32 devices in a mesh: stars: 8 (over z, x), seg: 4 (over y, core).
Axes of the slice: x: 2, y: 2, z: 4, core: 2. Of those that a mesh axis runs over, the one named last changes fastest.
Arguments:
- obs_star: int32 [4096, 128], P(('stars', 'seg')), may hold values from 0 to 8191
- obs_knot: int32 [4096, 128], P(('stars', 'seg')), may hold values from 0 to 8191
- obs_frac: float32 [4096, 128], P(('stars', 'seg')), may hold values from 0 to 1
- star_coef: float32 [5, 4096, 128], P(None, ('stars', 'seg')), may hold values from -6 to 6
- att_coef: float32 [4, 4096, 128], P(None, ('stars', 'seg')), may hold values from -3 to 3
- cal_coef: float32 [4096, 128], P(('stars', 'seg')), may hold values from -6 to 6
- tile_cal: int32 [4096], P(('stars', 'seg')), may hold values from 0 to 255
- live_tiles: int32 [32], P(('stars', 'seg')), may hold values from 1 to 128, as said below
- obs_value: float32 [4096, 128], P(('stars', 'seg')), may hold values from -8 to 8
Outputs:
- star_solution: float32 [5, 65536], P(None, 'stars')
- attitude_solution: float32 [4, 32768], P(None, 'seg')
- calibration_solution: float32 [1024, 128], P('seg')
- residual: float32 [4096, 128], P(('stars', 'seg'))
The draws below stay inside these ranges and needn't reach their ends.
Inputs may be any that keep to these rules, and one draw needn't show every extreme that they name: Entry d belongs to device d in the order of the stars axis, then seg; that device's first live_tiles[d] tile slots are live and the rest are padding; some device has all 128 slots live. `obs_knot`: knots past a segment's last knot are the next segment's first knots.
All inputs are finite; a program needn't handle non-finite values.
Results may differ from the reference program's by a relative error of at most 0.00017.
Values sent between devices are 32-bit elements; how exact they have to be, the bound alone decides.
No kernel may reach another device: no remote copies, remote signals or barrier semaphores. Data moves between devices by JAX's collectives and lax.ppermute only.
A program may use at most 128 MiB of HBM per device.

```python
import jax
import jax.numpy as jnp

STAR_DEV = 8192
KNOT_DEV = 8192
CALB_DEV = 256
TILE_DEV = 128
TILE_OBS = 128
ITERS = 2
NSTARS = 65536
NKNOTS = 32768
NCALB = 1024
NTILES = 4096
N_STARS = 8
N_SEG = 4
DEVICES = 32


def draw_live_tiles(key, part):
    load_key, jitter_key, chosen_key = jax.random.split(key, 3)
    seg_load = jax.random.randint(load_key, (N_SEG,), 1, 5)
    jitter = jax.random.randint(jitter_key, (DEVICES,), 0, TILE_DEV // 8 + 1)
    device = jnp.arange(DEVICES, dtype=jnp.int32)
    counts = jnp.maximum(TILE_DEV * seg_load[device % N_SEG] // 4 - jitter, 1)
    chosen = jax.random.randint(chosen_key, (), 0, DEVICES)
    return jnp.where(device == chosen, TILE_DEV, counts).astype(jnp.int32)


def draw_obs_value(key, part):
    noise_key = jax.random.fold_in(key, 0)
    rows = jnp.arange(NTILES, dtype=jnp.int32)
    block_pos = (rows // (TILE_DEV * N_SEG)).astype(jnp.float32)
    scale = 0.5 + 1.5 * block_pos / max(N_STARS - 1, 1)
    noise = jnp.clip(jax.random.normal(noise_key, (NTILES, TILE_OBS), jnp.float32), -4.0, 4.0)
    return (noise * scale[:, None]).astype(jnp.float32)


def set_ends(array, rng, low, high):
    spot = [jax.random.randint(jax.random.fold_in(rng, axis), (), 0, length) for axis, length in enumerate(array.shape)]
    widest = array.shape.index(max(array.shape))
    neighbour = spot[:widest] + [(spot[widest] + 1) % array.shape[widest]] + spot[widest + 1:]
    return array.at[tuple(spot)].set(low).at[tuple(neighbour)].set(high)


def level_of(stream_key, dims, cuts, smallest, high):
    loudness, own = 1.0, jax.random.fold_in(stream_key, 6)
    for position, shards_of in cuts:
        heights = jnp.exp(jax.random.uniform(jax.random.fold_in(own, position), (shards_of,), jnp.float32, smallest / len(cuts), high / len(cuts)))
        loudness = loudness * jnp.repeat(heights, dims[position] // shards_of).reshape([-1 if axis == position else 1 for axis in range(len(dims))])
    return loudness


def normal_values(key, dims, scale, limit, cuts=(), kind=jnp.bfloat16):
    values = scale * jax.random.normal(key, dims, jnp.float32)
    if cuts:
        values = values * level_of(key, dims, cuts, -0.22, 0.18)
    return jnp.clip(values, -limit, limit).astype(kind)


def setup_inputs(seed: int = 0) -> dict:
    key_of = jax.random.split(jax.random.key(seed), 10)
    return {
        "obs_star": set_ends(jax.random.randint(key_of[0], (NTILES, TILE_OBS), 0, STAR_DEV), jax.random.fold_in(key_of[0], 1), 0, STAR_DEV - 1).astype(jnp.int32),
        "obs_knot": set_ends(jax.random.randint(key_of[1], (NTILES, TILE_OBS), 0, KNOT_DEV), jax.random.fold_in(key_of[1], 1), 0, KNOT_DEV - 1).astype(jnp.int32),
        "obs_frac": jnp.clip(1.0 * jax.random.uniform(key_of[2], (NTILES, TILE_OBS), jnp.float32) ** level_of(key_of[2], (NTILES, TILE_OBS), ((0, 32),), -0.2, 0.2), 0.0, 1.0),
        "star_coef": normal_values(key_of[3], (5, NTILES, TILE_OBS), 1.0, 6.0, ((1, 32),), jnp.float32),
        "att_coef": normal_values(key_of[4], (4, NTILES, TILE_OBS), 0.5, 3.0, ((1, 32),), jnp.float32),
        "cal_coef": normal_values(key_of[5], (NTILES, TILE_OBS), 1.0, 6.0, ((0, 32),), jnp.float32),
        "tile_cal": set_ends(jax.random.randint(key_of[6], (NTILES,), 0, CALB_DEV), jax.random.fold_in(key_of[6], 1), 0, CALB_DEV - 1).astype(jnp.int32),
        "live_tiles": draw_live_tiles(jax.random.fold_in(key_of[9], 71), 0),
        "obs_value": draw_obs_value(jax.random.fold_in(key_of[9], 71), 0),
    }


def spline_weights(fraction):
    remain = 1.0 - fraction
    square = fraction * fraction
    cubed = square * fraction
    return (remain * remain * remain / 6.0,
            (3.0 * cubed - 6.0 * square + 4.0) / 6.0,
            (-3.0 * cubed + 3.0 * square + 3.0 * fraction + 1.0) / 6.0,
            cubed / 6.0)


def reference(obs_star, obs_knot, obs_frac, star_coef, att_coef, cal_coef, tile_cal, live_tiles, obs_value):
    tile_ids = jnp.arange(NTILES, dtype=jnp.int32)
    device = tile_ids // TILE_DEV
    block_ids = device // N_SEG
    segment = device % N_SEG
    live_mask = ((tile_ids % TILE_DEV) < live_tiles[device]).astype(jnp.float32)[:, None]
    star_ids = obs_star + (block_ids * STAR_DEV)[:, None]
    knot_ids = obs_knot + (segment * KNOT_DEV)[:, None]
    cal_rows = tile_cal + segment * CALB_DEV
    weights = spline_weights(obs_frac)

    def forward(star_x, att_x, cal_x):
        padded = jnp.concatenate([att_x, jnp.zeros((4, 3), jnp.float32)], axis=1)
        result = jnp.zeros((NTILES, TILE_OBS), jnp.float32)
        for comp in range(5):
            result = result + star_coef[comp] * star_x[comp][star_ids]
        for offset in range(4):
            for comp in range(4):
                result = result + weights[offset] * att_coef[comp] * padded[comp][knot_ids + offset]
        result = result + cal_coef * cal_x[cal_rows]
        return result * live_mask

    def backward(values):
        masked = values * live_mask
        flat_stars = star_ids.ravel()
        star_grad = jnp.stack([jax.ops.segment_sum((star_coef[comp] * masked).ravel(), flat_stars, num_segments=NSTARS) for comp in range(5)])
        att_rows = []
        for comp in range(4):
            acc = jnp.zeros((NKNOTS + 3,), jnp.float32)
            for offset in range(4):
                acc = acc + jax.ops.segment_sum((att_coef[comp] * weights[offset] * masked).ravel(), (knot_ids + offset).ravel(), num_segments=NKNOTS + 3)
            att_rows.append(acc[:NKNOTS])
        att_grad = jnp.stack(att_rows)
        cal_grad = jax.ops.segment_sum(cal_coef * masked, cal_rows, num_segments=NCALB)
        return (star_grad, att_grad, cal_grad)

    def squares(parts):
        return sum(jnp.sum(piece * piece) for piece in parts)

    residual = obs_value * live_mask
    gradient = backward(residual)
    grad_norm = squares(gradient)
    direction = gradient
    solution = tuple(jnp.zeros_like(piece) for piece in gradient)
    for iteration in range(ITERS):
        image = forward(*direction)
        step_size = grad_norm / jnp.sum(image * image)
        solution = tuple(current + step_size * moving for current, moving in zip(solution, direction))
        residual = residual - step_size * image
        gradient = backward(residual)
        new_norm = squares(gradient)
        direction = tuple(fresh + (new_norm / grad_norm) * moving for fresh, moving in zip(gradient, direction))
        grad_norm = new_norm
    return (solution[0], solution[1], solution[2], residual)
```

```python
import functools

import jax
import jax.numpy as jnp
from jax import lax
from jax.experimental import pallas as pl
from jax.experimental.pallas import tpu as pltpu
from jax.sharding import PartitionSpec as P

STAR_DEV = 8192
KNOT_DEV = 8192
CALB_DEV = 256
FINE = 32
COARSE = 256
GROUP = 8
STAR_ROWS = 5 * FINE
KNOT_ROWS = 4 * FINE
TABLE_ROWS = KNOT_ROWS + CALB_DEV // 2
BF16 = jnp.bfloat16
F32 = jnp.float32
SCALAR_LANE = 64


def two_parts(values):
    high = values.astype(BF16)
    return high, (values - high.astype(F32)).astype(BF16)


def rows_and_columns(shape):
    return lax.broadcasted_iota(jnp.int32, shape, 0), lax.broadcasted_iota(jnp.int32, shape, 1)


def one_hot(index_row, size):
    rows, _ = rows_and_columns((size, index_row.shape[1]))
    return jnp.where(rows == index_row, 1.0, 0.0).astype(BF16)


def spline_weights(fraction):
    remain = 1.0 - fraction
    square = fraction * fraction
    cubed = square * fraction
    return (
        remain * remain * remain / 6.0,
        (3.0 * cubed - 6.0 * square + 4.0) / 6.0,
        (-3.0 * cubed + 3.0 * square + 3.0 * fraction + 1.0) / 6.0,
        cubed / 6.0,
    )


def weight_columns(weights, fine, tile):
    rows, _ = rows_and_columns((FINE + 8, weights[0].shape[1]))
    behind = rows - fine[tile : tile + 1]
    result = jnp.zeros(behind.shape, F32)
    for offset in range(4):
        result = jnp.where(behind == offset, weights[offset][tile : tile + 1], result)
    return result


def product(left, right, contract):
    return lax.dot_general(left, right, (contract, ((), ())), preferred_element_type=F32)


def live_mask(live_ref, first, shape):
    rows, _ = rows_and_columns(shape)
    return (rows + first < live_ref[0]).astype(F32)


def backward_kernel(
    live_ref, star_ref, knot_ref, frac_ref, star_coef_ref, att_coef_ref, cal_coef_ref, tile_cal_ref,
    value_ref, scalar_ref, star_out, table_out, edge_out, star_acc, knot_acc,
):
    star_acc[...] = jnp.zeros_like(star_acc)
    knot_acc[...] = jnp.zeros_like(knot_acc)

    @pl.loop(0, star_ref.shape[0] // GROUP)
    def _(group):
        first = pl.multiple_of(group * GROUP, GROUP)
        rows = pl.ds(first, GROUP)
        star, knot = star_ref[rows, :], knot_ref[rows, :]
        values = value_ref[rows, :]
        values = values * live_mask(live_ref, first, values.shape)
        star_coarse, star_fine = star & (COARSE - 1), star >> 8
        knot_coarse, knot_fine = knot >> 5, knot & (FINE - 1)
        weights = spline_weights(frac_ref[rows, :])
        star_terms = [star_coef_ref[comp, rows, :] * values for comp in range(5)]
        knot_terms = [att_coef_ref[comp, rows, :] * values for comp in range(4)]
        star_parts = [two_parts(term) for term in star_terms]
        star_parts = [parts[half].astype(F32) for half in range(2) for parts in star_parts]
        star_left, star_right, knot_left, knot_right = [], [], [], []
        fine_rows, _ = rows_and_columns((FINE, star.shape[1]))
        for tile in range(GROUP):
            here = slice(tile, tile + 1)
            star_right.append(one_hot(star_coarse[here], COARSE))
            knot_right.append(one_hot(knot_coarse[here], COARSE))
            chosen = fine_rows == star_fine[here]
            star_left.append(
                jnp.concatenate(
                    [jnp.where(chosen, part[here], 0.0) for part in star_parts], axis=0
                ).astype(BF16)
            )
            columns = weight_columns(weights, knot_fine, tile)
            spread = jnp.concatenate(
                [term[here] * columns[:FINE] for term in knot_terms]
                + [term[here] * columns[FINE:] for term in knot_terms],
                axis=0,
            )
            knot_left.append(jnp.concatenate(two_parts(spread), axis=0))
        star_acc[...] += product(
            jnp.concatenate(star_left, axis=1), jnp.concatenate(star_right, axis=1), ((1,), (1,))
        )
        knot_acc[...] += product(
            jnp.concatenate(knot_left, axis=1), jnp.concatenate(knot_right, axis=1), ((1,), (1,))
        )

    star_out[...] = star_acc[:STAR_ROWS] + star_acc[STAR_ROWS:]

    half = KNOT_ROWS + 32
    lane = lax.broadcasted_iota(jnp.int32, (8, 128), 1)
    row = lax.broadcasted_iota(jnp.int32, (8, 128), 0)
    wide_lane = lax.broadcasted_iota(jnp.int32, (8, COARSE), 1)
    edges = scalar_ref[...]
    for comp in range(4):
        main = knot_acc[comp * FINE : (comp + 1) * FINE] + knot_acc[half + comp * FINE : half + (comp + 1) * FINE]
        past = KNOT_ROWS + comp * 8
        beyond = knot_acc[past : past + 8] + knot_acc[half + past : half + past + 8]
        moved = pltpu.roll(beyond, 1, 1)
        top = main[:8] + jnp.where(wide_lane > 0, moved, 0.0)
        table_out[comp * FINE : comp * FINE + 8, :] = top
        table_out[comp * FINE + 8 : (comp + 1) * FINE, :] = main[8:]
        tail, head = moved[:, :128], top[:, :128]
        if comp:
            tail = pltpu.roll(tail, 2 * comp, 1)
        head = pltpu.roll(head, 2 * comp + 1, 1)
        edges = jnp.where((lane == 2 * comp) & (row < 3), tail, edges)
        edges = jnp.where((lane == 2 * comp + 1) & (row < 3), head, edges)
    edge_out[...] = edges

    values = value_ref[...]
    values = values * live_mask(live_ref, 0, values.shape) * cal_coef_ref[...]
    blocks = product(
        one_hot(tile_cal_ref[...], CALB_DEV), jnp.concatenate(two_parts(values), axis=1), ((1,), (0,))
    )
    width = values.shape[1]
    blocks = blocks[:, :width] + blocks[:, width:]
    table_out[KNOT_ROWS:, :] = jnp.concatenate(
        [blocks[: CALB_DEV // 2], blocks[CALB_DEV // 2 :]], axis=1
    )


def forward_kernel(
    n_stars, n_seg, later, live_ref, place_ref, star_ref, knot_ref, frac_ref, star_coef_ref,
    att_coef_ref, cal_coef_ref, tile_cal_ref, other_ref, star_x_ref, table_x_ref, edges_ref, *refs,
):
    if later:
        star_0_ref, table_0_ref, ahead_0_ref, image_ref, star_out, table_out, scalar_out = refs[:7]
    else:
        image_ref, table_out, ahead_out, scalar_out = refs[:4]
    star_parts_ref, knot_parts_ref, cal_ref = refs[-3:]
    segment = place_ref[0]
    lane = lax.broadcasted_iota(jnp.int32, (8, 128), 1)
    row = lax.broadcasted_iota(jnp.int32, (8, 128), 0)
    wide_lane = lax.broadcasted_iota(jnp.int32, (8, COARSE), 1)

    before, own, after, everyone = [jnp.zeros((8, 128), F32) for _ in range(4)]
    for block in range(n_stars):
        start = block * n_seg
        before += edges_ref[start + jnp.maximum(segment - 1, 0)]
        own += edges_ref[start + segment]
        after += edges_ref[start + jnp.minimum(segment + 1, n_seg - 1)]
        if later:
            for other in range(n_seg):
                everyone += edges_ref[start + other]
    before = jnp.where(segment > 0, before, 0.0)
    ahead = jnp.where(lane % 2 == 0, own, 0.0) + pltpu.roll(jnp.where(lane % 2 == 1, after, 0.0), 127, 1)
    ahead = jnp.where((segment < n_seg - 1) & (lane < 8) & (row < 3), ahead, 0.0)

    table = table_x_ref[...]
    for comp in range(4):
        shifted = pltpu.roll(before, 128 - 2 * comp, 1) if comp else before
        shifted = jnp.where((lane == 0) & (row < 3), shifted, 0.0)
        top = table[comp * FINE : comp * FINE + 8]
        top = top + jnp.concatenate([shifted, jnp.zeros_like(shifted)], axis=1)
        table_out[comp * FINE : comp * FINE + 8, :] = top
        table_out[comp * FINE + 8 : (comp + 1) * FINE, :] = table[comp * FINE + 8 : (comp + 1) * FINE]
    table_out[KNOT_ROWS:, :] = table[KNOT_ROWS:]
    star_x = star_x_ref[...]
    if later:
        def total(which):
            return jnp.sum(jnp.where((row == 0) & (lane == SCALAR_LANE + which), everyone, 0.0), keepdims=True)

        step = total(0) / total(1)
        star_x = star_0_ref[...] - step * star_x
        star_out[...] = star_x
        table_out[...] = table_0_ref[...] - step * table_out[...]
        ahead = ahead_0_ref[...] - step * ahead
    else:
        ahead_out[...] = ahead
    table = table_out[...]
    norm = jnp.sum(star_x * star_x, keepdims=True) / n_seg + jnp.sum(table * table, keepdims=True) / n_stars

    star_high, star_low = two_parts(star_x)
    star_parts_ref[:STAR_ROWS] = star_high
    star_parts_ref[STAR_ROWS:] = star_low
    beyond = []
    for comp in range(4):
        moved = pltpu.roll(table[comp * FINE : comp * FINE + 8], COARSE - 1, 1)
        last = pltpu.roll(ahead, 127 - 2 * comp, 1)
        beyond.append(jnp.where(wide_lane == COARSE - 1, jnp.concatenate([last, last], axis=1), moved))
    knot_high, knot_low = two_parts(jnp.concatenate([table[:KNOT_ROWS]] + beyond, axis=0))
    half = KNOT_ROWS + 32
    knot_parts_ref[:half] = knot_high
    knot_parts_ref[half:] = knot_low

    blocks = jnp.concatenate([table[KNOT_ROWS:, :128], table[KNOT_ROWS:, 128:]], axis=0)
    rows = product(
        one_hot(tile_cal_ref[...], CALB_DEV), jnp.concatenate(two_parts(blocks), axis=1), ((0,), (0,))
    )
    cal_ref[...] = (rows[:, :128] + rows[:, 128:]) * cal_coef_ref[...]

    def one_group(group, sums):
        first = pl.multiple_of(group * GROUP, GROUP)
        rows = pl.ds(first, GROUP)
        star, knot = star_ref[rows, :], knot_ref[rows, :]
        star_coarse, star_fine = star & (COARSE - 1), star >> 8
        knot_coarse, knot_fine = knot >> 5, knot & (FINE - 1)
        weights = spline_weights(frac_ref[rows, :])
        star_coef = [star_coef_ref[comp, rows, :] for comp in range(5)]
        att_coef = [att_coef_ref[comp, rows, :] for comp in range(4)]
        tiles = [slice(tile, tile + 1) for tile in range(GROUP)]
        star_hot = jnp.concatenate([one_hot(star_coarse[here], COARSE) for here in tiles], axis=1)
        knot_hot = jnp.concatenate([one_hot(knot_coarse[here], COARSE) for here in tiles], axis=1)
        star_found = product(star_parts_ref[...], star_hot, ((1,), (0,)))
        knot_found = product(knot_parts_ref[...], knot_hot, ((1,), (0,)))
        width = star.shape[1]
        fine_rows, _ = rows_and_columns((FINE, width))
        image_rows = []
        for tile, here in enumerate(tiles):
            across = slice(tile * width, (tile + 1) * width)

            def star_part(comp):
                begin = comp * FINE
                return (
                    star_found[begin : begin + FINE, across]
                    + star_found[STAR_ROWS + begin : STAR_ROWS + begin + FINE, across]
                )

            def knot_part(begin, size):
                return (
                    knot_found[begin : begin + size, across]
                    + knot_found[half + begin : half + begin + size, across]
                )

            star_sum = sum(star_coef[comp][here] * star_part(comp) for comp in range(5))
            star_sum = jnp.where(fine_rows == star_fine[here], star_sum, 0.0)
            columns = weight_columns(weights, knot_fine, tile)
            main = sum(att_coef[comp][here] * knot_part(comp * FINE, FINE) for comp in range(4))
            past = sum(att_coef[comp][here] * knot_part(KNOT_ROWS + comp * 8, 8) for comp in range(4))
            both = star_sum + main * columns[:FINE]
            both = both[:8] + both[8:16] + both[16:24] + both[24:] + past * columns[FINE:]
            image_rows.append(jnp.sum(both, axis=0, keepdims=True))
        image = jnp.concatenate(image_rows, axis=0) + cal_ref[rows, :]
        image = image * live_mask(live_ref, first, image.shape)
        image_ref[rows, :] = image
        if later:
            return sums[0] + image * image, sums[1] + image * other_ref[rows, :]
        return (sums[0] + image * image,)

    zero = jnp.zeros((GROUP, star_ref.shape[1]), F32)
    sums = lax.fori_loop(0, star_ref.shape[0] // GROUP, one_group, (zero, zero) if later else (zero,))
    result = jnp.where((row == 0) & (lane == SCALAR_LANE), norm, 0.0)
    for which, part in enumerate(sums):
        result = jnp.where(
            (row == 0) & (lane == SCALAR_LANE + 1 + which), jnp.sum(part, keepdims=True), result
        )
    scalar_out[...] = result


def in_vmem(count):
    return [pl.BlockSpec(memory_space=pltpu.VMEM)] * count


def in_smem(count):
    return [pl.BlockSpec(memory_space=pltpu.SMEM)] * count


def table_shape(*shape, kind=F32):
    return jax.ShapeDtypeStruct(shape, kind)


PARAMS = pltpu.CompilerParams(vmem_limit_bytes=48 * 1024 * 1024)


def on_device(
    obs_star, obs_knot, obs_frac, star_coef, att_coef, cal_coef, tile_cal, live_tiles, obs_value
):
    n_stars, n_seg = lax.axis_size("stars"), lax.axis_size("seg")
    tile_count, width = obs_star.shape
    tile_row = tile_cal[None, :]
    place = lax.axis_index("seg").astype(jnp.int32)[None]
    observed = (obs_star, obs_knot, obs_frac, star_coef, att_coef, cal_coef, tile_row)
    half = KNOT_ROWS + 32

    def backward(values, scalars):
        return pl.pallas_call(
            backward_kernel,
            out_shape=(
                table_shape(STAR_ROWS, COARSE),
                table_shape(TABLE_ROWS, COARSE),
                table_shape(8, 128),
            ),
            in_specs=in_smem(1) + in_vmem(9),
            out_specs=tuple(in_vmem(3)),
            scratch_shapes=[
                pltpu.VMEM((2 * STAR_ROWS, COARSE), F32),
                pltpu.VMEM((2 * half, COARSE), F32),
            ],
            compiler_params=PARAMS,
            name="backward",
        )(live_tiles, *observed, values, scalars)

    def forward(later, other, *tables):
        image = table_shape(tile_count, width)
        if later:
            outs = (image, table_shape(STAR_ROWS, COARSE), table_shape(TABLE_ROWS, COARSE), table_shape(8, 128))
        else:
            outs = (image, table_shape(TABLE_ROWS, COARSE), table_shape(8, 128), table_shape(8, 128))
        return pl.pallas_call(
            functools.partial(forward_kernel, n_stars, n_seg, later),
            out_shape=outs,
            in_specs=in_smem(2) + in_vmem(8 + len(tables)),
            out_specs=tuple(in_vmem(len(outs))),
            scratch_shapes=[
                pltpu.VMEM((2 * STAR_ROWS, COARSE), BF16),
                pltpu.VMEM((2 * half, COARSE), BF16),
                pltpu.VMEM((tile_count, width), F32),
            ],
            compiler_params=PARAMS,
            name="forward",
        )(live_tiles, place, *observed, other, *tables)

    def swap(blocks, axes):
        return lax.all_to_all(blocks, axes, 0, 0)

    def all_sum(array, axis, count):
        rows, columns = array.shape
        blocks = swap(array.reshape(count, rows // count, columns), axis)
        part = jnp.sum(blocks, axis=0)
        return swap(jnp.broadcast_to(part[None], blocks.shape), axis).reshape(rows, columns)

    def everyones(array):
        count = n_stars * n_seg
        return swap(jnp.broadcast_to(array[None], (count, *array.shape)), ("stars", "seg"))

    def reduced(parts):
        star, table, edges = parts
        return all_sum(star, "seg", n_seg), all_sum(table, "stars", n_stars), everyones(edges)

    mask = (jnp.arange(tile_count, dtype=jnp.int32) < live_tiles[0]).astype(F32)[:, None]
    residual = obs_value * mask
    star_0, table_0, edges_0 = reduced(backward(obs_value, jnp.zeros((8, 128), F32)))
    image_0, table_0, ahead_0, scalars_0 = forward(False, obs_value, star_0, table_0, edges_0)
    star_h, table_h, edges_h = reduced(backward(image_0, scalars_0))
    image_1, star_1, table_1, scalars_1 = forward(
        True, image_0, star_h, table_h, edges_h, star_0, table_0, ahead_0
    )
    first = jnp.sum(edges_h[:, 0, SCALAR_LANE : SCALAR_LANE + 2], axis=0)
    second = jnp.sum(everyones(scalars_1)[:, 0, SCALAR_LANE : SCALAR_LANE + 3], axis=0)
    norm_0, square_0 = first[0], first[1]
    norm_1, square_1, cross = second[0], second[1], second[2]
    step_0 = norm_0 / square_0
    ratio = norm_1 / norm_0
    step_1 = norm_1 / (square_1 + 2.0 * ratio * cross + ratio * ratio * square_0)

    def combined(old, new):
        return (step_0 + step_1 * ratio) * old + step_1 * new

    star = combined(star_0, star_1).reshape(5, STAR_DEV)
    att = combined(table_0[:KNOT_ROWS], table_1[:KNOT_ROWS])
    att = att.reshape(4, FINE, COARSE).transpose(0, 2, 1).reshape(4, KNOT_DEV)
    cal = combined(table_0[KNOT_ROWS:], table_1[KNOT_ROWS:])
    cal = cal.reshape(CALB_DEV // 2, 2, width).transpose(1, 0, 2).reshape(CALB_DEV, width)
    return (star, att, cal, residual - combined(image_0, image_1))


def solution(mesh):
    placed = (
        P(("stars", "seg"), None),
        P(("stars", "seg"), None),
        P(("stars", "seg"), None),
        P(None, ("stars", "seg"), None),
        P(None, ("stars", "seg"), None),
        P(("stars", "seg"), None),
        P(("stars", "seg")),
        P(("stars", "seg")),
        P(("stars", "seg"), None),
    )
    return jax.shard_map(
        on_device,
        mesh=mesh,
        in_specs=placed,
        out_specs=(P(None, "stars"), P(None, "seg"), P("seg", None), P(("stars", "seg"), None)),
        check_vma=False,
    )
```

```python
import functools

import jax
import jax.numpy as jnp
from jax import lax
from jax.experimental import pallas as pl
from jax.experimental.pallas import tpu as pltpu
from jax.sharding import PartitionSpec as P

STAR_DEV = 8192
KNOT_DEV = 8192
CALB_DEV = 256
FINE = 32
COARSE = 256
GROUP = 8
STAR_ROWS = 5 * FINE
KNOT_ROWS = 4 * FINE
TABLE_ROWS = KNOT_ROWS + CALB_DEV // 2
BF16 = jnp.bfloat16
F32 = jnp.float32
SCALAR_LANE = 64
KNOT_HALF = KNOT_ROWS + 32


def two_parts(values):
    high = values.astype(BF16)
    return high, (values - high.astype(F32)).astype(BF16)


def rows_and_columns(shape):
    return lax.broadcasted_iota(jnp.int32, shape, 0), lax.broadcasted_iota(jnp.int32, shape, 1)


def one_hot(index_row, size):
    rows, _ = rows_and_columns((size, index_row.shape[1]))
    return jnp.where(rows == index_row, 1.0, 0.0).astype(BF16)


def spline_weights(fraction):
    remain = 1.0 - fraction
    square = fraction * fraction
    cubed = square * fraction
    return (
        remain * remain * remain / 6.0,
        (3.0 * cubed - 6.0 * square + 4.0) / 6.0,
        (-3.0 * cubed + 3.0 * square + 3.0 * fraction + 1.0) / 6.0,
        cubed / 6.0,
    )


def weight_columns(weights, fine, tile):
    rows, _ = rows_and_columns((FINE + 8, weights[0].shape[1]))
    behind = rows - fine[tile : tile + 1]
    result = jnp.zeros(behind.shape, F32)
    for offset in range(4):
        result = jnp.where(behind == offset, weights[offset][tile : tile + 1], result)
    return result


def product(left, right, contract):
    return lax.dot_general(left, right, (contract, ((), ())), preferred_element_type=F32)


def live_mask(live_ref, first, shape):
    rows, _ = rows_and_columns(shape)
    return (rows + first < live_ref[0]).astype(F32)


def knot_backward_kernel(arrive, live_ref, *refs):
    observed, (scalar_ref, table_out, edge_out, knot_acc) = refs[:6], refs[6:10]
    if arrive:
        buffers, sems = refs[10:16], refs[16]
        copies = [
            pltpu.make_async_copy(source, target, sems.at[which])
            for which, (source, target) in enumerate(zip(observed, buffers))
        ]
        for copy in copies:
            copy.start()
        observed = buffers
    knot_ref, frac_ref, att_coef_ref, value_ref, cal_coef_ref, tile_cal_ref = observed
    knot_acc[...] = jnp.zeros_like(knot_acc)
    if arrive:
        for copy in copies:
            copy.wait()

    @pl.loop(0, knot_ref.shape[0] // GROUP)
    def _(group):
        first = pl.multiple_of(group * GROUP, GROUP)
        rows = pl.ds(first, GROUP)
        knot = knot_ref[rows, :]
        values = value_ref[rows, :]
        values = values * live_mask(live_ref, first, values.shape)
        coarse, fine = knot >> 5, knot & (FINE - 1)
        weights = spline_weights(frac_ref[rows, :])
        terms = [att_coef_ref[comp, rows, :] * values for comp in range(4)]
        left, right = [], []
        for tile in range(GROUP):
            here = slice(tile, tile + 1)
            right.append(one_hot(coarse[here], COARSE))
            columns = weight_columns(weights, fine, tile)
            spread = jnp.concatenate(
                [term[here] * columns[:FINE] for term in terms]
                + [term[here] * columns[FINE:] for term in terms],
                axis=0,
            )
            left.append(jnp.concatenate(two_parts(spread), axis=0))
        knot_acc[...] += product(
            jnp.concatenate(left, axis=1), jnp.concatenate(right, axis=1), ((1,), (1,))
        )

    lane = lax.broadcasted_iota(jnp.int32, (8, 128), 1)
    row = lax.broadcasted_iota(jnp.int32, (8, 128), 0)
    wide_lane = lax.broadcasted_iota(jnp.int32, (8, COARSE), 1)
    edges = scalar_ref[...]
    for comp in range(4):
        begin, past = comp * FINE, KNOT_ROWS + comp * 8
        main = knot_acc[begin : begin + FINE] + knot_acc[KNOT_HALF + begin : KNOT_HALF + begin + FINE]
        beyond = knot_acc[past : past + 8] + knot_acc[KNOT_HALF + past : KNOT_HALF + past + 8]
        moved = pltpu.roll(beyond, 1, 1)
        top = main[:8] + jnp.where(wide_lane > 0, moved, 0.0)
        table_out[begin : begin + 8, :] = top
        table_out[begin + 8 : begin + FINE, :] = main[8:]
        tail, head = moved[:, :128], top[:, :128]
        if comp:
            tail = pltpu.roll(tail, 2 * comp, 1)
        head = pltpu.roll(head, 2 * comp + 1, 1)
        edges = jnp.where((lane == 2 * comp) & (row < 3), tail, edges)
        edges = jnp.where((lane == 2 * comp + 1) & (row < 3), head, edges)
    for device in range(edge_out.shape[0]):
        edge_out[device] = edges

    values = value_ref[...]
    values = values * live_mask(live_ref, 0, values.shape) * cal_coef_ref[...]
    blocks = product(
        one_hot(tile_cal_ref[...], CALB_DEV), jnp.concatenate(two_parts(values), axis=1), ((1,), (0,))
    )
    width = values.shape[1]
    blocks = blocks[:, :width] + blocks[:, width:]
    table_out[KNOT_ROWS:, :] = jnp.concatenate(
        [blocks[: CALB_DEV // 2], blocks[CALB_DEV // 2 :]], axis=1
    )


def star_backward_kernel(live_ref, star_ref, star_coef_ref, value_ref, after_ref, star_out, star_acc):
    star_acc[...] = jnp.zeros_like(star_acc)

    @pl.loop(0, star_ref.shape[0] // GROUP)
    def _(group):
        first = pl.multiple_of(group * GROUP, GROUP)
        rows = pl.ds(first, GROUP)
        star = star_ref[rows, :]
        values = value_ref[rows, :]
        values = values * live_mask(live_ref, first, values.shape)
        coarse, fine = star & (COARSE - 1), star >> 8
        parts = [two_parts(star_coef_ref[comp, rows, :] * values) for comp in range(5)]
        parts = [pair[half].astype(F32) for half in range(2) for pair in parts]
        left, right = [], []
        fine_rows, _ = rows_and_columns((FINE, star.shape[1]))
        for tile in range(GROUP):
            here = slice(tile, tile + 1)
            right.append(one_hot(coarse[here], COARSE))
            chosen = fine_rows == fine[here]
            left.append(
                jnp.concatenate([jnp.where(chosen, part[here], 0.0) for part in parts], axis=0).astype(BF16)
            )
        star_acc[...] += product(
            jnp.concatenate(left, axis=1), jnp.concatenate(right, axis=1), ((1,), (1,))
        )

    star_out[...] = star_acc[:STAR_ROWS] + star_acc[STAR_ROWS:]


def sum_kernel(block_ref, out_ref):
    total = block_ref[0]
    for device in range(1, block_ref.shape[0]):
        total = total + block_ref[device]
    for device in range(block_ref.shape[0]):
        out_ref[device] = total


def picked(array, which):
    row = lax.broadcasted_iota(jnp.int32, array.shape, 0)
    lane = lax.broadcasted_iota(jnp.int32, array.shape, 1)
    chosen = (row == 0) & (lane == SCALAR_LANE + which)
    return jnp.sum(jnp.where(chosen, array, 0.0), keepdims=True)


def with_scalars(array, scalars):
    row = lax.broadcasted_iota(jnp.int32, array.shape, 0)
    lane = lax.broadcasted_iota(jnp.int32, array.shape, 1)
    for which, value in scalars:
        array = jnp.where((row == 0) & (lane == SCALAR_LANE + which), value, array)
    return array


def over_devices(ref):
    total = ref[0]
    for device in range(1, ref.shape[0]):
        total = total + ref[device]
    return total


def first_step(edges_ref):
    everyone = over_devices(edges_ref)
    return picked(everyone, 0), picked(everyone, 1)


def star_forward_kernel(n_seg, later, star_ref, star_coef_ref, own_ref, other_ref, *refs):
    if later:
        edges_ref, star_0_ref = refs[:2]
    image_ref, star_out, scalar_out, star_parts_ref = refs[-4:]
    star_x = own_ref[...] + other_ref[...]
    if later:
        norm_0, square_0 = first_step(edges_ref)
        star_x = star_0_ref[...] - norm_0 / square_0 * star_x
    star_out[...] = star_x
    norm = jnp.sum(star_x * star_x, keepdims=True) / n_seg
    scalar_out[...] = with_scalars(jnp.zeros((8, 128), F32), [(0, norm)])
    star_high, star_low = two_parts(star_x)
    star_parts_ref[:STAR_ROWS] = star_high
    star_parts_ref[STAR_ROWS:] = star_low

    @pl.loop(0, star_ref.shape[0] // GROUP)
    def _(group):
        rows = pl.ds(pl.multiple_of(group * GROUP, GROUP), GROUP)
        star = star_ref[rows, :]
        coarse, fine = star & (COARSE - 1), star >> 8
        coef = [star_coef_ref[comp, rows, :] for comp in range(5)]
        tiles = [slice(tile, tile + 1) for tile in range(GROUP)]
        hot = jnp.concatenate([one_hot(coarse[here], COARSE) for here in tiles], axis=1)
        found = product(star_parts_ref[...], hot, ((1,), (0,)))
        width = star.shape[1]
        fine_rows, _ = rows_and_columns((FINE, width))
        image_rows = []
        for tile, here in enumerate(tiles):
            across = slice(tile * width, (tile + 1) * width)

            def part(comp):
                begin = comp * FINE
                return (
                    found[begin : begin + FINE, across]
                    + found[STAR_ROWS + begin : STAR_ROWS + begin + FINE, across]
                )

            both = sum(coef[comp][here] * part(comp) for comp in range(5))
            both = jnp.where(fine_rows == fine[here], both, 0.0)
            both = both[:8] + both[8:16] + both[16:24] + both[24:]
            image_rows.append(jnp.sum(both, axis=0, keepdims=True))
        image_ref[rows, :] = jnp.concatenate(image_rows, axis=0)


def knot_forward_kernel(
    n_stars, n_seg, later, live_ref, place_ref, knot_ref, frac_ref, att_coef_ref, cal_coef_ref,
    tile_cal_ref, star_image_ref, star_scalar_ref, table_x_ref, edges_ref, *refs,
):
    if later:
        table_0_ref, ahead_0_ref, image_0_ref, image_ref, table_out, scalar_out = refs[:6]
    else:
        image_ref, table_out, scalar_out, ahead_out = refs[:4]
    knot_parts_ref, cal_ref = refs[-2:]
    segment = place_ref[0]
    lane = lax.broadcasted_iota(jnp.int32, (8, 128), 1)
    row = lax.broadcasted_iota(jnp.int32, (8, 128), 0)
    wide_lane = lax.broadcasted_iota(jnp.int32, (8, COARSE), 1)

    before, own, after = [jnp.zeros((8, 128), F32) for _ in range(3)]
    for block in range(n_stars):
        start = block * n_seg
        before += edges_ref[start + jnp.maximum(segment - 1, 0)]
        own += edges_ref[start + segment]
        after += edges_ref[start + jnp.minimum(segment + 1, n_seg - 1)]
    before = jnp.where(segment > 0, before, 0.0)
    ahead = jnp.where(lane % 2 == 0, own, 0.0) + pltpu.roll(jnp.where(lane % 2 == 1, after, 0.0), 127, 1)
    ahead = jnp.where((segment < n_seg - 1) & (lane < 8) & (row < 3), ahead, 0.0)

    table = table_x_ref[...]
    pieces = []
    for comp in range(4):
        shifted = pltpu.roll(before, 128 - 2 * comp, 1) if comp else before
        shifted = jnp.where((lane == 0) & (row < 3), shifted, 0.0)
        top = table[comp * FINE : comp * FINE + 8]
        pieces.append(top + jnp.concatenate([shifted, jnp.zeros_like(shifted)], axis=1))
        pieces.append(table[comp * FINE + 8 : (comp + 1) * FINE])
    table = jnp.concatenate(pieces + [table[KNOT_ROWS:]], axis=0)
    if later:
        norm_0, square_0 = first_step(edges_ref)
        step = norm_0 / square_0
        table = table_0_ref[...] - step * table
        ahead = ahead_0_ref[...] - step * ahead
    else:
        ahead_out[...] = ahead
    table_out[...] = table
    norm = picked(star_scalar_ref[...], 0) + jnp.sum(table * table, keepdims=True) / n_stars

    beyond = []
    for comp in range(4):
        moved = pltpu.roll(table[comp * FINE : comp * FINE + 8], COARSE - 1, 1)
        last = pltpu.roll(ahead, 127 - 2 * comp, 1)
        beyond.append(jnp.where(wide_lane == COARSE - 1, jnp.concatenate([last, last], axis=1), moved))
    knot_high, knot_low = two_parts(jnp.concatenate([table[:KNOT_ROWS]] + beyond, axis=0))
    knot_parts_ref[:KNOT_HALF] = knot_high
    knot_parts_ref[KNOT_HALF:] = knot_low

    blocks = jnp.concatenate([table[KNOT_ROWS:, :128], table[KNOT_ROWS:, 128:]], axis=0)
    rows = product(
        one_hot(tile_cal_ref[...], CALB_DEV), jnp.concatenate(two_parts(blocks), axis=1), ((0,), (0,))
    )
    cal_ref[...] = (rows[:, :128] + rows[:, 128:]) * cal_coef_ref[...] + star_image_ref[...]

    def one_group(group, sums):
        first = pl.multiple_of(group * GROUP, GROUP)
        rows = pl.ds(first, GROUP)
        knot = knot_ref[rows, :]
        coarse, fine = knot >> 5, knot & (FINE - 1)
        weights = spline_weights(frac_ref[rows, :])
        coef = [att_coef_ref[comp, rows, :] for comp in range(4)]
        tiles = [slice(tile, tile + 1) for tile in range(GROUP)]
        hot = jnp.concatenate([one_hot(coarse[here], COARSE) for here in tiles], axis=1)
        found = product(knot_parts_ref[...], hot, ((1,), (0,)))
        width = knot.shape[1]
        image_rows = []
        for tile, here in enumerate(tiles):
            across = slice(tile * width, (tile + 1) * width)

            def part(begin, size):
                return (
                    found[begin : begin + size, across]
                    + found[KNOT_HALF + begin : KNOT_HALF + begin + size, across]
                )

            columns = weight_columns(weights, fine, tile)
            main = sum(coef[comp][here] * part(comp * FINE, FINE) for comp in range(4))
            past = sum(coef[comp][here] * part(KNOT_ROWS + comp * 8, 8) for comp in range(4))
            both = main * columns[:FINE]
            both = both[:8] + both[8:16] + both[16:24] + both[24:] + past * columns[FINE:]
            image_rows.append(jnp.sum(both, axis=0, keepdims=True))
        image = jnp.concatenate(image_rows, axis=0) + cal_ref[rows, :]
        image = image * live_mask(live_ref, first, image.shape)
        image_ref[rows, :] = image
        if later:
            return sums[0] + image * image, sums[1] + image * image_0_ref[rows, :]
        return (sums[0] + image * image,)

    zero = jnp.zeros((GROUP, knot_ref.shape[1]), F32)
    sums = lax.fori_loop(0, knot_ref.shape[0] // GROUP, one_group, (zero, zero) if later else (zero,))
    scalars = [(0, norm)] + [(1 + which, jnp.sum(part, keepdims=True)) for which, part in enumerate(sums)]
    result = with_scalars(jnp.zeros((8, 128), F32), scalars)
    for device in range(scalar_out.shape[0]):
        scalar_out[device] = result


def output_kernel(
    live_ref, edges_ref, scalar_ref, star_0_ref, star_1_ref, att_0_ref, att_1_ref, table_0_ref,
    table_1_ref, value_ref, image_0_ref, image_1_ref, star_out, att_out, cal_out, residual_out,
):
    norm_0, square_0 = first_step(edges_ref)
    everyone = over_devices(scalar_ref)
    norm_1, square_1, cross = [picked(everyone, which) for which in range(3)]
    ratio = norm_1 / norm_0
    step_1 = norm_1 / (square_1 + 2.0 * ratio * cross + ratio * ratio * square_0)
    scale = norm_0 / square_0 + step_1 * ratio

    def combined(old, new):
        return scale * old + step_1 * new

    star_out[...] = combined(star_0_ref[...], star_1_ref[...])
    att_out[...] = combined(att_0_ref[...], att_1_ref[...])
    cal = combined(table_0_ref[KNOT_ROWS:, :], table_1_ref[KNOT_ROWS:, :])
    cal_out[...] = jnp.concatenate([cal[:, :128], cal[:, 128:]], axis=0)
    values = value_ref[...] * live_mask(live_ref, 0, value_ref.shape)
    residual_out[...] = values - combined(image_0_ref[...], image_1_ref[...])


def in_vmem(count):
    return [pl.BlockSpec(memory_space=pltpu.VMEM)] * count


def in_smem(count):
    return [pl.BlockSpec(memory_space=pltpu.SMEM)] * count


def in_hbm(count):
    return [pl.BlockSpec(memory_space=pltpu.HBM)] * count


def shaped(*shape):
    return jax.ShapeDtypeStruct(shape, F32)


PARAMS = pltpu.CompilerParams(vmem_limit_bytes=40 * 1024 * 1024)
PASS_COST = pl.CostEstimate(flops=3_000_000_000, bytes_accessed=1_000_000, transcendentals=0)
SMALL_COST = pl.CostEstimate(flops=1_000_000, bytes_accessed=600_000, transcendentals=0)


def on_device(
    obs_star, obs_knot, obs_frac, star_coef, att_coef, cal_coef, tile_cal, live_tiles, obs_value
):
    n_stars, n_seg = lax.axis_size("stars"), lax.axis_size("seg")
    count = n_stars * n_seg
    tile_count, width = obs_star.shape
    tile_row = tile_cal[None, :]
    place = lax.axis_index("seg").astype(jnp.int32)[None]
    image_shape = shaped(tile_count, width)
    table_shape = shaped(TABLE_ROWS, COARSE)
    star_shape = shaped(STAR_ROWS, COARSE)
    scalar_shape, scalar_copies = shaped(8, 128), shaped(count, 8, 128)

    def knot_backward(values, scalars, arrive):
        observed = (obs_knot, obs_frac, att_coef, values, cal_coef, tile_row)
        scratch = [pltpu.VMEM((2 * KNOT_HALF, COARSE), F32)]
        if arrive:
            scratch += [pltpu.VMEM(array.shape, array.dtype) for array in observed]
            scratch += [pltpu.SemaphoreType.DMA((len(observed),))]
        return pl.pallas_call(
            functools.partial(knot_backward_kernel, arrive),
            out_shape=(table_shape, scalar_copies),
            in_specs=in_smem(1) + (in_hbm if arrive else in_vmem)(len(observed)) + in_vmem(1),
            out_specs=tuple(in_vmem(2)),
            scratch_shapes=scratch,
            compiler_params=PARAMS,
            cost_estimate=PASS_COST,
            name="knot_backward",
        )(live_tiles, *observed, scalars)

    def star_backward(values, after):
        return pl.pallas_call(
            star_backward_kernel,
            out_shape=star_shape,
            in_specs=in_smem(1) + in_vmem(3) + [pl.BlockSpec(memory_space=pl.ANY)],
            out_specs=in_vmem(1)[0],
            scratch_shapes=[pltpu.VMEM((2 * STAR_ROWS, COARSE), F32)],
            compiler_params=PARAMS,
            cost_estimate=PASS_COST,
            name="star_backward",
        )(live_tiles, obs_star, star_coef, values, after)

    def star_forward(own, other, *first):
        return pl.pallas_call(
            functools.partial(star_forward_kernel, n_seg, bool(first)),
            out_shape=(image_shape, star_shape, scalar_shape),
            in_specs=in_vmem(4 + len(first)),
            out_specs=tuple(in_vmem(3)),
            scratch_shapes=[pltpu.VMEM((2 * STAR_ROWS, COARSE), BF16)],
            compiler_params=PARAMS,
            cost_estimate=PASS_COST,
            name="star_forward",
        )(obs_star, star_coef, own, other, *first)

    def knot_forward(star_image, star_scalars, table, edges, *first):
        outs = (image_shape, table_shape) + ((scalar_copies,) if first else (shaped(1, 8, 128), scalar_shape))
        return pl.pallas_call(
            functools.partial(knot_forward_kernel, n_stars, n_seg, bool(first)),
            out_shape=outs,
            in_specs=in_smem(2) + in_vmem(9 + len(first)),
            out_specs=tuple(in_vmem(len(outs))),
            scratch_shapes=[
                pltpu.VMEM((2 * KNOT_HALF, COARSE), BF16),
                pltpu.VMEM((tile_count, width), F32),
            ],
            compiler_params=PARAMS,
            cost_estimate=PASS_COST,
            name="knot_forward",
        )(
            live_tiles, place, obs_knot, obs_frac, att_coef, cal_coef, tile_row, star_image,
            star_scalars, table, edges, *first,
        )

    def swap(blocks, axes):
        return lax.all_to_all(blocks, axes, 0, 0)

    def table_sum(table):
        blocks = swap(table.reshape(n_stars, TABLE_ROWS // n_stars, COARSE), "stars")
        copies = pl.pallas_call(
            sum_kernel,
            out_shape=shaped(*blocks.shape),
            in_specs=in_vmem(1),
            out_specs=in_vmem(1)[0],
            compiler_params=PARAMS,
            cost_estimate=SMALL_COST,
            name="table_sum",
        )(blocks)
        return swap(copies, "stars").reshape(TABLE_ROWS, COARSE)

    def star_terms(star):
        distance = 1
        while True:
            other = lax.ppermute(star, "seg", [(i, i ^ distance) for i in range(n_seg)])
            distance *= 2
            if distance >= n_seg:
                return star, other
            star = star + other

    def half(values, scalars, arrive):
        table, edges = knot_backward(values, scalars, arrive)
        star = star_backward(values, edges)
        return (*star_terms(star), table_sum(table), swap(edges, ("stars", "seg")))

    own, other, table, edges = half(obs_value, jnp.zeros((8, 128), F32), True)
    star_image, star_0, star_scalars = star_forward(own, other)
    image_0, table_0, scalars, ahead_0 = knot_forward(star_image, star_scalars, table, edges)
    own, other, table, edges = half(image_0, scalars[0], False)
    star_image, star_1, star_scalars = star_forward(own, other, edges, star_0)
    image_1, table_1, scalars = knot_forward(
        star_image, star_scalars, table, edges, table_0, ahead_0, image_0
    )

    def star_order(star):
        return star.reshape(5, STAR_DEV)

    def att_order(table):
        att = table[:KNOT_ROWS].reshape(4, FINE, COARSE)
        return att.transpose(0, 2, 1).reshape(4, KNOT_DEV)

    return pl.pallas_call(
        output_kernel,
        out_shape=(shaped(5, STAR_DEV), shaped(4, KNOT_DEV), shaped(CALB_DEV, width), image_shape),
        in_specs=in_smem(1) + in_vmem(11),
        out_specs=tuple(in_vmem(4)),
        compiler_params=PARAMS,
        cost_estimate=SMALL_COST,
        name="outputs",
    )(
        live_tiles, edges, swap(scalars, ("stars", "seg")), star_order(star_0), star_order(star_1),
        att_order(table_0), att_order(table_1), table_0, table_1, obs_value, image_0, image_1,
    )


def solution(mesh):
    placed = (
        P(("stars", "seg"), None),
        P(("stars", "seg"), None),
        P(("stars", "seg"), None),
        P(None, ("stars", "seg"), None),
        P(None, ("stars", "seg"), None),
        P(("stars", "seg"), None),
        P(("stars", "seg")),
        P(("stars", "seg")),
        P(("stars", "seg"), None),
    )
    return jax.shard_map(
        on_device,
        mesh=mesh,
        in_specs=placed,
        out_specs=(P(None, "stars"), P(None, "seg"), P("seg", None), P(("stars", "seg"), None)),
        check_vma=False,
    )
```

```python
import functools

import jax
import jax.numpy as jnp
from jax import lax
from jax.experimental import pallas as pl
from jax.experimental.pallas import tpu as pltpu
from jax.sharding import PartitionSpec as P

STAR_DEV = 8192
KNOT_DEV = 8192
CALB_DEV = 256
FINE = 32
COARSE = 256
GROUP = 8
WIDE_GROUP = 16
SLOT = 8
STAR_ROWS = 5 * FINE
KNOT_ROWS = 4 * FINE
TABLE_ROWS = KNOT_ROWS + CALB_DEV // 2
BF16 = jnp.bfloat16
F32 = jnp.float32
SCALAR_LANE = 64
KNOT_HALF = KNOT_ROWS + 32


def two_parts(values):
    high = values.astype(BF16)
    return high, (values - high.astype(F32)).astype(BF16)


def rows_and_columns(shape):
    return lax.broadcasted_iota(jnp.int32, shape, 0), lax.broadcasted_iota(jnp.int32, shape, 1)


def one_hot(index_row, size):
    rows, _ = rows_and_columns((size, index_row.shape[1]))
    return jnp.where(rows == index_row, 1.0, 0.0).astype(BF16)


def spline_weights(fraction):
    remain = 1.0 - fraction
    square = fraction * fraction
    cubed = square * fraction
    return (
        remain * remain * remain / 6.0,
        (3.0 * cubed - 6.0 * square + 4.0) / 6.0,
        (-3.0 * cubed + 3.0 * square + 3.0 * fraction + 1.0) / 6.0,
        cubed / 6.0,
    )


def weight_columns(weights, fine, tile):
    rows, _ = rows_and_columns((FINE + 8, weights[0].shape[1]))
    behind = rows - fine[tile : tile + 1]
    result = jnp.zeros(behind.shape, F32)
    for offset in range(4):
        result = jnp.where(behind == offset, weights[offset][tile : tile + 1], result)
    return result


def product(left, right, contract):
    return lax.dot_general(left, right, (contract, ((), ())), preferred_element_type=F32)


def live_mask(live_ref, first, shape):
    rows, _ = rows_and_columns(shape)
    return (rows + first < live_ref[0]).astype(F32)


def store_rows(out_ref, begin, rows):
    block = out_ref.shape[1] - 8
    for offset in range(0, rows.shape[0], 8):
        where = begin + offset
        out_ref[where // block, where % block : where % block + 8, :] = rows[offset : offset + 8]


def knot_backward_kernel(arrive, live_ref, place_ref, *refs):
    observed, (scalar_ref, table_out, knot_acc) = refs[:6], refs[6:9]
    if arrive:
        buffers, sems = refs[9:15], refs[15]
        copies = [
            pltpu.make_async_copy(source, target, sems.at[which])
            for which, (source, target) in enumerate(zip(observed, buffers))
        ]
        for copy in copies:
            copy.start()
        observed = buffers
    knot_ref, frac_ref, att_coef_ref, value_ref, cal_coef_ref, tile_cal_ref = observed
    knot_acc[...] = jnp.zeros_like(knot_acc)
    if arrive:
        for copy in copies:
            copy.wait()

    @pl.loop(0, knot_ref.shape[0] // WIDE_GROUP)
    def _(group):
        first = pl.multiple_of(group * WIDE_GROUP, WIDE_GROUP)
        rows = pl.ds(first, WIDE_GROUP)
        knot = knot_ref[rows, :]
        values = value_ref[rows, :]
        values = values * live_mask(live_ref, first, values.shape)
        coarse, fine = knot >> 5, knot & (FINE - 1)
        weights = spline_weights(frac_ref[rows, :])
        terms = [att_coef_ref[comp, rows, :] * values for comp in range(4)]
        left, right = [], []
        for tile in range(WIDE_GROUP):
            here = slice(tile, tile + 1)
            right.append(one_hot(coarse[here], COARSE))
            columns = weight_columns(weights, fine, tile)
            spread = jnp.concatenate(
                [term[here] * columns[:FINE] for term in terms]
                + [term[here] * columns[FINE:] for term in terms],
                axis=0,
            )
            left.append(jnp.concatenate(two_parts(spread), axis=0))
        knot_acc[...] += product(
            jnp.concatenate(left, axis=1), jnp.concatenate(right, axis=1), ((1,), (1,))
        )

    lane = lax.broadcasted_iota(jnp.int32, (8, 128), 1)
    row = lax.broadcasted_iota(jnp.int32, (8, 128), 0)
    wide_lane = lax.broadcasted_iota(jnp.int32, (8, COARSE), 1)
    edges = jnp.zeros((8, 128), F32)
    for comp in range(4):
        begin, past = comp * FINE, KNOT_ROWS + comp * 8
        main = knot_acc[begin : begin + FINE] + knot_acc[KNOT_HALF + begin : KNOT_HALF + begin + FINE]
        beyond = knot_acc[past : past + 8] + knot_acc[KNOT_HALF + past : KNOT_HALF + past + 8]
        moved = pltpu.roll(beyond, 1, 1)
        top = main[:8] + jnp.where(wide_lane > 0, moved, 0.0)
        store_rows(table_out, begin, top)
        store_rows(table_out, begin + 8, main[8:])
        tail, head = moved[:, :128], top[:, :128]
        if comp:
            tail = pltpu.roll(tail, 2 * comp, 1)
        head = pltpu.roll(head, 2 * comp + 1, 1)
        edges = jnp.where((lane == 2 * comp) & (row < 3), tail, edges)
        edges = jnp.where((lane == 2 * comp + 1) & (row < 3), head, edges)
    edges = scalar_ref[...] + pltpu.roll(edges, SLOT * place_ref[0], 1)
    edges = jnp.concatenate([edges, jnp.zeros_like(edges)], axis=1)
    for device in range(table_out.shape[0]):
        table_out[device, table_out.shape[1] - 8 :, :] = edges

    values = value_ref[...]
    values = values * live_mask(live_ref, 0, values.shape) * cal_coef_ref[...]
    blocks = product(
        one_hot(tile_cal_ref[...], CALB_DEV), jnp.concatenate(two_parts(values), axis=1), ((1,), (0,))
    )
    width = values.shape[1]
    blocks = blocks[:, :width] + blocks[:, width:]
    blocks = jnp.concatenate([blocks[: CALB_DEV // 2], blocks[CALB_DEV // 2 :]], axis=1)
    store_rows(table_out, KNOT_ROWS, blocks)


def star_backward_kernel(live_ref, star_ref, star_coef_ref, value_ref, after_ref, star_out, star_acc):
    star_acc[...] = jnp.zeros_like(star_acc)

    @pl.loop(0, star_ref.shape[0] // WIDE_GROUP)
    def _(group):
        first = pl.multiple_of(group * WIDE_GROUP, WIDE_GROUP)
        rows = pl.ds(first, WIDE_GROUP)
        star = star_ref[rows, :]
        values = value_ref[rows, :]
        values = values * live_mask(live_ref, first, values.shape)
        coarse, fine = star & (COARSE - 1), star >> 8
        parts = [two_parts(star_coef_ref[comp, rows, :] * values) for comp in range(5)]
        parts = [pair[half].astype(F32) for half in range(2) for pair in parts]
        left, right = [], []
        fine_rows, _ = rows_and_columns((FINE, star.shape[1]))
        for tile in range(WIDE_GROUP):
            here = slice(tile, tile + 1)
            right.append(one_hot(coarse[here], COARSE))
            chosen = fine_rows == fine[here]
            left.append(
                jnp.concatenate([jnp.where(chosen, part[here], 0.0) for part in parts], axis=0).astype(BF16)
            )
        star_acc[...] += product(
            jnp.concatenate(left, axis=1), jnp.concatenate(right, axis=1), ((1,), (1,))
        )

    star_out[...] = star_acc[:STAR_ROWS] + star_acc[STAR_ROWS:]


def sum_kernel(block_ref, out_ref, edge_out):
    total = block_ref[0]
    for device in range(1, block_ref.shape[0]):
        total = total + block_ref[device]
    rows = out_ref.shape[1]
    for device in range(block_ref.shape[0]):
        out_ref[device] = total[:rows]
    edge_out[...] = total[rows:, :128]


def picked(array, which):
    row = lax.broadcasted_iota(jnp.int32, array.shape, 0)
    lane = lax.broadcasted_iota(jnp.int32, array.shape, 1)
    chosen = (row == 0) & (lane == SCALAR_LANE + which)
    return jnp.sum(jnp.where(chosen, array, 0.0), keepdims=True)


def with_scalars(array, scalars):
    row = lax.broadcasted_iota(jnp.int32, array.shape, 0)
    lane = lax.broadcasted_iota(jnp.int32, array.shape, 1)
    for which, value in scalars:
        array = jnp.where((row == 0) & (lane == SCALAR_LANE + which), value, array)
    return array


def over_devices(ref):
    total = ref[0]
    for device in range(1, ref.shape[0]):
        total = total + ref[device]
    return total


def first_step(edges):
    return picked(edges, 0), picked(edges, 1)


def star_forward_kernel(n_seg, later, star_ref, star_coef_ref, own_ref, other_ref, *refs):
    if later:
        edge_ref, other_edge_ref, star_0_ref = refs[:3]
    image_ref, star_out, scalar_out, star_parts_ref = refs[-4:]
    star_x = own_ref[...] + other_ref[...]
    if later:
        norm_0, square_0 = first_step(edge_ref[...] + other_edge_ref[...])
        star_x = star_0_ref[...] - norm_0 / square_0 * star_x
    star_out[...] = star_x
    norm = jnp.sum(star_x * star_x, keepdims=True) / n_seg
    scalar_out[...] = with_scalars(jnp.zeros((8, 128), F32), [(0, norm)])
    star_high, star_low = two_parts(star_x)
    star_parts_ref[:STAR_ROWS] = star_high
    star_parts_ref[STAR_ROWS:] = star_low

    @pl.loop(0, star_ref.shape[0] // GROUP, unroll=2)
    def _(group):
        rows = pl.ds(pl.multiple_of(group * GROUP, GROUP), GROUP)
        star = star_ref[rows, :]
        coarse, fine = star & (COARSE - 1), star >> 8
        coef = [star_coef_ref[comp, rows, :] for comp in range(5)]
        tiles = [slice(tile, tile + 1) for tile in range(GROUP)]
        hot = jnp.concatenate([one_hot(coarse[here], COARSE) for here in tiles], axis=1)
        found = product(star_parts_ref[...], hot, ((1,), (0,)))
        width = star.shape[1]
        fine_rows, _ = rows_and_columns((FINE, width))
        image_rows = []
        for tile, here in enumerate(tiles):
            across = slice(tile * width, (tile + 1) * width)

            def part(comp):
                begin = comp * FINE
                return (
                    found[begin : begin + FINE, across]
                    + found[STAR_ROWS + begin : STAR_ROWS + begin + FINE, across]
                )

            both = sum(coef[comp][here] * part(comp) for comp in range(5))
            both = jnp.where(fine_rows == fine[here], both, 0.0)
            both = both[:8] + both[8:16] + both[16:24] + both[24:]
            image_rows.append(jnp.sum(both, axis=0, keepdims=True))
        image_ref[rows, :] = jnp.concatenate(image_rows, axis=0)


def knot_forward_kernel(
    n_stars, n_seg, later, live_ref, place_ref, knot_ref, frac_ref, att_coef_ref, cal_coef_ref,
    tile_cal_ref, star_image_ref, star_scalar_ref, table_x_ref, edge_ref, other_edge_ref, *refs,
):
    if later:
        table_0_ref, ahead_0_ref, image_0_ref, image_ref, table_out, scalar_out = refs[:6]
    else:
        image_ref, table_out, scalar_out, ahead_out = refs[:4]
    knot_parts_ref, cal_ref = refs[-2:]
    segment = place_ref[0]
    lane = lax.broadcasted_iota(jnp.int32, (8, 128), 1)
    row = lax.broadcasted_iota(jnp.int32, (8, 128), 0)
    wide_lane = lax.broadcasted_iota(jnp.int32, (8, COARSE), 1)

    edges = edge_ref[...] + other_edge_ref[...]

    def slot(which):
        return pltpu.roll(edges, 128 - SLOT * jnp.clip(which, 0, n_seg - 1), 1)

    before, own, after = slot(segment - 1), slot(segment), slot(segment + 1)
    before = jnp.where(segment > 0, before, 0.0)
    ahead = jnp.where(lane % 2 == 0, own, 0.0) + pltpu.roll(jnp.where(lane % 2 == 1, after, 0.0), 127, 1)
    ahead = jnp.where((segment < n_seg - 1) & (lane < 8) & (row < 3), ahead, 0.0)

    table = table_x_ref[...]
    pieces = []
    for comp in range(4):
        shifted = pltpu.roll(before, 128 - 2 * comp, 1) if comp else before
        shifted = jnp.where((lane == 0) & (row < 3), shifted, 0.0)
        top = table[comp * FINE : comp * FINE + 8]
        pieces.append(top + jnp.concatenate([shifted, jnp.zeros_like(shifted)], axis=1))
        pieces.append(table[comp * FINE + 8 : (comp + 1) * FINE])
    table = jnp.concatenate(pieces + [table[KNOT_ROWS:]], axis=0)
    if later:
        norm_0, square_0 = first_step(edges)
        step = norm_0 / square_0
        table = table_0_ref[...] - step * table
        ahead = ahead_0_ref[...] - step * ahead
    else:
        ahead_out[...] = ahead
    table_out[...] = table
    norm = picked(star_scalar_ref[...], 0) + jnp.sum(table * table, keepdims=True) / n_stars

    beyond = []
    for comp in range(4):
        moved = pltpu.roll(table[comp * FINE : comp * FINE + 8], COARSE - 1, 1)
        last = pltpu.roll(ahead, 127 - 2 * comp, 1)
        beyond.append(jnp.where(wide_lane == COARSE - 1, jnp.concatenate([last, last], axis=1), moved))
    knot_high, knot_low = two_parts(jnp.concatenate([table[:KNOT_ROWS]] + beyond, axis=0))
    knot_parts_ref[:KNOT_HALF] = knot_high
    knot_parts_ref[KNOT_HALF:] = knot_low

    blocks = jnp.concatenate([table[KNOT_ROWS:, :128], table[KNOT_ROWS:, 128:]], axis=0)
    rows = product(
        one_hot(tile_cal_ref[...], CALB_DEV), jnp.concatenate(two_parts(blocks), axis=1), ((0,), (0,))
    )
    cal_ref[...] = (rows[:, :128] + rows[:, 128:]) * cal_coef_ref[...] + star_image_ref[...]

    def one_group(group, sums):
        first = pl.multiple_of(group * GROUP, GROUP)
        rows = pl.ds(first, GROUP)
        knot = knot_ref[rows, :]
        coarse, fine = knot >> 5, knot & (FINE - 1)
        weights = spline_weights(frac_ref[rows, :])
        coef = [att_coef_ref[comp, rows, :] for comp in range(4)]
        tiles = [slice(tile, tile + 1) for tile in range(GROUP)]
        hot = jnp.concatenate([one_hot(coarse[here], COARSE) for here in tiles], axis=1)
        found = product(knot_parts_ref[...], hot, ((1,), (0,)))
        width = knot.shape[1]
        image_rows = []
        for tile, here in enumerate(tiles):
            across = slice(tile * width, (tile + 1) * width)

            def part(begin, size):
                return (
                    found[begin : begin + size, across]
                    + found[KNOT_HALF + begin : KNOT_HALF + begin + size, across]
                )

            columns = weight_columns(weights, fine, tile)
            main = sum(coef[comp][here] * part(comp * FINE, FINE) for comp in range(4))
            past = sum(coef[comp][here] * part(KNOT_ROWS + comp * 8, 8) for comp in range(4))
            both = main * columns[:FINE]
            both = both[:8] + both[8:16] + both[16:24] + both[24:] + past * columns[FINE:]
            image_rows.append(jnp.sum(both, axis=0, keepdims=True))
        image = jnp.concatenate(image_rows, axis=0) + cal_ref[rows, :]
        image = image * live_mask(live_ref, first, image.shape)
        image_ref[rows, :] = image
        if later:
            return sums[0] + image * image, sums[1] + image * image_0_ref[rows, :]
        return (sums[0] + image * image,)

    zero = jnp.zeros((GROUP, knot_ref.shape[1]), F32)
    start = (zero, zero) if later else (zero,)
    sums = lax.fori_loop(0, knot_ref.shape[0] // GROUP, one_group, start, unroll=2)
    scalars = [(0, norm)] + [(1 + which, jnp.sum(part, keepdims=True)) for which, part in enumerate(sums)]
    result = with_scalars(jnp.zeros((8, 128), F32), scalars)
    for device in range(scalar_out.shape[0]):
        scalar_out[device] = result


def output_kernel(
    live_ref, edge_ref, other_edge_ref, scalar_ref, star_0_ref, star_1_ref, att_0_ref, att_1_ref, table_0_ref,
    table_1_ref, value_ref, image_0_ref, image_1_ref, star_out, att_out, cal_out, residual_out,
):
    norm_0, square_0 = first_step(edge_ref[...] + other_edge_ref[...])
    everyone = over_devices(scalar_ref)
    norm_1, square_1, cross = [picked(everyone, which) for which in range(3)]
    ratio = norm_1 / norm_0
    step_1 = norm_1 / (square_1 + 2.0 * ratio * cross + ratio * ratio * square_0)
    scale = norm_0 / square_0 + step_1 * ratio

    def combined(old, new):
        return scale * old + step_1 * new

    star_out[...] = combined(star_0_ref[...], star_1_ref[...])
    att_out[...] = combined(att_0_ref[...], att_1_ref[...])
    cal = combined(table_0_ref[KNOT_ROWS:, :], table_1_ref[KNOT_ROWS:, :])
    cal_out[...] = jnp.concatenate([cal[:, :128], cal[:, 128:]], axis=0)
    values = value_ref[...] * live_mask(live_ref, 0, value_ref.shape)
    residual_out[...] = values - combined(image_0_ref[...], image_1_ref[...])


def in_vmem(count):
    return [pl.BlockSpec(memory_space=pltpu.VMEM)] * count


def in_smem(count):
    return [pl.BlockSpec(memory_space=pltpu.SMEM)] * count


def in_hbm(count):
    return [pl.BlockSpec(memory_space=pltpu.HBM)] * count


def shaped(*shape):
    return jax.ShapeDtypeStruct(shape, F32)


ARRIVE_PARAMS = pltpu.CompilerParams(vmem_limit_bytes=60 * 1024 * 1024)
PARAMS = pltpu.CompilerParams(vmem_limit_bytes=40 * 1024 * 1024)
PASS_COST = pl.CostEstimate(flops=3_000_000_000, bytes_accessed=1_000_000, transcendentals=0)
SMALL_COST = pl.CostEstimate(flops=1_000_000, bytes_accessed=600_000, transcendentals=0)


def on_device(
    obs_star, obs_knot, obs_frac, star_coef, att_coef, cal_coef, tile_cal, live_tiles, obs_value
):
    n_stars, n_seg = lax.axis_size("stars"), lax.axis_size("seg")
    count = n_stars * n_seg
    tile_count, width = obs_star.shape
    tile_row = tile_cal[None, :]
    place = lax.axis_index("seg").astype(jnp.int32)[None]
    image_shape = shaped(tile_count, width)
    table_shape = shaped(TABLE_ROWS, COARSE)
    star_shape = shaped(STAR_ROWS, COARSE)
    scalar_shape, scalar_copies = shaped(8, 128), shaped(count, 8, 128)

    def knot_backward(values, scalars, arrive):
        observed = (obs_knot, obs_frac, att_coef, values, cal_coef, tile_row)
        scratch = [pltpu.VMEM((2 * KNOT_HALF, COARSE), F32)]
        if arrive:
            scratch += [pltpu.VMEM(array.shape, array.dtype) for array in observed]
            scratch += [pltpu.SemaphoreType.DMA((len(observed),))]
        return pl.pallas_call(
            functools.partial(knot_backward_kernel, arrive),
            out_shape=shaped(n_stars, TABLE_ROWS // n_stars + 8, COARSE),
            in_specs=in_smem(2) + (in_hbm if arrive else in_vmem)(len(observed)) + in_vmem(1),
            out_specs=in_vmem(1)[0],
            scratch_shapes=scratch,
            compiler_params=ARRIVE_PARAMS if arrive else PARAMS,
            cost_estimate=PASS_COST,
            name="knot_backward",
        )(live_tiles, place, *observed, scalars)

    def star_backward(values, after):
        return pl.pallas_call(
            star_backward_kernel,
            out_shape=star_shape,
            in_specs=in_smem(1) + in_vmem(3) + [pl.BlockSpec(memory_space=pl.ANY)],
            out_specs=in_vmem(1)[0],
            scratch_shapes=[pltpu.VMEM((2 * STAR_ROWS, COARSE), F32)],
            compiler_params=PARAMS,
            cost_estimate=PASS_COST,
            name="star_backward",
        )(live_tiles, obs_star, star_coef, values, after)

    def star_forward(own, other, *first):
        return pl.pallas_call(
            functools.partial(star_forward_kernel, n_seg, bool(first)),
            out_shape=(image_shape, star_shape, scalar_shape),
            in_specs=in_vmem(4 + len(first)),
            out_specs=tuple(in_vmem(3)),
            scratch_shapes=[pltpu.VMEM((2 * STAR_ROWS, COARSE), BF16)],
            compiler_params=PARAMS,
            cost_estimate=PASS_COST,
            name="star_forward",
        )(obs_star, star_coef, own, other, *first)

    def knot_forward(star_image, star_scalars, table, edge, other_edge, *first):
        outs = (image_shape, table_shape) + ((scalar_copies,) if first else (shaped(1, 8, 128), scalar_shape))
        return pl.pallas_call(
            functools.partial(knot_forward_kernel, n_stars, n_seg, bool(first)),
            out_shape=outs,
            in_specs=in_smem(2) + in_vmem(10 + len(first)),
            out_specs=tuple(in_vmem(len(outs))),
            scratch_shapes=[
                pltpu.VMEM((2 * KNOT_HALF, COARSE), BF16),
                pltpu.VMEM((tile_count, width), F32),
            ],
            compiler_params=PARAMS,
            cost_estimate=PASS_COST,
            name="knot_forward",
        )(
            live_tiles, place, obs_knot, obs_frac, att_coef, cal_coef, tile_row, star_image,
            star_scalars, table, edge, other_edge, *first,
        )

    def swap(blocks, axes):
        return lax.all_to_all(blocks, axes, 0, 0)

    def seg_terms(array):
        distance = 1
        while True:
            other = lax.ppermute(array, "seg", [(i, i ^ distance) for i in range(n_seg)])
            distance *= 2
            if distance >= n_seg:
                return array, other
            array = array + other

    def table_sum(table):
        blocks = swap(table, "stars")
        copies, edge = pl.pallas_call(
            sum_kernel,
            out_shape=(shaped(n_stars, TABLE_ROWS // n_stars, COARSE), scalar_shape),
            in_specs=in_vmem(1),
            out_specs=tuple(in_vmem(2)),
            compiler_params=PARAMS,
            cost_estimate=SMALL_COST,
            name="table_sum",
        )(blocks)
        return (swap(copies, "stars").reshape(TABLE_ROWS, COARSE), *seg_terms(edge))

    def half(values, scalars, arrive):
        table = knot_backward(values, scalars, arrive)
        star = star_backward(values, table)
        return (*seg_terms(star), *table_sum(table))

    own, other, table, edge, other_edge = half(obs_value, jnp.zeros((8, 128), F32), True)
    star_image, star_0, star_scalars = star_forward(own, other)
    image_0, table_0, scalars, ahead_0 = knot_forward(star_image, star_scalars, table, edge, other_edge)
    own, other, table, edge, other_edge = half(image_0, scalars[0], False)
    star_image, star_1, star_scalars = star_forward(own, other, edge, other_edge, star_0)
    image_1, table_1, scalars = knot_forward(
        star_image, star_scalars, table, edge, other_edge, table_0, ahead_0, image_0
    )

    def star_order(star):
        return star.reshape(5, STAR_DEV)

    def att_order(table):
        att = table[:KNOT_ROWS].reshape(4, FINE, COARSE)
        return att.transpose(0, 2, 1).reshape(4, KNOT_DEV)

    return pl.pallas_call(
        output_kernel,
        out_shape=(shaped(5, STAR_DEV), shaped(4, KNOT_DEV), shaped(CALB_DEV, width), image_shape),
        in_specs=in_smem(1) + in_vmem(12),
        out_specs=tuple(in_vmem(4)),
        compiler_params=PARAMS,
        cost_estimate=SMALL_COST,
        name="outputs",
    )(
        live_tiles, edge, other_edge, swap(scalars, ("stars", "seg")), star_order(star_0),
        star_order(star_1), att_order(table_0), att_order(table_1), table_0, table_1, obs_value,
        image_0, image_1,
    )


def solution(mesh):
    placed = (
        P(("stars", "seg"), None),
        P(("stars", "seg"), None),
        P(("stars", "seg"), None),
        P(None, ("stars", "seg"), None),
        P(None, ("stars", "seg"), None),
        P(("stars", "seg"), None),
        P(("stars", "seg")),
        P(("stars", "seg")),
        P(("stars", "seg"), None),
    )
    return jax.shard_map(
        on_device,
        mesh=mesh,
        in_specs=placed,
        out_specs=(P(None, "stars"), P(None, "seg"), P("seg", None), P(("stars", "seg"), None)),
        check_vma=False,
    )
```

```python
import functools

import jax
import jax.numpy as jnp
from jax import lax
from jax.experimental import pallas as pl
from jax.experimental.pallas import tpu as pltpu
from jax.sharding import PartitionSpec as P

STAR_DEV = 8192
KNOT_DEV = 8192
CALB_DEV = 256
FINE = 32
COARSE = 256
GROUP = 8
WIDE_GROUP = 16
SLOT = 8
STAR_ROWS = 5 * FINE
KNOT_ROWS = 4 * FINE
TABLE_ROWS = KNOT_ROWS + CALB_DEV // 2
BF16 = jnp.bfloat16
F32 = jnp.float32
SCALAR_LANE = 64
KNOT_HALF = KNOT_ROWS + 32


def two_parts(values):
    high = values.astype(BF16)
    return high, (values - high.astype(F32)).astype(BF16)


def rows_and_columns(shape):
    return lax.broadcasted_iota(jnp.int32, shape, 0), lax.broadcasted_iota(jnp.int32, shape, 1)


def one_hot(index_row, size):
    rows, _ = rows_and_columns((size, index_row.shape[1]))
    return jnp.where(rows == index_row, 1.0, 0.0).astype(BF16)


def spline_weights(fraction):
    remain = 1.0 - fraction
    square = fraction * fraction
    cubed = square * fraction
    return (
        remain * remain * remain / 6.0,
        (3.0 * cubed - 6.0 * square + 4.0) / 6.0,
        (-3.0 * cubed + 3.0 * square + 3.0 * fraction + 1.0) / 6.0,
        cubed / 6.0,
    )


def weight_columns(weights, fine, tile):
    rows, _ = rows_and_columns((FINE + 8, weights[0].shape[1]))
    behind = rows - fine[tile : tile + 1]
    result = jnp.zeros(behind.shape, F32)
    for offset in range(4):
        result = jnp.where(behind == offset, weights[offset][tile : tile + 1], result)
    return result


def product(left, right, contract):
    return lax.dot_general(left, right, (contract, ((), ())), preferred_element_type=F32)


def live_mask(live_ref, first, shape):
    rows, _ = rows_and_columns(shape)
    return (rows + first < live_ref[0]).astype(F32)


def store_rows(out_ref, begin, rows):
    block = out_ref.shape[1] - 8
    for offset in range(0, rows.shape[0], 8):
        where = begin + offset
        out_ref[where // block, where % block : where % block + 8, :] = rows[offset : offset + 8]


def knot_backward_kernel(arrive, live_ref, place_ref, *refs):
    observed, refs = refs[:6], refs[6:]
    if arrive:
        table_out, knot_acc, *buffers, sems = refs
        copies = [
            pltpu.make_async_copy(source, target, sems.at[which])
            for which, (source, target) in enumerate(zip(observed, buffers))
        ]
        for copy in copies:
            copy.start()
        observed = buffers
    else:
        scalar_ref, table_out, knot_acc = refs
    value_ref, cal_coef_ref, tile_cal_ref, knot_ref, frac_ref, att_coef_ref = observed
    knot_acc[...] = jnp.zeros_like(knot_acc)
    if arrive:
        for copy in copies[:3]:
            copy.wait()

    values = value_ref[...]
    values = values * live_mask(live_ref, 0, values.shape) * cal_coef_ref[...]
    blocks = product(
        one_hot(tile_cal_ref[...], CALB_DEV), jnp.concatenate(two_parts(values), axis=1), ((1,), (0,))
    )
    width = values.shape[1]
    blocks = blocks[:, :width] + blocks[:, width:]
    blocks = jnp.concatenate([blocks[: CALB_DEV // 2], blocks[CALB_DEV // 2 :]], axis=1)
    store_rows(table_out, KNOT_ROWS, blocks)
    if arrive:
        for copy in copies[3:]:
            copy.wait()

    @pl.loop(0, knot_ref.shape[0] // WIDE_GROUP)
    def _(group):
        first = pl.multiple_of(group * WIDE_GROUP, WIDE_GROUP)
        rows = pl.ds(first, WIDE_GROUP)
        knot = knot_ref[rows, :]
        values = value_ref[rows, :]
        values = values * live_mask(live_ref, first, values.shape)
        coarse, fine = knot >> 5, knot & (FINE - 1)
        weights = spline_weights(frac_ref[rows, :])
        terms = [att_coef_ref[comp, rows, :] * values for comp in range(4)]
        left, right = [], []
        for tile in range(WIDE_GROUP):
            here = slice(tile, tile + 1)
            right.append(one_hot(coarse[here], COARSE))
            columns = weight_columns(weights, fine, tile)
            spread = jnp.concatenate(
                [term[here] * columns[:FINE] for term in terms]
                + [term[here] * columns[FINE:] for term in terms],
                axis=0,
            )
            left.append(jnp.concatenate(two_parts(spread), axis=0))
        knot_acc[...] += product(
            jnp.concatenate(left, axis=1), jnp.concatenate(right, axis=1), ((1,), (1,))
        )

    lane = lax.broadcasted_iota(jnp.int32, (8, 128), 1)
    row = lax.broadcasted_iota(jnp.int32, (8, 128), 0)
    wide_lane = lax.broadcasted_iota(jnp.int32, (8, COARSE), 1)
    edges = jnp.zeros((8, 128), F32)
    for comp in range(4):
        begin, past = comp * FINE, KNOT_ROWS + comp * 8
        main = knot_acc[begin : begin + FINE] + knot_acc[KNOT_HALF + begin : KNOT_HALF + begin + FINE]
        beyond = knot_acc[past : past + 8] + knot_acc[KNOT_HALF + past : KNOT_HALF + past + 8]
        moved = pltpu.roll(beyond, 1, 1)
        top = main[:8] + jnp.where(wide_lane > 0, moved, 0.0)
        store_rows(table_out, begin, top)
        store_rows(table_out, begin + 8, main[8:])
        tail, head = moved[:, :128], top[:, :128]
        if comp:
            tail = pltpu.roll(tail, 2 * comp, 1)
        head = pltpu.roll(head, 2 * comp + 1, 1)
        edges = jnp.where((lane == 2 * comp) & (row < 3), tail, edges)
        edges = jnp.where((lane == 2 * comp + 1) & (row < 3), head, edges)
    edges = pltpu.roll(edges, SLOT * place_ref[0], 1)
    if not arrive:
        edges = edges + scalar_ref[...]
    edges = jnp.concatenate([edges, jnp.zeros_like(edges)], axis=1)
    for device in range(table_out.shape[0]):
        table_out[device, table_out.shape[1] - 8 :, :] = edges


def star_backward_kernel(live_ref, star_ref, star_coef_ref, value_ref, after_ref, star_out, star_acc):
    star_acc[...] = jnp.zeros_like(star_acc)

    @pl.loop(0, star_ref.shape[0] // WIDE_GROUP)
    def _(group):
        first = pl.multiple_of(group * WIDE_GROUP, WIDE_GROUP)
        rows = pl.ds(first, WIDE_GROUP)
        star = star_ref[rows, :]
        values = value_ref[rows, :]
        values = values * live_mask(live_ref, first, values.shape)
        coarse, fine = star & (COARSE - 1), star >> 8
        parts = [two_parts(star_coef_ref[comp, rows, :] * values) for comp in range(5)]
        parts = [pair[half].astype(F32) for half in range(2) for pair in parts]
        left, right = [], []
        fine_rows, _ = rows_and_columns((FINE, star.shape[1]))
        for tile in range(WIDE_GROUP):
            here = slice(tile, tile + 1)
            right.append(one_hot(coarse[here], COARSE))
            chosen = fine_rows == fine[here]
            left.append(
                jnp.concatenate([jnp.where(chosen, part[here], 0.0) for part in parts], axis=0).astype(BF16)
            )
        star_acc[...] += product(
            jnp.concatenate(left, axis=1), jnp.concatenate(right, axis=1), ((1,), (1,))
        )

    star_out[...] = star_acc[:STAR_ROWS] + star_acc[STAR_ROWS:]


def sum_kernel(block_ref, out_ref, edge_out):
    total = block_ref[0]
    for device in range(1, block_ref.shape[0]):
        total = total + block_ref[device]
    rows = out_ref.shape[1]
    for device in range(block_ref.shape[0]):
        out_ref[device] = total[:rows]
    edge_out[...] = total[rows:, :128]


def picked(array, which):
    row = lax.broadcasted_iota(jnp.int32, array.shape, 0)
    lane = lax.broadcasted_iota(jnp.int32, array.shape, 1)
    chosen = (row == 0) & (lane == SCALAR_LANE + which)
    return jnp.sum(jnp.where(chosen, array, 0.0), keepdims=True)


def with_scalars(array, scalars):
    row = lax.broadcasted_iota(jnp.int32, array.shape, 0)
    lane = lax.broadcasted_iota(jnp.int32, array.shape, 1)
    for which, value in scalars:
        array = jnp.where((row == 0) & (lane == SCALAR_LANE + which), value, array)
    return array


def first_step(edges):
    return picked(edges, 0), picked(edges, 1)


def star_forward_kernel(n_seg, star_ref, star_coef_ref, *refs):
    term_refs, (image_ref, star_out, star_parts_ref) = refs[:n_seg], refs[n_seg:]
    star_x = term_refs[0][...]
    for term_ref in term_refs[1:]:
        star_x = star_x + term_ref[...]
    star_out[...] = star_x
    star_high, star_low = two_parts(star_x)
    star_parts_ref[:STAR_ROWS] = star_high
    star_parts_ref[STAR_ROWS:] = star_low

    @pl.loop(0, star_ref.shape[0] // GROUP, unroll=2)
    def _(group):
        rows = pl.ds(pl.multiple_of(group * GROUP, GROUP), GROUP)
        star = star_ref[rows, :]
        coarse, fine = star & (COARSE - 1), star >> 8
        coef = [star_coef_ref[comp, rows, :] for comp in range(5)]
        tiles = [slice(tile, tile + 1) for tile in range(GROUP)]
        hot = jnp.concatenate([one_hot(coarse[here], COARSE) for here in tiles], axis=1)
        found = product(star_parts_ref[...], hot, ((1,), (0,)))
        width = star.shape[1]
        fine_rows, _ = rows_and_columns((FINE, width))
        image_rows = []
        for tile, here in enumerate(tiles):
            across = slice(tile * width, (tile + 1) * width)

            def part(comp):
                begin = comp * FINE
                return (
                    found[begin : begin + FINE, across]
                    + found[STAR_ROWS + begin : STAR_ROWS + begin + FINE, across]
                )

            both = sum(coef[comp][here] * part(comp) for comp in range(5))
            both = jnp.where(fine_rows == fine[here], both, 0.0)
            both = both[:8] + both[8:16] + both[16:24] + both[24:]
            image_rows.append(jnp.sum(both, axis=0, keepdims=True))
        image_ref[rows, :] = jnp.concatenate(image_rows, axis=0)


def knot_forward_kernel(
    n_stars, n_seg, later, live_ref, place_ref, knot_ref, frac_ref, att_coef_ref, cal_coef_ref,
    tile_cal_ref, star_image_ref, star_x_ref, table_x_ref, edge_ref, other_edge_ref, *refs,
):
    if later:
        star_0_ref, table_0_ref, image_0_ref, image_ref, table_out, scalar_out = refs[:6]
    else:
        image_ref, table_out, scalar_out = refs[:3]
    knot_parts_ref, cal_ref = refs[-2:]
    segment = place_ref[0]
    lane = lax.broadcasted_iota(jnp.int32, (8, 128), 1)
    row = lax.broadcasted_iota(jnp.int32, (8, 128), 0)
    wide_lane = lax.broadcasted_iota(jnp.int32, (8, COARSE), 1)

    edges = edge_ref[...] + other_edge_ref[...]

    def slot(which):
        return pltpu.roll(edges, 128 - SLOT * jnp.clip(which, 0, n_seg - 1), 1)

    before, own, after = slot(segment - 1), slot(segment), slot(segment + 1)
    before = jnp.where(segment > 0, before, 0.0)
    ahead = jnp.where(lane % 2 == 0, own, 0.0) + pltpu.roll(jnp.where(lane % 2 == 1, after, 0.0), 127, 1)
    ahead = jnp.where((segment < n_seg - 1) & (lane < 8) & (row < 3), ahead, 0.0)

    table = table_x_ref[...]
    pieces = []
    for comp in range(4):
        shifted = pltpu.roll(before, 128 - 2 * comp, 1) if comp else before
        shifted = jnp.where((lane == 0) & (row < 3), shifted, 0.0)
        top = table[comp * FINE : comp * FINE + 8]
        pieces.append(top + jnp.concatenate([shifted, jnp.zeros_like(shifted)], axis=1))
        pieces.append(table[comp * FINE + 8 : (comp + 1) * FINE])
    table = jnp.concatenate(pieces + [table[KNOT_ROWS:]], axis=0)
    table_out[...] = table
    if later:
        norm_0, square_0 = first_step(edges)
        step = norm_0 / square_0
        star_change = star_0_ref[...] - step * star_x_ref[...]
        table_change = table_0_ref[...] - step * table
    else:
        star_change, table_change = star_x_ref[...], table
    norm = (
        jnp.sum(star_change * star_change, keepdims=True) / n_seg
        + jnp.sum(table_change * table_change, keepdims=True) / n_stars
    )

    beyond = []
    for comp in range(4):
        moved = pltpu.roll(table[comp * FINE : comp * FINE + 8], COARSE - 1, 1)
        last = pltpu.roll(ahead, 127 - 2 * comp, 1)
        beyond.append(jnp.where(wide_lane == COARSE - 1, jnp.concatenate([last, last], axis=1), moved))
    knot_high, knot_low = two_parts(jnp.concatenate([table[:KNOT_ROWS]] + beyond, axis=0))
    knot_parts_ref[:KNOT_HALF] = knot_high
    knot_parts_ref[KNOT_HALF:] = knot_low

    blocks = jnp.concatenate([table[KNOT_ROWS:, :128], table[KNOT_ROWS:, 128:]], axis=0)
    rows = product(
        one_hot(tile_cal_ref[...], CALB_DEV), jnp.concatenate(two_parts(blocks), axis=1), ((0,), (0,))
    )
    cal_ref[...] = (rows[:, :128] + rows[:, 128:]) * cal_coef_ref[...] + star_image_ref[...]

    def one_group(group, sums):
        first = pl.multiple_of(group * GROUP, GROUP)
        rows = pl.ds(first, GROUP)
        knot = knot_ref[rows, :]
        coarse, fine = knot >> 5, knot & (FINE - 1)
        weights = spline_weights(frac_ref[rows, :])
        coef = [att_coef_ref[comp, rows, :] for comp in range(4)]
        tiles = [slice(tile, tile + 1) for tile in range(GROUP)]
        hot = jnp.concatenate([one_hot(coarse[here], COARSE) for here in tiles], axis=1)
        found = product(knot_parts_ref[...], hot, ((1,), (0,)))
        width = knot.shape[1]
        image_rows = []
        for tile, here in enumerate(tiles):
            across = slice(tile * width, (tile + 1) * width)

            def part(begin, size):
                return (
                    found[begin : begin + size, across]
                    + found[KNOT_HALF + begin : KNOT_HALF + begin + size, across]
                )

            columns = weight_columns(weights, fine, tile)
            main = sum(coef[comp][here] * part(comp * FINE, FINE) for comp in range(4))
            past = sum(coef[comp][here] * part(KNOT_ROWS + comp * 8, 8) for comp in range(4))
            both = main * columns[:FINE]
            both = both[:8] + both[8:16] + both[16:24] + both[24:] + past * columns[FINE:]
            image_rows.append(jnp.sum(both, axis=0, keepdims=True))
        image = jnp.concatenate(image_rows, axis=0) + cal_ref[rows, :]
        image = image * live_mask(live_ref, first, image.shape)
        if later:
            image_0 = image_0_ref[rows, :]
            image = image_0 - step * image
            image_ref[rows, :] = image
            return sums[0] + image * image, sums[1] + image * image_0
        image_ref[rows, :] = image
        return (sums[0] + image * image,)

    zero = jnp.zeros((GROUP, knot_ref.shape[1]), F32)
    start = (zero, zero) if later else (zero,)
    sums = lax.fori_loop(0, knot_ref.shape[0] // GROUP, one_group, start, unroll=2)
    scalars = [(0, norm)] + [(1 + which, jnp.sum(part, keepdims=True)) for which, part in enumerate(sums)]
    scalar_out[...] = with_scalars(jnp.zeros((8, 128), F32), scalars)


def output_kernel(
    live_ref, edge_ref, other_edge_ref, scalar_ref, other_scalar_ref, star_0_ref, star_h_ref, att_0_ref,
    att_h_ref, table_0_ref, table_h_ref, value_ref, image_0_ref, image_1_ref, star_out, att_out, cal_out,
    residual_out,
):
    norm_0, square_0 = first_step(edge_ref[...] + other_edge_ref[...])
    everyone = scalar_ref[...] + other_scalar_ref[...]
    norm_1, square_1, cross = [picked(everyone, which) for which in range(3)]
    step_0 = norm_0 / square_0
    ratio = norm_1 / norm_0
    step_1 = norm_1 / (square_1 + 2.0 * ratio * cross + ratio * ratio * square_0)
    scale = step_0 + step_1 * ratio

    def combined(old, change):
        return scale * old + step_1 * (old - step_0 * change)

    star_out[...] = combined(star_0_ref[...], star_h_ref[...])
    att_out[...] = combined(att_0_ref[...], att_h_ref[...])
    cal = combined(table_0_ref[KNOT_ROWS:, :], table_h_ref[KNOT_ROWS:, :])
    cal_out[...] = jnp.concatenate([cal[:, :128], cal[:, 128:]], axis=0)
    values = value_ref[...] * live_mask(live_ref, 0, value_ref.shape)
    residual_out[...] = values - scale * image_0_ref[...] - step_1 * image_1_ref[...]


def in_vmem(count):
    return [pl.BlockSpec(memory_space=pltpu.VMEM)] * count


def in_smem(count):
    return [pl.BlockSpec(memory_space=pltpu.SMEM)] * count


def in_hbm(count):
    return [pl.BlockSpec(memory_space=pltpu.HBM)] * count


def shaped(*shape):
    return jax.ShapeDtypeStruct(shape, F32)


ARRIVE_PARAMS = pltpu.CompilerParams(vmem_limit_bytes=60 * 1024 * 1024)
PARAMS = pltpu.CompilerParams(vmem_limit_bytes=40 * 1024 * 1024)
PASS_COST = pl.CostEstimate(flops=3_000_000_000, bytes_accessed=1_000_000, transcendentals=0)
SMALL_COST = pl.CostEstimate(flops=1_000_000, bytes_accessed=600_000, transcendentals=0)


def on_device(
    obs_star, obs_knot, obs_frac, star_coef, att_coef, cal_coef, tile_cal, live_tiles, obs_value
):
    n_stars, n_seg = lax.axis_size("stars"), lax.axis_size("seg")
    tile_count, width = obs_star.shape
    tile_row = tile_cal[None, :]
    place = lax.axis_index("seg").astype(jnp.int32)[None]
    image_shape = shaped(tile_count, width)
    table_shape = shaped(TABLE_ROWS, COARSE)
    star_shape = shaped(STAR_ROWS, COARSE)
    scalar_shape = shaped(8, 128)

    def knot_backward(values, *scalars):
        arrive = not scalars
        observed = (values, cal_coef, tile_row, obs_knot, obs_frac, att_coef)
        scratch = [pltpu.VMEM((2 * KNOT_HALF, COARSE), F32)]
        if arrive:
            scratch += [pltpu.VMEM(array.shape, array.dtype) for array in observed]
            scratch += [pltpu.SemaphoreType.DMA((len(observed),))]
        return pl.pallas_call(
            functools.partial(knot_backward_kernel, arrive),
            out_shape=shaped(n_stars, TABLE_ROWS // n_stars + 8, COARSE),
            in_specs=in_smem(2) + (in_hbm if arrive else in_vmem)(len(observed)) + in_vmem(len(scalars)),
            out_specs=in_vmem(1)[0],
            scratch_shapes=scratch,
            compiler_params=ARRIVE_PARAMS if arrive else PARAMS,
            cost_estimate=PASS_COST,
            name="knot_backward",
        )(live_tiles, place, *observed, *scalars)

    def star_backward(values, after):
        return pl.pallas_call(
            star_backward_kernel,
            out_shape=star_shape,
            in_specs=in_smem(1) + in_vmem(3) + in_hbm(1),
            out_specs=in_vmem(1)[0],
            scratch_shapes=[pltpu.VMEM((2 * STAR_ROWS, COARSE), F32)],
            compiler_params=PARAMS,
            cost_estimate=PASS_COST,
            name="star_backward",
        )(live_tiles, obs_star, star_coef, values, after)

    def star_forward(*terms):
        return pl.pallas_call(
            functools.partial(star_forward_kernel, n_seg),
            out_shape=(image_shape, star_shape),
            in_specs=in_vmem(2 + n_seg),
            out_specs=tuple(in_vmem(2)),
            scratch_shapes=[pltpu.VMEM((2 * STAR_ROWS, COARSE), BF16)],
            compiler_params=PARAMS,
            cost_estimate=PASS_COST,
            name="star_forward",
        )(obs_star, star_coef, *terms)

    def knot_forward(*arrays):
        later = len(arrays) > 5
        return pl.pallas_call(
            functools.partial(knot_forward_kernel, n_stars, n_seg, later),
            out_shape=(image_shape, table_shape, scalar_shape),
            in_specs=in_smem(2) + in_vmem(5 + len(arrays)),
            out_specs=tuple(in_vmem(3)),
            scratch_shapes=[
                pltpu.VMEM((2 * KNOT_HALF, COARSE), BF16),
                pltpu.VMEM((tile_count, width), F32),
            ],
            compiler_params=PARAMS,
            cost_estimate=PASS_COST,
            name="knot_forward",
        )(live_tiles, place, obs_knot, obs_frac, att_coef, cal_coef, tile_row, *arrays)

    def swap(blocks, axes):
        return lax.all_to_all(blocks, axes, 0, 0)

    def partner(array, axis, distance):
        return lax.ppermute(array, axis, [(i, i ^ distance) for i in range(lax.axis_size(axis))])

    def last_terms(array, *axes):
        steps = [(axis, 1 << bit) for axis in axes for bit in range(lax.axis_size(axis).bit_length() - 1)]
        for axis, distance in steps[:-1]:
            array = array + partner(array, axis, distance)
        return array, partner(array, *steps[-1])

    def table_sum(table):
        blocks = swap(table, "stars")
        copies, edge = pl.pallas_call(
            sum_kernel,
            out_shape=(shaped(n_stars, TABLE_ROWS // n_stars, COARSE), scalar_shape),
            in_specs=in_vmem(1),
            out_specs=tuple(in_vmem(2)),
            compiler_params=PARAMS,
            cost_estimate=SMALL_COST,
            name="table_sum",
        )(blocks)
        return (swap(copies, "stars").reshape(TABLE_ROWS, COARSE), *last_terms(edge, "seg"))

    def half(values, *scalars):
        table = knot_backward(values, *scalars)
        star = star_backward(values, table)
        stars = [star] + [partner(star, "seg", distance) for distance in range(1, n_seg)]
        table, *edges = table_sum(table)
        star_image, star = star_forward(*stars)
        return star_image, star, table, edges

    star_image, star_0, table, edges = half(obs_value)
    image_0, table_0, scalars = knot_forward(star_image, star_0, table, *edges)
    star_image, star_h, table, edges = half(image_0, scalars)
    image_1, table_h, scalars = knot_forward(
        star_image, star_h, table, *edges, star_0, table_0, image_0
    )

    def star_order(star):
        return star.reshape(5, STAR_DEV)

    def att_order(table):
        att = table[:KNOT_ROWS].reshape(4, FINE, COARSE)
        return att.transpose(0, 2, 1).reshape(4, KNOT_DEV)

    return pl.pallas_call(
        output_kernel,
        out_shape=(shaped(5, STAR_DEV), shaped(4, KNOT_DEV), shaped(CALB_DEV, width), image_shape),
        in_specs=in_smem(1) + in_vmem(13),
        out_specs=tuple(in_vmem(4)),
        compiler_params=PARAMS,
        cost_estimate=SMALL_COST,
        name="outputs",
    )(
        live_tiles, *edges, *last_terms(scalars, "seg", "stars"), star_order(star_0), star_order(star_h),
        att_order(table_0), att_order(table_h), table_0, table_h, obs_value, image_0, image_1,
    )


def solution(mesh):
    placed = (
        P(("stars", "seg"), None),
        P(("stars", "seg"), None),
        P(("stars", "seg"), None),
        P(None, ("stars", "seg"), None),
        P(None, ("stars", "seg"), None),
        P(("stars", "seg"), None),
        P(("stars", "seg")),
        P(("stars", "seg")),
        P(("stars", "seg"), None),
    )
    return jax.shard_map(
        on_device,
        mesh=mesh,
        in_specs=placed,
        out_specs=(P(None, "stars"), P(None, "seg"), P("seg", None), P(("stars", "seg"), None)),
        check_vma=False,
    )
```

```python
import functools

import jax
import jax.numpy as jnp
from jax import lax
from jax.experimental import pallas as pl
from jax.experimental.pallas import tpu as pltpu
from jax.sharding import PartitionSpec as P

STAR_DEV = 8192
KNOT_DEV = 8192
CALB_DEV = 256
FINE = 32
COARSE = 256
GROUP = 8
WIDE_GROUP = 16
SLOT = 8
STAR_ROWS = 5 * FINE
KNOT_ROWS = 4 * FINE
TABLE_ROWS = KNOT_ROWS + CALB_DEV // 2
BF16 = jnp.bfloat16
F32 = jnp.float32
SCALAR_LANE = 64
KNOT_HALF = KNOT_ROWS + 32


def two_parts(values):
    high = values.astype(BF16)
    return high, (values - high.astype(F32)).astype(BF16)


def rows_and_columns(shape):
    return lax.broadcasted_iota(jnp.int32, shape, 0), lax.broadcasted_iota(jnp.int32, shape, 1)


def one_hot(index_row, size):
    rows, _ = rows_and_columns((size, index_row.shape[1]))
    return jnp.where(rows == index_row, 1.0, 0.0).astype(BF16)


def spline_weights(fraction):
    remain = 1.0 - fraction
    square = fraction * fraction
    cubed = square * fraction
    return (
        remain * remain * remain / 6.0,
        (3.0 * cubed - 6.0 * square + 4.0) / 6.0,
        (-3.0 * cubed + 3.0 * square + 3.0 * fraction + 1.0) / 6.0,
        cubed / 6.0,
    )


def weight_columns(weights, fine, tile):
    rows, _ = rows_and_columns((FINE + 8, weights[0].shape[1]))
    behind = rows - fine[tile : tile + 1]
    result = jnp.zeros(behind.shape, F32)
    for offset in range(4):
        result = jnp.where(behind == offset, weights[offset][tile : tile + 1], result)
    return result


def product(left, right, contract):
    return lax.dot_general(left, right, (contract, ((), ())), preferred_element_type=F32)


def live_mask(live_ref, first, shape):
    rows, _ = rows_and_columns(shape)
    return (rows + first < live_ref[0]).astype(F32)


def store_rows(out_ref, begin, rows):
    block = out_ref.shape[1]
    for offset in range(0, rows.shape[0], 8):
        where = begin + offset
        out_ref[where // block, where % block : where % block + 8, :] = rows[offset : offset + 8]


def knot_backward_kernel(n_stars, arrive, live_ref, place_ref, *refs):
    observed, refs = refs[:6], refs[6:]
    if not arrive:
        scalar_ref, *refs = refs
    block_outs, (table_out, knot_acc) = refs[:n_stars], refs[n_stars : n_stars + 2]
    if arrive:
        *buffers, sems = refs[n_stars + 2 :]
        copies = [
            pltpu.make_async_copy(source, target, sems.at[which])
            for which, (source, target) in enumerate(zip(observed, buffers))
        ]
        for copy in copies:
            copy.start()
        observed = buffers
    value_ref, cal_coef_ref, tile_cal_ref, knot_ref, frac_ref, att_coef_ref = observed
    knot_acc[...] = jnp.zeros_like(knot_acc)
    if arrive:
        for copy in copies[:3]:
            copy.wait()

    values = value_ref[...]
    values = values * live_mask(live_ref, 0, values.shape) * cal_coef_ref[...]
    blocks = product(
        one_hot(tile_cal_ref[...], CALB_DEV), jnp.concatenate(two_parts(values), axis=1), ((1,), (0,))
    )
    width = values.shape[1]
    blocks = blocks[:, :width] + blocks[:, width:]
    blocks = jnp.concatenate([blocks[: CALB_DEV // 2], blocks[CALB_DEV // 2 :]], axis=1)
    store_rows(table_out, KNOT_ROWS, blocks)
    if arrive:
        for copy in copies[3:]:
            copy.wait()

    @pl.loop(0, knot_ref.shape[0] // WIDE_GROUP)
    def _(group):
        first = pl.multiple_of(group * WIDE_GROUP, WIDE_GROUP)
        rows = pl.ds(first, WIDE_GROUP)
        knot = knot_ref[rows, :]
        values = value_ref[rows, :]
        values = values * live_mask(live_ref, first, values.shape)
        coarse, fine = knot >> 5, knot & (FINE - 1)
        weights = spline_weights(frac_ref[rows, :])
        terms = [att_coef_ref[comp, rows, :] * values for comp in range(4)]
        left, right = [], []
        for tile in range(WIDE_GROUP):
            here = slice(tile, tile + 1)
            right.append(one_hot(coarse[here], COARSE))
            columns = weight_columns(weights, fine, tile)
            spread = jnp.concatenate(
                [term[here] * columns[:FINE] for term in terms]
                + [term[here] * columns[FINE:] for term in terms],
                axis=0,
            )
            left.append(jnp.concatenate(two_parts(spread), axis=0))
        knot_acc[...] += product(
            jnp.concatenate(left, axis=1), jnp.concatenate(right, axis=1), ((1,), (1,))
        )

    lane = lax.broadcasted_iota(jnp.int32, (8, 128), 1)
    row = lax.broadcasted_iota(jnp.int32, (8, 128), 0)
    wide_lane = lax.broadcasted_iota(jnp.int32, (8, COARSE), 1)
    edges = jnp.zeros((8, 128), F32)
    for comp in range(4):
        begin, past = comp * FINE, KNOT_ROWS + comp * 8
        main = knot_acc[begin : begin + FINE] + knot_acc[KNOT_HALF + begin : KNOT_HALF + begin + FINE]
        beyond = knot_acc[past : past + 8] + knot_acc[KNOT_HALF + past : KNOT_HALF + past + 8]
        moved = pltpu.roll(beyond, 1, 1)
        top = main[:8] + jnp.where(wide_lane > 0, moved, 0.0)
        store_rows(table_out, begin, top)
        store_rows(table_out, begin + 8, main[8:])
        tail, head = moved[:, :128], top[:, :128]
        if comp:
            tail = pltpu.roll(tail, 2 * comp, 1)
        head = pltpu.roll(head, 2 * comp + 1, 1)
        edges = jnp.where((lane == 2 * comp) & (row < 3), tail, edges)
        edges = jnp.where((lane == 2 * comp + 1) & (row < 3), head, edges)
    edges = pltpu.roll(edges, SLOT * place_ref[0], 1)
    if not arrive:
        edges = edges + scalar_ref[...]
    edges = jnp.concatenate([edges, jnp.zeros_like(edges)], axis=1)
    for distance, block_out in enumerate(block_outs):
        block_out[:-8] = table_out[place_ref[1] ^ distance]
        block_out[-8:] = edges


def star_backward_kernel(
    live_ref, star_ref, star_coef_ref, value_ref, after_ref, star_out, token_out, star_acc
):
    token_out[...] = jnp.zeros_like(token_out)
    star_acc[...] = jnp.zeros_like(star_acc)

    @pl.loop(0, star_ref.shape[0] // WIDE_GROUP)
    def _(group):
        first = pl.multiple_of(group * WIDE_GROUP, WIDE_GROUP)
        rows = pl.ds(first, WIDE_GROUP)
        star = star_ref[rows, :]
        values = value_ref[rows, :]
        values = values * live_mask(live_ref, first, values.shape)
        coarse, fine = star & (COARSE - 1), star >> 8
        parts = [two_parts(star_coef_ref[comp, rows, :] * values) for comp in range(5)]
        parts = [pair[half].astype(F32) for half in range(2) for pair in parts]
        left, right = [], []
        fine_rows, _ = rows_and_columns((FINE, star.shape[1]))
        for tile in range(WIDE_GROUP):
            here = slice(tile, tile + 1)
            right.append(one_hot(coarse[here], COARSE))
            chosen = fine_rows == fine[here]
            left.append(
                jnp.concatenate([jnp.where(chosen, part[here], 0.0) for part in parts], axis=0).astype(BF16)
            )
        star_acc[...] += product(
            jnp.concatenate(left, axis=1), jnp.concatenate(right, axis=1), ((1,), (1,))
        )

    star_out[...] = star_acc[:STAR_ROWS] + star_acc[STAR_ROWS:]


def sum_kernel(n_stars, after_ref, *refs):
    block_refs, (part_out, edge_out) = refs[:n_stars], refs[n_stars:]
    total = block_refs[0][...]
    for block_ref in block_refs[1:]:
        total = total + block_ref[...]
    part_out[...] = total[:-8]
    edge_out[...] = total[-8:, :128]


def picked(array, which):
    row = lax.broadcasted_iota(jnp.int32, array.shape, 0)
    lane = lax.broadcasted_iota(jnp.int32, array.shape, 1)
    chosen = (row == 0) & (lane == SCALAR_LANE + which)
    return jnp.sum(jnp.where(chosen, array, 0.0), keepdims=True)


def with_scalars(array, scalars):
    row = lax.broadcasted_iota(jnp.int32, array.shape, 0)
    lane = lax.broadcasted_iota(jnp.int32, array.shape, 1)
    for which, value in scalars:
        array = jnp.where((row == 0) & (lane == SCALAR_LANE + which), value, array)
    return array


def first_step(edges):
    return picked(edges, 0), picked(edges, 1)


def star_forward_kernel(n_seg, star_ref, star_coef_ref, *refs):
    term_refs, (image_ref, star_out, star_parts_ref) = refs[:n_seg], refs[n_seg:]
    star_x = term_refs[0][...]
    for term_ref in term_refs[1:]:
        star_x = star_x + term_ref[...]
    star_out[...] = star_x
    star_high, star_low = two_parts(star_x)
    star_parts_ref[:STAR_ROWS] = star_high
    star_parts_ref[STAR_ROWS:] = star_low

    @pl.loop(0, star_ref.shape[0] // GROUP, unroll=2)
    def _(group):
        rows = pl.ds(pl.multiple_of(group * GROUP, GROUP), GROUP)
        star = star_ref[rows, :]
        coarse, fine = star & (COARSE - 1), star >> 8
        coef = [star_coef_ref[comp, rows, :] for comp in range(5)]
        tiles = [slice(tile, tile + 1) for tile in range(GROUP)]
        hot = jnp.concatenate([one_hot(coarse[here], COARSE) for here in tiles], axis=1)
        found = product(star_parts_ref[...], hot, ((1,), (0,)))
        width = star.shape[1]
        fine_rows, _ = rows_and_columns((FINE, width))
        image_rows = []
        for tile, here in enumerate(tiles):
            across = slice(tile * width, (tile + 1) * width)

            def part(comp):
                begin = comp * FINE
                return (
                    found[begin : begin + FINE, across]
                    + found[STAR_ROWS + begin : STAR_ROWS + begin + FINE, across]
                )

            both = sum(coef[comp][here] * part(comp) for comp in range(5))
            both = jnp.where(fine_rows == fine[here], both, 0.0)
            both = both[:8] + both[8:16] + both[16:24] + both[24:]
            image_rows.append(jnp.sum(both, axis=0, keepdims=True))
        image_ref[rows, :] = jnp.concatenate(image_rows, axis=0)


def knot_forward_kernel(
    n_stars, n_seg, later, live_ref, place_ref, knot_ref, frac_ref, att_coef_ref, cal_coef_ref,
    tile_cal_ref, star_image_ref, star_x_ref, edge_ref, other_edge_ref, *refs,
):
    part_refs, refs = refs[:n_stars], refs[n_stars:]
    if later:
        star_0_ref, table_0_ref, image_0_ref, image_ref, table_out, scalar_out = refs[:6]
    else:
        image_ref, table_out, scalar_out = refs[:3]
    table_ref, knot_parts_ref, cal_ref = refs[-3:]
    segment = place_ref[0]
    lane = lax.broadcasted_iota(jnp.int32, (8, 128), 1)
    row = lax.broadcasted_iota(jnp.int32, (8, 128), 0)
    wide_lane = lax.broadcasted_iota(jnp.int32, (8, COARSE), 1)

    edges = edge_ref[...] + other_edge_ref[...]

    def slot(which):
        return pltpu.roll(edges, 128 - SLOT * jnp.clip(which, 0, n_seg - 1), 1)

    before, own, after = slot(segment - 1), slot(segment), slot(segment + 1)
    before = jnp.where(segment > 0, before, 0.0)
    ahead = jnp.where(lane % 2 == 0, own, 0.0) + pltpu.roll(jnp.where(lane % 2 == 1, after, 0.0), 127, 1)
    ahead = jnp.where((segment < n_seg - 1) & (lane < 8) & (row < 3), ahead, 0.0)

    for distance, part_ref in enumerate(part_refs):
        table_ref[place_ref[1] ^ distance] = part_ref[...]
    table = table_ref[...].reshape(TABLE_ROWS, COARSE)
    pieces = []
    for comp in range(4):
        shifted = pltpu.roll(before, 128 - 2 * comp, 1) if comp else before
        shifted = jnp.where((lane == 0) & (row < 3), shifted, 0.0)
        top = table[comp * FINE : comp * FINE + 8]
        pieces.append(top + jnp.concatenate([shifted, jnp.zeros_like(shifted)], axis=1))
        pieces.append(table[comp * FINE + 8 : (comp + 1) * FINE])
    table = jnp.concatenate(pieces + [table[KNOT_ROWS:]], axis=0)
    table_out[...] = table
    if later:
        norm_0, square_0 = first_step(edges)
        step = norm_0 / square_0
        star_change = star_0_ref[...] - step * star_x_ref[...]
        table_change = table_0_ref[...] - step * table
    else:
        star_change, table_change = star_x_ref[...], table
    norm = (
        jnp.sum(star_change * star_change, keepdims=True) / n_seg
        + jnp.sum(table_change * table_change, keepdims=True) / n_stars
    )

    beyond = []
    for comp in range(4):
        moved = pltpu.roll(table[comp * FINE : comp * FINE + 8], COARSE - 1, 1)
        last = pltpu.roll(ahead, 127 - 2 * comp, 1)
        beyond.append(jnp.where(wide_lane == COARSE - 1, jnp.concatenate([last, last], axis=1), moved))
    knot_high, knot_low = two_parts(jnp.concatenate([table[:KNOT_ROWS]] + beyond, axis=0))
    knot_parts_ref[:KNOT_HALF] = knot_high
    knot_parts_ref[KNOT_HALF:] = knot_low

    blocks = jnp.concatenate([table[KNOT_ROWS:, :128], table[KNOT_ROWS:, 128:]], axis=0)
    rows = product(
        one_hot(tile_cal_ref[...], CALB_DEV), jnp.concatenate(two_parts(blocks), axis=1), ((0,), (0,))
    )
    cal_ref[...] = (rows[:, :128] + rows[:, 128:]) * cal_coef_ref[...] + star_image_ref[...]

    def one_group(group, sums):
        first = pl.multiple_of(group * GROUP, GROUP)
        rows = pl.ds(first, GROUP)
        knot = knot_ref[rows, :]
        coarse, fine = knot >> 5, knot & (FINE - 1)
        weights = spline_weights(frac_ref[rows, :])
        coef = [att_coef_ref[comp, rows, :] for comp in range(4)]
        tiles = [slice(tile, tile + 1) for tile in range(GROUP)]
        hot = jnp.concatenate([one_hot(coarse[here], COARSE) for here in tiles], axis=1)
        found = product(knot_parts_ref[...], hot, ((1,), (0,)))
        width = knot.shape[1]
        image_rows = []
        for tile, here in enumerate(tiles):
            across = slice(tile * width, (tile + 1) * width)

            def part(begin, size):
                return (
                    found[begin : begin + size, across]
                    + found[KNOT_HALF + begin : KNOT_HALF + begin + size, across]
                )

            columns = weight_columns(weights, fine, tile)
            main = sum(coef[comp][here] * part(comp * FINE, FINE) for comp in range(4))
            past = sum(coef[comp][here] * part(KNOT_ROWS + comp * 8, 8) for comp in range(4))
            both = main * columns[:FINE]
            both = both[:8] + both[8:16] + both[16:24] + both[24:] + past * columns[FINE:]
            image_rows.append(jnp.sum(both, axis=0, keepdims=True))
        image = jnp.concatenate(image_rows, axis=0) + cal_ref[rows, :]
        image = image * live_mask(live_ref, first, image.shape)
        if later:
            image_0 = image_0_ref[rows, :]
            image = image_0 - step * image
            image_ref[rows, :] = image
            return sums[0] + image * image, sums[1] + image * image_0
        image_ref[rows, :] = image
        return (sums[0] + image * image,)

    zero = jnp.zeros((GROUP, knot_ref.shape[1]), F32)
    start = (zero, zero) if later else (zero,)
    sums = lax.fori_loop(0, knot_ref.shape[0] // GROUP, one_group, start, unroll=2)
    scalars = [(0, norm)] + [(1 + which, jnp.sum(part, keepdims=True)) for which, part in enumerate(sums)]
    scalar_out[...] = with_scalars(jnp.zeros((8, 128), F32), scalars)


def output_kernel(
    live_ref, edge_ref, other_edge_ref, star_0_ref, star_h_ref, att_0_ref, att_h_ref, table_0_ref,
    table_h_ref, value_ref, image_0_ref, image_1_ref, *refs,
):
    *scalar_refs, star_out, att_out, cal_out, residual_out = refs
    norm_0, square_0 = first_step(edge_ref[...] + other_edge_ref[...])
    everyone = sum(scalar_ref[...] for scalar_ref in scalar_refs)
    norm_1, square_1, cross = [picked(everyone, which) for which in range(3)]
    step_0 = norm_0 / square_0
    ratio = norm_1 / norm_0
    step_1 = norm_1 / (square_1 + 2.0 * ratio * cross + ratio * ratio * square_0)
    scale = step_0 + step_1 * ratio

    def combined(old, change):
        return scale * old + step_1 * (old - step_0 * change)

    star_out[...] = combined(star_0_ref[...], star_h_ref[...])
    att_out[...] = combined(att_0_ref[...], att_h_ref[...])
    cal = combined(table_0_ref[KNOT_ROWS:, :], table_h_ref[KNOT_ROWS:, :])
    cal_out[...] = jnp.concatenate([cal[:, :128], cal[:, 128:]], axis=0)
    values = value_ref[...] * live_mask(live_ref, 0, value_ref.shape)
    residual_out[...] = values - scale * image_0_ref[...] - step_1 * image_1_ref[...]


def in_vmem(count):
    return [pl.BlockSpec(memory_space=pltpu.VMEM)] * count


def in_smem(count):
    return [pl.BlockSpec(memory_space=pltpu.SMEM)] * count


def in_hbm(count):
    return [pl.BlockSpec(memory_space=pltpu.HBM)] * count


def shaped(*shape):
    return jax.ShapeDtypeStruct(shape, F32)


ARRIVE_PARAMS = pltpu.CompilerParams(vmem_limit_bytes=60 * 1024 * 1024)
PARAMS = pltpu.CompilerParams(vmem_limit_bytes=40 * 1024 * 1024)
PASS_COST = pl.CostEstimate(flops=3_000_000_000, bytes_accessed=1_000_000, transcendentals=0)
SMALL_COST = pl.CostEstimate(flops=1_000_000, bytes_accessed=600_000, transcendentals=0)


def on_device(
    obs_star, obs_knot, obs_frac, star_coef, att_coef, cal_coef, tile_cal, live_tiles, obs_value
):
    n_stars, n_seg = lax.axis_size("stars"), lax.axis_size("seg")
    tile_count, width = obs_star.shape
    tile_row = tile_cal[None, :]
    place = jnp.stack([lax.axis_index("seg"), lax.axis_index("stars")]).astype(jnp.int32)
    block_rows = TABLE_ROWS // n_stars
    image_shape = shaped(tile_count, width)
    table_shape = shaped(TABLE_ROWS, COARSE)
    star_shape = shaped(STAR_ROWS, COARSE)
    scalar_shape = shaped(8, 128)

    def knot_backward(values, *scalars):
        arrive = not scalars
        observed = (values, cal_coef, tile_row, obs_knot, obs_frac, att_coef)
        scratch = [
            pltpu.VMEM((n_stars, block_rows, COARSE), F32),
            pltpu.VMEM((2 * KNOT_HALF, COARSE), F32),
        ]
        if arrive:
            scratch += [pltpu.VMEM(array.shape, array.dtype) for array in observed]
            scratch += [pltpu.SemaphoreType.DMA((len(observed),))]
        return pl.pallas_call(
            functools.partial(knot_backward_kernel, n_stars, arrive),
            out_shape=(shaped(block_rows + 8, COARSE),) * n_stars,
            in_specs=in_smem(2) + (in_hbm if arrive else in_vmem)(len(observed)) + in_vmem(len(scalars)),
            out_specs=tuple(in_vmem(n_stars)),
            scratch_shapes=scratch,
            compiler_params=ARRIVE_PARAMS if arrive else PARAMS,
            cost_estimate=PASS_COST,
            name="knot_backward",
        )(live_tiles, place, *observed, *scalars)

    def star_backward(values, after):
        return pl.pallas_call(
            star_backward_kernel,
            out_shape=(star_shape, scalar_shape),
            in_specs=in_smem(1) + in_vmem(3) + in_hbm(1),
            out_specs=tuple(in_vmem(2)),
            scratch_shapes=[pltpu.VMEM((2 * STAR_ROWS, COARSE), F32)],
            compiler_params=PARAMS,
            cost_estimate=PASS_COST,
            name="star_backward",
        )(live_tiles, obs_star, star_coef, values, after)

    def star_forward(*terms):
        return pl.pallas_call(
            functools.partial(star_forward_kernel, n_seg),
            out_shape=(image_shape, star_shape),
            in_specs=in_vmem(2 + n_seg),
            out_specs=tuple(in_vmem(2)),
            scratch_shapes=[pltpu.VMEM((2 * STAR_ROWS, COARSE), BF16)],
            compiler_params=PARAMS,
            cost_estimate=PASS_COST,
            name="star_forward",
        )(obs_star, star_coef, *terms)

    def knot_forward(*arrays):
        later = len(arrays) > 4 + n_stars
        return pl.pallas_call(
            functools.partial(knot_forward_kernel, n_stars, n_seg, later),
            out_shape=(image_shape, table_shape, scalar_shape),
            in_specs=in_smem(2) + in_vmem(5 + len(arrays)),
            out_specs=tuple(in_vmem(3)),
            scratch_shapes=[
                pltpu.VMEM((n_stars, block_rows, COARSE), F32),
                pltpu.VMEM((2 * KNOT_HALF, COARSE), BF16),
                pltpu.VMEM((tile_count, width), F32),
            ],
            compiler_params=PARAMS,
            cost_estimate=PASS_COST,
            name="knot_forward",
        )(live_tiles, place, obs_knot, obs_frac, att_coef, cal_coef, tile_row, *arrays)

    def partner(array, axis, distance):
        return lax.ppermute(array, axis, [(i, i ^ distance) for i in range(lax.axis_size(axis))])

    def everyones(array, axis):
        return [array] + [partner(array, axis, distance) for distance in range(1, lax.axis_size(axis))]

    def table_sum(blocks, token):
        return pl.pallas_call(
            functools.partial(sum_kernel, n_stars),
            out_shape=(shaped(block_rows, COARSE), scalar_shape),
            in_specs=in_hbm(1) + in_vmem(n_stars),
            out_specs=tuple(in_vmem(2)),
            compiler_params=PARAMS,
            cost_estimate=SMALL_COST,
            name="table_sum",
        )(token, *blocks)

    def half(values, *scalars):
        blocks = knot_backward(values, *scalars)
        star, token = star_backward(values, blocks[0])
        received = [partner(block, "stars", distance) for distance, block in enumerate(blocks) if distance]
        part, edge = table_sum([blocks[0]] + received, token)
        for distance in [1 << bit for bit in range(n_seg.bit_length() - 2)]:
            edge = edge + partner(edge, "seg", distance)
        star_image, star = star_forward(*everyones(star, "seg"))
        return star_image, star, edge, partner(edge, "seg", n_seg // 2), *everyones(part, "stars")

    first = half(obs_value)
    star_0 = first[1]
    image_0, table_0, scalars = knot_forward(*first)
    second = half(image_0, scalars)
    star_h, edges = second[1], second[2:4]
    image_1, table_h, scalars = knot_forward(*second, star_0, table_0, image_0)
    scalars = everyones(sum(everyones(scalars, "seg")), "stars")

    def star_order(star):
        return star.reshape(5, STAR_DEV)

    def att_order(table):
        att = table[:KNOT_ROWS].reshape(4, FINE, COARSE)
        return att.transpose(0, 2, 1).reshape(4, KNOT_DEV)

    return pl.pallas_call(
        output_kernel,
        out_shape=(shaped(5, STAR_DEV), shaped(4, KNOT_DEV), shaped(CALB_DEV, width), image_shape),
        in_specs=in_smem(1) + in_vmem(11 + n_stars),
        out_specs=tuple(in_vmem(4)),
        compiler_params=PARAMS,
        cost_estimate=SMALL_COST,
        name="outputs",
    )(
        live_tiles, *edges, star_order(star_0), star_order(star_h), att_order(table_0), att_order(table_h),
        table_0, table_h, obs_value, image_0, image_1, *scalars,
    )


def solution(mesh):
    placed = (
        P(("stars", "seg"), None),
        P(("stars", "seg"), None),
        P(("stars", "seg"), None),
        P(None, ("stars", "seg"), None),
        P(None, ("stars", "seg"), None),
        P(("stars", "seg"), None),
        P(("stars", "seg")),
        P(("stars", "seg")),
        P(("stars", "seg"), None),
    )
    return jax.shard_map(
        on_device,
        mesh=mesh,
        in_specs=placed,
        out_specs=(P(None, "stars"), P(None, "seg"), P("seg", None), P(("stars", "seg"), None)),
        check_vma=False,
    )
```

```python
import functools

import jax
import jax.numpy as jnp
from jax import lax
from jax.experimental import pallas as pl
from jax.experimental.pallas import tpu as pltpu
from jax.sharding import PartitionSpec as P

STAR_DEV = 8192
KNOT_DEV = 8192
CALB_DEV = 256
FINE = 32
COARSE = 256
GROUP = 8
WIDE_GROUP = 16
SLOT = 8
STAR_ROWS = 5 * FINE
KNOT_ROWS = 4 * FINE
TABLE_ROWS = KNOT_ROWS + CALB_DEV // 2
BF16 = jnp.bfloat16
F32 = jnp.float32
SCALAR_LANE = 64
KNOT_HALF = KNOT_ROWS + 32


def two_parts(values):
    high = values.astype(BF16)
    return high, (values - high.astype(F32)).astype(BF16)


def rows_and_columns(shape):
    return lax.broadcasted_iota(jnp.int32, shape, 0), lax.broadcasted_iota(jnp.int32, shape, 1)


def one_hot(index_row, size):
    rows, _ = rows_and_columns((size, index_row.shape[1]))
    return jnp.where(rows == index_row, 1.0, 0.0).astype(BF16)


def spline_weights(fraction):
    remain = 1.0 - fraction
    square = fraction * fraction
    cubed = square * fraction
    return (
        remain * remain * remain / 6.0,
        (3.0 * cubed - 6.0 * square + 4.0) / 6.0,
        (-3.0 * cubed + 3.0 * square + 3.0 * fraction + 1.0) / 6.0,
        cubed / 6.0,
    )


def weight_columns(weights, fine, tile):
    rows, _ = rows_and_columns((FINE + 8, weights[0].shape[1]))
    behind = rows - fine[tile : tile + 1]
    result = jnp.zeros(behind.shape, F32)
    for offset in range(4):
        result = jnp.where(behind == offset, weights[offset][tile : tile + 1], result)
    return result


def product(left, right, contract):
    return lax.dot_general(left, right, (contract, ((), ())), preferred_element_type=F32)


def live_mask(live_ref, first, shape):
    rows, _ = rows_and_columns(shape)
    return (rows + first < live_ref[0]).astype(F32)


def store_rows(out_ref, begin, rows):
    block = out_ref.shape[1] - 8
    for offset in range(0, rows.shape[0], 8):
        where = begin + offset
        out_ref[where // block, where % block : where % block + 8, :] = rows[offset : offset + 8]


def knot_backward_kernel(arrive, live_ref, place_ref, *refs):
    observed, refs = refs[:6], refs[6:]
    if arrive:
        table_out, knot_acc, *buffers, sems = refs
        copies = [
            pltpu.make_async_copy(source, target, sems.at[which])
            for which, (source, target) in enumerate(zip(observed, buffers))
        ]
        for copy in copies:
            copy.start()
        observed = buffers
    else:
        scalar_ref, table_out, knot_acc = refs
    value_ref, cal_coef_ref, tile_cal_ref, knot_ref, frac_ref, att_coef_ref = observed
    knot_acc[...] = jnp.zeros_like(knot_acc)
    if arrive:
        for copy in copies[:3]:
            copy.wait()

    values = value_ref[...]
    values = values * live_mask(live_ref, 0, values.shape) * cal_coef_ref[...]
    blocks = product(
        one_hot(tile_cal_ref[...], CALB_DEV), jnp.concatenate(two_parts(values), axis=1), ((1,), (0,))
    )
    width = values.shape[1]
    blocks = blocks[:, :width] + blocks[:, width:]
    blocks = jnp.concatenate([blocks[: CALB_DEV // 2], blocks[CALB_DEV // 2 :]], axis=1)
    store_rows(table_out, KNOT_ROWS, blocks)
    if arrive:
        for copy in copies[3:]:
            copy.wait()

    @pl.loop(0, knot_ref.shape[0] // WIDE_GROUP)
    def _(group):
        first = pl.multiple_of(group * WIDE_GROUP, WIDE_GROUP)
        rows = pl.ds(first, WIDE_GROUP)
        knot = knot_ref[rows, :]
        values = value_ref[rows, :]
        values = values * live_mask(live_ref, first, values.shape)
        coarse, fine = knot >> 5, knot & (FINE - 1)
        weights = spline_weights(frac_ref[rows, :])
        terms = [att_coef_ref[comp, rows, :] * values for comp in range(4)]
        left, right = [], []
        for tile in range(WIDE_GROUP):
            here = slice(tile, tile + 1)
            right.append(one_hot(coarse[here], COARSE))
            columns = weight_columns(weights, fine, tile)
            spread = jnp.concatenate(
                [term[here] * columns[:FINE] for term in terms]
                + [term[here] * columns[FINE:] for term in terms],
                axis=0,
            )
            left.append(jnp.concatenate(two_parts(spread), axis=0))
        knot_acc[...] += product(
            jnp.concatenate(left, axis=1), jnp.concatenate(right, axis=1), ((1,), (1,))
        )

    lane = lax.broadcasted_iota(jnp.int32, (8, 128), 1)
    row = lax.broadcasted_iota(jnp.int32, (8, 128), 0)
    wide_lane = lax.broadcasted_iota(jnp.int32, (8, COARSE), 1)
    edges = jnp.zeros((8, 128), F32)
    for comp in range(4):
        begin, past = comp * FINE, KNOT_ROWS + comp * 8
        main = knot_acc[begin : begin + FINE] + knot_acc[KNOT_HALF + begin : KNOT_HALF + begin + FINE]
        beyond = knot_acc[past : past + 8] + knot_acc[KNOT_HALF + past : KNOT_HALF + past + 8]
        moved = pltpu.roll(beyond, 1, 1)
        top = main[:8] + jnp.where(wide_lane > 0, moved, 0.0)
        store_rows(table_out, begin, top)
        store_rows(table_out, begin + 8, main[8:])
        tail, head = moved[:, :128], top[:, :128]
        if comp:
            tail = pltpu.roll(tail, 2 * comp, 1)
        head = pltpu.roll(head, 2 * comp + 1, 1)
        edges = jnp.where((lane == 2 * comp) & (row < 3), tail, edges)
        edges = jnp.where((lane == 2 * comp + 1) & (row < 3), head, edges)
    edges = pltpu.roll(edges, SLOT * place_ref[0], 1)
    if not arrive:
        edges = edges + scalar_ref[...]
    edges = jnp.concatenate([edges, jnp.zeros_like(edges)], axis=1)
    for device in range(table_out.shape[0]):
        table_out[device, table_out.shape[1] - 8 :, :] = edges


def star_backward_kernel(
    live_ref, star_ref, star_coef_ref, value_ref, after_ref, star_out, token_out, star_acc
):
    token_out[...] = jnp.zeros_like(token_out)
    star_acc[...] = jnp.zeros_like(star_acc)

    @pl.loop(0, star_ref.shape[0] // WIDE_GROUP)
    def _(group):
        first = pl.multiple_of(group * WIDE_GROUP, WIDE_GROUP)
        rows = pl.ds(first, WIDE_GROUP)
        star = star_ref[rows, :]
        values = value_ref[rows, :]
        values = values * live_mask(live_ref, first, values.shape)
        coarse, fine = star & (COARSE - 1), star >> 8
        parts = [two_parts(star_coef_ref[comp, rows, :] * values) for comp in range(5)]
        parts = [pair[half].astype(F32) for half in range(2) for pair in parts]
        left, right = [], []
        fine_rows, _ = rows_and_columns((FINE, star.shape[1]))
        for tile in range(WIDE_GROUP):
            here = slice(tile, tile + 1)
            right.append(one_hot(coarse[here], COARSE))
            chosen = fine_rows == fine[here]
            left.append(
                jnp.concatenate([jnp.where(chosen, part[here], 0.0) for part in parts], axis=0).astype(BF16)
            )
        star_acc[...] += product(
            jnp.concatenate(left, axis=1), jnp.concatenate(right, axis=1), ((1,), (1,))
        )

    star_out[...] = star_acc[:STAR_ROWS] + star_acc[STAR_ROWS:]


def sum_kernel(after_ref, block_ref, out_ref, edge_out):
    total = block_ref[0]
    for device in range(1, block_ref.shape[0]):
        total = total + block_ref[device]
    rows = out_ref.shape[1]
    for device in range(block_ref.shape[0]):
        out_ref[device] = total[:rows]
    edge_out[...] = total[rows:, :128]


def picked(array, which):
    row = lax.broadcasted_iota(jnp.int32, array.shape, 0)
    lane = lax.broadcasted_iota(jnp.int32, array.shape, 1)
    chosen = (row == 0) & (lane == SCALAR_LANE + which)
    return jnp.sum(jnp.where(chosen, array, 0.0), keepdims=True)


def with_scalars(array, scalars):
    row = lax.broadcasted_iota(jnp.int32, array.shape, 0)
    lane = lax.broadcasted_iota(jnp.int32, array.shape, 1)
    for which, value in scalars:
        array = jnp.where((row == 0) & (lane == SCALAR_LANE + which), value, array)
    return array


def first_step(edges):
    return picked(edges, 0), picked(edges, 1)


def star_forward_kernel(n_seg, star_ref, star_coef_ref, *refs):
    term_refs, (image_ref, star_out, star_parts_ref) = refs[:n_seg], refs[n_seg:]
    star_x = term_refs[0][...]
    for term_ref in term_refs[1:]:
        star_x = star_x + term_ref[...]
    star_out[...] = star_x
    star_high, star_low = two_parts(star_x)
    star_parts_ref[:STAR_ROWS] = star_high
    star_parts_ref[STAR_ROWS:] = star_low

    @pl.loop(0, star_ref.shape[0] // GROUP, unroll=2)
    def _(group):
        rows = pl.ds(pl.multiple_of(group * GROUP, GROUP), GROUP)
        star = star_ref[rows, :]
        coarse, fine = star & (COARSE - 1), star >> 8
        coef = [star_coef_ref[comp, rows, :] for comp in range(5)]
        tiles = [slice(tile, tile + 1) for tile in range(GROUP)]
        hot = jnp.concatenate([one_hot(coarse[here], COARSE) for here in tiles], axis=1)
        found = product(star_parts_ref[...], hot, ((1,), (0,)))
        width = star.shape[1]
        fine_rows, _ = rows_and_columns((FINE, width))
        image_rows = []
        for tile, here in enumerate(tiles):
            across = slice(tile * width, (tile + 1) * width)

            def part(comp):
                begin = comp * FINE
                return (
                    found[begin : begin + FINE, across]
                    + found[STAR_ROWS + begin : STAR_ROWS + begin + FINE, across]
                )

            both = sum(coef[comp][here] * part(comp) for comp in range(5))
            both = jnp.where(fine_rows == fine[here], both, 0.0)
            both = both[:8] + both[8:16] + both[16:24] + both[24:]
            image_rows.append(jnp.sum(both, axis=0, keepdims=True))
        image_ref[rows, :] = jnp.concatenate(image_rows, axis=0)


def knot_forward_kernel(
    n_stars, n_seg, later, live_ref, place_ref, knot_ref, frac_ref, att_coef_ref, cal_coef_ref,
    tile_cal_ref, star_image_ref, star_x_ref, table_x_ref, edge_ref, other_edge_ref, *refs,
):
    if later:
        star_0_ref, table_0_ref, image_0_ref, image_ref, table_out, scalar_out = refs[:6]
    else:
        image_ref, table_out, scalar_out = refs[:3]
    knot_parts_ref, cal_ref = refs[-2:]
    segment = place_ref[0]
    lane = lax.broadcasted_iota(jnp.int32, (8, 128), 1)
    row = lax.broadcasted_iota(jnp.int32, (8, 128), 0)
    wide_lane = lax.broadcasted_iota(jnp.int32, (8, COARSE), 1)

    edges = edge_ref[...] + other_edge_ref[...]

    def slot(which):
        return pltpu.roll(edges, 128 - SLOT * jnp.clip(which, 0, n_seg - 1), 1)

    before, own, after = slot(segment - 1), slot(segment), slot(segment + 1)
    before = jnp.where(segment > 0, before, 0.0)
    ahead = jnp.where(lane % 2 == 0, own, 0.0) + pltpu.roll(jnp.where(lane % 2 == 1, after, 0.0), 127, 1)
    ahead = jnp.where((segment < n_seg - 1) & (lane < 8) & (row < 3), ahead, 0.0)

    table = table_x_ref[...]
    pieces = []
    for comp in range(4):
        shifted = pltpu.roll(before, 128 - 2 * comp, 1) if comp else before
        shifted = jnp.where((lane == 0) & (row < 3), shifted, 0.0)
        top = table[comp * FINE : comp * FINE + 8]
        pieces.append(top + jnp.concatenate([shifted, jnp.zeros_like(shifted)], axis=1))
        pieces.append(table[comp * FINE + 8 : (comp + 1) * FINE])
    table = jnp.concatenate(pieces + [table[KNOT_ROWS:]], axis=0)
    table_out[...] = table
    if later:
        norm_0, square_0 = first_step(edges)
        step = norm_0 / square_0
        star_change = star_0_ref[...] - step * star_x_ref[...]
        table_change = table_0_ref[...] - step * table
    else:
        star_change, table_change = star_x_ref[...], table
    norm = (
        jnp.sum(star_change * star_change, keepdims=True) / n_seg
        + jnp.sum(table_change * table_change, keepdims=True) / n_stars
    )

    beyond = []
    for comp in range(4):
        moved = pltpu.roll(table[comp * FINE : comp * FINE + 8], COARSE - 1, 1)
        last = pltpu.roll(ahead, 127 - 2 * comp, 1)
        beyond.append(jnp.where(wide_lane == COARSE - 1, jnp.concatenate([last, last], axis=1), moved))
    knot_high, knot_low = two_parts(jnp.concatenate([table[:KNOT_ROWS]] + beyond, axis=0))
    knot_parts_ref[:KNOT_HALF] = knot_high
    knot_parts_ref[KNOT_HALF:] = knot_low

    blocks = jnp.concatenate([table[KNOT_ROWS:, :128], table[KNOT_ROWS:, 128:]], axis=0)
    rows = product(
        one_hot(tile_cal_ref[...], CALB_DEV), jnp.concatenate(two_parts(blocks), axis=1), ((0,), (0,))
    )
    cal_ref[...] = (rows[:, :128] + rows[:, 128:]) * cal_coef_ref[...] + star_image_ref[...]

    def one_group(group, sums):
        first = pl.multiple_of(group * GROUP, GROUP)
        rows = pl.ds(first, GROUP)
        knot = knot_ref[rows, :]
        coarse, fine = knot >> 5, knot & (FINE - 1)
        weights = spline_weights(frac_ref[rows, :])
        coef = [att_coef_ref[comp, rows, :] for comp in range(4)]
        tiles = [slice(tile, tile + 1) for tile in range(GROUP)]
        hot = jnp.concatenate([one_hot(coarse[here], COARSE) for here in tiles], axis=1)
        found = product(knot_parts_ref[...], hot, ((1,), (0,)))
        width = knot.shape[1]
        image_rows = []
        for tile, here in enumerate(tiles):
            across = slice(tile * width, (tile + 1) * width)

            def part(begin, size):
                return (
                    found[begin : begin + size, across]
                    + found[KNOT_HALF + begin : KNOT_HALF + begin + size, across]
                )

            columns = weight_columns(weights, fine, tile)
            main = sum(coef[comp][here] * part(comp * FINE, FINE) for comp in range(4))
            past = sum(coef[comp][here] * part(KNOT_ROWS + comp * 8, 8) for comp in range(4))
            both = main * columns[:FINE]
            both = both[:8] + both[8:16] + both[16:24] + both[24:] + past * columns[FINE:]
            image_rows.append(jnp.sum(both, axis=0, keepdims=True))
        image = jnp.concatenate(image_rows, axis=0) + cal_ref[rows, :]
        image = image * live_mask(live_ref, first, image.shape)
        if later:
            image_0 = image_0_ref[rows, :]
            image = image_0 - step * image
            image_ref[rows, :] = image
            return sums[0] + image * image, sums[1] + image * image_0
        image_ref[rows, :] = image
        return (sums[0] + image * image,)

    zero = jnp.zeros((GROUP, knot_ref.shape[1]), F32)
    start = (zero, zero) if later else (zero,)
    sums = lax.fori_loop(0, knot_ref.shape[0] // GROUP, one_group, start, unroll=2)
    scalars = [(0, norm)] + [(1 + which, jnp.sum(part, keepdims=True)) for which, part in enumerate(sums)]
    scalar_out[...] = with_scalars(jnp.zeros((8, 128), F32), scalars)


def output_kernel(
    live_ref, edge_ref, other_edge_ref, scalar_ref, star_0_ref, star_h_ref, att_0_ref, att_h_ref,
    table_0_ref, table_h_ref, value_ref, image_0_ref, image_1_ref, star_out, att_out, cal_out, residual_out,
):
    norm_0, square_0 = first_step(edge_ref[...] + other_edge_ref[...])
    everyone = scalar_ref[0]
    for device in range(1, scalar_ref.shape[0]):
        everyone = everyone + scalar_ref[device]
    norm_1, square_1, cross = [picked(everyone, which) for which in range(3)]
    step_0 = norm_0 / square_0
    ratio = norm_1 / norm_0
    step_1 = norm_1 / (square_1 + 2.0 * ratio * cross + ratio * ratio * square_0)
    scale = step_0 + step_1 * ratio

    def combined(old, change):
        return scale * old + step_1 * (old - step_0 * change)

    star_out[...] = combined(star_0_ref[...], star_h_ref[...])
    att_out[...] = combined(att_0_ref[...], att_h_ref[...])
    cal = combined(table_0_ref[KNOT_ROWS:, :], table_h_ref[KNOT_ROWS:, :])
    cal_out[...] = jnp.concatenate([cal[:, :128], cal[:, 128:]], axis=0)
    values = value_ref[...] * live_mask(live_ref, 0, value_ref.shape)
    residual_out[...] = values - scale * image_0_ref[...] - step_1 * image_1_ref[...]


def in_vmem(count):
    return [pl.BlockSpec(memory_space=pltpu.VMEM)] * count


def in_smem(count):
    return [pl.BlockSpec(memory_space=pltpu.SMEM)] * count


def in_hbm(count):
    return [pl.BlockSpec(memory_space=pltpu.HBM)] * count


def shaped(*shape):
    return jax.ShapeDtypeStruct(shape, F32)


ARRIVE_PARAMS = pltpu.CompilerParams(vmem_limit_bytes=60 * 1024 * 1024)
PARAMS = pltpu.CompilerParams(vmem_limit_bytes=40 * 1024 * 1024)
PASS_COST = pl.CostEstimate(flops=3_000_000_000, bytes_accessed=1_000_000, transcendentals=0)
SMALL_COST = pl.CostEstimate(flops=1_000_000, bytes_accessed=600_000, transcendentals=0)


def on_device(
    obs_star, obs_knot, obs_frac, star_coef, att_coef, cal_coef, tile_cal, live_tiles, obs_value
):
    n_stars, n_seg = lax.axis_size("stars"), lax.axis_size("seg")
    tile_count, width = obs_star.shape
    tile_row = tile_cal[None, :]
    place = lax.axis_index("seg").astype(jnp.int32)[None]
    image_shape = shaped(tile_count, width)
    table_shape = shaped(TABLE_ROWS, COARSE)
    star_shape = shaped(STAR_ROWS, COARSE)
    scalar_shape = shaped(8, 128)

    def knot_backward(values, *scalars):
        arrive = not scalars
        observed = (values, cal_coef, tile_row, obs_knot, obs_frac, att_coef)
        scratch = [pltpu.VMEM((2 * KNOT_HALF, COARSE), F32)]
        if arrive:
            scratch += [pltpu.VMEM(array.shape, array.dtype) for array in observed]
            scratch += [pltpu.SemaphoreType.DMA((len(observed),))]
        return pl.pallas_call(
            functools.partial(knot_backward_kernel, arrive),
            out_shape=shaped(n_stars, TABLE_ROWS // n_stars + 8, COARSE),
            in_specs=in_smem(2) + (in_hbm if arrive else in_vmem)(len(observed)) + in_vmem(len(scalars)),
            out_specs=in_vmem(1)[0],
            scratch_shapes=scratch,
            compiler_params=ARRIVE_PARAMS if arrive else PARAMS,
            cost_estimate=PASS_COST,
            name="knot_backward",
        )(live_tiles, place, *observed, *scalars)

    def star_backward(values, after):
        return pl.pallas_call(
            star_backward_kernel,
            out_shape=(star_shape, scalar_shape),
            in_specs=in_smem(1) + in_vmem(3) + in_hbm(1),
            out_specs=tuple(in_vmem(2)),
            scratch_shapes=[pltpu.VMEM((2 * STAR_ROWS, COARSE), F32)],
            compiler_params=PARAMS,
            cost_estimate=PASS_COST,
            name="star_backward",
        )(live_tiles, obs_star, star_coef, values, after)

    def star_forward(*terms):
        return pl.pallas_call(
            functools.partial(star_forward_kernel, n_seg),
            out_shape=(image_shape, star_shape),
            in_specs=in_vmem(2 + n_seg),
            out_specs=tuple(in_vmem(2)),
            scratch_shapes=[pltpu.VMEM((2 * STAR_ROWS, COARSE), BF16)],
            compiler_params=PARAMS,
            cost_estimate=PASS_COST,
            name="star_forward",
        )(obs_star, star_coef, *terms)

    def knot_forward(*arrays):
        later = len(arrays) > 5
        return pl.pallas_call(
            functools.partial(knot_forward_kernel, n_stars, n_seg, later),
            out_shape=(image_shape, table_shape, scalar_shape),
            in_specs=in_smem(2) + in_vmem(5 + len(arrays)),
            out_specs=tuple(in_vmem(3)),
            scratch_shapes=[
                pltpu.VMEM((2 * KNOT_HALF, COARSE), BF16),
                pltpu.VMEM((tile_count, width), F32),
            ],
            compiler_params=PARAMS,
            cost_estimate=PASS_COST,
            name="knot_forward",
        )(live_tiles, place, obs_knot, obs_frac, att_coef, cal_coef, tile_row, *arrays)

    def swap(blocks, axes):
        return lax.all_to_all(blocks, axes, 0, 0)

    def partner(array, axis, distance):
        return lax.ppermute(array, axis, [(i, i ^ distance) for i in range(lax.axis_size(axis))])

    def everyones(array, axis):
        return [array] + [partner(array, axis, distance) for distance in range(1, lax.axis_size(axis))]

    def table_sum(table, token):
        blocks = swap(table, "stars")
        copies, edge = pl.pallas_call(
            sum_kernel,
            out_shape=(shaped(n_stars, TABLE_ROWS // n_stars, COARSE), scalar_shape),
            in_specs=in_hbm(1) + in_vmem(1),
            out_specs=tuple(in_vmem(2)),
            compiler_params=PARAMS,
            cost_estimate=SMALL_COST,
            name="table_sum",
        )(token, blocks)
        for distance in [1 << bit for bit in range(n_seg.bit_length() - 2)]:
            edge = edge + partner(edge, "seg", distance)
        table = swap(copies, "stars").reshape(TABLE_ROWS, COARSE)
        return table, (edge, partner(edge, "seg", n_seg // 2))

    def half(values, *scalars):
        table = knot_backward(values, *scalars)
        star, token = star_backward(values, table)
        stars = everyones(star, "seg")
        table, edges = table_sum(table, token)
        star_image, star = star_forward(*stars)
        return star_image, star, table, edges

    star_image, star_0, table, edges = half(obs_value)
    image_0, table_0, scalars = knot_forward(star_image, star_0, table, *edges)
    star_image, star_h, table, edges = half(image_0, scalars)
    image_1, table_h, scalars = knot_forward(
        star_image, star_h, table, *edges, star_0, table_0, image_0
    )

    scalars = sum(everyones(scalars, "seg"))
    scalars = swap(jnp.broadcast_to(scalars[None], (n_stars, *scalars.shape)), "stars")

    def star_order(star):
        return star.reshape(5, STAR_DEV)

    def att_order(table):
        att = table[:KNOT_ROWS].reshape(4, FINE, COARSE)
        return att.transpose(0, 2, 1).reshape(4, KNOT_DEV)

    return pl.pallas_call(
        output_kernel,
        out_shape=(shaped(5, STAR_DEV), shaped(4, KNOT_DEV), shaped(CALB_DEV, width), image_shape),
        in_specs=in_smem(1) + in_vmem(12),
        out_specs=tuple(in_vmem(4)),
        compiler_params=PARAMS,
        cost_estimate=SMALL_COST,
        name="outputs",
    )(
        live_tiles, *edges, scalars, star_order(star_0), star_order(star_h), att_order(table_0),
        att_order(table_h), table_0, table_h, obs_value, image_0, image_1,
    )


def solution(mesh):
    placed = (
        P(("stars", "seg"), None),
        P(("stars", "seg"), None),
        P(("stars", "seg"), None),
        P(None, ("stars", "seg"), None),
        P(None, ("stars", "seg"), None),
        P(("stars", "seg"), None),
        P(("stars", "seg")),
        P(("stars", "seg")),
        P(("stars", "seg"), None),
    )
    return jax.shard_map(
        on_device,
        mesh=mesh,
        in_specs=placed,
        out_specs=(P(None, "stars"), P(None, "seg"), P("seg", None), P(("stars", "seg"), None)),
        check_vma=False,
    )
```

```python
import functools

import jax
import jax.numpy as jnp
from jax import lax
from jax.experimental import pallas as pl
from jax.experimental.pallas import tpu as pltpu
from jax.sharding import PartitionSpec as P

STAR_DEV = 8192
KNOT_DEV = 8192
CALB_DEV = 256
FINE = 32
COARSE = 256
GROUP = 8
WIDE_GROUP = 16
SLOT = 8
STAR_ROWS = 5 * FINE
KNOT_ROWS = 4 * FINE
TABLE_ROWS = KNOT_ROWS + CALB_DEV // 2
BF16 = jnp.bfloat16
F32 = jnp.float32
SCALAR_LANE = 64
KNOT_HALF = KNOT_ROWS + 32


def two_parts(values):
    high = values.astype(BF16)
    return high, (values - high.astype(F32)).astype(BF16)


def rows_and_columns(shape):
    return lax.broadcasted_iota(jnp.int32, shape, 0), lax.broadcasted_iota(jnp.int32, shape, 1)


def one_hot(index_row, size):
    rows, _ = rows_and_columns((size, index_row.shape[1]))
    return jnp.where(rows == index_row, 1.0, 0.0).astype(BF16)


def spline_weights(fraction):
    remain = 1.0 - fraction
    square = fraction * fraction
    cubed = square * fraction
    return (
        remain * remain * remain / 6.0,
        (3.0 * cubed - 6.0 * square + 4.0) / 6.0,
        (-3.0 * cubed + 3.0 * square + 3.0 * fraction + 1.0) / 6.0,
        cubed / 6.0,
    )


def weight_columns(weights, fine, tile):
    rows, _ = rows_and_columns((FINE + 8, weights[0].shape[1]))
    behind = rows - fine[tile : tile + 1]
    result = jnp.zeros(behind.shape, F32)
    for offset in range(4):
        result = jnp.where(behind == offset, weights[offset][tile : tile + 1], result)
    return result


def product(left, right, contract):
    return lax.dot_general(left, right, (contract, ((), ())), preferred_element_type=F32)


def live_mask(live_ref, first, shape):
    rows, _ = rows_and_columns(shape)
    return (rows + first < live_ref[0]).astype(F32)


def store_rows(out_ref, begin, rows):
    block = out_ref.shape[1]
    for offset in range(0, rows.shape[0], 8):
        where = begin + offset
        out_ref[where // block, where % block : where % block + 8, :] = rows[offset : offset + 8]


def knot_backward_kernel(arrive, live_ref, place_ref, *refs):
    observed, refs = refs[:6], refs[6:]
    if not arrive:
        scalar_ref, *refs = refs
    table_out, edge_out, knot_acc = refs[:3]
    if arrive:
        *buffers, sems = refs[3:]
        copies = [
            pltpu.make_async_copy(source, target, sems.at[which])
            for which, (source, target) in enumerate(zip(observed, buffers))
        ]
        for copy in copies:
            copy.start()
        observed = buffers
    value_ref, cal_coef_ref, tile_cal_ref, knot_ref, frac_ref, att_coef_ref = observed
    knot_acc[...] = jnp.zeros_like(knot_acc)
    if arrive:
        for copy in copies[:3]:
            copy.wait()

    values = value_ref[...]
    values = values * live_mask(live_ref, 0, values.shape) * cal_coef_ref[...]
    blocks = product(
        one_hot(tile_cal_ref[...], CALB_DEV), jnp.concatenate(two_parts(values), axis=1), ((1,), (0,))
    )
    width = values.shape[1]
    blocks = blocks[:, :width] + blocks[:, width:]
    blocks = jnp.concatenate([blocks[: CALB_DEV // 2], blocks[CALB_DEV // 2 :]], axis=1)
    store_rows(table_out, KNOT_ROWS, blocks)
    if arrive:
        for copy in copies[3:]:
            copy.wait()

    @pl.loop(0, knot_ref.shape[0] // WIDE_GROUP)
    def _(group):
        first = pl.multiple_of(group * WIDE_GROUP, WIDE_GROUP)
        rows = pl.ds(first, WIDE_GROUP)
        knot = knot_ref[rows, :]
        values = value_ref[rows, :]
        values = values * live_mask(live_ref, first, values.shape)
        coarse, fine = knot >> 5, knot & (FINE - 1)
        weights = spline_weights(frac_ref[rows, :])
        terms = [att_coef_ref[comp, rows, :] * values for comp in range(4)]
        left, right = [], []
        for tile in range(WIDE_GROUP):
            here = slice(tile, tile + 1)
            right.append(one_hot(coarse[here], COARSE))
            columns = weight_columns(weights, fine, tile)
            spread = jnp.concatenate(
                [term[here] * columns[:FINE] for term in terms]
                + [term[here] * columns[FINE:] for term in terms],
                axis=0,
            )
            left.append(jnp.concatenate(two_parts(spread), axis=0))
        knot_acc[...] += product(
            jnp.concatenate(left, axis=1), jnp.concatenate(right, axis=1), ((1,), (1,))
        )

    lane = lax.broadcasted_iota(jnp.int32, (8, 128), 1)
    row = lax.broadcasted_iota(jnp.int32, (8, 128), 0)
    wide_lane = lax.broadcasted_iota(jnp.int32, (8, COARSE), 1)
    edges = jnp.zeros((8, 128), F32)
    for comp in range(4):
        begin, past = comp * FINE, KNOT_ROWS + comp * 8
        main = knot_acc[begin : begin + FINE] + knot_acc[KNOT_HALF + begin : KNOT_HALF + begin + FINE]
        beyond = knot_acc[past : past + 8] + knot_acc[KNOT_HALF + past : KNOT_HALF + past + 8]
        moved = pltpu.roll(beyond, 1, 1)
        top = main[:8] + jnp.where(wide_lane > 0, moved, 0.0)
        store_rows(table_out, begin, top)
        store_rows(table_out, begin + 8, main[8:])
        tail, head = moved[:, :128], top[:, :128]
        if comp:
            tail = pltpu.roll(tail, 2 * comp, 1)
        head = pltpu.roll(head, 2 * comp + 1, 1)
        edges = jnp.where((lane == 2 * comp) & (row < 3), tail, edges)
        edges = jnp.where((lane == 2 * comp + 1) & (row < 3), head, edges)
    edges = pltpu.roll(edges, SLOT * place_ref[0], 1)
    if not arrive:
        edges = edges + scalar_ref[...]
    edge_out[...] = jnp.concatenate([edges, jnp.zeros_like(edges)], axis=1)


def star_backward_kernel(
    live_ref, star_ref, star_coef_ref, value_ref, edge_ref, star_out, star_acc
):
    star_acc[...] = jnp.zeros_like(star_acc)

    @pl.loop(0, star_ref.shape[0] // WIDE_GROUP)
    def _(group):
        first = pl.multiple_of(group * WIDE_GROUP, WIDE_GROUP)
        rows = pl.ds(first, WIDE_GROUP)
        star = star_ref[rows, :]
        values = value_ref[rows, :]
        values = values * live_mask(live_ref, first, values.shape)
        coarse, fine = star & (COARSE - 1), star >> 8
        parts = [two_parts(star_coef_ref[comp, rows, :] * values) for comp in range(5)]
        parts = [pair[half].astype(F32) for half in range(2) for pair in parts]
        left, right = [], []
        fine_rows, _ = rows_and_columns((FINE, star.shape[1]))
        for tile in range(WIDE_GROUP):
            here = slice(tile, tile + 1)
            right.append(one_hot(coarse[here], COARSE))
            chosen = fine_rows == fine[here]
            left.append(
                jnp.concatenate([jnp.where(chosen, part[here], 0.0) for part in parts], axis=0).astype(BF16)
            )
        star_acc[...] += product(
            jnp.concatenate(left, axis=1), jnp.concatenate(right, axis=1), ((1,), (1,))
        )

    star_out[:STAR_ROWS] = star_acc[:STAR_ROWS] + star_acc[STAR_ROWS:]
    star_out[STAR_ROWS:] = edge_ref[...]


def sum_kernel(block_ref, own_ref, other_ref, out_ref, star_out):
    total = block_ref[0]
    for device in range(1, block_ref.shape[0]):
        total = total + block_ref[device]
    star = own_ref[...] + other_ref[...]
    star_out[...] = star[:STAR_ROWS]
    for device in range(block_ref.shape[0]):
        out_ref[device, :-8] = total
        out_ref[device, -8:] = star[STAR_ROWS:]


def picked(array, which):
    row = lax.broadcasted_iota(jnp.int32, array.shape, 0)
    lane = lax.broadcasted_iota(jnp.int32, array.shape, 1)
    chosen = (row == 0) & (lane == SCALAR_LANE + which)
    return jnp.sum(jnp.where(chosen, array, 0.0), keepdims=True)


def with_scalars(array, scalars):
    row = lax.broadcasted_iota(jnp.int32, array.shape, 0)
    lane = lax.broadcasted_iota(jnp.int32, array.shape, 1)
    for which, value in scalars:
        array = jnp.where((row == 0) & (lane == SCALAR_LANE + which), value, array)
    return array


def first_step(edges):
    return picked(edges, 0), picked(edges, 1)


def star_forward_kernel(star_ref, star_coef_ref, star_x_ref, image_ref, star_parts_ref):
    star_x = star_x_ref[...]
    star_high, star_low = two_parts(star_x)
    star_parts_ref[:STAR_ROWS] = star_high
    star_parts_ref[STAR_ROWS:] = star_low

    @pl.loop(0, star_ref.shape[0] // GROUP, unroll=2)
    def _(group):
        rows = pl.ds(pl.multiple_of(group * GROUP, GROUP), GROUP)
        star = star_ref[rows, :]
        coarse, fine = star & (COARSE - 1), star >> 8
        coef = [star_coef_ref[comp, rows, :] for comp in range(5)]
        tiles = [slice(tile, tile + 1) for tile in range(GROUP)]
        hot = jnp.concatenate([one_hot(coarse[here], COARSE) for here in tiles], axis=1)
        found = product(star_parts_ref[...], hot, ((1,), (0,)))
        width = star.shape[1]
        fine_rows, _ = rows_and_columns((FINE, width))
        image_rows = []
        for tile, here in enumerate(tiles):
            across = slice(tile * width, (tile + 1) * width)

            def part(comp):
                begin = comp * FINE
                return (
                    found[begin : begin + FINE, across]
                    + found[STAR_ROWS + begin : STAR_ROWS + begin + FINE, across]
                )

            both = sum(coef[comp][here] * part(comp) for comp in range(5))
            both = jnp.where(fine_rows == fine[here], both, 0.0)
            both = both[:8] + both[8:16] + both[16:24] + both[24:]
            image_rows.append(jnp.sum(both, axis=0, keepdims=True))
        image_ref[rows, :] = jnp.concatenate(image_rows, axis=0)


def knot_forward_kernel(
    n_stars, n_seg, later, live_ref, place_ref, knot_ref, frac_ref, att_coef_ref, cal_coef_ref,
    tile_cal_ref, star_image_ref, star_x_ref, block_ref, *refs,
):
    if later:
        star_0_ref, table_0_ref, image_0_ref, image_ref, table_out, scalar_out = refs[:6]
    else:
        image_ref, table_out, scalar_out = refs[:3]
    knot_parts_ref, cal_ref = refs[-2:]
    segment = place_ref[0]
    lane = lax.broadcasted_iota(jnp.int32, (8, 128), 1)
    row = lax.broadcasted_iota(jnp.int32, (8, 128), 0)
    wide_lane = lax.broadcasted_iota(jnp.int32, (8, COARSE), 1)

    edges = block_ref[0, -8:, :128]
    for block in range(1, n_stars):
        edges = edges + block_ref[block, -8:, :128]

    def slot(which):
        return pltpu.roll(edges, 128 - SLOT * jnp.clip(which, 0, n_seg - 1), 1)

    before, own, after = slot(segment - 1), slot(segment), slot(segment + 1)
    before = jnp.where(segment > 0, before, 0.0)
    ahead = jnp.where(lane % 2 == 0, own, 0.0) + pltpu.roll(jnp.where(lane % 2 == 1, after, 0.0), 127, 1)
    ahead = jnp.where((segment < n_seg - 1) & (lane < 8) & (row < 3), ahead, 0.0)

    table = block_ref[:, :-8, :].reshape(TABLE_ROWS, COARSE)
    pieces = []
    for comp in range(4):
        shifted = pltpu.roll(before, 128 - 2 * comp, 1) if comp else before
        shifted = jnp.where((lane == 0) & (row < 3), shifted, 0.0)
        top = table[comp * FINE : comp * FINE + 8]
        pieces.append(top + jnp.concatenate([shifted, jnp.zeros_like(shifted)], axis=1))
        pieces.append(table[comp * FINE + 8 : (comp + 1) * FINE])
    table = jnp.concatenate(pieces + [table[KNOT_ROWS:]], axis=0)
    table_out[...] = table
    if later:
        norm_0, square_0 = first_step(edges)
        step = norm_0 / square_0
        star_change = star_0_ref[...] - step * star_x_ref[...]
        table_change = table_0_ref[...] - step * table
    else:
        star_change, table_change = star_x_ref[...], table
    norm = (
        jnp.sum(star_change * star_change, keepdims=True) / n_seg
        + jnp.sum(table_change * table_change, keepdims=True) / n_stars
    )

    beyond = []
    for comp in range(4):
        moved = pltpu.roll(table[comp * FINE : comp * FINE + 8], COARSE - 1, 1)
        last = pltpu.roll(ahead, 127 - 2 * comp, 1)
        beyond.append(jnp.where(wide_lane == COARSE - 1, jnp.concatenate([last, last], axis=1), moved))
    knot_high, knot_low = two_parts(jnp.concatenate([table[:KNOT_ROWS]] + beyond, axis=0))
    knot_parts_ref[:KNOT_HALF] = knot_high
    knot_parts_ref[KNOT_HALF:] = knot_low

    blocks = jnp.concatenate([table[KNOT_ROWS:, :128], table[KNOT_ROWS:, 128:]], axis=0)
    rows = product(
        one_hot(tile_cal_ref[...], CALB_DEV), jnp.concatenate(two_parts(blocks), axis=1), ((0,), (0,))
    )
    cal_ref[...] = (rows[:, :128] + rows[:, 128:]) * cal_coef_ref[...] + star_image_ref[...]

    def one_group(group, sums):
        first = pl.multiple_of(group * GROUP, GROUP)
        rows = pl.ds(first, GROUP)
        knot = knot_ref[rows, :]
        coarse, fine = knot >> 5, knot & (FINE - 1)
        weights = spline_weights(frac_ref[rows, :])
        coef = [att_coef_ref[comp, rows, :] for comp in range(4)]
        tiles = [slice(tile, tile + 1) for tile in range(GROUP)]
        hot = jnp.concatenate([one_hot(coarse[here], COARSE) for here in tiles], axis=1)
        found = product(knot_parts_ref[...], hot, ((1,), (0,)))
        width = knot.shape[1]
        image_rows = []
        for tile, here in enumerate(tiles):
            across = slice(tile * width, (tile + 1) * width)

            def part(begin, size):
                return (
                    found[begin : begin + size, across]
                    + found[KNOT_HALF + begin : KNOT_HALF + begin + size, across]
                )

            columns = weight_columns(weights, fine, tile)
            main = sum(coef[comp][here] * part(comp * FINE, FINE) for comp in range(4))
            past = sum(coef[comp][here] * part(KNOT_ROWS + comp * 8, 8) for comp in range(4))
            both = main * columns[:FINE]
            both = both[:8] + both[8:16] + both[16:24] + both[24:] + past * columns[FINE:]
            image_rows.append(jnp.sum(both, axis=0, keepdims=True))
        image = jnp.concatenate(image_rows, axis=0) + cal_ref[rows, :]
        image = image * live_mask(live_ref, first, image.shape)
        if later:
            image_0 = image_0_ref[rows, :]
            image = image_0 - step * image
            image_ref[rows, :] = image
            return sums[0] + image * image, sums[1] + image * image_0
        image_ref[rows, :] = image
        return (sums[0] + image * image,)

    zero = jnp.zeros((GROUP, knot_ref.shape[1]), F32)
    start = (zero, zero) if later else (zero,)
    sums = lax.fori_loop(0, knot_ref.shape[0] // GROUP, one_group, start, unroll=2)
    scalars = [norm] + [jnp.sum(part, keepdims=True) for part in sums]
    if later:
        scalars += [norm_0, square_0]
    scalars = with_scalars(jnp.zeros((8, 128), F32), list(enumerate(scalars)))
    for device in range(scalar_out.shape[0]):
        scalar_out[device] = scalars


def output_kernel(
    live_ref, own_scalar_ref, scalar_ref, star_0_ref, star_h_ref, att_0_ref, att_h_ref, table_0_ref,
    table_h_ref, value_ref, image_0_ref, image_1_ref, star_out, att_out, cal_out, residual_out,
):
    norm_0, square_0 = [picked(own_scalar_ref[0], which) for which in (3, 4)]
    everyone = scalar_ref[0]
    for device in range(1, scalar_ref.shape[0]):
        everyone = everyone + scalar_ref[device]
    norm_1, square_1, cross = [picked(everyone, which) for which in range(3)]
    step_0 = norm_0 / square_0
    ratio = norm_1 / norm_0
    step_1 = norm_1 / (square_1 + 2.0 * ratio * cross + ratio * ratio * square_0)
    scale = step_0 + step_1 * ratio

    def combined(old, change):
        return scale * old + step_1 * (old - step_0 * change)

    star_out[...] = combined(star_0_ref[...], star_h_ref[...])
    att_out[...] = combined(att_0_ref[...], att_h_ref[...])
    cal = combined(table_0_ref[KNOT_ROWS:, :], table_h_ref[KNOT_ROWS:, :])
    cal_out[...] = jnp.concatenate([cal[:, :128], cal[:, 128:]], axis=0)
    values = value_ref[...] * live_mask(live_ref, 0, value_ref.shape)
    residual_out[...] = values - scale * image_0_ref[...] - step_1 * image_1_ref[...]


def in_vmem(count):
    return [pl.BlockSpec(memory_space=pltpu.VMEM)] * count


def in_smem(count):
    return [pl.BlockSpec(memory_space=pltpu.SMEM)] * count


def in_hbm(count):
    return [pl.BlockSpec(memory_space=pltpu.HBM)] * count


def shaped(*shape):
    return jax.ShapeDtypeStruct(shape, F32)


ARRIVE_PARAMS = pltpu.CompilerParams(vmem_limit_bytes=60 * 1024 * 1024)
PARAMS = pltpu.CompilerParams(vmem_limit_bytes=40 * 1024 * 1024)
PASS_COST = pl.CostEstimate(flops=3_000_000_000, bytes_accessed=1_000_000, transcendentals=0)
SMALL_COST = pl.CostEstimate(flops=1_000_000, bytes_accessed=600_000, transcendentals=0)


def on_device(
    obs_star, obs_knot, obs_frac, star_coef, att_coef, cal_coef, tile_cal, live_tiles, obs_value
):
    n_stars, n_seg = lax.axis_size("stars"), lax.axis_size("seg")
    tile_count, width = obs_star.shape
    tile_row = tile_cal[None, :]
    place = lax.axis_index("seg").astype(jnp.int32)[None]
    image_shape = shaped(tile_count, width)
    table_shape = shaped(TABLE_ROWS, COARSE)
    star_shape = shaped(STAR_ROWS, COARSE)

    def knot_backward(values, *scalars):
        arrive = not scalars
        observed = (values, cal_coef, tile_row, obs_knot, obs_frac, att_coef)
        scratch = [pltpu.VMEM((2 * KNOT_HALF, COARSE), F32)]
        if arrive:
            scratch += [pltpu.VMEM(array.shape, array.dtype) for array in observed]
            scratch += [pltpu.SemaphoreType.DMA((len(observed),))]
        return pl.pallas_call(
            functools.partial(knot_backward_kernel, arrive),
            out_shape=(shaped(n_stars, TABLE_ROWS // n_stars, COARSE), shaped(8, COARSE)),
            in_specs=in_smem(2) + (in_hbm if arrive else in_vmem)(len(observed)) + in_vmem(len(scalars)),
            out_specs=tuple(in_vmem(2)),
            scratch_shapes=scratch,
            compiler_params=ARRIVE_PARAMS if arrive else PARAMS,
            cost_estimate=PASS_COST,
            name="knot_backward",
        )(live_tiles, place, *observed, *scalars)

    def star_backward(values, edges):
        return pl.pallas_call(
            star_backward_kernel,
            out_shape=shaped(STAR_ROWS + 8, COARSE),
            in_specs=in_smem(1) + in_vmem(4),
            out_specs=in_vmem(1)[0],
            scratch_shapes=[pltpu.VMEM((2 * STAR_ROWS, COARSE), F32)],
            compiler_params=PARAMS,
            cost_estimate=PASS_COST,
            name="star_backward",
        )(live_tiles, obs_star, star_coef, values, edges)

    def star_forward(star):
        return pl.pallas_call(
            star_forward_kernel,
            out_shape=image_shape,
            in_specs=in_vmem(3),
            out_specs=in_vmem(1)[0],
            scratch_shapes=[pltpu.VMEM((2 * STAR_ROWS, COARSE), BF16)],
            compiler_params=PARAMS,
            cost_estimate=PASS_COST,
            name="star_forward",
        )(obs_star, star_coef, star)

    def knot_forward(*arrays):
        later = len(arrays) > 3
        return pl.pallas_call(
            functools.partial(knot_forward_kernel, n_stars, n_seg, later),
            out_shape=(image_shape, table_shape, shaped(n_stars * n_seg if later else 1, 8, 128)),
            in_specs=in_smem(2) + in_vmem(5 + len(arrays)),
            out_specs=tuple(in_vmem(3)),
            scratch_shapes=[
                pltpu.VMEM((2 * KNOT_HALF, COARSE), BF16),
                pltpu.VMEM((tile_count, width), F32),
            ],
            compiler_params=PARAMS,
            cost_estimate=PASS_COST,
            name="knot_forward",
        )(live_tiles, place, obs_knot, obs_frac, att_coef, cal_coef, tile_row, *arrays)

    def swap(blocks, axes):
        return lax.all_to_all(blocks, axes, 0, 0)

    def partner(array, axis, distance):
        return lax.ppermute(array, axis, [(i, i ^ distance) for i in range(lax.axis_size(axis))])

    def half(values, *scalars):
        table, edges = knot_backward(values, *scalars)
        star = star_backward(values, edges)
        distances = [1 << bit for bit in range(n_seg.bit_length() - 1)]
        for distance in distances[:-1]:
            star = star + partner(star, "seg", distance)
        blocks, star = pl.pallas_call(
            sum_kernel,
            out_shape=(shaped(n_stars, TABLE_ROWS // n_stars + 8, COARSE), star_shape),
            in_specs=in_vmem(3),
            out_specs=tuple(in_vmem(2)),
            compiler_params=PARAMS,
            cost_estimate=SMALL_COST,
            name="table_sum",
        )(swap(table, "stars"), star, partner(star, "seg", distances[-1]))
        return star_forward(star), star, swap(blocks, "stars")

    star_image, star_0, blocks = half(obs_value)
    image_0, table_0, scalars = knot_forward(star_image, star_0, blocks)
    star_image, star_h, blocks = half(image_0, scalars[0])
    image_1, table_h, scalars = knot_forward(star_image, star_h, blocks, star_0, table_0, image_0)

    def star_order(star):
        return star.reshape(5, STAR_DEV)

    def att_order(table):
        att = table[:KNOT_ROWS].reshape(4, FINE, COARSE)
        return att.transpose(0, 2, 1).reshape(4, KNOT_DEV)

    return pl.pallas_call(
        output_kernel,
        out_shape=(shaped(5, STAR_DEV), shaped(4, KNOT_DEV), shaped(CALB_DEV, width), image_shape),
        in_specs=in_smem(1) + in_vmem(11),
        out_specs=tuple(in_vmem(4)),
        compiler_params=PARAMS,
        cost_estimate=SMALL_COST,
        name="outputs",
    )(
        live_tiles, scalars, swap(scalars, ("stars", "seg")), star_order(star_0), star_order(star_h),
        att_order(table_0), att_order(table_h), table_0, table_h, obs_value, image_0, image_1,
    )


def solution(mesh):
    placed = (
        P(("stars", "seg"), None),
        P(("stars", "seg"), None),
        P(("stars", "seg"), None),
        P(None, ("stars", "seg"), None),
        P(None, ("stars", "seg"), None),
        P(("stars", "seg"), None),
        P(("stars", "seg")),
        P(("stars", "seg")),
        P(("stars", "seg"), None),
    )
    return jax.shard_map(
        on_device,
        mesh=mesh,
        in_specs=placed,
        out_specs=(P(None, "stars"), P(None, "seg"), P("seg", None), P(("stars", "seg"), None)),
        check_vma=False,
    )
```

```python
import functools

import jax
import jax.numpy as jnp
from jax import lax
from jax.experimental import pallas as pl
from jax.experimental.pallas import tpu as pltpu
from jax.sharding import PartitionSpec as P

STAR_DEV = 8192
KNOT_DEV = 8192
CALB_DEV = 256
FINE = 32
COARSE = 256
GROUP = 16
SLOT = 8
STAR_ROWS = 5 * FINE
KNOT_ROWS = 4 * FINE
TABLE_ROWS = KNOT_ROWS + CALB_DEV // 2
BF16 = jnp.bfloat16
F32 = jnp.float32
SCALAR_LANE = 64
KNOT_HALF = KNOT_ROWS + 32


def two_parts(values):
    high = values.astype(BF16)
    return high, (values - high.astype(F32)).astype(BF16)


def rows_and_columns(shape):
    return lax.broadcasted_iota(jnp.int32, shape, 0), lax.broadcasted_iota(jnp.int32, shape, 1)


def one_hot(index_row, size):
    width = index_row.shape[1]
    row = jnp.broadcast_to(index_row.astype(F32), (16, width)).astype(BF16)
    rows = jnp.concatenate([row] * (size // 16), axis=0)
    places, _ = rows_and_columns((size, width))
    places = places.astype(F32).astype(BF16)
    return jnp.where(places == rows, jnp.ones((), BF16), jnp.zeros((), BF16))


def spline_weights(fraction):
    remain = 1.0 - fraction
    square = fraction * fraction
    cubed = square * fraction
    return (
        remain * remain * remain / 6.0,
        (3.0 * cubed - 6.0 * square + 4.0) / 6.0,
        (-3.0 * cubed + 3.0 * square + 3.0 * fraction + 1.0) / 6.0,
        cubed / 6.0,
    )


def weight_columns(weights, fine, tile):
    rows, _ = rows_and_columns((FINE + 8, weights[0].shape[1]))
    behind = rows - fine[tile : tile + 1]
    result = jnp.zeros(behind.shape, F32)
    for offset in range(4):
        result = jnp.where(behind == offset, weights[offset][tile : tile + 1], result)
    return result


def product(left, right, contract):
    return lax.dot_general(left, right, (contract, ((), ())), preferred_element_type=F32)


def live_mask(live_ref, first, shape):
    rows, _ = rows_and_columns(shape)
    return (rows + first < live_ref[0]).astype(F32)


def store_rows(out_ref, begin, rows):
    block = out_ref.shape[1]
    for offset in range(0, rows.shape[0], 8):
        where = begin + offset
        out_ref[where // block, where % block : where % block + 8, :] = rows[offset : offset + 8]


def scatter(first, values, observed, knot_acc, star_acc):
    knot_ref, frac_ref, att_coef_ref, star_ref, star_coef_ref = observed
    rows = pl.ds(first, GROUP)
    knot, star = knot_ref[rows, :], star_ref[rows, :]
    knot_coarse, knot_fine = knot >> 5, knot & (FINE - 1)
    star_coarse, star_fine = star & (COARSE - 1), star >> 8
    weights = spline_weights(frac_ref[rows, :])
    terms = [att_coef_ref[comp, rows, :] * values for comp in range(4)]
    parts = [two_parts(star_coef_ref[comp, rows, :] * values) for comp in range(5)]
    parts = [pair[half].astype(F32) for half in range(2) for pair in parts]
    width = knot.shape[1]
    fine_rows, _ = rows_and_columns((FINE, width))
    knot_left, knot_right, star_left, star_right = [], [], [], []
    for tile in range(GROUP):
        here = slice(tile, tile + 1)
        knot_right.append(one_hot(knot_coarse[here], COARSE))
        columns = weight_columns(weights, knot_fine, tile)
        spread = jnp.concatenate(
            [term[here] * columns[:FINE] for term in terms]
            + [term[here] * columns[FINE:] for term in terms],
            axis=0,
        )
        knot_left.append(jnp.concatenate(two_parts(spread), axis=0))
        star_right.append(one_hot(star_coarse[here], COARSE))
        chosen = fine_rows == star_fine[here]
        star_left.append(
            jnp.concatenate([jnp.where(chosen, part[here], 0.0) for part in parts], axis=0).astype(BF16)
        )
    knot_acc[...] += product(
        jnp.concatenate(knot_left, axis=1), jnp.concatenate(knot_right, axis=1), ((1,), (1,))
    )
    star_acc[...] += product(
        jnp.concatenate(star_left, axis=1), jnp.concatenate(star_right, axis=1), ((1,), (1,))
    )


def scatter_calibration(values, tile_cal_ref, table_out):
    blocks = product(
        one_hot(tile_cal_ref[...], CALB_DEV), jnp.concatenate(two_parts(values), axis=1), ((1,), (0,))
    )
    width = values.shape[1]
    blocks = blocks[:, :width] + blocks[:, width:]
    blocks = jnp.concatenate([blocks[: CALB_DEV // 2], blocks[CALB_DEV // 2 :]], axis=1)
    store_rows(table_out, KNOT_ROWS, blocks)


def scatter_end(place_ref, scalars, knot_acc, star_acc, table_out, star_out):
    lane = lax.broadcasted_iota(jnp.int32, (8, 128), 1)
    row = lax.broadcasted_iota(jnp.int32, (8, 128), 0)
    wide_lane = lax.broadcasted_iota(jnp.int32, (8, COARSE), 1)
    edges = jnp.zeros((8, 128), F32)
    for comp in range(4):
        begin, past = comp * FINE, KNOT_ROWS + comp * 8
        main = knot_acc[begin : begin + FINE] + knot_acc[KNOT_HALF + begin : KNOT_HALF + begin + FINE]
        beyond = knot_acc[past : past + 8] + knot_acc[KNOT_HALF + past : KNOT_HALF + past + 8]
        moved = pltpu.roll(beyond, 1, 1)
        top = main[:8] + jnp.where(wide_lane > 0, moved, 0.0)
        store_rows(table_out, begin, top)
        store_rows(table_out, begin + 8, main[8:])
        tail, head = moved[:, :128], top[:, :128]
        if comp:
            tail = pltpu.roll(tail, 2 * comp, 1)
        head = pltpu.roll(head, 2 * comp + 1, 1)
        edges = jnp.where((lane == 2 * comp) & (row < 3), tail, edges)
        edges = jnp.where((lane == 2 * comp + 1) & (row < 3), head, edges)
    edges = with_scalars(pltpu.roll(edges, SLOT * place_ref[0], 1), scalars)
    star_out[:STAR_ROWS] = star_acc[:STAR_ROWS] + star_acc[STAR_ROWS:]
    star_out[STAR_ROWS:] = jnp.concatenate([edges, jnp.zeros_like(edges)], axis=1)


def first_kernel(live_ref, place_ref, *refs):
    sources, (table_out, star_out, knot_acc, star_acc) = refs[:8], refs[8:12]
    buffers, sems = refs[12:20], refs[20]
    copies = [
        pltpu.make_async_copy(source, target, sems.at[which])
        for which, (source, target) in enumerate(zip(sources, buffers))
    ]
    for copy in copies:
        copy.start()
    value_ref, cal_coef_ref, tile_cal_ref, *observed = buffers
    knot_acc[...] = jnp.zeros_like(knot_acc)
    star_acc[...] = jnp.zeros_like(star_acc)
    for copy in copies[:3]:
        copy.wait()
    values = value_ref[...] * live_mask(live_ref, 0, value_ref.shape)
    scatter_calibration(values * cal_coef_ref[...], tile_cal_ref, table_out)
    for copy in copies[3:]:
        copy.wait()

    @pl.loop(0, value_ref.shape[0] // GROUP)
    def _(group):
        first = pl.multiple_of(group * GROUP, GROUP)
        values = value_ref[pl.ds(first, GROUP), :]
        scatter(first, values * live_mask(live_ref, first, values.shape), observed, knot_acc, star_acc)

    scatter_end(place_ref, [], knot_acc, star_acc, table_out, star_out)


def sum_kernel(block_ref, own_ref, other_ref, out_ref, star_out):
    total = block_ref[0]
    for device in range(1, block_ref.shape[0]):
        total = total + block_ref[device]
    star = own_ref[...] + other_ref[...]
    star_out[...] = star[:STAR_ROWS]
    for device in range(block_ref.shape[0]):
        out_ref[device, :-8] = total
        out_ref[device, -8:] = star[STAR_ROWS:]


def picked(array, which):
    row = lax.broadcasted_iota(jnp.int32, array.shape, 0)
    lane = lax.broadcasted_iota(jnp.int32, array.shape, 1)
    chosen = (row == 0) & (lane == SCALAR_LANE + which)
    return jnp.sum(jnp.where(chosen, array, 0.0), keepdims=True)


def with_scalars(array, scalars):
    row = lax.broadcasted_iota(jnp.int32, array.shape, 0)
    lane = lax.broadcasted_iota(jnp.int32, array.shape, 1)
    for which, value in scalars:
        array = jnp.where((row == 0) & (lane == SCALAR_LANE + which), value, array)
    return array


def first_step(edges):
    return picked(edges, 0), picked(edges, 1)


def star_forward_kernel(star_ref, star_coef_ref, star_x_ref, image_ref, star_parts_ref):
    star_x = star_x_ref[...]
    star_high, star_low = two_parts(star_x)
    star_parts_ref[:STAR_ROWS] = star_high
    star_parts_ref[STAR_ROWS:] = star_low

    @pl.loop(0, star_ref.shape[0] // GROUP)
    def _(group):
        rows = pl.ds(pl.multiple_of(group * GROUP, GROUP), GROUP)
        star = star_ref[rows, :]
        coarse, fine = star & (COARSE - 1), star >> 8
        coef = [star_coef_ref[comp, rows, :] for comp in range(5)]
        tiles = [slice(tile, tile + 1) for tile in range(GROUP)]
        hot = jnp.concatenate([one_hot(coarse[here], COARSE) for here in tiles], axis=1)
        found = product(star_parts_ref[...], hot, ((1,), (0,)))
        width = star.shape[1]
        fine_rows, _ = rows_and_columns((FINE, width))
        image_rows = []
        for tile, here in enumerate(tiles):
            across = slice(tile * width, (tile + 1) * width)

            def part(comp):
                begin = comp * FINE
                return (
                    found[begin : begin + FINE, across]
                    + found[STAR_ROWS + begin : STAR_ROWS + begin + FINE, across]
                )

            both = sum(coef[comp][here] * part(comp) for comp in range(5))
            both = jnp.where(fine_rows == fine[here], both, 0.0)
            both = both[:8] + both[8:16] + both[16:24] + both[24:]
            image_rows.append(jnp.sum(both, axis=0, keepdims=True))
        image_ref[rows, :] = jnp.concatenate(image_rows, axis=0)


def received_table(n_stars, n_seg, place_ref, block_ref):
    segment = place_ref[0]
    lane = lax.broadcasted_iota(jnp.int32, (8, 128), 1)
    row = lax.broadcasted_iota(jnp.int32, (8, 128), 0)
    edges = block_ref[0, -8:, :128]
    for block in range(1, n_stars):
        edges = edges + block_ref[block, -8:, :128]

    def slot(which):
        return pltpu.roll(edges, 128 - SLOT * jnp.clip(which, 0, n_seg - 1), 1)

    before, own, after = slot(segment - 1), slot(segment), slot(segment + 1)
    before = jnp.where(segment > 0, before, 0.0)
    ahead = jnp.where(lane % 2 == 0, own, 0.0) + pltpu.roll(jnp.where(lane % 2 == 1, after, 0.0), 127, 1)
    ahead = jnp.where((segment < n_seg - 1) & (lane < 8) & (row < 3), ahead, 0.0)

    table = block_ref[:, :-8, :].reshape(TABLE_ROWS, COARSE)
    pieces = []
    for comp in range(4):
        shifted = pltpu.roll(before, 128 - 2 * comp, 1) if comp else before
        shifted = jnp.where((lane == 0) & (row < 3), shifted, 0.0)
        top = table[comp * FINE : comp * FINE + 8]
        pieces.append(top + jnp.concatenate([shifted, jnp.zeros_like(shifted)], axis=1))
        pieces.append(table[comp * FINE + 8 : (comp + 1) * FINE])
    return jnp.concatenate(pieces + [table[KNOT_ROWS:]], axis=0), ahead, edges


def gather_ready(table, ahead, cal_coef_ref, tile_cal_ref, star_image_ref, knot_parts_ref, cal_ref):
    wide_lane = lax.broadcasted_iota(jnp.int32, (8, COARSE), 1)
    beyond = []
    for comp in range(4):
        moved = pltpu.roll(table[comp * FINE : comp * FINE + 8], COARSE - 1, 1)
        last = pltpu.roll(ahead, 127 - 2 * comp, 1)
        beyond.append(jnp.where(wide_lane == COARSE - 1, jnp.concatenate([last, last], axis=1), moved))
    knot_high, knot_low = two_parts(jnp.concatenate([table[:KNOT_ROWS]] + beyond, axis=0))
    knot_parts_ref[:KNOT_HALF] = knot_high
    knot_parts_ref[KNOT_HALF:] = knot_low

    blocks = jnp.concatenate([table[KNOT_ROWS:, :128], table[KNOT_ROWS:, 128:]], axis=0)
    rows = product(
        one_hot(tile_cal_ref[...], CALB_DEV), jnp.concatenate(two_parts(blocks), axis=1), ((0,), (0,))
    )
    cal_ref[...] = (rows[:, :128] + rows[:, 128:]) * cal_coef_ref[...] + star_image_ref[...]


def gather(first, live_ref, observed, knot_parts_ref, cal_ref):
    knot_ref, frac_ref, att_coef_ref = observed
    rows = pl.ds(first, GROUP)
    knot = knot_ref[rows, :]
    coarse, fine = knot >> 5, knot & (FINE - 1)
    weights = spline_weights(frac_ref[rows, :])
    coef = [att_coef_ref[comp, rows, :] for comp in range(4)]
    tiles = [slice(tile, tile + 1) for tile in range(GROUP)]
    hot = jnp.concatenate([one_hot(coarse[here], COARSE) for here in tiles], axis=1)
    found = product(knot_parts_ref[...], hot, ((1,), (0,)))
    width = knot.shape[1]
    image_rows = []
    for tile, here in enumerate(tiles):
        across = slice(tile * width, (tile + 1) * width)

        def part(begin, size):
            return (
                found[begin : begin + size, across]
                + found[KNOT_HALF + begin : KNOT_HALF + begin + size, across]
            )

        columns = weight_columns(weights, fine, tile)
        main = sum(coef[comp][here] * part(comp * FINE, FINE) for comp in range(4))
        past = sum(coef[comp][here] * part(KNOT_ROWS + comp * 8, 8) for comp in range(4))
        both = main * columns[:FINE]
        both = both[:8] + both[8:16] + both[16:24] + both[24:] + past * columns[FINE:]
        image_rows.append(jnp.sum(both, axis=0, keepdims=True))
    image = jnp.concatenate(image_rows, axis=0) + cal_ref[rows, :]
    return image * live_mask(live_ref, first, image.shape)


def squares(array):
    return jnp.sum(array * array, keepdims=True)


def middle_kernel(
    n_stars, n_seg, live_ref, place_ref, knot_ref, frac_ref, att_coef_ref, star_ref, star_coef_ref,
    cal_coef_ref, tile_cal_ref, star_image_ref, star_x_ref, block_ref, image_ref, table_out, scatter_out,
    star_out, knot_parts_ref, cal_ref, knot_acc, star_acc,
):
    table, ahead, _ = received_table(n_stars, n_seg, place_ref, block_ref)
    table_out[...] = table
    norm = squares(star_x_ref[...]) / n_seg + squares(table) / n_stars
    gather_ready(table, ahead, cal_coef_ref, tile_cal_ref, star_image_ref, knot_parts_ref, cal_ref)
    knot_acc[...] = jnp.zeros_like(knot_acc)
    star_acc[...] = jnp.zeros_like(star_acc)
    observed = (knot_ref, frac_ref, att_coef_ref)
    every = (knot_ref, frac_ref, att_coef_ref, star_ref, star_coef_ref)
    groups = knot_ref.shape[0] // GROUP
    image = gather(0, live_ref, observed, knot_parts_ref, cal_ref)
    image_ref[:GROUP, :] = image

    def one_group(group, total):
        first = pl.multiple_of(group * GROUP, GROUP)
        following = pl.multiple_of(first + GROUP, GROUP)
        values = image_ref[pl.ds(first, GROUP), :]
        image = gather(following, live_ref, observed, knot_parts_ref, cal_ref)
        scatter(first, values, every, knot_acc, star_acc)
        image_ref[pl.ds(following, GROUP), :] = image
        return total + image * image

    total = lax.fori_loop(0, groups - 1, one_group, image * image)
    first = (groups - 1) * GROUP
    scatter(first, image_ref[first:, :], every, knot_acc, star_acc)
    scatter_calibration(image_ref[...] * cal_coef_ref[...], tile_cal_ref, scatter_out)
    scalars = [(0, norm), (1, jnp.sum(total, keepdims=True))]
    scatter_end(place_ref, scalars, knot_acc, star_acc, scatter_out, star_out)


def last_kernel(
    n_stars, n_seg, live_ref, place_ref, knot_ref, frac_ref, att_coef_ref, cal_coef_ref, tile_cal_ref,
    star_image_ref, star_x_ref, block_ref, star_0_ref, table_0_ref, image_0_ref, image_ref, table_out,
    scalar_out, knot_parts_ref, cal_ref,
):
    table, ahead, edges = received_table(n_stars, n_seg, place_ref, block_ref)
    table_out[...] = table
    norm_0, square_0 = first_step(edges)
    step = norm_0 / square_0
    norm = (
        squares(star_0_ref[...] - step * star_x_ref[...]) / n_seg
        + squares(table_0_ref[...] - step * table) / n_stars
    )
    gather_ready(table, ahead, cal_coef_ref, tile_cal_ref, star_image_ref, knot_parts_ref, cal_ref)

    def one_group(group, sums):
        first = pl.multiple_of(group * GROUP, GROUP)
        rows = pl.ds(first, GROUP)
        image_0 = image_0_ref[rows, :]
        image = gather(first, live_ref, (knot_ref, frac_ref, att_coef_ref), knot_parts_ref, cal_ref)
        image = image_0 - step * image
        image_ref[rows, :] = image
        return sums[0] + image * image, sums[1] + image * image_0

    zero = jnp.zeros((GROUP, knot_ref.shape[1]), F32)
    sums = lax.fori_loop(0, knot_ref.shape[0] // GROUP, one_group, (zero, zero))
    scalars = [norm] + [jnp.sum(part, keepdims=True) for part in sums] + [norm_0, square_0]
    scalars = with_scalars(jnp.zeros((8, 128), F32), list(enumerate(scalars)))
    for device in range(scalar_out.shape[0]):
        scalar_out[device] = scalars


def output_kernel(
    live_ref, own_scalar_ref, scalar_ref, star_0_ref, star_h_ref, att_0_ref, att_h_ref, table_0_ref,
    table_h_ref, value_ref, image_0_ref, image_1_ref, star_out, att_out, cal_out, residual_out,
):
    norm_0, square_0 = [picked(own_scalar_ref[0], which) for which in (3, 4)]
    everyone = scalar_ref[0]
    for device in range(1, scalar_ref.shape[0]):
        everyone = everyone + scalar_ref[device]
    norm_1, square_1, cross = [picked(everyone, which) for which in range(3)]
    step_0 = norm_0 / square_0
    ratio = norm_1 / norm_0
    step_1 = norm_1 / (square_1 + 2.0 * ratio * cross + ratio * ratio * square_0)
    scale = step_0 + step_1 * ratio

    def combined(old, change):
        return scale * old + step_1 * (old - step_0 * change)

    star_out[...] = combined(star_0_ref[...], star_h_ref[...])
    att_out[...] = combined(att_0_ref[...], att_h_ref[...])
    cal = combined(table_0_ref[KNOT_ROWS:, :], table_h_ref[KNOT_ROWS:, :])
    cal_out[...] = jnp.concatenate([cal[:, :128], cal[:, 128:]], axis=0)
    values = value_ref[...] * live_mask(live_ref, 0, value_ref.shape)
    residual_out[...] = values - scale * image_0_ref[...] - step_1 * image_1_ref[...]


def in_vmem(count):
    return [pl.BlockSpec(memory_space=pltpu.VMEM)] * count


def in_smem(count):
    return [pl.BlockSpec(memory_space=pltpu.SMEM)] * count


def in_hbm(count):
    return [pl.BlockSpec(memory_space=pltpu.HBM)] * count


def shaped(*shape):
    return jax.ShapeDtypeStruct(shape, F32)


ARRIVE_PARAMS = pltpu.CompilerParams(vmem_limit_bytes=60 * 1024 * 1024)
PARAMS = pltpu.CompilerParams(vmem_limit_bytes=40 * 1024 * 1024)
PASS_COST = pl.CostEstimate(flops=3_000_000_000, bytes_accessed=1_000_000, transcendentals=0)
SMALL_COST = pl.CostEstimate(flops=1_000_000, bytes_accessed=600_000, transcendentals=0)


def on_device(
    obs_star, obs_knot, obs_frac, star_coef, att_coef, cal_coef, tile_cal, live_tiles, obs_value
):
    n_stars, n_seg = lax.axis_size("stars"), lax.axis_size("seg")
    tile_count, width = obs_star.shape
    tile_row = tile_cal[None, :]
    place = lax.axis_index("seg").astype(jnp.int32)[None]
    image_shape = shaped(tile_count, width)
    table_shape = shaped(TABLE_ROWS, COARSE)
    star_shape = shaped(STAR_ROWS, COARSE)
    sent_shapes = (shaped(n_stars, TABLE_ROWS // n_stars, COARSE), shaped(STAR_ROWS + 8, COARSE))
    sums = [pltpu.VMEM((2 * KNOT_HALF, COARSE), F32), pltpu.VMEM((2 * STAR_ROWS, COARSE), F32)]
    ready = [pltpu.VMEM((2 * KNOT_HALF, COARSE), BF16), pltpu.VMEM((tile_count, width), F32)]

    def first_scatter():
        observed = (obs_value, cal_coef, tile_row, obs_knot, obs_frac, att_coef, obs_star, star_coef)
        buffers = [pltpu.VMEM(array.shape, array.dtype) for array in observed]
        return pl.pallas_call(
            first_kernel,
            out_shape=sent_shapes,
            in_specs=in_smem(2) + in_hbm(len(observed)),
            out_specs=tuple(in_vmem(2)),
            scratch_shapes=sums + buffers + [pltpu.SemaphoreType.DMA((len(observed),))],
            compiler_params=ARRIVE_PARAMS,
            cost_estimate=PASS_COST,
            name="first_scatter",
        )(live_tiles, place, *observed)

    def middle(*received):
        observed = (obs_knot, obs_frac, att_coef, obs_star, star_coef, cal_coef, tile_row)
        return pl.pallas_call(
            functools.partial(middle_kernel, n_stars, n_seg),
            out_shape=(image_shape, table_shape, *sent_shapes),
            in_specs=in_smem(2) + in_vmem(len(observed) + len(received)),
            out_specs=tuple(in_vmem(4)),
            scratch_shapes=ready + sums,
            compiler_params=PARAMS,
            cost_estimate=PASS_COST,
            name="gather_and_scatter",
        )(live_tiles, place, *observed, *received)

    def last_gather(*received):
        observed = (obs_knot, obs_frac, att_coef, cal_coef, tile_row)
        return pl.pallas_call(
            functools.partial(last_kernel, n_stars, n_seg),
            out_shape=(image_shape, table_shape, shaped(n_stars * n_seg, 8, 128)),
            in_specs=in_smem(2) + in_vmem(len(observed) + len(received)),
            out_specs=tuple(in_vmem(3)),
            scratch_shapes=ready,
            compiler_params=PARAMS,
            cost_estimate=PASS_COST,
            name="last_gather",
        )(live_tiles, place, *observed, *received)

    def star_forward(star):
        return pl.pallas_call(
            star_forward_kernel,
            out_shape=image_shape,
            in_specs=in_vmem(3),
            out_specs=in_vmem(1)[0],
            scratch_shapes=[pltpu.VMEM((2 * STAR_ROWS, COARSE), BF16)],
            compiler_params=PARAMS,
            cost_estimate=PASS_COST,
            name="star_forward",
        )(obs_star, star_coef, star)

    def swap(blocks, axes):
        return lax.all_to_all(blocks, axes, 0, 0)

    def partner(array, axis, distance):
        return lax.ppermute(array, axis, [(i, i ^ distance) for i in range(lax.axis_size(axis))])

    def reduced(table, star):
        distances = [1 << bit for bit in range(n_seg.bit_length() - 1)]
        for distance in distances[:-1]:
            star = star + partner(star, "seg", distance)
        blocks, star = pl.pallas_call(
            sum_kernel,
            out_shape=(shaped(n_stars, TABLE_ROWS // n_stars + 8, COARSE), star_shape),
            in_specs=in_vmem(3),
            out_specs=tuple(in_vmem(2)),
            compiler_params=PARAMS,
            cost_estimate=SMALL_COST,
            name="table_sum",
        )(swap(table, "stars"), star, partner(star, "seg", distances[-1]))
        return star_forward(star), star, swap(blocks, "stars")

    first = reduced(*first_scatter())
    star_0 = first[1]
    image_0, table_0, *sent = middle(*first)
    second = reduced(*sent)
    star_h = second[1]
    image_1, table_h, scalars = last_gather(*second, star_0, table_0, image_0)

    def star_order(star):
        return star.reshape(5, STAR_DEV)

    def att_order(table):
        att = table[:KNOT_ROWS].reshape(4, FINE, COARSE)
        return att.transpose(0, 2, 1).reshape(4, KNOT_DEV)

    return pl.pallas_call(
        output_kernel,
        out_shape=(shaped(5, STAR_DEV), shaped(4, KNOT_DEV), shaped(CALB_DEV, width), image_shape),
        in_specs=in_smem(1) + in_vmem(11),
        out_specs=tuple(in_vmem(4)),
        compiler_params=PARAMS,
        cost_estimate=SMALL_COST,
        name="outputs",
    )(
        live_tiles, scalars, swap(scalars, ("stars", "seg")), star_order(star_0), star_order(star_h),
        att_order(table_0), att_order(table_h), table_0, table_h, obs_value, image_0, image_1,
    )


def solution(mesh):
    placed = (
        P(("stars", "seg"), None),
        P(("stars", "seg"), None),
        P(("stars", "seg"), None),
        P(None, ("stars", "seg"), None),
        P(None, ("stars", "seg"), None),
        P(("stars", "seg"), None),
        P(("stars", "seg")),
        P(("stars", "seg")),
        P(("stars", "seg"), None),
    )
    return jax.shard_map(
        on_device,
        mesh=mesh,
        in_specs=placed,
        out_specs=(P(None, "stars"), P(None, "seg"), P("seg", None), P(("stars", "seg"), None)),
        check_vma=False,
    )
```

```python
import functools

import jax
import jax.numpy as jnp
from jax import lax
from jax.experimental import pallas as pl
from jax.experimental.pallas import tpu as pltpu
from jax.sharding import PartitionSpec as P

STAR_DEV = 8192
KNOT_DEV = 8192
CALB_DEV = 256
FINE = 32
COARSE = 256
GROUP = 16
SLOT = 8
STAR_ROWS = 5 * FINE
KNOT_ROWS = 4 * FINE
TABLE_ROWS = KNOT_ROWS + CALB_DEV // 2
BF16 = jnp.bfloat16
F32 = jnp.float32
SCALAR_LANE = 64
PAST_ROWS = 16
KNOT_HALF = KNOT_ROWS + PAST_ROWS


def two_parts(values):
    high = values.astype(BF16)
    return high, (values - high.astype(F32)).astype(BF16)


def rows_and_columns(shape):
    return lax.broadcasted_iota(jnp.int32, shape, 0), lax.broadcasted_iota(jnp.int32, shape, 1)


def packed_rows(row, size):
    wide = jnp.broadcast_to(row.astype(F32), (16, row.shape[1])).astype(BF16)
    return jnp.concatenate([wide] * (size // 16), axis=0)


def matches(index_row, size):
    places, _ = rows_and_columns((size, index_row.shape[1]))
    return places.astype(F32).astype(BF16) == packed_rows(index_row, size)


def one_hot(index_row, size):
    return jnp.where(matches(index_row, size), jnp.ones((), BF16), jnp.zeros((), BF16))


def spline_weights(fraction):
    remain = 1.0 - fraction
    square = fraction * fraction
    cubed = square * fraction
    return (
        remain * remain * remain / 6.0,
        (3.0 * cubed - 6.0 * square + 4.0) / 6.0,
        (-3.0 * cubed + 3.0 * square + 3.0 * fraction + 1.0) / 6.0,
        cubed / 6.0,
    )


def weight_columns(weights, fine_row, tile, places):
    behind = places - fine_row
    result = jnp.zeros(behind.shape, F32)
    for offset in range(4):
        result = jnp.where(behind == offset, weights[offset][tile : tile + 1], result)
    return result


def near_and_past(weights, fine, tile):
    width = fine.shape[1]
    fine_row = fine[tile : tile + 1]
    near, _ = rows_and_columns((FINE, width))
    past, _ = rows_and_columns((PAST_ROWS, width))
    past = FINE + (past & 3)
    return weight_columns(weights, fine_row, tile, near), weight_columns(weights, fine_row, tile, past)


def past_terms(terms, here):
    rows, _ = rows_and_columns((PAST_ROWS, terms[0].shape[1]))
    result = jnp.broadcast_to(terms[3][here], rows.shape)
    for comp in range(2, -1, -1):
        result = jnp.where(rows < 4 * (comp + 1), terms[comp][here], result)
    return result


def product(left, right, contract):
    return lax.dot_general(left, right, (contract, ((), ())), preferred_element_type=F32)


def live_mask(live_ref, first, shape):
    rows, _ = rows_and_columns(shape)
    return (rows + first < live_ref[0]).astype(F32)


def store_rows(out_ref, begin, rows):
    block = out_ref.shape[1]
    for offset in range(0, rows.shape[0], 8):
        where = begin + offset
        out_ref[where // block, where % block : where % block + 8, :] = rows[offset : offset + 8]


def scatter(first, values, observed, knot_acc, star_acc):
    knot_ref, frac_ref, att_coef_ref, star_ref, star_coef_ref = observed
    rows = pl.ds(first, GROUP)
    knot, star = knot_ref[rows, :], star_ref[rows, :]
    knot_coarse, knot_fine = knot >> 5, knot & (FINE - 1)
    star_coarse, star_fine = star & (COARSE - 1), star >> 8
    weights = spline_weights(frac_ref[rows, :])
    terms = [att_coef_ref[comp, rows, :] * values for comp in range(4)]
    parts = [two_parts(star_coef_ref[comp, rows, :] * values) for comp in range(5)]
    parts = [pair[half].astype(F32) for half in range(2) for pair in parts]
    knot_left, knot_right, star_left, star_right = [], [], [], []
    for tile in range(GROUP):
        here = slice(tile, tile + 1)
        knot_right.append(one_hot(knot_coarse[here], COARSE))
        near, past = near_and_past(weights, knot_fine, tile)
        spread = jnp.concatenate(
            [term[here] * near for term in terms] + [past_terms(terms, here) * past], axis=0
        )
        knot_left.append(jnp.concatenate(two_parts(spread), axis=0))
        star_right.append(one_hot(star_coarse[here], COARSE))
        chosen = matches(star_fine[here], FINE)
        star_left.append(
            jnp.concatenate(
                [jnp.where(chosen, packed_rows(part[here], FINE), jnp.zeros((), BF16)) for part in parts],
                axis=0,
            )
        )
    knot_acc[...] += product(
        jnp.concatenate(knot_left, axis=1), jnp.concatenate(knot_right, axis=1), ((1,), (1,))
    )
    star_acc[...] += product(
        jnp.concatenate(star_left, axis=1), jnp.concatenate(star_right, axis=1), ((1,), (1,))
    )


def scatter_calibration(values, tile_cal_ref, table_out):
    blocks = product(
        one_hot(tile_cal_ref[...], CALB_DEV), jnp.concatenate(two_parts(values), axis=1), ((1,), (0,))
    )
    width = values.shape[1]
    blocks = blocks[:, :width] + blocks[:, width:]
    blocks = jnp.concatenate([blocks[: CALB_DEV // 2], blocks[CALB_DEV // 2 :]], axis=1)
    store_rows(table_out, KNOT_ROWS, blocks)


def scatter_end(place_ref, scalars, knot_acc, star_acc, table_out, star_out):
    lane = lax.broadcasted_iota(jnp.int32, (8, 128), 1)
    row = lax.broadcasted_iota(jnp.int32, (8, 128), 0)
    wide_lane = lax.broadcasted_iota(jnp.int32, (8, COARSE), 1)
    wide_row = lax.broadcasted_iota(jnp.int32, (8, COARSE), 0)
    edges = jnp.zeros((8, 128), F32)
    for comp in range(4):
        begin, past = comp * FINE, KNOT_ROWS + comp // 2 * 8
        main = knot_acc[begin : begin + FINE] + knot_acc[KNOT_HALF + begin : KNOT_HALF + begin + FINE]
        beyond = knot_acc[past : past + 8] + knot_acc[KNOT_HALF + past : KNOT_HALF + past + 8]
        if comp % 2:
            beyond = pltpu.roll(beyond, 4, 0)
        moved = pltpu.roll(jnp.where(wide_row < 3, beyond, 0.0), 1, 1)
        top = main[:8] + jnp.where(wide_lane > 0, moved, 0.0)
        store_rows(table_out, begin, top)
        store_rows(table_out, begin + 8, main[8:])
        tail, head = moved[:, :128], top[:, :128]
        if comp:
            tail = pltpu.roll(tail, 2 * comp, 1)
        head = pltpu.roll(head, 2 * comp + 1, 1)
        edges = jnp.where((lane == 2 * comp) & (row < 3), tail, edges)
        edges = jnp.where((lane == 2 * comp + 1) & (row < 3), head, edges)
    edges = with_scalars(pltpu.roll(edges, SLOT * place_ref[0], 1), scalars)
    star_out[:STAR_ROWS] = star_acc[:STAR_ROWS] + star_acc[STAR_ROWS:]
    star_out[STAR_ROWS:] = jnp.concatenate([edges, jnp.zeros_like(edges)], axis=1)


def first_kernel(live_ref, place_ref, *refs):
    sources, (table_out, star_out, knot_acc, star_acc) = refs[:8], refs[8:12]
    buffers, sems = refs[12:20], refs[20]
    copies = [
        pltpu.make_async_copy(source, target, sems.at[which])
        for which, (source, target) in enumerate(zip(sources, buffers))
    ]
    for copy in copies:
        copy.start()
    value_ref, cal_coef_ref, tile_cal_ref, *observed = buffers
    knot_acc[...] = jnp.zeros_like(knot_acc)
    star_acc[...] = jnp.zeros_like(star_acc)
    for copy in copies[:3]:
        copy.wait()
    values = value_ref[...] * live_mask(live_ref, 0, value_ref.shape)
    scatter_calibration(values * cal_coef_ref[...], tile_cal_ref, table_out)
    for copy in copies[3:]:
        copy.wait()

    @pl.loop(0, value_ref.shape[0] // GROUP)
    def _(group):
        first = pl.multiple_of(group * GROUP, GROUP)
        values = value_ref[pl.ds(first, GROUP), :]
        scatter(first, values * live_mask(live_ref, first, values.shape), observed, knot_acc, star_acc)

    scatter_end(place_ref, [], knot_acc, star_acc, table_out, star_out)


def sum_kernel(block_ref, own_ref, other_ref, out_ref, star_out):
    total = block_ref[0]
    for device in range(1, block_ref.shape[0]):
        total = total + block_ref[device]
    star = own_ref[...] + other_ref[...]
    star_out[...] = star[:STAR_ROWS]
    total = jnp.concatenate([total[:, :128], total[:, 128:], star[STAR_ROWS:, :128]], axis=0)
    for device in range(block_ref.shape[0]):
        out_ref[device] = total


def picked(array, which):
    row = lax.broadcasted_iota(jnp.int32, array.shape, 0)
    lane = lax.broadcasted_iota(jnp.int32, array.shape, 1)
    chosen = (row == 0) & (lane == SCALAR_LANE + which)
    return jnp.sum(jnp.where(chosen, array, 0.0), keepdims=True)


def with_scalars(array, scalars):
    row = lax.broadcasted_iota(jnp.int32, array.shape, 0)
    lane = lax.broadcasted_iota(jnp.int32, array.shape, 1)
    for which, value in scalars:
        array = jnp.where((row == 0) & (lane == SCALAR_LANE + which), value, array)
    return array


def first_step(edges):
    return picked(edges, 0), picked(edges, 1)


def star_forward_kernel(star_ref, star_coef_ref, star_x_ref, image_ref, star_parts_ref):
    star_x = star_x_ref[...]
    star_high, star_low = two_parts(star_x)
    star_parts_ref[:STAR_ROWS] = star_high
    star_parts_ref[STAR_ROWS:] = star_low

    @pl.loop(0, star_ref.shape[0] // GROUP)
    def _(group):
        rows = pl.ds(pl.multiple_of(group * GROUP, GROUP), GROUP)
        star = star_ref[rows, :]
        coarse, fine = star & (COARSE - 1), star >> 8
        coef = [star_coef_ref[comp, rows, :] for comp in range(5)]
        tiles = [slice(tile, tile + 1) for tile in range(GROUP)]
        hot = jnp.concatenate([one_hot(coarse[here], COARSE) for here in tiles], axis=1)
        found = product(star_parts_ref[...], hot, ((1,), (0,)))
        width = star.shape[1]
        fine_rows, _ = rows_and_columns((FINE, width))
        image_rows = []
        for tile, here in enumerate(tiles):
            across = slice(tile * width, (tile + 1) * width)

            def part(comp):
                begin = comp * FINE
                return (
                    found[begin : begin + FINE, across]
                    + found[STAR_ROWS + begin : STAR_ROWS + begin + FINE, across]
                )

            both = sum(coef[comp][here] * part(comp) for comp in range(5))
            both = jnp.where(fine_rows == fine[here], both, 0.0)
            both = both[:8] + both[8:16] + both[16:24] + both[24:]
            image_rows.append(jnp.sum(both, axis=0, keepdims=True))
        image_ref[rows, :] = jnp.concatenate(image_rows, axis=0)


def received_table(n_stars, n_seg, place_ref, block_ref):
    segment = place_ref[0]
    lane = lax.broadcasted_iota(jnp.int32, (8, 128), 1)
    row = lax.broadcasted_iota(jnp.int32, (8, 128), 0)
    edges = block_ref[0, -8:, :]
    for block in range(1, n_stars):
        edges = edges + block_ref[block, -8:, :]

    def slot(which):
        return pltpu.roll(edges, 128 - SLOT * jnp.clip(which, 0, n_seg - 1), 1)

    before, own, after = slot(segment - 1), slot(segment), slot(segment + 1)
    before = jnp.where(segment > 0, before, 0.0)
    ahead = jnp.where(lane % 2 == 0, own, 0.0) + pltpu.roll(jnp.where(lane % 2 == 1, after, 0.0), 127, 1)
    ahead = jnp.where((segment < n_seg - 1) & (lane < 8) & (row < 3), ahead, 0.0)

    size = TABLE_ROWS // n_stars
    table = jnp.concatenate([block_ref[:, :size, :], block_ref[:, size : 2 * size, :]], axis=2)
    table = table.reshape(TABLE_ROWS, COARSE)
    pieces = []
    for comp in range(4):
        shifted = pltpu.roll(before, 128 - 2 * comp, 1) if comp else before
        shifted = jnp.where((lane == 0) & (row < 3), shifted, 0.0)
        top = table[comp * FINE : comp * FINE + 8]
        pieces.append(top + jnp.concatenate([shifted, jnp.zeros_like(shifted)], axis=1))
        pieces.append(table[comp * FINE + 8 : (comp + 1) * FINE])
    return jnp.concatenate(pieces + [table[KNOT_ROWS:]], axis=0), ahead, edges


def gather_ready(table, ahead, cal_coef_ref, tile_cal_ref, star_image_ref, knot_parts_ref, cal_ref):
    wide_lane = lax.broadcasted_iota(jnp.int32, (8, COARSE), 1)
    row = lax.broadcasted_iota(jnp.int32, (8, COARSE), 0)
    beyond = []
    for comp in range(4):
        moved = pltpu.roll(table[comp * FINE : comp * FINE + 8], COARSE - 1, 1)
        last = pltpu.roll(ahead, 127 - 2 * comp, 1)
        moved = jnp.where(wide_lane == COARSE - 1, jnp.concatenate([last, last], axis=1), moved)
        beyond.append(pltpu.roll(moved, 4, 0) if comp % 2 else moved)
    beyond = [jnp.where(row < 4, beyond[0], beyond[1]), jnp.where(row < 4, beyond[2], beyond[3])]
    knot_high, knot_low = two_parts(jnp.concatenate([table[:KNOT_ROWS]] + beyond, axis=0))
    knot_parts_ref[:KNOT_HALF] = knot_high
    knot_parts_ref[KNOT_HALF:] = knot_low

    blocks = jnp.concatenate([table[KNOT_ROWS:, :128], table[KNOT_ROWS:, 128:]], axis=0)
    rows = product(
        one_hot(tile_cal_ref[...], CALB_DEV), jnp.concatenate(two_parts(blocks), axis=1), ((0,), (0,))
    )
    cal_ref[...] = (rows[:, :128] + rows[:, 128:]) * cal_coef_ref[...] + star_image_ref[...]


def gather(first, live_ref, observed, knot_parts_ref, cal_ref):
    knot_ref, frac_ref, att_coef_ref = observed
    rows = pl.ds(first, GROUP)
    knot = knot_ref[rows, :]
    coarse, fine = knot >> 5, knot & (FINE - 1)
    weights = spline_weights(frac_ref[rows, :])
    coef = [att_coef_ref[comp, rows, :] for comp in range(4)]
    tiles = [slice(tile, tile + 1) for tile in range(GROUP)]
    hot = jnp.concatenate([one_hot(coarse[here], COARSE) for here in tiles], axis=1)
    found = product(knot_parts_ref[...], hot, ((1,), (0,)))
    width = knot.shape[1]
    image_rows = []
    for tile, here in enumerate(tiles):
        across = slice(tile * width, (tile + 1) * width)

        def part(begin, size):
            return (
                found[begin : begin + size, across]
                + found[KNOT_HALF + begin : KNOT_HALF + begin + size, across]
            )

        near, past = near_and_past(weights, fine, tile)
        near = near * sum(coef[comp][here] * part(comp * FINE, FINE) for comp in range(4))
        past = past * past_terms(coef, here) * part(KNOT_ROWS, PAST_ROWS)
        both = near[:8] + near[8:16] + near[16:24] + near[24:] + past[:8] + past[8:]
        image_rows.append(jnp.sum(both, axis=0, keepdims=True))
    image = jnp.concatenate(image_rows, axis=0) + cal_ref[rows, :]
    return image * live_mask(live_ref, first, image.shape)


def squares(array):
    return jnp.sum(array * array, keepdims=True)


def middle_kernel(
    n_stars, n_seg, live_ref, place_ref, knot_ref, frac_ref, att_coef_ref, star_ref, star_coef_ref,
    cal_coef_ref, tile_cal_ref, star_image_ref, star_x_ref, block_ref, image_ref, table_out, scatter_out,
    star_out, knot_parts_ref, cal_ref, knot_acc, star_acc,
):
    table, ahead, _ = received_table(n_stars, n_seg, place_ref, block_ref)
    table_out[...] = table
    norm = squares(star_x_ref[...]) / n_seg + squares(table) / n_stars
    gather_ready(table, ahead, cal_coef_ref, tile_cal_ref, star_image_ref, knot_parts_ref, cal_ref)
    knot_acc[...] = jnp.zeros_like(knot_acc)
    star_acc[...] = jnp.zeros_like(star_acc)
    observed = (knot_ref, frac_ref, att_coef_ref)
    every = (knot_ref, frac_ref, att_coef_ref, star_ref, star_coef_ref)
    groups = knot_ref.shape[0] // GROUP
    image = gather(0, live_ref, observed, knot_parts_ref, cal_ref)
    image_ref[:GROUP, :] = image

    def one_group(group, total):
        first = pl.multiple_of(group * GROUP, GROUP)
        following = pl.multiple_of(first + GROUP, GROUP)
        values = image_ref[pl.ds(first, GROUP), :]
        image = gather(following, live_ref, observed, knot_parts_ref, cal_ref)
        scatter(first, values, every, knot_acc, star_acc)
        image_ref[pl.ds(following, GROUP), :] = image
        return total + image * image

    total = lax.fori_loop(0, groups - 1, one_group, image * image)
    first = (groups - 1) * GROUP
    scatter(first, image_ref[first:, :], every, knot_acc, star_acc)
    scatter_calibration(image_ref[...] * cal_coef_ref[...], tile_cal_ref, scatter_out)
    scalars = [(0, norm), (1, jnp.sum(total, keepdims=True))]
    scatter_end(place_ref, scalars, knot_acc, star_acc, scatter_out, star_out)


def last_kernel(
    n_stars, n_seg, live_ref, place_ref, knot_ref, frac_ref, att_coef_ref, cal_coef_ref, tile_cal_ref,
    star_image_ref, star_x_ref, block_ref, star_0_ref, table_0_ref, image_0_ref, image_ref, table_out,
    scalar_out, own_scalar_out, knot_parts_ref, cal_ref,
):
    table, ahead, edges = received_table(n_stars, n_seg, place_ref, block_ref)
    table_out[...] = table
    norm_0, square_0 = first_step(edges)
    step = norm_0 / square_0
    norm = (
        squares(star_0_ref[...] - step * star_x_ref[...]) / n_seg
        + squares(table_0_ref[...] - step * table) / n_stars
    )
    gather_ready(table, ahead, cal_coef_ref, tile_cal_ref, star_image_ref, knot_parts_ref, cal_ref)

    def one_group(group, sums):
        first = pl.multiple_of(group * GROUP, GROUP)
        rows = pl.ds(first, GROUP)
        image_0 = image_0_ref[rows, :]
        image = gather(first, live_ref, (knot_ref, frac_ref, att_coef_ref), knot_parts_ref, cal_ref)
        image = image_0 - step * image
        image_ref[rows, :] = image
        return sums[0] + image * image, sums[1] + image * image_0

    zero = jnp.zeros((GROUP, knot_ref.shape[1]), F32)
    sums = lax.fori_loop(0, knot_ref.shape[0] // GROUP, one_group, (zero, zero))
    scalars = [norm] + [jnp.sum(part, keepdims=True) for part in sums] + [norm_0, square_0]
    scalars = with_scalars(jnp.zeros((8, 128), F32), list(enumerate(scalars)))
    own_scalar_out[...] = scalars
    for device in range(scalar_out.shape[0]):
        scalar_out[device] = scalars


def output_kernel(
    live_ref, own_scalar_ref, scalar_ref, star_0_ref, star_h_ref, att_0_ref, att_h_ref, table_0_ref,
    table_h_ref, value_ref, image_0_ref, image_1_ref, star_out, att_out, cal_out, residual_out,
):
    norm_0, square_0 = [picked(own_scalar_ref[...], which) for which in (3, 4)]
    everyone = scalar_ref[0]
    for device in range(1, scalar_ref.shape[0]):
        everyone = everyone + scalar_ref[device]
    norm_1, square_1, cross = [picked(everyone, which) for which in range(3)]
    step_0 = norm_0 / square_0
    ratio = norm_1 / norm_0
    step_1 = norm_1 / (square_1 + 2.0 * ratio * cross + ratio * ratio * square_0)
    scale = step_0 + step_1 * ratio

    def combined(old, change):
        return scale * old + step_1 * (old - step_0 * change)

    star_out[...] = combined(star_0_ref[...], star_h_ref[...])
    att_out[...] = combined(att_0_ref[...], att_h_ref[...])
    cal = combined(table_0_ref[KNOT_ROWS:, :], table_h_ref[KNOT_ROWS:, :])
    cal_out[...] = jnp.concatenate([cal[:, :128], cal[:, 128:]], axis=0)
    values = value_ref[...] * live_mask(live_ref, 0, value_ref.shape)
    residual_out[...] = values - scale * image_0_ref[...] - step_1 * image_1_ref[...]


def in_vmem(count):
    return [pl.BlockSpec(memory_space=pltpu.VMEM)] * count


def in_smem(count):
    return [pl.BlockSpec(memory_space=pltpu.SMEM)] * count


def in_hbm(count):
    return [pl.BlockSpec(memory_space=pltpu.HBM)] * count


def shaped(*shape):
    return jax.ShapeDtypeStruct(shape, F32)


ARRIVE_PARAMS = pltpu.CompilerParams(vmem_limit_bytes=60 * 1024 * 1024)
PARAMS = pltpu.CompilerParams(vmem_limit_bytes=40 * 1024 * 1024)
PASS_COST = pl.CostEstimate(flops=3_000_000_000, bytes_accessed=1_000_000, transcendentals=0)
SMALL_COST = pl.CostEstimate(flops=1_000_000, bytes_accessed=600_000, transcendentals=0)


def on_device(
    obs_star, obs_knot, obs_frac, star_coef, att_coef, cal_coef, tile_cal, live_tiles, obs_value
):
    n_stars, n_seg = lax.axis_size("stars"), lax.axis_size("seg")
    tile_count, width = obs_star.shape
    tile_row = tile_cal[None, :]
    place = lax.axis_index("seg").astype(jnp.int32)[None]
    image_shape = shaped(tile_count, width)
    table_shape = shaped(TABLE_ROWS, COARSE)
    star_shape = shaped(STAR_ROWS, COARSE)
    sent_shapes = (shaped(n_stars, TABLE_ROWS // n_stars, COARSE), shaped(STAR_ROWS + 8, COARSE))
    sums = [pltpu.VMEM((2 * KNOT_HALF, COARSE), F32), pltpu.VMEM((2 * STAR_ROWS, COARSE), F32)]
    ready = [pltpu.VMEM((2 * KNOT_HALF, COARSE), BF16), pltpu.VMEM((tile_count, width), F32)]

    def first_scatter():
        observed = (obs_value, cal_coef, tile_row, obs_knot, obs_frac, att_coef, obs_star, star_coef)
        buffers = [pltpu.VMEM(array.shape, array.dtype) for array in observed]
        return pl.pallas_call(
            first_kernel,
            out_shape=sent_shapes,
            in_specs=in_smem(2) + in_hbm(len(observed)),
            out_specs=tuple(in_vmem(2)),
            scratch_shapes=sums + buffers + [pltpu.SemaphoreType.DMA((len(observed),))],
            compiler_params=ARRIVE_PARAMS,
            cost_estimate=PASS_COST,
            name="first_scatter",
        )(live_tiles, place, *observed)

    def middle(*received):
        observed = (obs_knot, obs_frac, att_coef, obs_star, star_coef, cal_coef, tile_row)
        return pl.pallas_call(
            functools.partial(middle_kernel, n_stars, n_seg),
            out_shape=(image_shape, table_shape, *sent_shapes),
            in_specs=in_smem(2) + in_vmem(len(observed) + len(received)),
            out_specs=tuple(in_vmem(4)),
            scratch_shapes=ready + sums,
            compiler_params=PARAMS,
            cost_estimate=PASS_COST,
            name="gather_and_scatter",
        )(live_tiles, place, *observed, *received)

    def last_gather(*received):
        observed = (obs_knot, obs_frac, att_coef, cal_coef, tile_row)
        return pl.pallas_call(
            functools.partial(last_kernel, n_stars, n_seg),
            out_shape=(image_shape, table_shape, shaped(n_stars * n_seg, 8, 128), shaped(8, 128)),
            in_specs=in_smem(2) + in_vmem(len(observed) + len(received)),
            out_specs=tuple(in_vmem(4)),
            scratch_shapes=ready,
            compiler_params=PARAMS,
            cost_estimate=PASS_COST,
            name="last_gather",
        )(live_tiles, place, *observed, *received)

    def star_forward(star):
        return pl.pallas_call(
            star_forward_kernel,
            out_shape=image_shape,
            in_specs=in_vmem(3),
            out_specs=in_vmem(1)[0],
            scratch_shapes=[pltpu.VMEM((2 * STAR_ROWS, COARSE), BF16)],
            compiler_params=PARAMS,
            cost_estimate=PASS_COST,
            name="star_forward",
        )(obs_star, star_coef, star)

    def swap(blocks, axes):
        return lax.all_to_all(blocks, axes, 0, 0)

    def partner(array, axis, distance):
        return lax.ppermute(array, axis, [(i, i ^ distance) for i in range(lax.axis_size(axis))])

    def reduced(table, star):
        distances = [1 << bit for bit in range(n_seg.bit_length() - 1)]
        for distance in distances[:-1]:
            star = star + partner(star, "seg", distance)
        blocks, star = pl.pallas_call(
            sum_kernel,
            out_shape=(shaped(n_stars, 2 * TABLE_ROWS // n_stars + 8, 128), star_shape),
            in_specs=in_vmem(3),
            out_specs=tuple(in_vmem(2)),
            compiler_params=PARAMS,
            cost_estimate=SMALL_COST,
            name="table_sum",
        )(swap(table, "stars"), star, partner(star, "seg", distances[-1]))
        return star_forward(star), star, swap(blocks, "stars")

    first = reduced(*first_scatter())
    star_0 = first[1]
    image_0, table_0, *sent = middle(*first)
    second = reduced(*sent)
    star_h = second[1]
    image_1, table_h, scalars, own_scalars = last_gather(*second, star_0, table_0, image_0)

    def star_order(star):
        return star.reshape(5, STAR_DEV)

    def att_order(table):
        att = table[:KNOT_ROWS].reshape(4, FINE, COARSE)
        return att.transpose(0, 2, 1).reshape(4, KNOT_DEV)

    return pl.pallas_call(
        output_kernel,
        out_shape=(shaped(5, STAR_DEV), shaped(4, KNOT_DEV), shaped(CALB_DEV, width), image_shape),
        in_specs=in_smem(1) + in_vmem(11),
        out_specs=tuple(in_vmem(4)),
        compiler_params=PARAMS,
        cost_estimate=SMALL_COST,
        name="outputs",
    )(
        live_tiles, own_scalars, swap(scalars, ("stars", "seg")), star_order(star_0), star_order(star_h),
        att_order(table_0), att_order(table_h), table_0, table_h, obs_value, image_0, image_1,
    )


def solution(mesh):
    placed = (
        P(("stars", "seg"), None),
        P(("stars", "seg"), None),
        P(("stars", "seg"), None),
        P(None, ("stars", "seg"), None),
        P(None, ("stars", "seg"), None),
        P(("stars", "seg"), None),
        P(("stars", "seg")),
        P(("stars", "seg")),
        P(("stars", "seg"), None),
    )
    return jax.shard_map(
        on_device,
        mesh=mesh,
        in_specs=placed,
        out_specs=(P(None, "stars"), P(None, "seg"), P("seg", None), P(("stars", "seg"), None)),
        check_vma=False,
    )
```

```python
import functools

import jax
import jax.numpy as jnp
from jax import lax
from jax.experimental import pallas as pl
from jax.experimental.pallas import tpu as pltpu
from jax.sharding import PartitionSpec as P

STAR_DEV = 8192
KNOT_DEV = 8192
CALB_DEV = 256
FINE = 32
COARSE = 256
GROUP = 16
SLOT = 8
STAR_ROWS = 5 * FINE
KNOT_ROWS = 4 * FINE
TABLE_ROWS = KNOT_ROWS + CALB_DEV // 2
BF16 = jnp.bfloat16
F32 = jnp.float32
SCALAR_LANE = 64
PAST_ROWS = 16
KNOT_HALF = KNOT_ROWS + PAST_ROWS


def two_parts(values):
    high = values.astype(BF16)
    return high, (values - high.astype(F32)).astype(BF16)


def rows_and_columns(shape):
    return lax.broadcasted_iota(jnp.int32, shape, 0), lax.broadcasted_iota(jnp.int32, shape, 1)


def packed_rows(row, size):
    wide = jnp.broadcast_to(row.astype(F32), (16, row.shape[1])).astype(BF16)
    return jnp.concatenate([wide] * (size // 16), axis=0)


def matches(index_row, size):
    places, _ = rows_and_columns((size, index_row.shape[1]))
    return places.astype(F32).astype(BF16) == packed_rows(index_row, size)


def one_hot(index_row, size):
    return jnp.where(matches(index_row, size), jnp.ones((), BF16), jnp.zeros((), BF16))


def spline_weights(fraction):
    remain = 1.0 - fraction
    square = fraction * fraction
    cubed = square * fraction
    return (
        remain * remain * remain / 6.0,
        (3.0 * cubed - 6.0 * square + 4.0) / 6.0,
        (-3.0 * cubed + 3.0 * square + 3.0 * fraction + 1.0) / 6.0,
        cubed / 6.0,
    )


def weight_columns(weights, fine_row, tile, places):
    behind = places - fine_row
    result = jnp.zeros(behind.shape, F32)
    for offset in range(4):
        result = jnp.where(behind == offset, weights[offset][tile : tile + 1], result)
    return result


def near_and_past(weights, fine, tile):
    width = fine.shape[1]
    fine_row = fine[tile : tile + 1]
    near, _ = rows_and_columns((FINE, width))
    past, _ = rows_and_columns((PAST_ROWS, width))
    past = FINE + (past & 3)
    return weight_columns(weights, fine_row, tile, near), weight_columns(weights, fine_row, tile, past)


def past_terms(terms, here):
    rows, _ = rows_and_columns((PAST_ROWS, terms[0].shape[1]))
    result = jnp.broadcast_to(terms[3][here], rows.shape)
    for comp in range(2, -1, -1):
        result = jnp.where(rows < 4 * (comp + 1), terms[comp][here], result)
    return result


def product(left, right, contract):
    return lax.dot_general(left, right, (contract, ((), ())), preferred_element_type=F32)


def live_mask(live_ref, first, shape):
    rows, _ = rows_and_columns(shape)
    return (rows + first < live_ref[0]).astype(F32)


def store_rows(out_ref, begin, rows):
    block = out_ref.shape[1]
    for offset in range(0, rows.shape[0], 8):
        where = begin + offset
        out_ref[where // block, where % block : where % block + 8, :] = rows[offset : offset + 8]


def prepare(first, values, observed, buffers):
    knot_ref, frac_ref, att_coef_ref, star_ref, star_coef_ref = observed
    rows = pl.ds(first, GROUP)
    knot, star = knot_ref[rows, :], star_ref[rows, :]
    knot_coarse, knot_fine = knot >> 5, knot & (FINE - 1)
    star_coarse, star_fine = star & (COARSE - 1), star >> 8
    weights = spline_weights(frac_ref[rows, :])
    terms = [att_coef_ref[comp, rows, :] * values for comp in range(4)]
    parts = [two_parts(star_coef_ref[comp, rows, :] * values) for comp in range(5)]
    parts = [pair[half].astype(F32) for half in range(2) for pair in parts]
    width = knot.shape[1]
    knot_left, knot_right, star_left, star_right = buffers
    for tile in range(GROUP):
        here = slice(tile, tile + 1)
        across = slice(tile * width, (tile + 1) * width)
        knot_right[:, across] = one_hot(knot_coarse[here], COARSE)
        near, past = near_and_past(weights, knot_fine, tile)
        spread = jnp.concatenate(
            [term[here] * near for term in terms] + [past_terms(terms, here) * past], axis=0
        )
        knot_left[:, across] = jnp.concatenate(two_parts(spread), axis=0)
        star_right[:, across] = one_hot(star_coarse[here], COARSE)
        chosen = matches(star_fine[here], FINE)
        star_left[:, across] = jnp.concatenate(
            [jnp.where(chosen, packed_rows(part[here], FINE), jnp.zeros((), BF16)) for part in parts], axis=0
        )


def multiply(buffers, knot_acc, star_acc):
    knot_left, knot_right, star_left, star_right = buffers
    knot_acc[...] += product(knot_left[...], knot_right[...], ((1,), (1,)))
    star_acc[...] += product(star_left[...], star_right[...], ((1,), (1,)))


def scatter_calibration(values, tile_cal_ref, table_out):
    blocks = product(
        one_hot(tile_cal_ref[...], CALB_DEV), jnp.concatenate(two_parts(values), axis=1), ((1,), (0,))
    )
    width = values.shape[1]
    blocks = blocks[:, :width] + blocks[:, width:]
    blocks = jnp.concatenate([blocks[: CALB_DEV // 2], blocks[CALB_DEV // 2 :]], axis=1)
    store_rows(table_out, KNOT_ROWS, blocks)


def scatter_end(place_ref, scalars, knot_acc, star_acc, table_out, star_out):
    lane = lax.broadcasted_iota(jnp.int32, (8, 128), 1)
    row = lax.broadcasted_iota(jnp.int32, (8, 128), 0)
    wide_lane = lax.broadcasted_iota(jnp.int32, (8, COARSE), 1)
    wide_row = lax.broadcasted_iota(jnp.int32, (8, COARSE), 0)
    edges = jnp.zeros((8, 128), F32)
    for comp in range(4):
        begin, past = comp * FINE, KNOT_ROWS + comp // 2 * 8
        main = knot_acc[begin : begin + FINE] + knot_acc[KNOT_HALF + begin : KNOT_HALF + begin + FINE]
        beyond = knot_acc[past : past + 8] + knot_acc[KNOT_HALF + past : KNOT_HALF + past + 8]
        if comp % 2:
            beyond = pltpu.roll(beyond, 4, 0)
        moved = pltpu.roll(jnp.where(wide_row < 3, beyond, 0.0), 1, 1)
        top = main[:8] + jnp.where(wide_lane > 0, moved, 0.0)
        store_rows(table_out, begin, top)
        store_rows(table_out, begin + 8, main[8:])
        tail, head = moved[:, :128], top[:, :128]
        if comp:
            tail = pltpu.roll(tail, 2 * comp, 1)
        head = pltpu.roll(head, 2 * comp + 1, 1)
        edges = jnp.where((lane == 2 * comp) & (row < 3), tail, edges)
        edges = jnp.where((lane == 2 * comp + 1) & (row < 3), head, edges)
    edges = with_scalars(pltpu.roll(edges, SLOT * place_ref[0], 1), scalars)
    star_out[:STAR_ROWS] = star_acc[:STAR_ROWS] + star_acc[STAR_ROWS:]
    star_out[STAR_ROWS:] = jnp.concatenate([edges, jnp.zeros_like(edges)], axis=1)


def first_kernel(live_ref, place_ref, *refs):
    sources, (table_out, star_out, knot_acc, star_acc) = refs[:8], refs[8:12]
    even, odd, buffers, sems = refs[12:16], refs[16:20], refs[20:28], refs[28]
    copies = [
        pltpu.make_async_copy(source, target, sems.at[which])
        for which, (source, target) in enumerate(zip(sources, buffers))
    ]
    for copy in copies:
        copy.start()
    value_ref, cal_coef_ref, tile_cal_ref, *observed = buffers
    knot_acc[...] = jnp.zeros_like(knot_acc)
    star_acc[...] = jnp.zeros_like(star_acc)
    for copy in copies[:3]:
        copy.wait()
    values = value_ref[...] * live_mask(live_ref, 0, value_ref.shape)
    scatter_calibration(values * cal_coef_ref[...], tile_cal_ref, table_out)
    for copy in copies[3:]:
        copy.wait()

    def build(group, target):
        first = group * GROUP if isinstance(group, int) else pl.multiple_of(group * GROUP, GROUP)
        values = value_ref[pl.ds(first, GROUP), :]
        prepare(first, values * live_mask(live_ref, first, values.shape), observed, target)

    groups = value_ref.shape[0] // GROUP
    build(0, even)

    @pl.loop(0, groups // 2 - 1)
    def _(pair):
        multiply(even, knot_acc, star_acc)
        build(2 * pair + 1, odd)
        multiply(odd, knot_acc, star_acc)
        build(2 * pair + 2, even)

    multiply(even, knot_acc, star_acc)
    build(groups - 1, odd)
    multiply(odd, knot_acc, star_acc)
    scatter_end(place_ref, [], knot_acc, star_acc, table_out, star_out)


def sum_kernel(block_ref, own_ref, other_ref, out_ref, star_out):
    total = block_ref[0]
    for device in range(1, block_ref.shape[0]):
        total = total + block_ref[device]
    star = own_ref[...] + other_ref[...]
    star_out[...] = star[:STAR_ROWS]
    total = jnp.concatenate([total[:, :128], total[:, 128:], star[STAR_ROWS:, :128]], axis=0)
    for device in range(block_ref.shape[0]):
        out_ref[device] = total


def picked(array, which):
    row = lax.broadcasted_iota(jnp.int32, array.shape, 0)
    lane = lax.broadcasted_iota(jnp.int32, array.shape, 1)
    chosen = (row == 0) & (lane == SCALAR_LANE + which)
    return jnp.sum(jnp.where(chosen, array, 0.0), keepdims=True)


def with_scalars(array, scalars):
    row = lax.broadcasted_iota(jnp.int32, array.shape, 0)
    lane = lax.broadcasted_iota(jnp.int32, array.shape, 1)
    for which, value in scalars:
        array = jnp.where((row == 0) & (lane == SCALAR_LANE + which), value, array)
    return array


def first_step(edges):
    return picked(edges, 0), picked(edges, 1)


def in_turn(groups, make, use, even, odd, sums=()):
    make(0, even)

    def pair(index, sums):
        first = 2 * index
        make(first + 1, odd)
        sums = use(first, even, sums)
        make(first + 2, even)
        return use(first + 1, odd, sums)

    sums = lax.fori_loop(0, groups // 2 - 1, pair, sums)
    make(groups - 1, odd)
    return use(groups - 1, odd, use(groups - 2, even, sums))


def group_rows(group):
    return pl.ds(group * GROUP if isinstance(group, int) else pl.multiple_of(group * GROUP, GROUP), GROUP)


def star_forward_kernel(star_ref, star_coef_ref, star_x_ref, image_ref, star_parts_ref, even, odd):
    star_high, star_low = two_parts(star_x_ref[...])
    star_parts_ref[:STAR_ROWS] = star_high
    star_parts_ref[STAR_ROWS:] = star_low
    tiles = [slice(tile, tile + 1) for tile in range(GROUP)]

    def make(group, target):
        coarse = star_ref[group_rows(group), :] & (COARSE - 1)
        hot = jnp.concatenate([one_hot(coarse[here], COARSE) for here in tiles], axis=1)
        target[...] = product(star_parts_ref[...], hot, ((1,), (0,)))

    def use(group, found, sums):
        rows = group_rows(group)
        fine = star_ref[rows, :] >> 8
        coef = [star_coef_ref[comp, rows, :] for comp in range(5)]
        width = fine.shape[1]
        fine_rows, _ = rows_and_columns((FINE, width))
        image_rows = []
        for tile, here in enumerate(tiles):
            across = slice(tile * width, (tile + 1) * width)

            def part(comp):
                begin = comp * FINE
                return (
                    found[begin : begin + FINE, across]
                    + found[STAR_ROWS + begin : STAR_ROWS + begin + FINE, across]
                )

            both = sum(coef[comp][here] * part(comp) for comp in range(5))
            both = jnp.where(fine_rows == fine[here], both, 0.0)
            both = both[:8] + both[8:16] + both[16:24] + both[24:]
            image_rows.append(jnp.sum(both, axis=0, keepdims=True))
        image_ref[rows, :] = jnp.concatenate(image_rows, axis=0)
        return sums

    in_turn(star_ref.shape[0] // GROUP, make, use, even, odd)


def received_table(n_stars, n_seg, place_ref, block_ref):
    segment = place_ref[0]
    lane = lax.broadcasted_iota(jnp.int32, (8, 128), 1)
    row = lax.broadcasted_iota(jnp.int32, (8, 128), 0)
    edges = block_ref[0, -8:, :]
    for block in range(1, n_stars):
        edges = edges + block_ref[block, -8:, :]

    def slot(which):
        return pltpu.roll(edges, 128 - SLOT * jnp.clip(which, 0, n_seg - 1), 1)

    before, own, after = slot(segment - 1), slot(segment), slot(segment + 1)
    before = jnp.where(segment > 0, before, 0.0)
    ahead = jnp.where(lane % 2 == 0, own, 0.0) + pltpu.roll(jnp.where(lane % 2 == 1, after, 0.0), 127, 1)
    ahead = jnp.where((segment < n_seg - 1) & (lane < 8) & (row < 3), ahead, 0.0)

    size = TABLE_ROWS // n_stars
    table = jnp.concatenate([block_ref[:, :size, :], block_ref[:, size : 2 * size, :]], axis=2)
    table = table.reshape(TABLE_ROWS, COARSE)
    pieces = []
    for comp in range(4):
        shifted = pltpu.roll(before, 128 - 2 * comp, 1) if comp else before
        shifted = jnp.where((lane == 0) & (row < 3), shifted, 0.0)
        top = table[comp * FINE : comp * FINE + 8]
        pieces.append(top + jnp.concatenate([shifted, jnp.zeros_like(shifted)], axis=1))
        pieces.append(table[comp * FINE + 8 : (comp + 1) * FINE])
    return jnp.concatenate(pieces + [table[KNOT_ROWS:]], axis=0), ahead, edges


def gather_ready(table, ahead, cal_coef_ref, tile_cal_ref, star_image_ref, knot_parts_ref, cal_ref):
    wide_lane = lax.broadcasted_iota(jnp.int32, (8, COARSE), 1)
    row = lax.broadcasted_iota(jnp.int32, (8, COARSE), 0)
    beyond = []
    for comp in range(4):
        moved = pltpu.roll(table[comp * FINE : comp * FINE + 8], COARSE - 1, 1)
        last = pltpu.roll(ahead, 127 - 2 * comp, 1)
        moved = jnp.where(wide_lane == COARSE - 1, jnp.concatenate([last, last], axis=1), moved)
        beyond.append(pltpu.roll(moved, 4, 0) if comp % 2 else moved)
    beyond = [jnp.where(row < 4, beyond[0], beyond[1]), jnp.where(row < 4, beyond[2], beyond[3])]
    knot_high, knot_low = two_parts(jnp.concatenate([table[:KNOT_ROWS]] + beyond, axis=0))
    knot_parts_ref[:KNOT_HALF] = knot_high
    knot_parts_ref[KNOT_HALF:] = knot_low

    blocks = jnp.concatenate([table[KNOT_ROWS:, :128], table[KNOT_ROWS:, 128:]], axis=0)
    rows = product(
        one_hot(tile_cal_ref[...], CALB_DEV), jnp.concatenate(two_parts(blocks), axis=1), ((0,), (0,))
    )
    cal_ref[...] = (rows[:, :128] + rows[:, 128:]) * cal_coef_ref[...] + star_image_ref[...]


def gather_products(group, knot_ref, knot_parts_ref):
    coarse = knot_ref[group_rows(group), :] >> 5
    hot = [one_hot(coarse[tile : tile + 1], COARSE) for tile in range(GROUP)]
    return product(knot_parts_ref[...], jnp.concatenate(hot, axis=1), ((1,), (0,)))


def gather_image(group, found, live_ref, observed, cal_ref):
    knot_ref, frac_ref, att_coef_ref = observed
    rows = group_rows(group)
    fine = knot_ref[rows, :] & (FINE - 1)
    weights = spline_weights(frac_ref[rows, :])
    coef = [att_coef_ref[comp, rows, :] for comp in range(4)]
    width = fine.shape[1]
    image_rows = []
    for tile in range(GROUP):
        here = slice(tile, tile + 1)
        across = slice(tile * width, (tile + 1) * width)

        def part(begin, size):
            return (
                found[begin : begin + size, across]
                + found[KNOT_HALF + begin : KNOT_HALF + begin + size, across]
            )

        near, past = near_and_past(weights, fine, tile)
        near = near * sum(coef[comp][here] * part(comp * FINE, FINE) for comp in range(4))
        past = past * past_terms(coef, here) * part(KNOT_ROWS, PAST_ROWS)
        both = near[:8] + near[8:16] + near[16:24] + near[24:] + past[:8] + past[8:]
        image_rows.append(jnp.sum(both, axis=0, keepdims=True))
    image = jnp.concatenate(image_rows, axis=0) + cal_ref[rows, :]
    return image * live_mask(live_ref, group * GROUP, image.shape)


def squares(array):
    return jnp.sum(array * array, keepdims=True)


def middle_kernel(
    n_stars, n_seg, live_ref, place_ref, knot_ref, frac_ref, att_coef_ref, star_ref, star_coef_ref,
    cal_coef_ref, tile_cal_ref, star_image_ref, star_x_ref, block_ref, image_ref, table_out, scatter_out,
    star_out, knot_parts_ref, cal_ref, knot_acc, star_acc, *buffers,
):
    table, ahead, _ = received_table(n_stars, n_seg, place_ref, block_ref)
    table_out[...] = table
    norm = squares(star_x_ref[...]) / n_seg + squares(table) / n_stars
    gather_ready(table, ahead, cal_coef_ref, tile_cal_ref, star_image_ref, knot_parts_ref, cal_ref)
    knot_acc[...] = jnp.zeros_like(knot_acc)
    star_acc[...] = jnp.zeros_like(star_acc)
    observed = (knot_ref, frac_ref, att_coef_ref)
    every = (knot_ref, frac_ref, att_coef_ref, star_ref, star_coef_ref)
    groups = knot_ref.shape[0] // GROUP
    even, odd = buffers[:4], buffers[4:]

    def build(group, target):
        found = gather_products(group, knot_ref, knot_parts_ref)
        image = gather_image(group, found, live_ref, observed, cal_ref)
        image_ref[group_rows(group), :] = image
        prepare(group_rows(group).start, image, every, target)
        return image * image

    total = build(0, even)

    def pair(index, total):
        multiply(even, knot_acc, star_acc)
        total = total + build(2 * index + 1, odd)
        multiply(odd, knot_acc, star_acc)
        return total + build(2 * index + 2, even)

    total = lax.fori_loop(0, groups // 2 - 1, pair, total)
    multiply(even, knot_acc, star_acc)
    total = total + build(groups - 1, odd)
    multiply(odd, knot_acc, star_acc)
    scatter_calibration(image_ref[...] * cal_coef_ref[...], tile_cal_ref, scatter_out)
    scalars = [(0, norm), (1, jnp.sum(total, keepdims=True))]
    scatter_end(place_ref, scalars, knot_acc, star_acc, scatter_out, star_out)


def last_kernel(
    n_stars, n_seg, live_ref, place_ref, knot_ref, frac_ref, att_coef_ref, cal_coef_ref, tile_cal_ref,
    star_image_ref, star_x_ref, block_ref, star_0_ref, table_0_ref, image_0_ref, image_ref, table_out,
    scalar_out, own_scalar_out, knot_parts_ref, cal_ref, even, odd,
):
    table, ahead, edges = received_table(n_stars, n_seg, place_ref, block_ref)
    table_out[...] = table
    norm_0, square_0 = first_step(edges)
    step = norm_0 / square_0
    norm = (
        squares(star_0_ref[...] - step * star_x_ref[...]) / n_seg
        + squares(table_0_ref[...] - step * table) / n_stars
    )
    gather_ready(table, ahead, cal_coef_ref, tile_cal_ref, star_image_ref, knot_parts_ref, cal_ref)

    def make(group, target):
        target[...] = gather_products(group, knot_ref, knot_parts_ref)

    def use(group, found, sums):
        rows = group_rows(group)
        image_0 = image_0_ref[rows, :]
        image = gather_image(group, found, live_ref, (knot_ref, frac_ref, att_coef_ref), cal_ref)
        image = image_0 - step * image
        image_ref[rows, :] = image
        return sums[0] + image * image, sums[1] + image * image_0

    zero = jnp.zeros((GROUP, knot_ref.shape[1]), F32)
    sums = in_turn(knot_ref.shape[0] // GROUP, make, use, even, odd, (zero, zero))
    scalars = [norm] + [jnp.sum(part, keepdims=True) for part in sums] + [norm_0, square_0]
    scalars = with_scalars(jnp.zeros((8, 128), F32), list(enumerate(scalars)))
    own_scalar_out[...] = scalars
    for device in range(scalar_out.shape[0]):
        scalar_out[device] = scalars


def output_kernel(
    live_ref, own_scalar_ref, scalar_ref, star_0_ref, star_h_ref, att_0_ref, att_h_ref, table_0_ref,
    table_h_ref, value_ref, image_0_ref, image_1_ref, star_out, att_out, cal_out, residual_out,
):
    norm_0, square_0 = [picked(own_scalar_ref[...], which) for which in (3, 4)]
    everyone = scalar_ref[0]
    for device in range(1, scalar_ref.shape[0]):
        everyone = everyone + scalar_ref[device]
    norm_1, square_1, cross = [picked(everyone, which) for which in range(3)]
    step_0 = norm_0 / square_0
    ratio = norm_1 / norm_0
    step_1 = norm_1 / (square_1 + 2.0 * ratio * cross + ratio * ratio * square_0)
    scale = step_0 + step_1 * ratio

    def combined(old, change):
        return scale * old + step_1 * (old - step_0 * change)

    star_out[...] = combined(star_0_ref[...], star_h_ref[...])
    att_out[...] = combined(att_0_ref[...], att_h_ref[...])
    cal = combined(table_0_ref[KNOT_ROWS:, :], table_h_ref[KNOT_ROWS:, :])
    cal_out[...] = jnp.concatenate([cal[:, :128], cal[:, 128:]], axis=0)
    values = value_ref[...] * live_mask(live_ref, 0, value_ref.shape)
    residual_out[...] = values - scale * image_0_ref[...] - step_1 * image_1_ref[...]


def in_vmem(count):
    return [pl.BlockSpec(memory_space=pltpu.VMEM)] * count


def in_smem(count):
    return [pl.BlockSpec(memory_space=pltpu.SMEM)] * count


def in_hbm(count):
    return [pl.BlockSpec(memory_space=pltpu.HBM)] * count


def shaped(*shape):
    return jax.ShapeDtypeStruct(shape, F32)


ARRIVE_PARAMS = pltpu.CompilerParams(vmem_limit_bytes=60 * 1024 * 1024)
PARAMS = pltpu.CompilerParams(vmem_limit_bytes=40 * 1024 * 1024)
PASS_COST = pl.CostEstimate(flops=3_000_000_000, bytes_accessed=1_000_000, transcendentals=0)
SMALL_COST = pl.CostEstimate(flops=1_000_000, bytes_accessed=600_000, transcendentals=0)


def on_device(
    obs_star, obs_knot, obs_frac, star_coef, att_coef, cal_coef, tile_cal, live_tiles, obs_value
):
    n_stars, n_seg = lax.axis_size("stars"), lax.axis_size("seg")
    tile_count, width = obs_star.shape
    tile_row = tile_cal[None, :]
    place = lax.axis_index("seg").astype(jnp.int32)[None]
    image_shape = shaped(tile_count, width)
    table_shape = shaped(TABLE_ROWS, COARSE)
    star_shape = shaped(STAR_ROWS, COARSE)
    sent_shapes = (shaped(n_stars, TABLE_ROWS // n_stars, COARSE), shaped(STAR_ROWS + 8, COARSE))
    sums = [pltpu.VMEM((2 * KNOT_HALF, COARSE), F32), pltpu.VMEM((2 * STAR_ROWS, COARSE), F32)]
    lanes = GROUP * width
    sizes = (2 * KNOT_HALF, COARSE, 2 * STAR_ROWS, COARSE)
    turns = [pltpu.VMEM((size, lanes), BF16) for size in sizes] * 2
    ready = [pltpu.VMEM((2 * KNOT_HALF, COARSE), BF16), pltpu.VMEM((tile_count, width), F32)]

    def first_scatter():
        observed = (obs_value, cal_coef, tile_row, obs_knot, obs_frac, att_coef, obs_star, star_coef)
        buffers = [pltpu.VMEM(array.shape, array.dtype) for array in observed]
        return pl.pallas_call(
            first_kernel,
            out_shape=sent_shapes,
            in_specs=in_smem(2) + in_hbm(len(observed)),
            out_specs=tuple(in_vmem(2)),
            scratch_shapes=sums + turns + buffers + [pltpu.SemaphoreType.DMA((len(observed),))],
            compiler_params=ARRIVE_PARAMS,
            cost_estimate=PASS_COST,
            name="first_scatter",
        )(live_tiles, place, *observed)

    def middle(*received):
        observed = (obs_knot, obs_frac, att_coef, obs_star, star_coef, cal_coef, tile_row)
        return pl.pallas_call(
            functools.partial(middle_kernel, n_stars, n_seg),
            out_shape=(image_shape, table_shape, *sent_shapes),
            in_specs=in_smem(2) + in_vmem(len(observed) + len(received)),
            out_specs=tuple(in_vmem(4)),
            scratch_shapes=ready + sums + turns,
            compiler_params=PARAMS,
            cost_estimate=PASS_COST,
            name="gather_and_scatter",
        )(live_tiles, place, *observed, *received)

    def last_gather(*received):
        observed = (obs_knot, obs_frac, att_coef, cal_coef, tile_row)
        return pl.pallas_call(
            functools.partial(last_kernel, n_stars, n_seg),
            out_shape=(image_shape, table_shape, shaped(n_stars * n_seg, 8, 128), shaped(8, 128)),
            in_specs=in_smem(2) + in_vmem(len(observed) + len(received)),
            out_specs=tuple(in_vmem(4)),
            scratch_shapes=ready + [pltpu.VMEM((2 * KNOT_HALF, lanes), F32)] * 2,
            compiler_params=PARAMS,
            cost_estimate=PASS_COST,
            name="last_gather",
        )(live_tiles, place, *observed, *received)

    def star_forward(star):
        return pl.pallas_call(
            star_forward_kernel,
            out_shape=image_shape,
            in_specs=in_vmem(3),
            out_specs=in_vmem(1)[0],
            scratch_shapes=[pltpu.VMEM((2 * STAR_ROWS, COARSE), BF16)] + [pltpu.VMEM((2 * STAR_ROWS, lanes), F32)] * 2,
            compiler_params=PARAMS,
            cost_estimate=PASS_COST,
            name="star_forward",
        )(obs_star, star_coef, star)

    def swap(blocks, axes):
        return lax.all_to_all(blocks, axes, 0, 0)

    def partner(array, axis, distance):
        return lax.ppermute(array, axis, [(i, i ^ distance) for i in range(lax.axis_size(axis))])

    def reduced(table, star):
        distances = [1 << bit for bit in range(n_seg.bit_length() - 1)]
        for distance in distances[:-1]:
            star = star + partner(star, "seg", distance)
        blocks, star = pl.pallas_call(
            sum_kernel,
            out_shape=(shaped(n_stars, 2 * TABLE_ROWS // n_stars + 8, 128), star_shape),
            in_specs=in_vmem(3),
            out_specs=tuple(in_vmem(2)),
            compiler_params=PARAMS,
            cost_estimate=SMALL_COST,
            name="table_sum",
        )(swap(table, "stars"), star, partner(star, "seg", distances[-1]))
        return star_forward(star), star, swap(blocks, "stars")

    first = reduced(*first_scatter())
    star_0 = first[1]
    image_0, table_0, *sent = middle(*first)
    second = reduced(*sent)
    star_h = second[1]
    image_1, table_h, scalars, own_scalars = last_gather(*second, star_0, table_0, image_0)

    def star_order(star):
        return star.reshape(5, STAR_DEV)

    def att_order(table):
        att = table[:KNOT_ROWS].reshape(4, FINE, COARSE)
        return att.transpose(0, 2, 1).reshape(4, KNOT_DEV)

    return pl.pallas_call(
        output_kernel,
        out_shape=(shaped(5, STAR_DEV), shaped(4, KNOT_DEV), shaped(CALB_DEV, width), image_shape),
        in_specs=in_smem(1) + in_vmem(11),
        out_specs=tuple(in_vmem(4)),
        compiler_params=PARAMS,
        cost_estimate=SMALL_COST,
        name="outputs",
    )(
        live_tiles, own_scalars, swap(scalars, ("stars", "seg")), star_order(star_0), star_order(star_h),
        att_order(table_0), att_order(table_h), table_0, table_h, obs_value, image_0, image_1,
    )


def solution(mesh):
    placed = (
        P(("stars", "seg"), None),
        P(("stars", "seg"), None),
        P(("stars", "seg"), None),
        P(None, ("stars", "seg"), None),
        P(None, ("stars", "seg"), None),
        P(("stars", "seg"), None),
        P(("stars", "seg")),
        P(("stars", "seg")),
        P(("stars", "seg"), None),
    )
    return jax.shard_map(
        on_device,
        mesh=mesh,
        in_specs=placed,
        out_specs=(P(None, "stars"), P(None, "seg"), P("seg", None), P(("stars", "seg"), None)),
        check_vma=False,
    )
```

```python
import functools

import jax
import jax.numpy as jnp
from jax import lax
from jax.experimental import pallas as pl
from jax.experimental.pallas import tpu as pltpu
from jax.sharding import PartitionSpec as P

STAR_DEV = 8192
KNOT_DEV = 8192
CALB_DEV = 256
FINE = 32
COARSE = 256
GROUP = 16
SLOT = 8
STAR_ROWS = 5 * FINE
KNOT_ROWS = 4 * FINE
TABLE_ROWS = KNOT_ROWS + CALB_DEV // 2
BF16 = jnp.bfloat16
F32 = jnp.float32
SCALAR_LANE = 64
PAST_ROWS = 16
KNOT_HALF = KNOT_ROWS + PAST_ROWS


def two_parts(values):
    high = values.astype(BF16)
    return high, (values - high.astype(F32)).astype(BF16)


def rows_and_columns(shape):
    return lax.broadcasted_iota(jnp.int32, shape, 0), lax.broadcasted_iota(jnp.int32, shape, 1)


def packed_rows(row, size):
    wide = jnp.broadcast_to(row.astype(F32), (16, row.shape[1])).astype(BF16)
    return jnp.concatenate([wide] * (size // 16), axis=0)


def matches(index_row, size):
    places, _ = rows_and_columns((size, index_row.shape[1]))
    return places.astype(F32).astype(BF16) == packed_rows(index_row, size)


def one_hot(index_row, size):
    return jnp.where(matches(index_row, size), jnp.ones((), BF16), jnp.zeros((), BF16))


def spline_weights(fraction):
    remain = 1.0 - fraction
    square = fraction * fraction
    cubed = square * fraction
    return (
        remain * remain * remain / 6.0,
        (3.0 * cubed - 6.0 * square + 4.0) / 6.0,
        (-3.0 * cubed + 3.0 * square + 3.0 * fraction + 1.0) / 6.0,
        cubed / 6.0,
    )


def weight_columns(weights, fine_row, tile, places):
    behind = places - fine_row
    result = jnp.zeros(behind.shape, F32)
    for offset in range(4):
        result = jnp.where(behind == offset, weights[offset][tile : tile + 1], result)
    return result


def near_and_past(weights, fine, tile):
    width = fine.shape[1]
    fine_row = fine[tile : tile + 1]
    near, _ = rows_and_columns((FINE, width))
    past, _ = rows_and_columns((PAST_ROWS, width))
    past = FINE + (past & 3)
    return weight_columns(weights, fine_row, tile, near), weight_columns(weights, fine_row, tile, past)


def past_terms(terms, here):
    rows, _ = rows_and_columns((PAST_ROWS, terms[0].shape[1]))
    result = jnp.broadcast_to(terms[3][here], rows.shape)
    for comp in range(2, -1, -1):
        result = jnp.where(rows < 4 * (comp + 1), terms[comp][here], result)
    return result


def product(left, right, contract):
    return lax.dot_general(left, right, (contract, ((), ())), preferred_element_type=F32)


def live_mask(live_ref, first, shape):
    rows, _ = rows_and_columns(shape)
    return (rows + first < live_ref[0]).astype(F32)


def store_rows(out_ref, begin, rows):
    block = out_ref.shape[1]
    for offset in range(0, rows.shape[0], 8):
        where = begin + offset
        out_ref[where // block, where % block : where % block + 8, :] = rows[offset : offset + 8]


class Fresh:
    def __init__(self, knot_ref, frac_ref, star_ref):
        self.refs = knot_ref, frac_ref, star_ref

    def at(self, group):
        rows = group_rows(group)
        knot_ref, frac_ref, star_ref = self.refs
        knot, star = knot_ref[rows, :], star_ref[rows, :]
        weights = spline_weights(frac_ref[rows, :])
        knot_hot = [one_hot((knot >> 5)[tile : tile + 1], COARSE) for tile in range(GROUP)]
        star_hot = [one_hot((star & (COARSE - 1))[tile : tile + 1], COARSE) for tile in range(GROUP)]
        columns = [near_and_past(weights, knot & (FINE - 1), tile) for tile in range(GROUP)]
        return columns, jnp.concatenate(knot_hot, axis=1), jnp.concatenate(star_hot, axis=1)


class Stored:
    def __init__(self, column_ref, knot_hot_ref, star_hot_ref):
        self.refs = column_ref, knot_hot_ref, star_hot_ref

    def columns(self, group):
        column_ref = self.refs[0]
        result = []
        for tile in range(GROUP):
            both = column_ref[group * GROUP + tile]
            result.append((both[:FINE], both[FINE:]))
        return result

    def at(self, group):
        return self.columns(group), self.refs[1][group], self.refs[2][group]


def group_rows(group):
    return pl.ds(group * GROUP if isinstance(group, int) else pl.multiple_of(group * GROUP, GROUP), GROUP)


def factor_kernel(knot_ref, frac_ref, star_ref, after_ref, column_out, knot_hot_out, star_hot_out):
    @pl.loop(0, knot_ref.shape[0] // GROUP)
    def _(group):
        columns, knot_hot, star_hot = Fresh(knot_ref, frac_ref, star_ref).at(group)
        knot_hot_out[group] = knot_hot
        star_hot_out[group] = star_hot
        for tile in range(GROUP):
            column_out[group * GROUP + tile] = jnp.concatenate(columns[tile], axis=0)


def scatter(group, values, factors, coefs, knot_acc, star_acc):
    att_coef_ref, star_ref, star_coef_ref = coefs
    rows = group_rows(group)
    star_fine = star_ref[rows, :] >> 8
    columns, knot_hot, star_hot = factors.at(group)
    terms = [att_coef_ref[comp, rows, :] * values for comp in range(4)]
    parts = [two_parts(star_coef_ref[comp, rows, :] * values) for comp in range(5)]
    parts = [pair[half].astype(F32) for half in range(2) for pair in parts]
    knot_left, star_left = [], []
    for tile in range(GROUP):
        here = slice(tile, tile + 1)
        near, past = columns[tile]
        spread = jnp.concatenate(
            [term[here] * near for term in terms] + [past_terms(terms, here) * past], axis=0
        )
        knot_left.append(jnp.concatenate(two_parts(spread), axis=0))
        chosen = matches(star_fine[here], FINE)
        star_left.append(
            jnp.concatenate(
                [jnp.where(chosen, packed_rows(part[here], FINE), jnp.zeros((), BF16)) for part in parts],
                axis=0,
            )
        )
    knot_acc[...] += product(
        jnp.concatenate(knot_left, axis=1), knot_hot, ((1,), (1,))
    )
    star_acc[...] += product(
        jnp.concatenate(star_left, axis=1), star_hot, ((1,), (1,))
    )


def scatter_calibration(values, tile_cal_ref, table_out):
    blocks = product(
        one_hot(tile_cal_ref[...], CALB_DEV), jnp.concatenate(two_parts(values), axis=1), ((1,), (0,))
    )
    width = values.shape[1]
    blocks = blocks[:, :width] + blocks[:, width:]
    blocks = jnp.concatenate([blocks[: CALB_DEV // 2], blocks[CALB_DEV // 2 :]], axis=1)
    store_rows(table_out, KNOT_ROWS, blocks)


def scatter_end(place_ref, scalars, knot_acc, star_acc, table_out, star_out):
    lane = lax.broadcasted_iota(jnp.int32, (8, 128), 1)
    row = lax.broadcasted_iota(jnp.int32, (8, 128), 0)
    wide_lane = lax.broadcasted_iota(jnp.int32, (8, COARSE), 1)
    wide_row = lax.broadcasted_iota(jnp.int32, (8, COARSE), 0)
    edges = jnp.zeros((8, 128), F32)
    for comp in range(4):
        begin, past = comp * FINE, KNOT_ROWS + comp // 2 * 8
        main = knot_acc[begin : begin + FINE] + knot_acc[KNOT_HALF + begin : KNOT_HALF + begin + FINE]
        beyond = knot_acc[past : past + 8] + knot_acc[KNOT_HALF + past : KNOT_HALF + past + 8]
        if comp % 2:
            beyond = pltpu.roll(beyond, 4, 0)
        moved = pltpu.roll(jnp.where(wide_row < 3, beyond, 0.0), 1, 1)
        top = main[:8] + jnp.where(wide_lane > 0, moved, 0.0)
        store_rows(table_out, begin, top)
        store_rows(table_out, begin + 8, main[8:])
        tail, head = moved[:, :128], top[:, :128]
        if comp:
            tail = pltpu.roll(tail, 2 * comp, 1)
        head = pltpu.roll(head, 2 * comp + 1, 1)
        edges = jnp.where((lane == 2 * comp) & (row < 3), tail, edges)
        edges = jnp.where((lane == 2 * comp + 1) & (row < 3), head, edges)
    edges = with_scalars(pltpu.roll(edges, SLOT * place_ref[0], 1), scalars)
    star_out[:STAR_ROWS] = star_acc[:STAR_ROWS] + star_acc[STAR_ROWS:]
    star_out[STAR_ROWS:] = jnp.concatenate([edges, jnp.zeros_like(edges)], axis=1)


def first_kernel(live_ref, place_ref, *refs):
    sources, (table_out, star_out, knot_acc, star_acc) = refs[:8], refs[8:12]
    buffers, sems = refs[12:20], refs[20]
    copies = [
        pltpu.make_async_copy(source, target, sems.at[which])
        for which, (source, target) in enumerate(zip(sources, buffers))
    ]
    for copy in copies:
        copy.start()
    value_ref, cal_coef_ref, tile_cal_ref, knot_ref, frac_ref, att_coef_ref, star_ref, star_coef_ref = buffers
    factors, coefs = Fresh(knot_ref, frac_ref, star_ref), (att_coef_ref, star_ref, star_coef_ref)
    knot_acc[...] = jnp.zeros_like(knot_acc)
    star_acc[...] = jnp.zeros_like(star_acc)
    for copy in copies[:3]:
        copy.wait()
    values = value_ref[...] * live_mask(live_ref, 0, value_ref.shape)
    scatter_calibration(values * cal_coef_ref[...], tile_cal_ref, table_out)
    for copy in copies[3:]:
        copy.wait()

    @pl.loop(0, value_ref.shape[0] // GROUP)
    def _(group):
        values = value_ref[group_rows(group), :]
        values = values * live_mask(live_ref, group * GROUP, values.shape)
        scatter(group, values, factors, coefs, knot_acc, star_acc)

    scatter_end(place_ref, [], knot_acc, star_acc, table_out, star_out)


def sum_kernel(block_ref, own_ref, other_ref, out_ref, star_out):
    total = block_ref[0]
    for device in range(1, block_ref.shape[0]):
        total = total + block_ref[device]
    star = own_ref[...] + other_ref[...]
    star_out[...] = star[:STAR_ROWS]
    total = jnp.concatenate([total[:, :128], total[:, 128:], star[STAR_ROWS:, :128]], axis=0)
    for device in range(block_ref.shape[0]):
        out_ref[device] = total


def picked(array, which):
    row = lax.broadcasted_iota(jnp.int32, array.shape, 0)
    lane = lax.broadcasted_iota(jnp.int32, array.shape, 1)
    chosen = (row == 0) & (lane == SCALAR_LANE + which)
    return jnp.sum(jnp.where(chosen, array, 0.0), keepdims=True)


def with_scalars(array, scalars):
    row = lax.broadcasted_iota(jnp.int32, array.shape, 0)
    lane = lax.broadcasted_iota(jnp.int32, array.shape, 1)
    for which, value in scalars:
        array = jnp.where((row == 0) & (lane == SCALAR_LANE + which), value, array)
    return array


def first_step(edges):
    return picked(edges, 0), picked(edges, 1)


def star_forward_kernel(star_ref, star_coef_ref, star_hot_ref, star_x_ref, image_ref, star_parts_ref):
    star_x = star_x_ref[...]
    star_high, star_low = two_parts(star_x)
    star_parts_ref[:STAR_ROWS] = star_high
    star_parts_ref[STAR_ROWS:] = star_low

    @pl.loop(0, star_ref.shape[0] // GROUP)
    def _(group):
        rows = pl.ds(pl.multiple_of(group * GROUP, GROUP), GROUP)
        star = star_ref[rows, :]
        fine = star >> 8
        coef = [star_coef_ref[comp, rows, :] for comp in range(5)]
        tiles = [slice(tile, tile + 1) for tile in range(GROUP)]
        found = product(star_parts_ref[...], star_hot_ref[group], ((1,), (0,)))
        width = star.shape[1]
        fine_rows, _ = rows_and_columns((FINE, width))
        image_rows = []
        for tile, here in enumerate(tiles):
            across = slice(tile * width, (tile + 1) * width)

            def part(comp):
                begin = comp * FINE
                return (
                    found[begin : begin + FINE, across]
                    + found[STAR_ROWS + begin : STAR_ROWS + begin + FINE, across]
                )

            both = sum(coef[comp][here] * part(comp) for comp in range(5))
            both = jnp.where(fine_rows == fine[here], both, 0.0)
            both = both[:8] + both[8:16] + both[16:24] + both[24:]
            image_rows.append(jnp.sum(both, axis=0, keepdims=True))
        image_ref[rows, :] = jnp.concatenate(image_rows, axis=0)


def received_table(n_stars, n_seg, place_ref, block_ref):
    segment = place_ref[0]
    lane = lax.broadcasted_iota(jnp.int32, (8, 128), 1)
    row = lax.broadcasted_iota(jnp.int32, (8, 128), 0)
    edges = block_ref[0, -8:, :]
    for block in range(1, n_stars):
        edges = edges + block_ref[block, -8:, :]

    def slot(which):
        return pltpu.roll(edges, 128 - SLOT * jnp.clip(which, 0, n_seg - 1), 1)

    before, own, after = slot(segment - 1), slot(segment), slot(segment + 1)
    before = jnp.where(segment > 0, before, 0.0)
    ahead = jnp.where(lane % 2 == 0, own, 0.0) + pltpu.roll(jnp.where(lane % 2 == 1, after, 0.0), 127, 1)
    ahead = jnp.where((segment < n_seg - 1) & (lane < 8) & (row < 3), ahead, 0.0)

    size = TABLE_ROWS // n_stars
    table = jnp.concatenate([block_ref[:, :size, :], block_ref[:, size : 2 * size, :]], axis=2)
    table = table.reshape(TABLE_ROWS, COARSE)
    pieces = []
    for comp in range(4):
        shifted = pltpu.roll(before, 128 - 2 * comp, 1) if comp else before
        shifted = jnp.where((lane == 0) & (row < 3), shifted, 0.0)
        top = table[comp * FINE : comp * FINE + 8]
        pieces.append(top + jnp.concatenate([shifted, jnp.zeros_like(shifted)], axis=1))
        pieces.append(table[comp * FINE + 8 : (comp + 1) * FINE])
    return jnp.concatenate(pieces + [table[KNOT_ROWS:]], axis=0), ahead, edges


def gather_ready(table, ahead, cal_coef_ref, tile_cal_ref, star_image_ref, knot_parts_ref, cal_ref):
    wide_lane = lax.broadcasted_iota(jnp.int32, (8, COARSE), 1)
    row = lax.broadcasted_iota(jnp.int32, (8, COARSE), 0)
    beyond = []
    for comp in range(4):
        moved = pltpu.roll(table[comp * FINE : comp * FINE + 8], COARSE - 1, 1)
        last = pltpu.roll(ahead, 127 - 2 * comp, 1)
        moved = jnp.where(wide_lane == COARSE - 1, jnp.concatenate([last, last], axis=1), moved)
        beyond.append(pltpu.roll(moved, 4, 0) if comp % 2 else moved)
    beyond = [jnp.where(row < 4, beyond[0], beyond[1]), jnp.where(row < 4, beyond[2], beyond[3])]
    knot_high, knot_low = two_parts(jnp.concatenate([table[:KNOT_ROWS]] + beyond, axis=0))
    knot_parts_ref[:KNOT_HALF] = knot_high
    knot_parts_ref[KNOT_HALF:] = knot_low

    blocks = jnp.concatenate([table[KNOT_ROWS:, :128], table[KNOT_ROWS:, 128:]], axis=0)
    rows = product(
        one_hot(tile_cal_ref[...], CALB_DEV), jnp.concatenate(two_parts(blocks), axis=1), ((0,), (0,))
    )
    cal_ref[...] = (rows[:, :128] + rows[:, 128:]) * cal_coef_ref[...] + star_image_ref[...]


def gather(group, live_ref, factors, att_coef_ref, knot_parts_ref, cal_ref):
    rows = group_rows(group)
    coef = [att_coef_ref[comp, rows, :] for comp in range(4)]
    columns = factors.columns(group)
    found = product(knot_parts_ref[...], factors.refs[1][group], ((1,), (0,)))
    width = cal_ref.shape[1]
    image_rows = []
    for tile in range(GROUP):
        here = slice(tile, tile + 1)
        across = slice(tile * width, (tile + 1) * width)

        def part(begin, size):
            return (
                found[begin : begin + size, across]
                + found[KNOT_HALF + begin : KNOT_HALF + begin + size, across]
            )

        near, past = columns[tile]
        near = near * sum(coef[comp][here] * part(comp * FINE, FINE) for comp in range(4))
        past = past * past_terms(coef, here) * part(KNOT_ROWS, PAST_ROWS)
        both = near[:8] + near[8:16] + near[16:24] + near[24:] + past[:8] + past[8:]
        image_rows.append(jnp.sum(both, axis=0, keepdims=True))
    image = jnp.concatenate(image_rows, axis=0) + cal_ref[rows, :]
    return image * live_mask(live_ref, group * GROUP, image.shape)


def squares(array):
    return jnp.sum(array * array, keepdims=True)


def middle_kernel(
    n_stars, n_seg, live_ref, place_ref, column_ref, knot_hot_ref, star_hot_ref, att_coef_ref, star_ref,
    star_coef_ref, cal_coef_ref, tile_cal_ref, star_image_ref, star_x_ref, block_ref, image_ref, table_out, scatter_out,
    star_out, knot_parts_ref, cal_ref, knot_acc, star_acc,
):
    table, ahead, _ = received_table(n_stars, n_seg, place_ref, block_ref)
    table_out[...] = table
    norm = squares(star_x_ref[...]) / n_seg + squares(table) / n_stars
    gather_ready(table, ahead, cal_coef_ref, tile_cal_ref, star_image_ref, knot_parts_ref, cal_ref)
    knot_acc[...] = jnp.zeros_like(knot_acc)
    star_acc[...] = jnp.zeros_like(star_acc)
    factors = Stored(column_ref, knot_hot_ref, star_hot_ref)
    coefs = (att_coef_ref, star_ref, star_coef_ref)
    groups = star_ref.shape[0] // GROUP
    image = gather(0, live_ref, factors, att_coef_ref, knot_parts_ref, cal_ref)
    image_ref[:GROUP, :] = image

    def one_group(group, total):
        values = image_ref[group_rows(group), :]
        image = gather(group + 1, live_ref, factors, att_coef_ref, knot_parts_ref, cal_ref)
        scatter(group, values, factors, coefs, knot_acc, star_acc)
        image_ref[group_rows(group + 1), :] = image
        return total + image * image

    total = lax.fori_loop(0, groups - 1, one_group, image * image)
    scatter(groups - 1, image_ref[group_rows(groups - 1), :], factors, coefs, knot_acc, star_acc)
    scatter_calibration(image_ref[...] * cal_coef_ref[...], tile_cal_ref, scatter_out)
    scalars = [(0, norm), (1, jnp.sum(total, keepdims=True))]
    scatter_end(place_ref, scalars, knot_acc, star_acc, scatter_out, star_out)


def last_kernel(
    n_stars, n_seg, live_ref, place_ref, column_ref, knot_hot_ref, att_coef_ref, cal_coef_ref, tile_cal_ref,
    star_image_ref, star_x_ref, block_ref, star_0_ref, table_0_ref, image_0_ref, image_ref, table_out,
    scalar_out, own_scalar_out, knot_parts_ref, cal_ref,
):
    table, ahead, edges = received_table(n_stars, n_seg, place_ref, block_ref)
    table_out[...] = table
    norm_0, square_0 = first_step(edges)
    step = norm_0 / square_0
    norm = (
        squares(star_0_ref[...] - step * star_x_ref[...]) / n_seg
        + squares(table_0_ref[...] - step * table) / n_stars
    )
    gather_ready(table, ahead, cal_coef_ref, tile_cal_ref, star_image_ref, knot_parts_ref, cal_ref)

    factors = Stored(column_ref, knot_hot_ref, None)

    def one_group(group, sums):
        rows = group_rows(group)
        image_0 = image_0_ref[rows, :]
        image = gather(group, live_ref, factors, att_coef_ref, knot_parts_ref, cal_ref)
        image = image_0 - step * image
        image_ref[rows, :] = image
        return sums[0] + image * image, sums[1] + image * image_0

    zero = jnp.zeros((GROUP, image_ref.shape[1]), F32)
    sums = lax.fori_loop(0, image_ref.shape[0] // GROUP, one_group, (zero, zero))
    scalars = [norm] + [jnp.sum(part, keepdims=True) for part in sums] + [norm_0, square_0]
    scalars = with_scalars(jnp.zeros((8, 128), F32), list(enumerate(scalars)))
    own_scalar_out[...] = scalars
    for device in range(scalar_out.shape[0]):
        scalar_out[device] = scalars


def output_kernel(
    live_ref, own_scalar_ref, scalar_ref, star_0_ref, star_h_ref, att_0_ref, att_h_ref, table_0_ref,
    table_h_ref, value_ref, image_0_ref, image_1_ref, star_out, att_out, cal_out, residual_out,
):
    norm_0, square_0 = [picked(own_scalar_ref[...], which) for which in (3, 4)]
    everyone = scalar_ref[0]
    for device in range(1, scalar_ref.shape[0]):
        everyone = everyone + scalar_ref[device]
    norm_1, square_1, cross = [picked(everyone, which) for which in range(3)]
    step_0 = norm_0 / square_0
    ratio = norm_1 / norm_0
    step_1 = norm_1 / (square_1 + 2.0 * ratio * cross + ratio * ratio * square_0)
    scale = step_0 + step_1 * ratio

    def combined(old, change):
        return scale * old + step_1 * (old - step_0 * change)

    star_out[...] = combined(star_0_ref[...], star_h_ref[...])
    att_out[...] = combined(att_0_ref[...], att_h_ref[...])
    cal = combined(table_0_ref[KNOT_ROWS:, :], table_h_ref[KNOT_ROWS:, :])
    cal_out[...] = jnp.concatenate([cal[:, :128], cal[:, 128:]], axis=0)
    values = value_ref[...] * live_mask(live_ref, 0, value_ref.shape)
    residual_out[...] = values - scale * image_0_ref[...] - step_1 * image_1_ref[...]


def in_vmem(count):
    return [pl.BlockSpec(memory_space=pltpu.VMEM)] * count


def in_smem(count):
    return [pl.BlockSpec(memory_space=pltpu.SMEM)] * count


def in_hbm(count):
    return [pl.BlockSpec(memory_space=pltpu.HBM)] * count


def shaped(*shape):
    return jax.ShapeDtypeStruct(shape, F32)


ARRIVE_PARAMS = pltpu.CompilerParams(vmem_limit_bytes=60 * 1024 * 1024)
PARAMS = pltpu.CompilerParams(vmem_limit_bytes=32 * 1024 * 1024)
PASS_COST = pl.CostEstimate(flops=3_000_000_000, bytes_accessed=1_000_000, transcendentals=0)
SMALL_COST = pl.CostEstimate(flops=1_000_000, bytes_accessed=600_000, transcendentals=0)


def on_device(
    obs_star, obs_knot, obs_frac, star_coef, att_coef, cal_coef, tile_cal, live_tiles, obs_value
):
    n_stars, n_seg = lax.axis_size("stars"), lax.axis_size("seg")
    tile_count, width = obs_star.shape
    tile_row = tile_cal[None, :]
    place = lax.axis_index("seg").astype(jnp.int32)[None]
    image_shape = shaped(tile_count, width)
    table_shape = shaped(TABLE_ROWS, COARSE)
    star_shape = shaped(STAR_ROWS, COARSE)
    sent_shapes = (shaped(n_stars, TABLE_ROWS // n_stars, COARSE), shaped(STAR_ROWS + 8, COARSE))
    sums = [pltpu.VMEM((2 * KNOT_HALF, COARSE), F32), pltpu.VMEM((2 * STAR_ROWS, COARSE), F32)]
    ready = [pltpu.VMEM((2 * KNOT_HALF, COARSE), BF16), pltpu.VMEM((tile_count, width), F32)]

    def first_scatter():
        observed = (obs_value, cal_coef, tile_row, obs_knot, obs_frac, att_coef, obs_star, star_coef)
        buffers = [pltpu.VMEM(array.shape, array.dtype) for array in observed]
        return pl.pallas_call(
            first_kernel,
            out_shape=sent_shapes,
            in_specs=in_smem(2) + in_hbm(len(observed)),
            out_specs=tuple(in_vmem(2)),
            scratch_shapes=sums + buffers + [pltpu.SemaphoreType.DMA((len(observed),))],
            compiler_params=ARRIVE_PARAMS,
            cost_estimate=PASS_COST,
            name="first_scatter",
        )(live_tiles, place, *observed)

    def factors(after):
        groups = tile_count // GROUP
        hot_shape = jax.ShapeDtypeStruct((groups, COARSE, GROUP * width), BF16)
        return pl.pallas_call(
            factor_kernel,
            out_shape=(shaped(tile_count, FINE + PAST_ROWS, width), hot_shape, hot_shape),
            in_specs=in_vmem(3) + [pl.BlockSpec(memory_space=pl.ANY)],
            out_specs=tuple(in_vmem(3)),
            compiler_params=PARAMS,
            cost_estimate=PASS_COST,
            name="factors",
        )(obs_knot, obs_frac, obs_star, after)

    def middle(*received):
        observed = (*made, att_coef, obs_star, star_coef, cal_coef, tile_row)
        return pl.pallas_call(
            functools.partial(middle_kernel, n_stars, n_seg),
            out_shape=(image_shape, table_shape, *sent_shapes),
            in_specs=in_smem(2) + in_vmem(len(observed) + len(received)),
            out_specs=tuple(in_vmem(4)),
            scratch_shapes=ready + sums,
            compiler_params=PARAMS,
            cost_estimate=PASS_COST,
            name="gather_and_scatter",
        )(live_tiles, place, *observed, *received)

    def last_gather(*received):
        observed = (*made[:2], att_coef, cal_coef, tile_row)
        return pl.pallas_call(
            functools.partial(last_kernel, n_stars, n_seg),
            out_shape=(image_shape, table_shape, shaped(n_stars * n_seg, 8, 128), shaped(8, 128)),
            in_specs=in_smem(2) + in_vmem(len(observed) + len(received)),
            out_specs=tuple(in_vmem(4)),
            scratch_shapes=ready,
            compiler_params=PARAMS,
            cost_estimate=PASS_COST,
            name="last_gather",
        )(live_tiles, place, *observed, *received)

    def star_forward(star):
        return pl.pallas_call(
            star_forward_kernel,
            out_shape=image_shape,
            in_specs=in_vmem(4),
            out_specs=in_vmem(1)[0],
            scratch_shapes=[pltpu.VMEM((2 * STAR_ROWS, COARSE), BF16)],
            compiler_params=PARAMS,
            cost_estimate=PASS_COST,
            name="star_forward",
        )(obs_star, star_coef, made[2], star)

    def swap(blocks, axes):
        return lax.all_to_all(blocks, axes, 0, 0)

    def partner(array, axis, distance):
        return lax.ppermute(array, axis, [(i, i ^ distance) for i in range(lax.axis_size(axis))])

    def reduced(table, star):
        distances = [1 << bit for bit in range(n_seg.bit_length() - 1)]
        for distance in distances[:-1]:
            star = star + partner(star, "seg", distance)
        blocks, star = pl.pallas_call(
            sum_kernel,
            out_shape=(shaped(n_stars, 2 * TABLE_ROWS // n_stars + 8, 128), star_shape),
            in_specs=in_vmem(3),
            out_specs=tuple(in_vmem(2)),
            compiler_params=PARAMS,
            cost_estimate=SMALL_COST,
            name="table_sum",
        )(swap(table, "stars"), star, partner(star, "seg", distances[-1]))
        return star_forward(star), star, swap(blocks, "stars")

    sent = first_scatter()
    made = factors(sent[1])
    first = reduced(*sent)
    star_0 = first[1]
    image_0, table_0, *sent = middle(*first)
    second = reduced(*sent)
    star_h = second[1]
    image_1, table_h, scalars, own_scalars = last_gather(*second, star_0, table_0, image_0)

    def star_order(star):
        return star.reshape(5, STAR_DEV)

    def att_order(table):
        att = table[:KNOT_ROWS].reshape(4, FINE, COARSE)
        return att.transpose(0, 2, 1).reshape(4, KNOT_DEV)

    return pl.pallas_call(
        output_kernel,
        out_shape=(shaped(5, STAR_DEV), shaped(4, KNOT_DEV), shaped(CALB_DEV, width), image_shape),
        in_specs=in_smem(1) + in_vmem(11),
        out_specs=tuple(in_vmem(4)),
        compiler_params=PARAMS,
        cost_estimate=SMALL_COST,
        name="outputs",
    )(
        live_tiles, own_scalars, swap(scalars, ("stars", "seg")), star_order(star_0), star_order(star_h),
        att_order(table_0), att_order(table_h), table_0, table_h, obs_value, image_0, image_1,
    )


def solution(mesh):
    placed = (
        P(("stars", "seg"), None),
        P(("stars", "seg"), None),
        P(("stars", "seg"), None),
        P(None, ("stars", "seg"), None),
        P(None, ("stars", "seg"), None),
        P(("stars", "seg"), None),
        P(("stars", "seg")),
        P(("stars", "seg")),
        P(("stars", "seg"), None),
    )
    return jax.shard_map(
        on_device,
        mesh=mesh,
        in_specs=placed,
        out_specs=(P(None, "stars"), P(None, "seg"), P("seg", None), P(("stars", "seg"), None)),
        check_vma=False,
    )
```

```python
import functools

import jax
import jax.numpy as jnp
from jax import lax
from jax.experimental import pallas as pl
from jax.experimental.pallas import tpu as pltpu
from jax.sharding import PartitionSpec as P

STAR_DEV = 8192
KNOT_DEV = 8192
CALB_DEV = 256
FINE = 32
COARSE = 256
GROUP = 16
FIRST_GROUP = 32
SLOT = 8
STAR_ROWS = 5 * FINE
KNOT_ROWS = 4 * FINE
TABLE_ROWS = KNOT_ROWS + CALB_DEV // 2
BF16 = jnp.bfloat16
F32 = jnp.float32
SCALAR_LANE = 64
PAST_ROWS = 16
KNOT_HALF = KNOT_ROWS + PAST_ROWS


def two_parts(values):
    high = values.astype(BF16)
    return high, (values - high.astype(F32)).astype(BF16)


def rows_and_columns(shape):
    return lax.broadcasted_iota(jnp.int32, shape, 0), lax.broadcasted_iota(jnp.int32, shape, 1)


def packed_rows(row, size):
    wide = jnp.broadcast_to(row.astype(F32), (16, row.shape[1])).astype(BF16)
    return jnp.concatenate([wide] * (size // 16), axis=0)


def matches(index_row, size):
    places, _ = rows_and_columns((size, index_row.shape[1]))
    return places.astype(F32).astype(BF16) == packed_rows(index_row, size)


def one_hot(index_row, size):
    return jnp.where(matches(index_row, size), jnp.ones((), BF16), jnp.zeros((), BF16))


def spline_weights(fraction):
    remain = 1.0 - fraction
    square = fraction * fraction
    cubed = square * fraction
    return (
        remain * remain * remain / 6.0,
        (3.0 * cubed - 6.0 * square + 4.0) / 6.0,
        (-3.0 * cubed + 3.0 * square + 3.0 * fraction + 1.0) / 6.0,
        cubed / 6.0,
    )


def weight_columns(weights, fine_row, tile, places):
    behind = places - fine_row
    result = jnp.zeros(behind.shape, F32)
    for offset in range(4):
        result = jnp.where(behind == offset, weights[offset][tile : tile + 1], result)
    return result


def near_and_past(weights, fine, tile):
    width = fine.shape[1]
    fine_row = fine[tile : tile + 1]
    near, _ = rows_and_columns((FINE, width))
    past, _ = rows_and_columns((PAST_ROWS, width))
    past = FINE + (past & 3)
    return weight_columns(weights, fine_row, tile, near), weight_columns(weights, fine_row, tile, past)


def past_terms(terms, here):
    rows, _ = rows_and_columns((PAST_ROWS, terms[0].shape[1]))
    result = jnp.broadcast_to(terms[3][here], rows.shape)
    for comp in range(2, -1, -1):
        result = jnp.where(rows < 4 * (comp + 1), terms[comp][here], result)
    return result


def product(left, right, contract):
    return lax.dot_general(left, right, (contract, ((), ())), preferred_element_type=F32)


def live_mask(live_ref, first, shape):
    rows, _ = rows_and_columns(shape)
    return (rows + first < live_ref[0]).astype(F32)


def store_rows(out_ref, begin, rows):
    block = out_ref.shape[1]
    for offset in range(0, rows.shape[0], 8):
        where = begin + offset
        out_ref[where // block, where % block : where % block + 8, :] = rows[offset : offset + 8]


def scatter(first, size, values, observed, knot_acc, star_acc):
    knot_ref, frac_ref, att_coef_ref, star_ref, star_coef_ref = observed
    rows = pl.ds(first, size)
    knot, star = knot_ref[rows, :], star_ref[rows, :]
    knot_coarse, knot_fine = knot >> 5, knot & (FINE - 1)
    star_coarse, star_fine = star & (COARSE - 1), star >> 8
    weights = spline_weights(frac_ref[rows, :])
    terms = [att_coef_ref[comp, rows, :] * values for comp in range(4)]
    parts = [two_parts(star_coef_ref[comp, rows, :] * values) for comp in range(5)]
    parts = [pair[half].astype(F32) for half in range(2) for pair in parts]
    knot_left, knot_right, star_left, star_right = [], [], [], []
    for tile in range(size):
        here = slice(tile, tile + 1)
        knot_right.append(one_hot(knot_coarse[here], COARSE))
        near, past = near_and_past(weights, knot_fine, tile)
        spread = jnp.concatenate(
            [term[here] * near for term in terms] + [past_terms(terms, here) * past], axis=0
        )
        knot_left.append(jnp.concatenate(two_parts(spread), axis=0))
        star_right.append(one_hot(star_coarse[here], COARSE))
        chosen = matches(star_fine[here], FINE)
        star_left.append(
            jnp.concatenate(
                [jnp.where(chosen, packed_rows(part[here], FINE), jnp.zeros((), BF16)) for part in parts],
                axis=0,
            )
        )
    knot_acc[...] += product(
        jnp.concatenate(knot_left, axis=1), jnp.concatenate(knot_right, axis=1), ((1,), (1,))
    )
    star_acc[...] += product(
        jnp.concatenate(star_left, axis=1), jnp.concatenate(star_right, axis=1), ((1,), (1,))
    )


def scatter_calibration(values, tile_cal_ref, table_out):
    blocks = product(
        one_hot(tile_cal_ref[...], CALB_DEV), jnp.concatenate(two_parts(values), axis=1), ((1,), (0,))
    )
    width = values.shape[1]
    blocks = blocks[:, :width] + blocks[:, width:]
    blocks = jnp.concatenate([blocks[: CALB_DEV // 2], blocks[CALB_DEV // 2 :]], axis=1)
    store_rows(table_out, KNOT_ROWS, blocks)


def scatter_end(place_ref, scalars, knot_acc, star_acc, table_out, star_out):
    lane = lax.broadcasted_iota(jnp.int32, (8, 128), 1)
    row = lax.broadcasted_iota(jnp.int32, (8, 128), 0)
    wide_lane = lax.broadcasted_iota(jnp.int32, (8, COARSE), 1)
    wide_row = lax.broadcasted_iota(jnp.int32, (8, COARSE), 0)
    edges = jnp.zeros((8, 128), F32)
    for comp in range(4):
        begin, past = comp * FINE, KNOT_ROWS + comp // 2 * 8
        main = knot_acc[begin : begin + FINE] + knot_acc[KNOT_HALF + begin : KNOT_HALF + begin + FINE]
        beyond = knot_acc[past : past + 8] + knot_acc[KNOT_HALF + past : KNOT_HALF + past + 8]
        if comp % 2:
            beyond = pltpu.roll(beyond, 4, 0)
        moved = pltpu.roll(jnp.where(wide_row < 3, beyond, 0.0), 1, 1)
        top = main[:8] + jnp.where(wide_lane > 0, moved, 0.0)
        store_rows(table_out, begin, top)
        store_rows(table_out, begin + 8, main[8:])
        tail, head = moved[:, :128], top[:, :128]
        if comp:
            tail = pltpu.roll(tail, 2 * comp, 1)
        head = pltpu.roll(head, 2 * comp + 1, 1)
        edges = jnp.where((lane == 2 * comp) & (row < 3), tail, edges)
        edges = jnp.where((lane == 2 * comp + 1) & (row < 3), head, edges)
    edges = with_scalars(pltpu.roll(edges, SLOT * place_ref[0], 1), scalars)
    star_out[:STAR_ROWS] = star_acc[:STAR_ROWS] + star_acc[STAR_ROWS:]
    star_out[STAR_ROWS:] = jnp.concatenate([edges, jnp.zeros_like(edges)], axis=1)


def first_kernel(live_ref, place_ref, *refs):
    sources, (table_out, star_out, knot_acc, star_acc) = refs[:8], refs[8:12]
    buffers, sems = refs[12:20], refs[20]
    half = sources[0].shape[0] // 2
    copies = []

    def begin(source, target, *place):
        source, target = (source.at[place], target.at[place]) if place else (source, target)
        copies.append(pltpu.make_async_copy(source, target, sems.at[len(copies)]))
        copies[-1].start()

    for source, target in zip(sources[:3], buffers):
        begin(source, target)
    for rows in (slice(0, half), slice(half, 2 * half)):
        for source, target in zip(sources[3:], buffers[3:]):
            begin(source, target, *[slice(None)] * (len(source.shape) - 2), rows)
    value_ref, cal_coef_ref, tile_cal_ref, *observed = buffers
    knot_acc[...] = jnp.zeros_like(knot_acc)
    star_acc[...] = jnp.zeros_like(star_acc)
    for copy in copies[:3]:
        copy.wait()
    values = value_ref[...] * live_mask(live_ref, 0, value_ref.shape)
    scatter_calibration(values * cal_coef_ref[...], tile_cal_ref, table_out)
    for copy in copies[3:8]:
        copy.wait()

    @pl.loop(0, value_ref.shape[0] // FIRST_GROUP)
    def _(group):
        @pl.when(group * FIRST_GROUP == half)
        def _():
            for copy in copies[8:]:
                copy.wait()

        first = pl.multiple_of(group * FIRST_GROUP, FIRST_GROUP)
        values = value_ref[pl.ds(first, FIRST_GROUP), :]
        values = values * live_mask(live_ref, first, values.shape)
        scatter(first, FIRST_GROUP, values, observed, knot_acc, star_acc)

    scatter_end(place_ref, [], knot_acc, star_acc, table_out, star_out)


def sum_kernel(block_ref, own_ref, other_ref, out_ref, star_out):
    total = block_ref[0]
    for device in range(1, block_ref.shape[0]):
        total = total + block_ref[device]
    star = own_ref[...] + other_ref[...]
    star_out[...] = star[:STAR_ROWS]
    total = jnp.concatenate([total[:, :128], total[:, 128:], star[STAR_ROWS:, :128]], axis=0)
    for device in range(block_ref.shape[0]):
        out_ref[device] = total


def picked(array, which):
    row = lax.broadcasted_iota(jnp.int32, array.shape, 0)
    lane = lax.broadcasted_iota(jnp.int32, array.shape, 1)
    chosen = (row == 0) & (lane == SCALAR_LANE + which)
    return jnp.sum(jnp.where(chosen, array, 0.0), keepdims=True)


def with_scalars(array, scalars):
    row = lax.broadcasted_iota(jnp.int32, array.shape, 0)
    lane = lax.broadcasted_iota(jnp.int32, array.shape, 1)
    for which, value in scalars:
        array = jnp.where((row == 0) & (lane == SCALAR_LANE + which), value, array)
    return array


def first_step(edges):
    return picked(edges, 0), picked(edges, 1)


def star_forward_kernel(star_ref, star_coef_ref, star_x_ref, image_ref, star_parts_ref):
    star_x = star_x_ref[...]
    star_high, star_low = two_parts(star_x)
    star_parts_ref[:STAR_ROWS] = star_high
    star_parts_ref[STAR_ROWS:] = star_low

    @pl.loop(0, star_ref.shape[0] // GROUP)
    def _(group):
        rows = pl.ds(pl.multiple_of(group * GROUP, GROUP), GROUP)
        star = star_ref[rows, :]
        coarse, fine = star & (COARSE - 1), star >> 8
        coef = [star_coef_ref[comp, rows, :] for comp in range(5)]
        tiles = [slice(tile, tile + 1) for tile in range(GROUP)]
        hot = jnp.concatenate([one_hot(coarse[here], COARSE) for here in tiles], axis=1)
        found = product(star_parts_ref[...], hot, ((1,), (0,)))
        width = star.shape[1]
        fine_rows, _ = rows_and_columns((FINE, width))
        image_rows = []
        for tile, here in enumerate(tiles):
            across = slice(tile * width, (tile + 1) * width)

            def part(comp):
                begin = comp * FINE
                return (
                    found[begin : begin + FINE, across]
                    + found[STAR_ROWS + begin : STAR_ROWS + begin + FINE, across]
                )

            both = sum(coef[comp][here] * part(comp) for comp in range(5))
            both = jnp.where(fine_rows == fine[here], both, 0.0)
            both = both[:8] + both[8:16] + both[16:24] + both[24:]
            image_rows.append(jnp.sum(both, axis=0, keepdims=True))
        image_ref[rows, :] = jnp.concatenate(image_rows, axis=0)


def received_table(n_stars, n_seg, place_ref, block_ref):
    segment = place_ref[0]
    lane = lax.broadcasted_iota(jnp.int32, (8, 128), 1)
    row = lax.broadcasted_iota(jnp.int32, (8, 128), 0)
    edges = block_ref[0, -8:, :]
    for block in range(1, n_stars):
        edges = edges + block_ref[block, -8:, :]

    def slot(which):
        return pltpu.roll(edges, 128 - SLOT * jnp.clip(which, 0, n_seg - 1), 1)

    before, own, after = slot(segment - 1), slot(segment), slot(segment + 1)
    before = jnp.where(segment > 0, before, 0.0)
    ahead = jnp.where(lane % 2 == 0, own, 0.0) + pltpu.roll(jnp.where(lane % 2 == 1, after, 0.0), 127, 1)
    ahead = jnp.where((segment < n_seg - 1) & (lane < 8) & (row < 3), ahead, 0.0)

    size = TABLE_ROWS // n_stars
    table = jnp.concatenate([block_ref[:, :size, :], block_ref[:, size : 2 * size, :]], axis=2)
    table = table.reshape(TABLE_ROWS, COARSE)
    pieces = []
    for comp in range(4):
        shifted = pltpu.roll(before, 128 - 2 * comp, 1) if comp else before
        shifted = jnp.where((lane == 0) & (row < 3), shifted, 0.0)
        top = table[comp * FINE : comp * FINE + 8]
        pieces.append(top + jnp.concatenate([shifted, jnp.zeros_like(shifted)], axis=1))
        pieces.append(table[comp * FINE + 8 : (comp + 1) * FINE])
    return jnp.concatenate(pieces + [table[KNOT_ROWS:]], axis=0), ahead, edges


def gather_ready(table, ahead, cal_coef_ref, tile_cal_ref, star_image_ref, knot_parts_ref, cal_ref):
    wide_lane = lax.broadcasted_iota(jnp.int32, (8, COARSE), 1)
    row = lax.broadcasted_iota(jnp.int32, (8, COARSE), 0)
    beyond = []
    for comp in range(4):
        moved = pltpu.roll(table[comp * FINE : comp * FINE + 8], COARSE - 1, 1)
        last = pltpu.roll(ahead, 127 - 2 * comp, 1)
        moved = jnp.where(wide_lane == COARSE - 1, jnp.concatenate([last, last], axis=1), moved)
        beyond.append(pltpu.roll(moved, 4, 0) if comp % 2 else moved)
    beyond = [jnp.where(row < 4, beyond[0], beyond[1]), jnp.where(row < 4, beyond[2], beyond[3])]
    knot_high, knot_low = two_parts(jnp.concatenate([table[:KNOT_ROWS]] + beyond, axis=0))
    knot_parts_ref[:KNOT_HALF] = knot_high
    knot_parts_ref[KNOT_HALF:] = knot_low

    blocks = jnp.concatenate([table[KNOT_ROWS:, :128], table[KNOT_ROWS:, 128:]], axis=0)
    rows = product(
        one_hot(tile_cal_ref[...], CALB_DEV), jnp.concatenate(two_parts(blocks), axis=1), ((0,), (0,))
    )
    cal_ref[...] = (rows[:, :128] + rows[:, 128:]) * cal_coef_ref[...] + star_image_ref[...]


def gather(first, live_ref, observed, knot_parts_ref, cal_ref):
    knot_ref, frac_ref, att_coef_ref = observed
    rows = pl.ds(first, GROUP)
    knot = knot_ref[rows, :]
    coarse, fine = knot >> 5, knot & (FINE - 1)
    weights = spline_weights(frac_ref[rows, :])
    coef = [att_coef_ref[comp, rows, :] for comp in range(4)]
    tiles = [slice(tile, tile + 1) for tile in range(GROUP)]
    hot = jnp.concatenate([one_hot(coarse[here], COARSE) for here in tiles], axis=1)
    found = product(knot_parts_ref[...], hot, ((1,), (0,)))
    width = knot.shape[1]
    image_rows = []
    for tile, here in enumerate(tiles):
        across = slice(tile * width, (tile + 1) * width)

        def part(begin, size):
            return (
                found[begin : begin + size, across]
                + found[KNOT_HALF + begin : KNOT_HALF + begin + size, across]
            )

        near, past = near_and_past(weights, fine, tile)
        near = near * sum(coef[comp][here] * part(comp * FINE, FINE) for comp in range(4))
        past = past * past_terms(coef, here) * part(KNOT_ROWS, PAST_ROWS)
        both = near[:8] + near[8:16] + near[16:24] + near[24:] + past[:8] + past[8:]
        image_rows.append(jnp.sum(both, axis=0, keepdims=True))
    image = jnp.concatenate(image_rows, axis=0) + cal_ref[rows, :]
    return image * live_mask(live_ref, first, image.shape)


def squares(array):
    return jnp.sum(array * array, keepdims=True)


def middle_kernel(
    n_stars, n_seg, live_ref, place_ref, knot_ref, frac_ref, att_coef_ref, star_ref, star_coef_ref,
    cal_coef_ref, tile_cal_ref, star_image_ref, star_x_ref, block_ref, image_ref, table_out, scatter_out,
    star_out, knot_parts_ref, cal_ref, knot_acc, star_acc,
):
    table, ahead, _ = received_table(n_stars, n_seg, place_ref, block_ref)
    table_out[...] = table
    norm = squares(star_x_ref[...]) / n_seg + squares(table) / n_stars
    gather_ready(table, ahead, cal_coef_ref, tile_cal_ref, star_image_ref, knot_parts_ref, cal_ref)
    knot_acc[...] = jnp.zeros_like(knot_acc)
    star_acc[...] = jnp.zeros_like(star_acc)
    observed = (knot_ref, frac_ref, att_coef_ref)
    every = (knot_ref, frac_ref, att_coef_ref, star_ref, star_coef_ref)
    groups = knot_ref.shape[0] // GROUP
    image = gather(0, live_ref, observed, knot_parts_ref, cal_ref)
    image_ref[:GROUP, :] = image

    def one_group(group, total):
        first = pl.multiple_of(group * GROUP, GROUP)
        following = pl.multiple_of(first + GROUP, GROUP)
        values = image_ref[pl.ds(first, GROUP), :]
        image = gather(following, live_ref, observed, knot_parts_ref, cal_ref)
        scatter(first, GROUP, values, every, knot_acc, star_acc)
        image_ref[pl.ds(following, GROUP), :] = image
        return total + image * image

    total = lax.fori_loop(0, groups - 1, one_group, image * image)
    first = (groups - 1) * GROUP
    scatter(first, GROUP, image_ref[first:, :], every, knot_acc, star_acc)
    scatter_calibration(image_ref[...] * cal_coef_ref[...], tile_cal_ref, scatter_out)
    scalars = [(0, norm), (1, jnp.sum(total, keepdims=True))]
    scatter_end(place_ref, scalars, knot_acc, star_acc, scatter_out, star_out)


def last_kernel(
    n_stars, n_seg, live_ref, place_ref, knot_ref, frac_ref, att_coef_ref, cal_coef_ref, tile_cal_ref,
    star_image_ref, star_x_ref, block_ref, star_0_ref, table_0_ref, image_0_ref, image_ref, table_out,
    scalar_out, own_scalar_out, knot_parts_ref, cal_ref,
):
    table, ahead, edges = received_table(n_stars, n_seg, place_ref, block_ref)
    table_out[...] = table
    norm_0, square_0 = first_step(edges)
    step = norm_0 / square_0
    norm = (
        squares(star_0_ref[...] - step * star_x_ref[...]) / n_seg
        + squares(table_0_ref[...] - step * table) / n_stars
    )
    gather_ready(table, ahead, cal_coef_ref, tile_cal_ref, star_image_ref, knot_parts_ref, cal_ref)

    def one_group(group, sums):
        first = pl.multiple_of(group * GROUP, GROUP)
        rows = pl.ds(first, GROUP)
        image_0 = image_0_ref[rows, :]
        image = gather(first, live_ref, (knot_ref, frac_ref, att_coef_ref), knot_parts_ref, cal_ref)
        image = image_0 - step * image
        image_ref[rows, :] = image
        return sums[0] + image * image, sums[1] + image * image_0

    zero = jnp.zeros((GROUP, knot_ref.shape[1]), F32)
    sums = lax.fori_loop(0, knot_ref.shape[0] // GROUP, one_group, (zero, zero))
    scalars = [norm] + [jnp.sum(part, keepdims=True) for part in sums] + [norm_0, square_0]
    scalars = with_scalars(jnp.zeros((8, 128), F32), list(enumerate(scalars)))
    own_scalar_out[...] = scalars
    for device in range(scalar_out.shape[0]):
        scalar_out[device] = scalars


def output_kernel(
    live_ref, own_scalar_ref, scalar_ref, star_0_ref, star_h_ref, att_0_ref, att_h_ref, table_0_ref,
    table_h_ref, value_ref, image_0_ref, image_1_ref, star_out, att_out, cal_out, residual_out,
):
    norm_0, square_0 = [picked(own_scalar_ref[...], which) for which in (3, 4)]
    everyone = scalar_ref[0]
    for device in range(1, scalar_ref.shape[0]):
        everyone = everyone + scalar_ref[device]
    norm_1, square_1, cross = [picked(everyone, which) for which in range(3)]
    step_0 = norm_0 / square_0
    ratio = norm_1 / norm_0
    step_1 = norm_1 / (square_1 + 2.0 * ratio * cross + ratio * ratio * square_0)
    scale = step_0 + step_1 * ratio

    def combined(old, change):
        return scale * old + step_1 * (old - step_0 * change)

    star_out[...] = combined(star_0_ref[...], star_h_ref[...])
    att_out[...] = combined(att_0_ref[...], att_h_ref[...])
    cal = combined(table_0_ref[KNOT_ROWS:, :], table_h_ref[KNOT_ROWS:, :])
    cal_out[...] = jnp.concatenate([cal[:, :128], cal[:, 128:]], axis=0)
    values = value_ref[...] * live_mask(live_ref, 0, value_ref.shape)
    residual_out[...] = values - scale * image_0_ref[...] - step_1 * image_1_ref[...]


def in_vmem(count):
    return [pl.BlockSpec(memory_space=pltpu.VMEM)] * count


def in_smem(count):
    return [pl.BlockSpec(memory_space=pltpu.SMEM)] * count


def in_hbm(count):
    return [pl.BlockSpec(memory_space=pltpu.HBM)] * count


def shaped(*shape):
    return jax.ShapeDtypeStruct(shape, F32)


ARRIVE_PARAMS = pltpu.CompilerParams(vmem_limit_bytes=60 * 1024 * 1024)
PARAMS = pltpu.CompilerParams(vmem_limit_bytes=40 * 1024 * 1024)
PASS_COST = pl.CostEstimate(flops=3_000_000_000, bytes_accessed=1_000_000, transcendentals=0)
SMALL_COST = pl.CostEstimate(flops=1_000_000, bytes_accessed=600_000, transcendentals=0)


def on_device(
    obs_star, obs_knot, obs_frac, star_coef, att_coef, cal_coef, tile_cal, live_tiles, obs_value
):
    n_stars, n_seg = lax.axis_size("stars"), lax.axis_size("seg")
    tile_count, width = obs_star.shape
    tile_row = tile_cal[None, :]
    place = lax.axis_index("seg").astype(jnp.int32)[None]
    image_shape = shaped(tile_count, width)
    table_shape = shaped(TABLE_ROWS, COARSE)
    star_shape = shaped(STAR_ROWS, COARSE)
    sent_shapes = (shaped(n_stars, TABLE_ROWS // n_stars, COARSE), shaped(STAR_ROWS + 8, COARSE))
    sums = [pltpu.VMEM((2 * KNOT_HALF, COARSE), F32), pltpu.VMEM((2 * STAR_ROWS, COARSE), F32)]
    ready = [pltpu.VMEM((2 * KNOT_HALF, COARSE), BF16), pltpu.VMEM((tile_count, width), F32)]

    def first_scatter():
        observed = (obs_value, cal_coef, tile_row, obs_knot, obs_frac, att_coef, obs_star, star_coef)
        buffers = [pltpu.VMEM(array.shape, array.dtype) for array in observed]
        return pl.pallas_call(
            first_kernel,
            out_shape=sent_shapes,
            in_specs=in_smem(2) + in_hbm(len(observed)),
            out_specs=tuple(in_vmem(2)),
            scratch_shapes=sums + buffers + [pltpu.SemaphoreType.DMA((13,))],
            compiler_params=ARRIVE_PARAMS,
            cost_estimate=PASS_COST,
            name="first_scatter",
        )(live_tiles, place, *observed)

    def middle(*received):
        observed = (obs_knot, obs_frac, att_coef, obs_star, star_coef, cal_coef, tile_row)
        return pl.pallas_call(
            functools.partial(middle_kernel, n_stars, n_seg),
            out_shape=(image_shape, table_shape, *sent_shapes),
            in_specs=in_smem(2) + in_vmem(len(observed) + len(received)),
            out_specs=tuple(in_vmem(4)),
            scratch_shapes=ready + sums,
            compiler_params=PARAMS,
            cost_estimate=PASS_COST,
            name="gather_and_scatter",
        )(live_tiles, place, *observed, *received)

    def last_gather(*received):
        observed = (obs_knot, obs_frac, att_coef, cal_coef, tile_row)
        return pl.pallas_call(
            functools.partial(last_kernel, n_stars, n_seg),
            out_shape=(image_shape, table_shape, shaped(n_stars * n_seg, 8, 128), shaped(8, 128)),
            in_specs=in_smem(2) + in_vmem(len(observed) + len(received)),
            out_specs=tuple(in_vmem(4)),
            scratch_shapes=ready,
            compiler_params=PARAMS,
            cost_estimate=PASS_COST,
            name="last_gather",
        )(live_tiles, place, *observed, *received)

    def star_forward(star):
        return pl.pallas_call(
            star_forward_kernel,
            out_shape=image_shape,
            in_specs=in_vmem(3),
            out_specs=in_vmem(1)[0],
            scratch_shapes=[pltpu.VMEM((2 * STAR_ROWS, COARSE), BF16)],
            compiler_params=PARAMS,
            cost_estimate=PASS_COST,
            name="star_forward",
        )(obs_star, star_coef, star)

    def swap(blocks, axes):
        return lax.all_to_all(blocks, axes, 0, 0)

    def partner(array, axis, distance):
        return lax.ppermute(array, axis, [(i, i ^ distance) for i in range(lax.axis_size(axis))])

    def reduced(table, star):
        distances = [1 << bit for bit in range(n_seg.bit_length() - 1)]
        for distance in distances[:-1]:
            star = star + partner(star, "seg", distance)
        blocks, star = pl.pallas_call(
            sum_kernel,
            out_shape=(shaped(n_stars, 2 * TABLE_ROWS // n_stars + 8, 128), star_shape),
            in_specs=in_vmem(3),
            out_specs=tuple(in_vmem(2)),
            compiler_params=PARAMS,
            cost_estimate=SMALL_COST,
            name="table_sum",
        )(swap(table, "stars"), star, partner(star, "seg", distances[-1]))
        return star_forward(star), star, swap(blocks, "stars")

    first = reduced(*first_scatter())
    star_0 = first[1]
    image_0, table_0, *sent = middle(*first)
    second = reduced(*sent)
    star_h = second[1]
    image_1, table_h, scalars, own_scalars = last_gather(*second, star_0, table_0, image_0)

    def star_order(star):
        return star.reshape(5, STAR_DEV)

    def att_order(table):
        att = table[:KNOT_ROWS].reshape(4, FINE, COARSE)
        return att.transpose(0, 2, 1).reshape(4, KNOT_DEV)

    return pl.pallas_call(
        output_kernel,
        out_shape=(shaped(5, STAR_DEV), shaped(4, KNOT_DEV), shaped(CALB_DEV, width), image_shape),
        in_specs=in_smem(1) + in_vmem(11),
        out_specs=tuple(in_vmem(4)),
        compiler_params=PARAMS,
        cost_estimate=SMALL_COST,
        name="outputs",
    )(
        live_tiles, own_scalars, swap(scalars, ("stars", "seg")), star_order(star_0), star_order(star_h),
        att_order(table_0), att_order(table_h), table_0, table_h, obs_value, image_0, image_1,
    )


def solution(mesh):
    placed = (
        P(("stars", "seg"), None),
        P(("stars", "seg"), None),
        P(("stars", "seg"), None),
        P(None, ("stars", "seg"), None),
        P(None, ("stars", "seg"), None),
        P(("stars", "seg"), None),
        P(("stars", "seg")),
        P(("stars", "seg")),
        P(("stars", "seg"), None),
    )
    return jax.shard_map(
        on_device,
        mesh=mesh,
        in_specs=placed,
        out_specs=(P(None, "stars"), P(None, "seg"), P("seg", None), P(("stars", "seg"), None)),
        check_vma=False,
    )
```

```python
import functools

import jax
import jax.numpy as jnp
from jax import lax
from jax.experimental import pallas as pl
from jax.experimental.pallas import tpu as pltpu
from jax.sharding import PartitionSpec as P

STAR_DEV = 8192
KNOT_DEV = 8192
CALB_DEV = 256
FINE = 32
COARSE = 256
GROUP = 16
WIDE_GROUP = 32
SLOT = 8
STAR_ROWS = 5 * FINE
KNOT_ROWS = 4 * FINE
TABLE_ROWS = KNOT_ROWS + CALB_DEV // 2
BF16 = jnp.bfloat16
F32 = jnp.float32
SCALAR_LANE = 64
PAST_ROWS = 16
KNOT_HALF = KNOT_ROWS + PAST_ROWS


def two_parts(values):
    high = values.astype(BF16)
    return high, (values - high.astype(F32)).astype(BF16)


def rows_and_columns(shape):
    return lax.broadcasted_iota(jnp.int32, shape, 0), lax.broadcasted_iota(jnp.int32, shape, 1)


def packed_rows(row, size):
    wide = jnp.broadcast_to(row.astype(F32), (16, row.shape[1])).astype(BF16)
    return jnp.concatenate([wide] * (size // 16), axis=0)


def matches(index_row, size):
    places, _ = rows_and_columns((size, index_row.shape[1]))
    return places.astype(F32).astype(BF16) == packed_rows(index_row, size)


def one_hot(index_row, size):
    return jnp.where(matches(index_row, size), jnp.ones((), BF16), jnp.zeros((), BF16))


def spline_weights(fraction):
    remain = 1.0 - fraction
    square = fraction * fraction
    cubed = square * fraction
    return (
        remain * remain * remain / 6.0,
        (3.0 * cubed - 6.0 * square + 4.0) / 6.0,
        (-3.0 * cubed + 3.0 * square + 3.0 * fraction + 1.0) / 6.0,
        cubed / 6.0,
    )


def weight_columns(weights, fine_row, tile, places):
    behind = places - fine_row
    result = jnp.zeros(behind.shape, F32)
    for offset in range(4):
        result = jnp.where(behind == offset, weights[offset][tile : tile + 1], result)
    return result


def near_and_past(weights, fine, tile):
    width = fine.shape[1]
    fine_row = fine[tile : tile + 1]
    near, _ = rows_and_columns((FINE, width))
    past, _ = rows_and_columns((PAST_ROWS, width))
    past = FINE + (past & 3)
    return weight_columns(weights, fine_row, tile, near), weight_columns(weights, fine_row, tile, past)


def past_terms(terms, here):
    rows, _ = rows_and_columns((PAST_ROWS, terms[0].shape[1]))
    result = jnp.broadcast_to(terms[3][here], rows.shape)
    for comp in range(2, -1, -1):
        result = jnp.where(rows < 4 * (comp + 1), terms[comp][here], result)
    return result


def product(left, right, contract):
    return lax.dot_general(left, right, (contract, ((), ())), preferred_element_type=F32)


def live_mask(live_ref, first, shape):
    rows, _ = rows_and_columns(shape)
    return (rows + first < live_ref[0]).astype(F32)


def store_rows(out_ref, begin, rows):
    block = out_ref.shape[1]
    for offset in range(0, rows.shape[0], 8):
        where = begin + offset
        out_ref[where // block, where % block : where % block + 8, :] = rows[offset : offset + 8]


def knot_factors(first, knot_ref, frac_ref):
    rows = pl.ds(first, WIDE_GROUP)
    knot = knot_ref[rows, :]
    coarse, fine = knot >> 5, knot & (FINE - 1)
    weights = spline_weights(frac_ref[rows, :])
    hot = [one_hot(coarse[tile : tile + 1], COARSE) for tile in range(WIDE_GROUP)]
    columns = [near_and_past(weights, fine, tile) for tile in range(WIDE_GROUP)]
    return jnp.concatenate(hot, axis=1), columns


def scatter(first, factors, values, observed, knot_acc, star_acc):
    att_coef_ref, star_ref, star_coef_ref = observed
    rows = pl.ds(first, WIDE_GROUP)
    knot_hot, columns = factors
    star = star_ref[rows, :]
    star_coarse, star_fine = star & (COARSE - 1), star >> 8
    terms = [att_coef_ref[comp, rows, :] * values for comp in range(4)]
    parts = [two_parts(star_coef_ref[comp, rows, :] * values) for comp in range(5)]
    parts = [pair[half].astype(F32) for half in range(2) for pair in parts]
    knot_left, star_left, star_right = [], [], []
    for tile in range(WIDE_GROUP):
        here = slice(tile, tile + 1)
        near, past = columns[tile]
        spread = jnp.concatenate(
            [term[here] * near for term in terms] + [past_terms(terms, here) * past], axis=0
        )
        knot_left.append(jnp.concatenate(two_parts(spread), axis=0))
        star_right.append(one_hot(star_coarse[here], COARSE))
        chosen = matches(star_fine[here], FINE)
        star_left.append(
            jnp.concatenate(
                [jnp.where(chosen, packed_rows(part[here], FINE), jnp.zeros((), BF16)) for part in parts],
                axis=0,
            )
        )
    knot_acc[...] += product(
        jnp.concatenate(knot_left, axis=1), knot_hot, ((1,), (1,))
    )
    star_acc[...] += product(
        jnp.concatenate(star_left, axis=1), jnp.concatenate(star_right, axis=1), ((1,), (1,))
    )


def scatter_calibration(values, tile_cal_ref, table_out):
    blocks = product(
        one_hot(tile_cal_ref[...], CALB_DEV), jnp.concatenate(two_parts(values), axis=1), ((1,), (0,))
    )
    width = values.shape[1]
    blocks = blocks[:, :width] + blocks[:, width:]
    blocks = jnp.concatenate([blocks[: CALB_DEV // 2], blocks[CALB_DEV // 2 :]], axis=1)
    store_rows(table_out, KNOT_ROWS, blocks)


def scatter_end(place_ref, scalars, knot_acc, star_acc, table_out, star_out):
    lane = lax.broadcasted_iota(jnp.int32, (8, 128), 1)
    row = lax.broadcasted_iota(jnp.int32, (8, 128), 0)
    wide_lane = lax.broadcasted_iota(jnp.int32, (8, COARSE), 1)
    wide_row = lax.broadcasted_iota(jnp.int32, (8, COARSE), 0)
    edges = jnp.zeros((8, 128), F32)
    for comp in range(4):
        begin, past = comp * FINE, KNOT_ROWS + comp // 2 * 8
        main = knot_acc[begin : begin + FINE] + knot_acc[KNOT_HALF + begin : KNOT_HALF + begin + FINE]
        beyond = knot_acc[past : past + 8] + knot_acc[KNOT_HALF + past : KNOT_HALF + past + 8]
        if comp % 2:
            beyond = pltpu.roll(beyond, 4, 0)
        moved = pltpu.roll(jnp.where(wide_row < 3, beyond, 0.0), 1, 1)
        top = main[:8] + jnp.where(wide_lane > 0, moved, 0.0)
        store_rows(table_out, begin, top)
        store_rows(table_out, begin + 8, main[8:])
        tail, head = moved[:, :128], top[:, :128]
        if comp:
            tail = pltpu.roll(tail, 2 * comp, 1)
        head = pltpu.roll(head, 2 * comp + 1, 1)
        edges = jnp.where((lane == 2 * comp) & (row < 3), tail, edges)
        edges = jnp.where((lane == 2 * comp + 1) & (row < 3), head, edges)
    edges = with_scalars(pltpu.roll(edges, SLOT * place_ref[0], 1), scalars)
    star_out[:STAR_ROWS] = star_acc[:STAR_ROWS] + star_acc[STAR_ROWS:]
    star_out[STAR_ROWS:] = jnp.concatenate([edges, jnp.zeros_like(edges)], axis=1)


def first_kernel(live_ref, place_ref, *refs):
    sources, (table_out, star_out, knot_acc, star_acc) = refs[:8], refs[8:12]
    buffers, sems = refs[12:20], refs[20]
    half = sources[0].shape[0] // 2
    copies = []

    def begin(source, target, *place):
        source, target = (source.at[place], target.at[place]) if place else (source, target)
        copies.append(pltpu.make_async_copy(source, target, sems.at[len(copies)]))
        copies[-1].start()

    for source, target in zip(sources[:3], buffers):
        begin(source, target)
    for rows in (slice(0, half), slice(half, 2 * half)):
        for source, target in zip(sources[3:], buffers[3:]):
            begin(source, target, *[slice(None)] * (len(source.shape) - 2), rows)
    value_ref, cal_coef_ref, tile_cal_ref, knot_ref, frac_ref, *observed = buffers
    knot_acc[...] = jnp.zeros_like(knot_acc)
    star_acc[...] = jnp.zeros_like(star_acc)
    for copy in copies[:3]:
        copy.wait()
    values = value_ref[...] * live_mask(live_ref, 0, value_ref.shape)
    scatter_calibration(values * cal_coef_ref[...], tile_cal_ref, table_out)
    for copy in copies[3:8]:
        copy.wait()

    @pl.loop(0, value_ref.shape[0] // WIDE_GROUP)
    def _(group):
        @pl.when(group * WIDE_GROUP == half)
        def _():
            for copy in copies[8:]:
                copy.wait()

        first = pl.multiple_of(group * WIDE_GROUP, WIDE_GROUP)
        values = value_ref[pl.ds(first, WIDE_GROUP), :]
        values = values * live_mask(live_ref, first, values.shape)
        scatter(first, knot_factors(first, knot_ref, frac_ref), values, observed, knot_acc, star_acc)

    scatter_end(place_ref, [], knot_acc, star_acc, table_out, star_out)


def sum_kernel(block_ref, own_ref, other_ref, out_ref, star_out):
    total = block_ref[0]
    for device in range(1, block_ref.shape[0]):
        total = total + block_ref[device]
    star = own_ref[...] + other_ref[...]
    star_out[...] = star[:STAR_ROWS]
    total = jnp.concatenate([total[:, :128], total[:, 128:], star[STAR_ROWS:, :128]], axis=0)
    for device in range(block_ref.shape[0]):
        out_ref[device] = total


def picked(array, which):
    row = lax.broadcasted_iota(jnp.int32, array.shape, 0)
    lane = lax.broadcasted_iota(jnp.int32, array.shape, 1)
    chosen = (row == 0) & (lane == SCALAR_LANE + which)
    return jnp.sum(jnp.where(chosen, array, 0.0), keepdims=True)


def with_scalars(array, scalars):
    row = lax.broadcasted_iota(jnp.int32, array.shape, 0)
    lane = lax.broadcasted_iota(jnp.int32, array.shape, 1)
    for which, value in scalars:
        array = jnp.where((row == 0) & (lane == SCALAR_LANE + which), value, array)
    return array


def first_step(edges):
    return picked(edges, 0), picked(edges, 1)


def star_forward_kernel(star_ref, star_coef_ref, star_x_ref, image_ref, star_parts_ref):
    star_x = star_x_ref[...]
    star_high, star_low = two_parts(star_x)
    star_parts_ref[:STAR_ROWS] = star_high
    star_parts_ref[STAR_ROWS:] = star_low

    @pl.loop(0, star_ref.shape[0] // GROUP)
    def _(group):
        rows = pl.ds(pl.multiple_of(group * GROUP, GROUP), GROUP)
        star = star_ref[rows, :]
        coarse, fine = star & (COARSE - 1), star >> 8
        coef = [star_coef_ref[comp, rows, :] for comp in range(5)]
        tiles = [slice(tile, tile + 1) for tile in range(GROUP)]
        hot = jnp.concatenate([one_hot(coarse[here], COARSE) for here in tiles], axis=1)
        found = product(star_parts_ref[...], hot, ((1,), (0,)))
        width = star.shape[1]
        fine_rows, _ = rows_and_columns((FINE, width))
        image_rows = []
        for tile, here in enumerate(tiles):
            across = slice(tile * width, (tile + 1) * width)

            def part(comp):
                begin = comp * FINE
                return (
                    found[begin : begin + FINE, across]
                    + found[STAR_ROWS + begin : STAR_ROWS + begin + FINE, across]
                )

            both = sum(coef[comp][here] * part(comp) for comp in range(5))
            both = jnp.where(fine_rows == fine[here], both, 0.0)
            both = both[:8] + both[8:16] + both[16:24] + both[24:]
            image_rows.append(jnp.sum(both, axis=0, keepdims=True))
        image_ref[rows, :] = jnp.concatenate(image_rows, axis=0)


def received_table(n_stars, n_seg, place_ref, block_ref):
    segment = place_ref[0]
    lane = lax.broadcasted_iota(jnp.int32, (8, 128), 1)
    row = lax.broadcasted_iota(jnp.int32, (8, 128), 0)
    edges = block_ref[0, -8:, :]
    for block in range(1, n_stars):
        edges = edges + block_ref[block, -8:, :]

    def slot(which):
        return pltpu.roll(edges, 128 - SLOT * jnp.clip(which, 0, n_seg - 1), 1)

    before, own, after = slot(segment - 1), slot(segment), slot(segment + 1)
    before = jnp.where(segment > 0, before, 0.0)
    ahead = jnp.where(lane % 2 == 0, own, 0.0) + pltpu.roll(jnp.where(lane % 2 == 1, after, 0.0), 127, 1)
    ahead = jnp.where((segment < n_seg - 1) & (lane < 8) & (row < 3), ahead, 0.0)

    size = TABLE_ROWS // n_stars
    table = jnp.concatenate([block_ref[:, :size, :], block_ref[:, size : 2 * size, :]], axis=2)
    table = table.reshape(TABLE_ROWS, COARSE)
    pieces = []
    for comp in range(4):
        shifted = pltpu.roll(before, 128 - 2 * comp, 1) if comp else before
        shifted = jnp.where((lane == 0) & (row < 3), shifted, 0.0)
        top = table[comp * FINE : comp * FINE + 8]
        pieces.append(top + jnp.concatenate([shifted, jnp.zeros_like(shifted)], axis=1))
        pieces.append(table[comp * FINE + 8 : (comp + 1) * FINE])
    return jnp.concatenate(pieces + [table[KNOT_ROWS:]], axis=0), ahead, edges


def gather_ready(table, ahead, cal_coef_ref, tile_cal_ref, star_image_ref, knot_parts_ref, cal_ref):
    wide_lane = lax.broadcasted_iota(jnp.int32, (8, COARSE), 1)
    row = lax.broadcasted_iota(jnp.int32, (8, COARSE), 0)
    beyond = []
    for comp in range(4):
        moved = pltpu.roll(table[comp * FINE : comp * FINE + 8], COARSE - 1, 1)
        last = pltpu.roll(ahead, 127 - 2 * comp, 1)
        moved = jnp.where(wide_lane == COARSE - 1, jnp.concatenate([last, last], axis=1), moved)
        beyond.append(pltpu.roll(moved, 4, 0) if comp % 2 else moved)
    beyond = [jnp.where(row < 4, beyond[0], beyond[1]), jnp.where(row < 4, beyond[2], beyond[3])]
    knot_high, knot_low = two_parts(jnp.concatenate([table[:KNOT_ROWS]] + beyond, axis=0))
    knot_parts_ref[:KNOT_HALF] = knot_high
    knot_parts_ref[KNOT_HALF:] = knot_low

    blocks = jnp.concatenate([table[KNOT_ROWS:, :128], table[KNOT_ROWS:, 128:]], axis=0)
    rows = product(
        one_hot(tile_cal_ref[...], CALB_DEV), jnp.concatenate(two_parts(blocks), axis=1), ((0,), (0,))
    )
    cal_ref[...] = (rows[:, :128] + rows[:, 128:]) * cal_coef_ref[...] + star_image_ref[...]


def gather(first, live_ref, factors, att_coef_ref, knot_parts_ref, cal_ref):
    rows = pl.ds(first, WIDE_GROUP)
    coef = [att_coef_ref[comp, rows, :] for comp in range(4)]
    hot, columns = factors
    found = product(knot_parts_ref[...], hot, ((1,), (0,)))
    width = cal_ref.shape[1]
    image_rows = []
    for tile in range(WIDE_GROUP):
        here = slice(tile, tile + 1)
        across = slice(tile * width, (tile + 1) * width)

        def part(begin, size):
            return (
                found[begin : begin + size, across]
                + found[KNOT_HALF + begin : KNOT_HALF + begin + size, across]
            )

        near, past = columns[tile]
        near = near * sum(coef[comp][here] * part(comp * FINE, FINE) for comp in range(4))
        past = past * past_terms(coef, here) * part(KNOT_ROWS, PAST_ROWS)
        both = near[:8] + near[8:16] + near[16:24] + near[24:] + past[:8] + past[8:]
        image_rows.append(jnp.sum(both, axis=0, keepdims=True))
    image = jnp.concatenate(image_rows, axis=0) + cal_ref[rows, :]
    return image * live_mask(live_ref, first, image.shape)


def squares(array):
    return jnp.sum(array * array, keepdims=True)


def middle_kernel(
    n_stars, n_seg, live_ref, place_ref, knot_ref, frac_ref, att_coef_ref, star_ref, star_coef_ref,
    cal_coef_ref, tile_cal_ref, star_image_ref, star_x_ref, block_ref, image_ref, table_out, scatter_out,
    star_out, knot_parts_ref, cal_ref, knot_acc, star_acc,
):
    table, ahead, _ = received_table(n_stars, n_seg, place_ref, block_ref)
    table_out[...] = table
    norm = squares(star_x_ref[...]) / n_seg + squares(table) / n_stars
    gather_ready(table, ahead, cal_coef_ref, tile_cal_ref, star_image_ref, knot_parts_ref, cal_ref)
    knot_acc[...] = jnp.zeros_like(knot_acc)
    star_acc[...] = jnp.zeros_like(star_acc)
    def one_group(group, total):
        first = pl.multiple_of(group * WIDE_GROUP, WIDE_GROUP)
        factors = knot_factors(first, knot_ref, frac_ref)
        image = gather(first, live_ref, factors, att_coef_ref, knot_parts_ref, cal_ref)
        image_ref[pl.ds(first, WIDE_GROUP), :] = image
        scatter(first, factors, image, (att_coef_ref, star_ref, star_coef_ref), knot_acc, star_acc)
        return total + image * image

    zero = jnp.zeros((WIDE_GROUP, knot_ref.shape[1]), F32)
    total = lax.fori_loop(0, knot_ref.shape[0] // WIDE_GROUP, one_group, zero)
    scatter_calibration(image_ref[...] * cal_coef_ref[...], tile_cal_ref, scatter_out)
    scalars = [(0, norm), (1, jnp.sum(total, keepdims=True))]
    scatter_end(place_ref, scalars, knot_acc, star_acc, scatter_out, star_out)


def last_kernel(
    n_stars, n_seg, live_ref, place_ref, knot_ref, frac_ref, att_coef_ref, cal_coef_ref, tile_cal_ref,
    star_image_ref, star_x_ref, block_ref, star_0_ref, table_0_ref, image_0_ref, image_ref, table_out,
    scalar_out, own_scalar_out, knot_parts_ref, cal_ref,
):
    table, ahead, edges = received_table(n_stars, n_seg, place_ref, block_ref)
    table_out[...] = table
    norm_0, square_0 = first_step(edges)
    step = norm_0 / square_0
    norm = (
        squares(star_0_ref[...] - step * star_x_ref[...]) / n_seg
        + squares(table_0_ref[...] - step * table) / n_stars
    )
    gather_ready(table, ahead, cal_coef_ref, tile_cal_ref, star_image_ref, knot_parts_ref, cal_ref)

    def one_group(group, sums):
        first = pl.multiple_of(group * WIDE_GROUP, WIDE_GROUP)
        rows = pl.ds(first, WIDE_GROUP)
        image_0 = image_0_ref[rows, :]
        factors = knot_factors(first, knot_ref, frac_ref)
        image = gather(first, live_ref, factors, att_coef_ref, knot_parts_ref, cal_ref)
        image = image_0 - step * image
        image_ref[rows, :] = image
        return sums[0] + image * image, sums[1] + image * image_0

    zero = jnp.zeros((WIDE_GROUP, knot_ref.shape[1]), F32)
    sums = lax.fori_loop(0, knot_ref.shape[0] // WIDE_GROUP, one_group, (zero, zero))
    scalars = [norm] + [jnp.sum(part, keepdims=True) for part in sums] + [norm_0, square_0]
    scalars = with_scalars(jnp.zeros((8, 128), F32), list(enumerate(scalars)))
    own_scalar_out[...] = scalars
    for device in range(scalar_out.shape[0]):
        scalar_out[device] = scalars


def output_kernel(
    live_ref, own_scalar_ref, scalar_ref, star_0_ref, star_h_ref, att_0_ref, att_h_ref, table_0_ref,
    table_h_ref, value_ref, image_0_ref, image_1_ref, star_out, att_out, cal_out, residual_out,
):
    norm_0, square_0 = [picked(own_scalar_ref[...], which) for which in (3, 4)]
    everyone = scalar_ref[0]
    for device in range(1, scalar_ref.shape[0]):
        everyone = everyone + scalar_ref[device]
    norm_1, square_1, cross = [picked(everyone, which) for which in range(3)]
    step_0 = norm_0 / square_0
    ratio = norm_1 / norm_0
    step_1 = norm_1 / (square_1 + 2.0 * ratio * cross + ratio * ratio * square_0)
    scale = step_0 + step_1 * ratio

    def combined(old, change):
        return scale * old + step_1 * (old - step_0 * change)

    star_out[...] = combined(star_0_ref[...], star_h_ref[...])
    att_out[...] = combined(att_0_ref[...], att_h_ref[...])
    cal = combined(table_0_ref[KNOT_ROWS:, :], table_h_ref[KNOT_ROWS:, :])
    cal_out[...] = jnp.concatenate([cal[:, :128], cal[:, 128:]], axis=0)
    values = value_ref[...] * live_mask(live_ref, 0, value_ref.shape)
    residual_out[...] = values - scale * image_0_ref[...] - step_1 * image_1_ref[...]


def in_vmem(count):
    return [pl.BlockSpec(memory_space=pltpu.VMEM)] * count


def in_smem(count):
    return [pl.BlockSpec(memory_space=pltpu.SMEM)] * count


def in_hbm(count):
    return [pl.BlockSpec(memory_space=pltpu.HBM)] * count


def shaped(*shape):
    return jax.ShapeDtypeStruct(shape, F32)


ARRIVE_PARAMS = pltpu.CompilerParams(vmem_limit_bytes=60 * 1024 * 1024)
PARAMS = pltpu.CompilerParams(vmem_limit_bytes=40 * 1024 * 1024)
PASS_COST = pl.CostEstimate(flops=3_000_000_000, bytes_accessed=1_000_000, transcendentals=0)
SMALL_COST = pl.CostEstimate(flops=1_000_000, bytes_accessed=600_000, transcendentals=0)


def on_device(
    obs_star, obs_knot, obs_frac, star_coef, att_coef, cal_coef, tile_cal, live_tiles, obs_value
):
    n_stars, n_seg = lax.axis_size("stars"), lax.axis_size("seg")
    tile_count, width = obs_star.shape
    tile_row = tile_cal[None, :]
    place = lax.axis_index("seg").astype(jnp.int32)[None]
    image_shape = shaped(tile_count, width)
    table_shape = shaped(TABLE_ROWS, COARSE)
    star_shape = shaped(STAR_ROWS, COARSE)
    sent_shapes = (shaped(n_stars, TABLE_ROWS // n_stars, COARSE), shaped(STAR_ROWS + 8, COARSE))
    sums = [pltpu.VMEM((2 * KNOT_HALF, COARSE), F32), pltpu.VMEM((2 * STAR_ROWS, COARSE), F32)]
    ready = [pltpu.VMEM((2 * KNOT_HALF, COARSE), BF16), pltpu.VMEM((tile_count, width), F32)]

    def first_scatter():
        observed = (obs_value, cal_coef, tile_row, obs_knot, obs_frac, att_coef, obs_star, star_coef)
        buffers = [pltpu.VMEM(array.shape, array.dtype) for array in observed]
        return pl.pallas_call(
            first_kernel,
            out_shape=sent_shapes,
            in_specs=in_smem(2) + in_hbm(len(observed)),
            out_specs=tuple(in_vmem(2)),
            scratch_shapes=sums + buffers + [pltpu.SemaphoreType.DMA((13,))],
            compiler_params=ARRIVE_PARAMS,
            cost_estimate=PASS_COST,
            name="first_scatter",
        )(live_tiles, place, *observed)

    def middle(*received):
        observed = (obs_knot, obs_frac, att_coef, obs_star, star_coef, cal_coef, tile_row)
        return pl.pallas_call(
            functools.partial(middle_kernel, n_stars, n_seg),
            out_shape=(image_shape, table_shape, *sent_shapes),
            in_specs=in_smem(2) + in_vmem(len(observed) + len(received)),
            out_specs=tuple(in_vmem(4)),
            scratch_shapes=ready + sums,
            compiler_params=PARAMS,
            cost_estimate=PASS_COST,
            name="gather_and_scatter",
        )(live_tiles, place, *observed, *received)

    def last_gather(*received):
        observed = (obs_knot, obs_frac, att_coef, cal_coef, tile_row)
        return pl.pallas_call(
            functools.partial(last_kernel, n_stars, n_seg),
            out_shape=(image_shape, table_shape, shaped(n_stars * n_seg, 8, 128), shaped(8, 128)),
            in_specs=in_smem(2) + in_vmem(len(observed) + len(received)),
            out_specs=tuple(in_vmem(4)),
            scratch_shapes=ready,
            compiler_params=PARAMS,
            cost_estimate=PASS_COST,
            name="last_gather",
        )(live_tiles, place, *observed, *received)

    def star_forward(star):
        return pl.pallas_call(
            star_forward_kernel,
            out_shape=image_shape,
            in_specs=in_vmem(3),
            out_specs=in_vmem(1)[0],
            scratch_shapes=[pltpu.VMEM((2 * STAR_ROWS, COARSE), BF16)],
            compiler_params=PARAMS,
            cost_estimate=PASS_COST,
            name="star_forward",
        )(obs_star, star_coef, star)

    def swap(blocks, axes):
        return lax.all_to_all(blocks, axes, 0, 0)

    def partner(array, axis, distance):
        return lax.ppermute(array, axis, [(i, i ^ distance) for i in range(lax.axis_size(axis))])

    def reduced(table, star):
        distances = [1 << bit for bit in range(n_seg.bit_length() - 1)]
        for distance in distances[:-1]:
            star = star + partner(star, "seg", distance)
        blocks, star = pl.pallas_call(
            sum_kernel,
            out_shape=(shaped(n_stars, 2 * TABLE_ROWS // n_stars + 8, 128), star_shape),
            in_specs=in_vmem(3),
            out_specs=tuple(in_vmem(2)),
            compiler_params=PARAMS,
            cost_estimate=SMALL_COST,
            name="table_sum",
        )(swap(table, "stars"), star, partner(star, "seg", distances[-1]))
        return star_forward(star), star, swap(blocks, "stars")

    first = reduced(*first_scatter())
    star_0 = first[1]
    image_0, table_0, *sent = middle(*first)
    second = reduced(*sent)
    star_h = second[1]
    image_1, table_h, scalars, own_scalars = last_gather(*second, star_0, table_0, image_0)

    def star_order(star):
        return star.reshape(5, STAR_DEV)

    def att_order(table):
        att = table[:KNOT_ROWS].reshape(4, FINE, COARSE)
        return att.transpose(0, 2, 1).reshape(4, KNOT_DEV)

    return pl.pallas_call(
        output_kernel,
        out_shape=(shaped(5, STAR_DEV), shaped(4, KNOT_DEV), shaped(CALB_DEV, width), image_shape),
        in_specs=in_smem(1) + in_vmem(11),
        out_specs=tuple(in_vmem(4)),
        compiler_params=PARAMS,
        cost_estimate=SMALL_COST,
        name="outputs",
    )(
        live_tiles, own_scalars, swap(scalars, ("stars", "seg")), star_order(star_0), star_order(star_h),
        att_order(table_0), att_order(table_h), table_0, table_h, obs_value, image_0, image_1,
    )


def solution(mesh):
    placed = (
        P(("stars", "seg"), None),
        P(("stars", "seg"), None),
        P(("stars", "seg"), None),
        P(None, ("stars", "seg"), None),
        P(None, ("stars", "seg"), None),
        P(("stars", "seg"), None),
        P(("stars", "seg")),
        P(("stars", "seg")),
        P(("stars", "seg"), None),
    )
    return jax.shard_map(
        on_device,
        mesh=mesh,
        in_specs=placed,
        out_specs=(P(None, "stars"), P(None, "seg"), P("seg", None), P(("stars", "seg"), None)),
        check_vma=False,
    )
```

```python
import functools

import jax
import jax.numpy as jnp
from jax import lax
from jax.experimental import pallas as pl
from jax.experimental.pallas import tpu as pltpu
from jax.sharding import PartitionSpec as P

STAR_DEV = 8192
KNOT_DEV = 8192
CALB_DEV = 256
FINE = 32
COARSE = 256
GROUP = 16
WIDE_GROUP = 64
SLOT = 8
STAR_ROWS = 5 * FINE
KNOT_ROWS = 4 * FINE
TABLE_ROWS = KNOT_ROWS + CALB_DEV // 2
BF16 = jnp.bfloat16
F32 = jnp.float32
SCALAR_LANE = 64
PAST_ROWS = 16
KNOT_HALF = KNOT_ROWS + PAST_ROWS


def two_parts(values):
    high = values.astype(BF16)
    return high, (values - high.astype(F32)).astype(BF16)


def rows_and_columns(shape):
    return lax.broadcasted_iota(jnp.int32, shape, 0), lax.broadcasted_iota(jnp.int32, shape, 1)


def packed_rows(row, size):
    wide = jnp.broadcast_to(row.astype(F32), (16, row.shape[1])).astype(BF16)
    return jnp.concatenate([wide] * (size // 16), axis=0)


def matches(index_row, size):
    places, _ = rows_and_columns((size, index_row.shape[1]))
    return places.astype(F32).astype(BF16) == packed_rows(index_row, size)


def one_hot(index_row, size):
    return jnp.where(matches(index_row, size), jnp.ones((), BF16), jnp.zeros((), BF16))


def spline_weights(fraction):
    remain = 1.0 - fraction
    square = fraction * fraction
    cubed = square * fraction
    return (
        remain * remain * remain / 6.0,
        (3.0 * cubed - 6.0 * square + 4.0) / 6.0,
        (-3.0 * cubed + 3.0 * square + 3.0 * fraction + 1.0) / 6.0,
        cubed / 6.0,
    )


def weight_columns(weights, fine_row, tile, places):
    behind = places - fine_row
    result = jnp.zeros(behind.shape, F32)
    for offset in range(4):
        result = jnp.where(behind == offset, weights[offset][tile : tile + 1], result)
    return result


def near_and_past(weights, fine, tile):
    width = fine.shape[1]
    fine_row = fine[tile : tile + 1]
    near, _ = rows_and_columns((FINE, width))
    past, _ = rows_and_columns((PAST_ROWS, width))
    past = FINE + (past & 3)
    return weight_columns(weights, fine_row, tile, near), weight_columns(weights, fine_row, tile, past)


def past_terms(terms, here):
    rows, _ = rows_and_columns((PAST_ROWS, terms[0].shape[1]))
    result = jnp.broadcast_to(terms[3][here], rows.shape)
    for comp in range(2, -1, -1):
        result = jnp.where(rows < 4 * (comp + 1), terms[comp][here], result)
    return result


def product(left, right, contract):
    return lax.dot_general(left, right, (contract, ((), ())), preferred_element_type=F32)


def live_mask(live_ref, first, shape):
    rows, _ = rows_and_columns(shape)
    return (rows + first < live_ref[0]).astype(F32)


def store_rows(out_ref, begin, rows):
    block = out_ref.shape[1]
    for offset in range(0, rows.shape[0], 8):
        where = begin + offset
        out_ref[where // block, where % block : where % block + 8, :] = rows[offset : offset + 8]


def knot_factors(first, knot_ref, frac_ref):
    rows = pl.ds(first, WIDE_GROUP)
    knot = knot_ref[rows, :]
    coarse, fine = knot >> 5, knot & (FINE - 1)
    weights = spline_weights(frac_ref[rows, :])
    hot = [one_hot(coarse[tile : tile + 1], COARSE) for tile in range(WIDE_GROUP)]
    columns = [near_and_past(weights, fine, tile) for tile in range(WIDE_GROUP)]
    return jnp.concatenate(hot, axis=1), columns


def scatter(first, factors, values, observed, knot_acc, star_acc):
    att_coef_ref, star_ref, star_coef_ref = observed
    rows = pl.ds(first, WIDE_GROUP)
    knot_hot, columns = factors
    star = star_ref[rows, :]
    star_coarse, star_fine = star & (COARSE - 1), star >> 8
    terms = [att_coef_ref[comp, rows, :] * values for comp in range(4)]
    parts = [two_parts(star_coef_ref[comp, rows, :] * values) for comp in range(5)]
    parts = [pair[half].astype(F32) for half in range(2) for pair in parts]
    knot_left, star_left, star_right = [], [], []
    for tile in range(WIDE_GROUP):
        here = slice(tile, tile + 1)
        near, past = columns[tile]
        spread = jnp.concatenate(
            [term[here] * near for term in terms] + [past_terms(terms, here) * past], axis=0
        )
        knot_left.append(jnp.concatenate(two_parts(spread), axis=0))
        star_right.append(one_hot(star_coarse[here], COARSE))
        chosen = matches(star_fine[here], FINE)
        star_left.append(
            jnp.concatenate(
                [jnp.where(chosen, packed_rows(part[here], FINE), jnp.zeros((), BF16)) for part in parts],
                axis=0,
            )
        )
    knot_acc[...] += product(
        jnp.concatenate(knot_left, axis=1), knot_hot, ((1,), (1,))
    )
    star_acc[...] += product(
        jnp.concatenate(star_left, axis=1), jnp.concatenate(star_right, axis=1), ((1,), (1,))
    )


def scatter_calibration(values, tile_cal_ref, table_out):
    blocks = product(
        one_hot(tile_cal_ref[...], CALB_DEV), jnp.concatenate(two_parts(values), axis=1), ((1,), (0,))
    )
    width = values.shape[1]
    blocks = blocks[:, :width] + blocks[:, width:]
    blocks = jnp.concatenate([blocks[: CALB_DEV // 2], blocks[CALB_DEV // 2 :]], axis=1)
    store_rows(table_out, KNOT_ROWS, blocks)


def scatter_end(place_ref, scalars, knot_acc, star_acc, table_out, star_out):
    lane = lax.broadcasted_iota(jnp.int32, (8, 128), 1)
    row = lax.broadcasted_iota(jnp.int32, (8, 128), 0)
    wide_lane = lax.broadcasted_iota(jnp.int32, (8, COARSE), 1)
    wide_row = lax.broadcasted_iota(jnp.int32, (8, COARSE), 0)
    edges = jnp.zeros((8, 128), F32)
    for comp in range(4):
        begin, past = comp * FINE, KNOT_ROWS + comp // 2 * 8
        main = knot_acc[begin : begin + FINE] + knot_acc[KNOT_HALF + begin : KNOT_HALF + begin + FINE]
        beyond = knot_acc[past : past + 8] + knot_acc[KNOT_HALF + past : KNOT_HALF + past + 8]
        if comp % 2:
            beyond = pltpu.roll(beyond, 4, 0)
        moved = pltpu.roll(jnp.where(wide_row < 3, beyond, 0.0), 1, 1)
        top = main[:8] + jnp.where(wide_lane > 0, moved, 0.0)
        store_rows(table_out, begin, top)
        store_rows(table_out, begin + 8, main[8:])
        tail, head = moved[:, :128], top[:, :128]
        if comp:
            tail = pltpu.roll(tail, 2 * comp, 1)
        head = pltpu.roll(head, 2 * comp + 1, 1)
        edges = jnp.where((lane == 2 * comp) & (row < 3), tail, edges)
        edges = jnp.where((lane == 2 * comp + 1) & (row < 3), head, edges)
    edges = with_scalars(pltpu.roll(edges, SLOT * place_ref[0], 1), scalars)
    star_out[:STAR_ROWS] = star_acc[:STAR_ROWS] + star_acc[STAR_ROWS:]
    star_out[STAR_ROWS:] = jnp.concatenate([edges, jnp.zeros_like(edges)], axis=1)


def first_kernel(live_ref, place_ref, *refs):
    sources, (table_out, star_out, knot_acc, star_acc) = refs[:8], refs[8:12]
    buffers, sems = refs[12:20], refs[20]
    half = sources[0].shape[0] // 2
    copies = []

    def begin(source, target, *place):
        source, target = (source.at[place], target.at[place]) if place else (source, target)
        copies.append(pltpu.make_async_copy(source, target, sems.at[len(copies)]))
        copies[-1].start()

    for source, target in zip(sources[:3], buffers):
        begin(source, target)
    for rows in (slice(0, half), slice(half, 2 * half)):
        for source, target in zip(sources[3:], buffers[3:]):
            begin(source, target, *[slice(None)] * (len(source.shape) - 2), rows)
    value_ref, cal_coef_ref, tile_cal_ref, knot_ref, frac_ref, *observed = buffers
    knot_acc[...] = jnp.zeros_like(knot_acc)
    star_acc[...] = jnp.zeros_like(star_acc)
    for copy in copies[:3]:
        copy.wait()
    values = value_ref[...] * live_mask(live_ref, 0, value_ref.shape)
    scatter_calibration(values * cal_coef_ref[...], tile_cal_ref, table_out)
    for copy in copies[3:8]:
        copy.wait()

    @pl.loop(0, value_ref.shape[0] // WIDE_GROUP)
    def _(group):
        @pl.when(group * WIDE_GROUP == half)
        def _():
            for copy in copies[8:]:
                copy.wait()

        first = pl.multiple_of(group * WIDE_GROUP, WIDE_GROUP)
        values = value_ref[pl.ds(first, WIDE_GROUP), :]
        values = values * live_mask(live_ref, first, values.shape)
        scatter(first, knot_factors(first, knot_ref, frac_ref), values, observed, knot_acc, star_acc)

    scatter_end(place_ref, [], knot_acc, star_acc, table_out, star_out)


def sum_kernel(block_ref, own_ref, other_ref, out_ref, star_out):
    total = block_ref[0]
    for device in range(1, block_ref.shape[0]):
        total = total + block_ref[device]
    star = own_ref[...] + other_ref[...]
    star_out[...] = star[:STAR_ROWS]
    total = jnp.concatenate([total[:, :128], total[:, 128:], star[STAR_ROWS:, :128]], axis=0)
    for device in range(block_ref.shape[0]):
        out_ref[device] = total


def picked(array, which):
    row = lax.broadcasted_iota(jnp.int32, array.shape, 0)
    lane = lax.broadcasted_iota(jnp.int32, array.shape, 1)
    chosen = (row == 0) & (lane == SCALAR_LANE + which)
    return jnp.sum(jnp.where(chosen, array, 0.0), keepdims=True)


def with_scalars(array, scalars):
    row = lax.broadcasted_iota(jnp.int32, array.shape, 0)
    lane = lax.broadcasted_iota(jnp.int32, array.shape, 1)
    for which, value in scalars:
        array = jnp.where((row == 0) & (lane == SCALAR_LANE + which), value, array)
    return array


def first_step(edges):
    return picked(edges, 0), picked(edges, 1)


def star_forward_kernel(star_ref, star_coef_ref, star_x_ref, image_ref, star_parts_ref):
    star_x = star_x_ref[...]
    star_high, star_low = two_parts(star_x)
    star_parts_ref[:STAR_ROWS] = star_high
    star_parts_ref[STAR_ROWS:] = star_low

    @pl.loop(0, star_ref.shape[0] // GROUP)
    def _(group):
        rows = pl.ds(pl.multiple_of(group * GROUP, GROUP), GROUP)
        star = star_ref[rows, :]
        coarse, fine = star & (COARSE - 1), star >> 8
        coef = [star_coef_ref[comp, rows, :] for comp in range(5)]
        tiles = [slice(tile, tile + 1) for tile in range(GROUP)]
        hot = jnp.concatenate([one_hot(coarse[here], COARSE) for here in tiles], axis=1)
        found = product(star_parts_ref[...], hot, ((1,), (0,)))
        width = star.shape[1]
        fine_rows, _ = rows_and_columns((FINE, width))
        image_rows = []
        for tile, here in enumerate(tiles):
            across = slice(tile * width, (tile + 1) * width)

            def part(comp):
                begin = comp * FINE
                return (
                    found[begin : begin + FINE, across]
                    + found[STAR_ROWS + begin : STAR_ROWS + begin + FINE, across]
                )

            both = sum(coef[comp][here] * part(comp) for comp in range(5))
            both = jnp.where(fine_rows == fine[here], both, 0.0)
            both = both[:8] + both[8:16] + both[16:24] + both[24:]
            image_rows.append(jnp.sum(both, axis=0, keepdims=True))
        image_ref[rows, :] = jnp.concatenate(image_rows, axis=0)


def received_table(n_stars, n_seg, place_ref, block_ref):
    segment = place_ref[0]
    lane = lax.broadcasted_iota(jnp.int32, (8, 128), 1)
    row = lax.broadcasted_iota(jnp.int32, (8, 128), 0)
    edges = block_ref[0, -8:, :]
    for block in range(1, n_stars):
        edges = edges + block_ref[block, -8:, :]

    def slot(which):
        return pltpu.roll(edges, 128 - SLOT * jnp.clip(which, 0, n_seg - 1), 1)

    before, own, after = slot(segment - 1), slot(segment), slot(segment + 1)
    before = jnp.where(segment > 0, before, 0.0)
    ahead = jnp.where(lane % 2 == 0, own, 0.0) + pltpu.roll(jnp.where(lane % 2 == 1, after, 0.0), 127, 1)
    ahead = jnp.where((segment < n_seg - 1) & (lane < 8) & (row < 3), ahead, 0.0)

    size = TABLE_ROWS // n_stars
    table = jnp.concatenate([block_ref[:, :size, :], block_ref[:, size : 2 * size, :]], axis=2)
    table = table.reshape(TABLE_ROWS, COARSE)
    pieces = []
    for comp in range(4):
        shifted = pltpu.roll(before, 128 - 2 * comp, 1) if comp else before
        shifted = jnp.where((lane == 0) & (row < 3), shifted, 0.0)
        top = table[comp * FINE : comp * FINE + 8]
        pieces.append(top + jnp.concatenate([shifted, jnp.zeros_like(shifted)], axis=1))
        pieces.append(table[comp * FINE + 8 : (comp + 1) * FINE])
    return jnp.concatenate(pieces + [table[KNOT_ROWS:]], axis=0), ahead, edges


def gather_ready(table, ahead, cal_coef_ref, tile_cal_ref, star_image_ref, knot_parts_ref, cal_ref):
    wide_lane = lax.broadcasted_iota(jnp.int32, (8, COARSE), 1)
    row = lax.broadcasted_iota(jnp.int32, (8, COARSE), 0)
    beyond = []
    for comp in range(4):
        moved = pltpu.roll(table[comp * FINE : comp * FINE + 8], COARSE - 1, 1)
        last = pltpu.roll(ahead, 127 - 2 * comp, 1)
        moved = jnp.where(wide_lane == COARSE - 1, jnp.concatenate([last, last], axis=1), moved)
        beyond.append(pltpu.roll(moved, 4, 0) if comp % 2 else moved)
    beyond = [jnp.where(row < 4, beyond[0], beyond[1]), jnp.where(row < 4, beyond[2], beyond[3])]
    knot_high, knot_low = two_parts(jnp.concatenate([table[:KNOT_ROWS]] + beyond, axis=0))
    knot_parts_ref[:KNOT_HALF] = knot_high
    knot_parts_ref[KNOT_HALF:] = knot_low

    blocks = jnp.concatenate([table[KNOT_ROWS:, :128], table[KNOT_ROWS:, 128:]], axis=0)
    rows = product(
        one_hot(tile_cal_ref[...], CALB_DEV), jnp.concatenate(two_parts(blocks), axis=1), ((0,), (0,))
    )
    cal_ref[...] = (rows[:, :128] + rows[:, 128:]) * cal_coef_ref[...] + star_image_ref[...]


def gather(first, live_ref, factors, att_coef_ref, knot_parts_ref, cal_ref):
    rows = pl.ds(first, WIDE_GROUP)
    coef = [att_coef_ref[comp, rows, :] for comp in range(4)]
    hot, columns = factors
    found = product(knot_parts_ref[...], hot, ((1,), (0,)))
    width = cal_ref.shape[1]
    image_rows = []
    for tile in range(WIDE_GROUP):
        here = slice(tile, tile + 1)
        across = slice(tile * width, (tile + 1) * width)

        def part(begin, size):
            return (
                found[begin : begin + size, across]
                + found[KNOT_HALF + begin : KNOT_HALF + begin + size, across]
            )

        near, past = columns[tile]
        near = near * sum(coef[comp][here] * part(comp * FINE, FINE) for comp in range(4))
        past = past * past_terms(coef, here) * part(KNOT_ROWS, PAST_ROWS)
        both = near[:8] + near[8:16] + near[16:24] + near[24:] + past[:8] + past[8:]
        image_rows.append(jnp.sum(both, axis=0, keepdims=True))
    image = jnp.concatenate(image_rows, axis=0) + cal_ref[rows, :]
    return image * live_mask(live_ref, first, image.shape)


def squares(array):
    return jnp.sum(array * array, keepdims=True)


def middle_kernel(
    n_stars, n_seg, live_ref, place_ref, knot_ref, frac_ref, att_coef_ref, star_ref, star_coef_ref,
    cal_coef_ref, tile_cal_ref, star_image_ref, star_x_ref, block_ref, image_ref, table_out, scatter_out,
    star_out, knot_parts_ref, cal_ref, knot_acc, star_acc,
):
    table, ahead, _ = received_table(n_stars, n_seg, place_ref, block_ref)
    table_out[...] = table
    norm = squares(star_x_ref[...]) / n_seg + squares(table) / n_stars
    gather_ready(table, ahead, cal_coef_ref, tile_cal_ref, star_image_ref, knot_parts_ref, cal_ref)
    knot_acc[...] = jnp.zeros_like(knot_acc)
    star_acc[...] = jnp.zeros_like(star_acc)
    def one_group(group, total):
        first = pl.multiple_of(group * WIDE_GROUP, WIDE_GROUP)
        factors = knot_factors(first, knot_ref, frac_ref)
        image = gather(first, live_ref, factors, att_coef_ref, knot_parts_ref, cal_ref)
        image_ref[pl.ds(first, WIDE_GROUP), :] = image
        scatter(first, factors, image, (att_coef_ref, star_ref, star_coef_ref), knot_acc, star_acc)
        return total + image * image

    zero = jnp.zeros((WIDE_GROUP, knot_ref.shape[1]), F32)
    total = lax.fori_loop(0, knot_ref.shape[0] // WIDE_GROUP, one_group, zero)
    scatter_calibration(image_ref[...] * cal_coef_ref[...], tile_cal_ref, scatter_out)
    scalars = [(0, norm), (1, jnp.sum(total, keepdims=True))]
    scatter_end(place_ref, scalars, knot_acc, star_acc, scatter_out, star_out)


def last_kernel(
    n_stars, n_seg, live_ref, place_ref, knot_ref, frac_ref, att_coef_ref, cal_coef_ref, tile_cal_ref,
    star_image_ref, star_x_ref, block_ref, star_0_ref, table_0_ref, image_0_ref, image_ref, table_out,
    scalar_out, own_scalar_out, knot_parts_ref, cal_ref,
):
    table, ahead, edges = received_table(n_stars, n_seg, place_ref, block_ref)
    table_out[...] = table
    norm_0, square_0 = first_step(edges)
    step = norm_0 / square_0
    norm = (
        squares(star_0_ref[...] - step * star_x_ref[...]) / n_seg
        + squares(table_0_ref[...] - step * table) / n_stars
    )
    gather_ready(table, ahead, cal_coef_ref, tile_cal_ref, star_image_ref, knot_parts_ref, cal_ref)

    def one_group(group, sums):
        first = pl.multiple_of(group * WIDE_GROUP, WIDE_GROUP)
        rows = pl.ds(first, WIDE_GROUP)
        image_0 = image_0_ref[rows, :]
        factors = knot_factors(first, knot_ref, frac_ref)
        image = gather(first, live_ref, factors, att_coef_ref, knot_parts_ref, cal_ref)
        image = image_0 - step * image
        image_ref[rows, :] = image
        return sums[0] + image * image, sums[1] + image * image_0

    zero = jnp.zeros((WIDE_GROUP, knot_ref.shape[1]), F32)
    sums = lax.fori_loop(0, knot_ref.shape[0] // WIDE_GROUP, one_group, (zero, zero))
    scalars = [norm] + [jnp.sum(part, keepdims=True) for part in sums] + [norm_0, square_0]
    scalars = with_scalars(jnp.zeros((8, 128), F32), list(enumerate(scalars)))
    own_scalar_out[...] = scalars
    for device in range(scalar_out.shape[0]):
        scalar_out[device] = scalars


def output_kernel(
    live_ref, own_scalar_ref, scalar_ref, star_0_ref, star_h_ref, att_0_ref, att_h_ref, table_0_ref,
    table_h_ref, value_ref, image_0_ref, image_1_ref, star_out, att_out, cal_out, residual_out,
):
    norm_0, square_0 = [picked(own_scalar_ref[...], which) for which in (3, 4)]
    everyone = scalar_ref[0]
    for device in range(1, scalar_ref.shape[0]):
        everyone = everyone + scalar_ref[device]
    norm_1, square_1, cross = [picked(everyone, which) for which in range(3)]
    step_0 = norm_0 / square_0
    ratio = norm_1 / norm_0
    step_1 = norm_1 / (square_1 + 2.0 * ratio * cross + ratio * ratio * square_0)
    scale = step_0 + step_1 * ratio

    def combined(old, change):
        return scale * old + step_1 * (old - step_0 * change)

    star_out[...] = combined(star_0_ref[...], star_h_ref[...])
    att_out[...] = combined(att_0_ref[...], att_h_ref[...])
    cal = combined(table_0_ref[KNOT_ROWS:, :], table_h_ref[KNOT_ROWS:, :])
    cal_out[...] = jnp.concatenate([cal[:, :128], cal[:, 128:]], axis=0)
    values = value_ref[...] * live_mask(live_ref, 0, value_ref.shape)
    residual_out[...] = values - scale * image_0_ref[...] - step_1 * image_1_ref[...]


def in_vmem(count):
    return [pl.BlockSpec(memory_space=pltpu.VMEM)] * count


def in_smem(count):
    return [pl.BlockSpec(memory_space=pltpu.SMEM)] * count


def in_hbm(count):
    return [pl.BlockSpec(memory_space=pltpu.HBM)] * count


def shaped(*shape):
    return jax.ShapeDtypeStruct(shape, F32)


ARRIVE_PARAMS = pltpu.CompilerParams(vmem_limit_bytes=60 * 1024 * 1024)
PARAMS = pltpu.CompilerParams(vmem_limit_bytes=40 * 1024 * 1024)
PASS_COST = pl.CostEstimate(flops=3_000_000_000, bytes_accessed=1_000_000, transcendentals=0)
SMALL_COST = pl.CostEstimate(flops=1_000_000, bytes_accessed=600_000, transcendentals=0)


def on_device(
    obs_star, obs_knot, obs_frac, star_coef, att_coef, cal_coef, tile_cal, live_tiles, obs_value
):
    n_stars, n_seg = lax.axis_size("stars"), lax.axis_size("seg")
    tile_count, width = obs_star.shape
    tile_row = tile_cal[None, :]
    place = lax.axis_index("seg").astype(jnp.int32)[None]
    image_shape = shaped(tile_count, width)
    table_shape = shaped(TABLE_ROWS, COARSE)
    star_shape = shaped(STAR_ROWS, COARSE)
    sent_shapes = (shaped(n_stars, TABLE_ROWS // n_stars, COARSE), shaped(STAR_ROWS + 8, COARSE))
    sums = [pltpu.VMEM((2 * KNOT_HALF, COARSE), F32), pltpu.VMEM((2 * STAR_ROWS, COARSE), F32)]
    ready = [pltpu.VMEM((2 * KNOT_HALF, COARSE), BF16), pltpu.VMEM((tile_count, width), F32)]

    def first_scatter():
        observed = (obs_value, cal_coef, tile_row, obs_knot, obs_frac, att_coef, obs_star, star_coef)
        buffers = [pltpu.VMEM(array.shape, array.dtype) for array in observed]
        return pl.pallas_call(
            first_kernel,
            out_shape=sent_shapes,
            in_specs=in_smem(2) + in_hbm(len(observed)),
            out_specs=tuple(in_vmem(2)),
            scratch_shapes=sums + buffers + [pltpu.SemaphoreType.DMA((13,))],
            compiler_params=ARRIVE_PARAMS,
            cost_estimate=PASS_COST,
            name="first_scatter",
        )(live_tiles, place, *observed)

    def middle(*received):
        observed = (obs_knot, obs_frac, att_coef, obs_star, star_coef, cal_coef, tile_row)
        return pl.pallas_call(
            functools.partial(middle_kernel, n_stars, n_seg),
            out_shape=(image_shape, table_shape, *sent_shapes),
            in_specs=in_smem(2) + in_vmem(len(observed) + len(received)),
            out_specs=tuple(in_vmem(4)),
            scratch_shapes=ready + sums,
            compiler_params=PARAMS,
            cost_estimate=PASS_COST,
            name="gather_and_scatter",
        )(live_tiles, place, *observed, *received)

    def last_gather(*received):
        observed = (obs_knot, obs_frac, att_coef, cal_coef, tile_row)
        return pl.pallas_call(
            functools.partial(last_kernel, n_stars, n_seg),
            out_shape=(image_shape, table_shape, shaped(n_stars * n_seg, 8, 128), shaped(8, 128)),
            in_specs=in_smem(2) + in_vmem(len(observed) + len(received)),
            out_specs=tuple(in_vmem(4)),
            scratch_shapes=ready,
            compiler_params=PARAMS,
            cost_estimate=PASS_COST,
            name="last_gather",
        )(live_tiles, place, *observed, *received)

    def star_forward(star):
        return pl.pallas_call(
            star_forward_kernel,
            out_shape=image_shape,
            in_specs=in_vmem(3),
            out_specs=in_vmem(1)[0],
            scratch_shapes=[pltpu.VMEM((2 * STAR_ROWS, COARSE), BF16)],
            compiler_params=PARAMS,
            cost_estimate=PASS_COST,
            name="star_forward",
        )(obs_star, star_coef, star)

    def swap(blocks, axes):
        return lax.all_to_all(blocks, axes, 0, 0)

    def partner(array, axis, distance):
        return lax.ppermute(array, axis, [(i, i ^ distance) for i in range(lax.axis_size(axis))])

    def reduced(table, star):
        distances = [1 << bit for bit in range(n_seg.bit_length() - 1)]
        for distance in distances[:-1]:
            star = star + partner(star, "seg", distance)
        blocks, star = pl.pallas_call(
            sum_kernel,
            out_shape=(shaped(n_stars, 2 * TABLE_ROWS // n_stars + 8, 128), star_shape),
            in_specs=in_vmem(3),
            out_specs=tuple(in_vmem(2)),
            compiler_params=PARAMS,
            cost_estimate=SMALL_COST,
            name="table_sum",
        )(swap(table, "stars"), star, partner(star, "seg", distances[-1]))
        return star_forward(star), star, swap(blocks, "stars")

    first = reduced(*first_scatter())
    star_0 = first[1]
    image_0, table_0, *sent = middle(*first)
    second = reduced(*sent)
    star_h = second[1]
    image_1, table_h, scalars, own_scalars = last_gather(*second, star_0, table_0, image_0)

    def star_order(star):
        return star.reshape(5, STAR_DEV)

    def att_order(table):
        att = table[:KNOT_ROWS].reshape(4, FINE, COARSE)
        return att.transpose(0, 2, 1).reshape(4, KNOT_DEV)

    return pl.pallas_call(
        output_kernel,
        out_shape=(shaped(5, STAR_DEV), shaped(4, KNOT_DEV), shaped(CALB_DEV, width), image_shape),
        in_specs=in_smem(1) + in_vmem(11),
        out_specs=tuple(in_vmem(4)),
        compiler_params=PARAMS,
        cost_estimate=SMALL_COST,
        name="outputs",
    )(
        live_tiles, own_scalars, swap(scalars, ("stars", "seg")), star_order(star_0), star_order(star_h),
        att_order(table_0), att_order(table_h), table_0, table_h, obs_value, image_0, image_1,
    )


def solution(mesh):
    placed = (
        P(("stars", "seg"), None),
        P(("stars", "seg"), None),
        P(("stars", "seg"), None),
        P(None, ("stars", "seg"), None),
        P(None, ("stars", "seg"), None),
        P(("stars", "seg"), None),
        P(("stars", "seg")),
        P(("stars", "seg")),
        P(("stars", "seg"), None),
    )
    return jax.shard_map(
        on_device,
        mesh=mesh,
        in_specs=placed,
        out_specs=(P(None, "stars"), P(None, "seg"), P("seg", None), P(("stars", "seg"), None)),
        check_vma=False,
    )
```

```python
import functools

import jax
import jax.numpy as jnp
from jax import lax
from jax.experimental import pallas as pl
from jax.experimental.pallas import tpu as pltpu
from jax.sharding import PartitionSpec as P

STAR_DEV = 8192
KNOT_DEV = 8192
CALB_DEV = 256
FINE = 32
COARSE = 256
GROUP = 16
WIDE_GROUP = 64
SLOT = 8
STAR_ROWS = 5 * FINE
KNOT_ROWS = 4 * FINE
TABLE_ROWS = KNOT_ROWS + CALB_DEV // 2
BF16 = jnp.bfloat16
F32 = jnp.float32
SCALAR_LANE = 64
PAST_ROWS = 16
KNOT_HALF = KNOT_ROWS + PAST_ROWS


def two_parts(values):
    high = values.astype(BF16)
    return high, (values - high.astype(F32)).astype(BF16)


def rows_and_columns(shape):
    return lax.broadcasted_iota(jnp.int32, shape, 0), lax.broadcasted_iota(jnp.int32, shape, 1)


def packed_rows(row, size):
    wide = jnp.broadcast_to(row.astype(F32), (16, row.shape[1])).astype(BF16)
    return jnp.concatenate([wide] * (size // 16), axis=0)


def matches(index_row, size):
    places, _ = rows_and_columns((size, index_row.shape[1]))
    return places.astype(F32).astype(BF16) == packed_rows(index_row, size)


def one_hot(index_row, size):
    return jnp.where(matches(index_row, size), jnp.ones((), BF16), jnp.zeros((), BF16))


def spline_weights(fraction):
    remain = 1.0 - fraction
    square = fraction * fraction
    cubed = square * fraction
    return (
        remain * remain * remain / 6.0,
        (3.0 * cubed - 6.0 * square + 4.0) / 6.0,
        (-3.0 * cubed + 3.0 * square + 3.0 * fraction + 1.0) / 6.0,
        cubed / 6.0,
    )


def weight_columns(weights, fine_row, tile, places):
    behind = places - fine_row
    result = jnp.zeros(behind.shape, F32)
    for offset in range(4):
        result = jnp.where(behind == offset, weights[offset][tile : tile + 1], result)
    return result


def near_and_past(weights, fine, tile):
    width = fine.shape[1]
    fine_row = fine[tile : tile + 1]
    near, _ = rows_and_columns((FINE, width))
    past, _ = rows_and_columns((PAST_ROWS, width))
    past = FINE + (past & 3)
    return weight_columns(weights, fine_row, tile, near), weight_columns(weights, fine_row, tile, past)


def past_terms(terms, here):
    rows, _ = rows_and_columns((PAST_ROWS, terms[0].shape[1]))
    result = jnp.broadcast_to(terms[3][here], rows.shape)
    for comp in range(2, -1, -1):
        result = jnp.where(rows < 4 * (comp + 1), terms[comp][here], result)
    return result


def product(left, right, contract):
    return lax.dot_general(left, right, (contract, ((), ())), preferred_element_type=F32)


def live_mask(live_ref, first, shape):
    rows, _ = rows_and_columns(shape)
    return (rows + first < live_ref[0]).astype(F32)


def store_rows(out_ref, begin, rows):
    block = out_ref.shape[1]
    for offset in range(0, rows.shape[0], 8):
        where = begin + offset
        out_ref[where // block, where % block : where % block + 8, :] = rows[offset : offset + 8]


def knot_factors(first, knot_ref, frac_ref):
    rows = pl.ds(first, WIDE_GROUP)
    knot = knot_ref[rows, :]
    coarse, fine = knot >> 5, knot & (FINE - 1)
    weights = spline_weights(frac_ref[rows, :])
    hot = [one_hot(coarse[tile : tile + 1], COARSE) for tile in range(WIDE_GROUP)]
    columns = [near_and_past(weights, fine, tile) for tile in range(WIDE_GROUP)]
    return jnp.concatenate(hot, axis=1), columns


def scatter(first, factors, values, observed, knot_acc, star_acc):
    att_coef_ref, star_ref, star_coef_ref = observed
    rows = pl.ds(first, WIDE_GROUP)
    knot_hot, columns = factors
    star = star_ref[rows, :]
    star_coarse, star_fine = star & (COARSE - 1), star >> 8
    terms = [att_coef_ref[comp, rows, :] * values for comp in range(4)]
    parts = [two_parts(star_coef_ref[comp, rows, :] * values) for comp in range(5)]
    parts = [pair[half].astype(F32) for half in range(2) for pair in parts]
    knot_left, star_left, star_right = [], [], []
    for tile in range(WIDE_GROUP):
        here = slice(tile, tile + 1)
        near, past = columns[tile]
        spread = jnp.concatenate(
            [term[here] * near for term in terms] + [past_terms(terms, here) * past], axis=0
        )
        knot_left.append(jnp.concatenate(two_parts(spread), axis=0))
        star_right.append(one_hot(star_coarse[here], COARSE))
        chosen = matches(star_fine[here], FINE)
        star_left.append(
            jnp.concatenate(
                [jnp.where(chosen, packed_rows(part[here], FINE), jnp.zeros((), BF16)) for part in parts],
                axis=0,
            )
        )
    knot_acc[...] += product(
        jnp.concatenate(knot_left, axis=1), knot_hot, ((1,), (1,))
    )
    star_acc[...] += product(
        jnp.concatenate(star_left, axis=1), jnp.concatenate(star_right, axis=1), ((1,), (1,))
    )


def scatter_calibration(values, tile_cal_ref, table_out):
    blocks = product(
        one_hot(tile_cal_ref[...], CALB_DEV), jnp.concatenate(two_parts(values), axis=1), ((1,), (0,))
    )
    width = values.shape[1]
    blocks = blocks[:, :width] + blocks[:, width:]
    blocks = jnp.concatenate([blocks[: CALB_DEV // 2], blocks[CALB_DEV // 2 :]], axis=1)
    store_rows(table_out, KNOT_ROWS, blocks)


def scatter_end(place_ref, scalars, knot_acc, star_acc, table_out, star_out):
    lane = lax.broadcasted_iota(jnp.int32, (8, 128), 1)
    row = lax.broadcasted_iota(jnp.int32, (8, 128), 0)
    wide_lane = lax.broadcasted_iota(jnp.int32, (8, COARSE), 1)
    wide_row = lax.broadcasted_iota(jnp.int32, (8, COARSE), 0)
    edges = jnp.zeros((8, 128), F32)
    for comp in range(4):
        begin, past = comp * FINE, KNOT_ROWS + comp // 2 * 8
        main = knot_acc[begin : begin + FINE] + knot_acc[KNOT_HALF + begin : KNOT_HALF + begin + FINE]
        beyond = knot_acc[past : past + 8] + knot_acc[KNOT_HALF + past : KNOT_HALF + past + 8]
        if comp % 2:
            beyond = pltpu.roll(beyond, 4, 0)
        moved = pltpu.roll(jnp.where(wide_row < 3, beyond, 0.0), 1, 1)
        top = main[:8] + jnp.where(wide_lane > 0, moved, 0.0)
        store_rows(table_out, begin, top)
        store_rows(table_out, begin + 8, main[8:])
        tail, head = moved[:, :128], top[:, :128]
        if comp:
            tail = pltpu.roll(tail, 2 * comp, 1)
        head = pltpu.roll(head, 2 * comp + 1, 1)
        edges = jnp.where((lane == 2 * comp) & (row < 3), tail, edges)
        edges = jnp.where((lane == 2 * comp + 1) & (row < 3), head, edges)
    edges = with_scalars(pltpu.roll(edges, SLOT * place_ref[0], 1), scalars)
    star_out[:STAR_ROWS] = star_acc[:STAR_ROWS] + star_acc[STAR_ROWS:]
    star_out[STAR_ROWS:] = jnp.concatenate([edges, jnp.zeros_like(edges)], axis=1)


def first_kernel(live_ref, place_ref, *refs):
    sources, (table_out, star_out, knot_acc, star_acc) = refs[:8], refs[8:12]
    buffers, sems = refs[12:20], refs[20]
    half = sources[0].shape[0] // 2
    copies = []

    def begin(source, target, *place):
        source, target = (source.at[place], target.at[place]) if place else (source, target)
        copies.append(pltpu.make_async_copy(source, target, sems.at[len(copies)]))
        copies[-1].start()

    for source, target in zip(sources[:3], buffers):
        begin(source, target)
    for rows in (slice(0, half), slice(half, 2 * half)):
        for source, target in zip(sources[3:], buffers[3:]):
            begin(source, target, *[slice(None)] * (len(source.shape) - 2), rows)
    value_ref, cal_coef_ref, tile_cal_ref, knot_ref, frac_ref, *observed = buffers
    knot_acc[...] = jnp.zeros_like(knot_acc)
    star_acc[...] = jnp.zeros_like(star_acc)
    for copy in copies[:3]:
        copy.wait()
    values = value_ref[...] * live_mask(live_ref, 0, value_ref.shape)
    scatter_calibration(values * cal_coef_ref[...], tile_cal_ref, table_out)
    for copy in copies[3:8]:
        copy.wait()

    @pl.loop(0, value_ref.shape[0] // WIDE_GROUP)
    def _(group):
        @pl.when(group * WIDE_GROUP == half)
        def _():
            for copy in copies[8:]:
                copy.wait()

        first = pl.multiple_of(group * WIDE_GROUP, WIDE_GROUP)
        values = value_ref[pl.ds(first, WIDE_GROUP), :]
        values = values * live_mask(live_ref, first, values.shape)
        scatter(first, knot_factors(first, knot_ref, frac_ref), values, observed, knot_acc, star_acc)

    scatter_end(place_ref, [], knot_acc, star_acc, table_out, star_out)


def sum_kernel(block_ref, own_ref, other_ref, out_ref, star_out):
    total = block_ref[0]
    for device in range(1, block_ref.shape[0]):
        total = total + block_ref[device]
    star = own_ref[...] + other_ref[...]
    star_out[...] = star[:STAR_ROWS]
    total = jnp.concatenate([total[:, :128], total[:, 128:], star[STAR_ROWS:, :128]], axis=0)
    for device in range(block_ref.shape[0]):
        out_ref[device] = total


def picked(array, which):
    row = lax.broadcasted_iota(jnp.int32, array.shape, 0)
    lane = lax.broadcasted_iota(jnp.int32, array.shape, 1)
    chosen = (row == 0) & (lane == SCALAR_LANE + which)
    return jnp.sum(jnp.where(chosen, array, 0.0), keepdims=True)


def with_scalars(array, scalars):
    row = lax.broadcasted_iota(jnp.int32, array.shape, 0)
    lane = lax.broadcasted_iota(jnp.int32, array.shape, 1)
    for which, value in scalars:
        array = jnp.where((row == 0) & (lane == SCALAR_LANE + which), value, array)
    return array


def first_step(edges):
    return picked(edges, 0), picked(edges, 1)


def star_forward_kernel(star_ref, star_coef_ref, star_x_ref, image_ref, star_parts_ref):
    star_x = star_x_ref[...]
    star_high, star_low = two_parts(star_x)
    star_parts_ref[:STAR_ROWS] = star_high
    star_parts_ref[STAR_ROWS:] = star_low

    @pl.loop(0, star_ref.shape[0] // GROUP)
    def _(group):
        rows = pl.ds(pl.multiple_of(group * GROUP, GROUP), GROUP)
        star = star_ref[rows, :]
        coarse, fine = star & (COARSE - 1), star >> 8
        coef = [star_coef_ref[comp, rows, :] for comp in range(5)]
        tiles = [slice(tile, tile + 1) for tile in range(GROUP)]
        hot = jnp.concatenate([one_hot(coarse[here], COARSE) for here in tiles], axis=1)
        found = product(star_parts_ref[...], hot, ((1,), (0,)))
        width = star.shape[1]
        fine_rows, _ = rows_and_columns((FINE, width))
        image_rows = []
        for tile, here in enumerate(tiles):
            across = slice(tile * width, (tile + 1) * width)

            def part(comp):
                begin = comp * FINE
                return (
                    found[begin : begin + FINE, across]
                    + found[STAR_ROWS + begin : STAR_ROWS + begin + FINE, across]
                )

            both = sum(coef[comp][here] * part(comp) for comp in range(5))
            both = jnp.where(fine_rows == fine[here], both, 0.0)
            both = both[:8] + both[8:16] + both[16:24] + both[24:]
            image_rows.append(jnp.sum(both, axis=0, keepdims=True))
        image_ref[rows, :] = jnp.concatenate(image_rows, axis=0)


def received_table(n_stars, n_seg, place_ref, block_ref):
    segment = place_ref[0]
    lane = lax.broadcasted_iota(jnp.int32, (8, 128), 1)
    row = lax.broadcasted_iota(jnp.int32, (8, 128), 0)
    edges = block_ref[0, -8:, :]
    for block in range(1, n_stars):
        edges = edges + block_ref[block, -8:, :]

    def slot(which):
        return pltpu.roll(edges, 128 - SLOT * jnp.clip(which, 0, n_seg - 1), 1)

    before, own, after = slot(segment - 1), slot(segment), slot(segment + 1)
    before = jnp.where(segment > 0, before, 0.0)
    ahead = jnp.where(lane % 2 == 0, own, 0.0) + pltpu.roll(jnp.where(lane % 2 == 1, after, 0.0), 127, 1)
    ahead = jnp.where((segment < n_seg - 1) & (lane < 8) & (row < 3), ahead, 0.0)

    size = TABLE_ROWS // n_stars
    table = jnp.concatenate([block_ref[:, :size, :], block_ref[:, size : 2 * size, :]], axis=2)
    table = table.reshape(TABLE_ROWS, COARSE)
    pieces = []
    for comp in range(4):
        shifted = pltpu.roll(before, 128 - 2 * comp, 1) if comp else before
        shifted = jnp.where((lane == 0) & (row < 3), shifted, 0.0)
        top = table[comp * FINE : comp * FINE + 8]
        pieces.append(top + jnp.concatenate([shifted, jnp.zeros_like(shifted)], axis=1))
        pieces.append(table[comp * FINE + 8 : (comp + 1) * FINE])
    return jnp.concatenate(pieces + [table[KNOT_ROWS:]], axis=0), ahead, edges


def gather_ready(table, ahead, cal_coef_ref, tile_cal_ref, star_image_ref, knot_parts_ref, cal_ref):
    wide_lane = lax.broadcasted_iota(jnp.int32, (8, COARSE), 1)
    row = lax.broadcasted_iota(jnp.int32, (8, COARSE), 0)
    beyond = []
    for comp in range(4):
        moved = pltpu.roll(table[comp * FINE : comp * FINE + 8], COARSE - 1, 1)
        last = pltpu.roll(ahead, 127 - 2 * comp, 1)
        moved = jnp.where(wide_lane == COARSE - 1, jnp.concatenate([last, last], axis=1), moved)
        beyond.append(pltpu.roll(moved, 4, 0) if comp % 2 else moved)
    beyond = [jnp.where(row < 4, beyond[0], beyond[1]), jnp.where(row < 4, beyond[2], beyond[3])]
    knot_high, knot_low = two_parts(jnp.concatenate([table[:KNOT_ROWS]] + beyond, axis=0))
    knot_parts_ref[:, :COARSE] = knot_high
    knot_parts_ref[:, COARSE:] = knot_low

    blocks = jnp.concatenate([table[KNOT_ROWS:, :128], table[KNOT_ROWS:, 128:]], axis=0)
    rows = product(
        one_hot(tile_cal_ref[...], CALB_DEV), jnp.concatenate(two_parts(blocks), axis=1), ((0,), (0,))
    )
    cal_ref[...] = (rows[:, :128] + rows[:, 128:]) * cal_coef_ref[...] + star_image_ref[...]


def gather(first, live_ref, factors, att_coef_ref, knot_parts_ref, cal_ref):
    rows = pl.ds(first, WIDE_GROUP)
    coef = [att_coef_ref[comp, rows, :] for comp in range(4)]
    hot, columns = factors
    found = product(knot_parts_ref[...], jnp.concatenate([hot, hot], axis=0), ((1,), (0,)))
    width = cal_ref.shape[1]
    image_rows = []
    for tile in range(WIDE_GROUP):
        here = slice(tile, tile + 1)
        across = slice(tile * width, (tile + 1) * width)

        def part(begin, size):
            return found[begin : begin + size, across]

        near, past = columns[tile]
        near = near * sum(coef[comp][here] * part(comp * FINE, FINE) for comp in range(4))
        past = past * past_terms(coef, here) * part(KNOT_ROWS, PAST_ROWS)
        both = near[:8] + near[8:16] + near[16:24] + near[24:] + past[:8] + past[8:]
        image_rows.append(jnp.sum(both, axis=0, keepdims=True))
    image = jnp.concatenate(image_rows, axis=0) + cal_ref[rows, :]
    return image * live_mask(live_ref, first, image.shape)


def squares(array):
    return jnp.sum(array * array, keepdims=True)


def middle_kernel(
    n_stars, n_seg, live_ref, place_ref, knot_ref, frac_ref, att_coef_ref, star_ref, star_coef_ref,
    cal_coef_ref, tile_cal_ref, star_image_ref, star_x_ref, block_ref, image_ref, table_out, scatter_out,
    star_out, knot_parts_ref, cal_ref, knot_acc, star_acc,
):
    table, ahead, _ = received_table(n_stars, n_seg, place_ref, block_ref)
    table_out[...] = table
    norm = squares(star_x_ref[...]) / n_seg + squares(table) / n_stars
    gather_ready(table, ahead, cal_coef_ref, tile_cal_ref, star_image_ref, knot_parts_ref, cal_ref)
    knot_acc[...] = jnp.zeros_like(knot_acc)
    star_acc[...] = jnp.zeros_like(star_acc)
    def one_group(group, total):
        first = pl.multiple_of(group * WIDE_GROUP, WIDE_GROUP)
        factors = knot_factors(first, knot_ref, frac_ref)
        image = gather(first, live_ref, factors, att_coef_ref, knot_parts_ref, cal_ref)
        image_ref[pl.ds(first, WIDE_GROUP), :] = image
        scatter(first, factors, image, (att_coef_ref, star_ref, star_coef_ref), knot_acc, star_acc)
        return total + image * image

    zero = jnp.zeros((WIDE_GROUP, knot_ref.shape[1]), F32)
    total = lax.fori_loop(0, knot_ref.shape[0] // WIDE_GROUP, one_group, zero)
    scatter_calibration(image_ref[...] * cal_coef_ref[...], tile_cal_ref, scatter_out)
    scalars = [(0, norm), (1, jnp.sum(total, keepdims=True))]
    scatter_end(place_ref, scalars, knot_acc, star_acc, scatter_out, star_out)


def last_kernel(
    n_stars, n_seg, live_ref, place_ref, knot_ref, frac_ref, att_coef_ref, cal_coef_ref, tile_cal_ref,
    star_image_ref, star_x_ref, block_ref, star_0_ref, table_0_ref, image_0_ref, image_ref, table_out,
    scalar_out, own_scalar_out, knot_parts_ref, cal_ref,
):
    table, ahead, edges = received_table(n_stars, n_seg, place_ref, block_ref)
    table_out[...] = table
    norm_0, square_0 = first_step(edges)
    step = norm_0 / square_0
    norm = (
        squares(star_0_ref[...] - step * star_x_ref[...]) / n_seg
        + squares(table_0_ref[...] - step * table) / n_stars
    )
    gather_ready(table, ahead, cal_coef_ref, tile_cal_ref, star_image_ref, knot_parts_ref, cal_ref)

    def one_group(group, sums):
        first = pl.multiple_of(group * WIDE_GROUP, WIDE_GROUP)
        rows = pl.ds(first, WIDE_GROUP)
        image_0 = image_0_ref[rows, :]
        factors = knot_factors(first, knot_ref, frac_ref)
        image = gather(first, live_ref, factors, att_coef_ref, knot_parts_ref, cal_ref)
        image = image_0 - step * image
        image_ref[rows, :] = image
        return sums[0] + image * image, sums[1] + image * image_0

    zero = jnp.zeros((WIDE_GROUP, knot_ref.shape[1]), F32)
    sums = lax.fori_loop(0, knot_ref.shape[0] // WIDE_GROUP, one_group, (zero, zero))
    scalars = [norm] + [jnp.sum(part, keepdims=True) for part in sums] + [norm_0, square_0]
    scalars = with_scalars(jnp.zeros((8, 128), F32), list(enumerate(scalars)))
    own_scalar_out[...] = scalars
    for device in range(scalar_out.shape[0]):
        scalar_out[device] = scalars


def output_kernel(
    live_ref, own_scalar_ref, scalar_ref, star_0_ref, star_h_ref, att_0_ref, att_h_ref, table_0_ref,
    table_h_ref, value_ref, image_0_ref, image_1_ref, star_out, att_out, cal_out, residual_out,
):
    norm_0, square_0 = [picked(own_scalar_ref[...], which) for which in (3, 4)]
    everyone = scalar_ref[0]
    for device in range(1, scalar_ref.shape[0]):
        everyone = everyone + scalar_ref[device]
    norm_1, square_1, cross = [picked(everyone, which) for which in range(3)]
    step_0 = norm_0 / square_0
    ratio = norm_1 / norm_0
    step_1 = norm_1 / (square_1 + 2.0 * ratio * cross + ratio * ratio * square_0)
    scale = step_0 + step_1 * ratio

    def combined(old, change):
        return scale * old + step_1 * (old - step_0 * change)

    star_out[...] = combined(star_0_ref[...], star_h_ref[...])
    att_out[...] = combined(att_0_ref[...], att_h_ref[...])
    cal = combined(table_0_ref[KNOT_ROWS:, :], table_h_ref[KNOT_ROWS:, :])
    cal_out[...] = jnp.concatenate([cal[:, :128], cal[:, 128:]], axis=0)
    values = value_ref[...] * live_mask(live_ref, 0, value_ref.shape)
    residual_out[...] = values - scale * image_0_ref[...] - step_1 * image_1_ref[...]


def in_vmem(count):
    return [pl.BlockSpec(memory_space=pltpu.VMEM)] * count


def in_smem(count):
    return [pl.BlockSpec(memory_space=pltpu.SMEM)] * count


def in_hbm(count):
    return [pl.BlockSpec(memory_space=pltpu.HBM)] * count


def shaped(*shape):
    return jax.ShapeDtypeStruct(shape, F32)


ARRIVE_PARAMS = pltpu.CompilerParams(vmem_limit_bytes=60 * 1024 * 1024)
PARAMS = pltpu.CompilerParams(vmem_limit_bytes=40 * 1024 * 1024)
PASS_COST = pl.CostEstimate(flops=3_000_000_000, bytes_accessed=1_000_000, transcendentals=0)
SMALL_COST = pl.CostEstimate(flops=1_000_000, bytes_accessed=600_000, transcendentals=0)


def on_device(
    obs_star, obs_knot, obs_frac, star_coef, att_coef, cal_coef, tile_cal, live_tiles, obs_value
):
    n_stars, n_seg = lax.axis_size("stars"), lax.axis_size("seg")
    tile_count, width = obs_star.shape
    tile_row = tile_cal[None, :]
    place = lax.axis_index("seg").astype(jnp.int32)[None]
    image_shape = shaped(tile_count, width)
    table_shape = shaped(TABLE_ROWS, COARSE)
    star_shape = shaped(STAR_ROWS, COARSE)
    sent_shapes = (shaped(n_stars, TABLE_ROWS // n_stars, COARSE), shaped(STAR_ROWS + 8, COARSE))
    sums = [pltpu.VMEM((2 * KNOT_HALF, COARSE), F32), pltpu.VMEM((2 * STAR_ROWS, COARSE), F32)]
    ready = [pltpu.VMEM((KNOT_HALF, 2 * COARSE), BF16), pltpu.VMEM((tile_count, width), F32)]

    def first_scatter():
        observed = (obs_value, cal_coef, tile_row, obs_knot, obs_frac, att_coef, obs_star, star_coef)
        buffers = [pltpu.VMEM(array.shape, array.dtype) for array in observed]
        return pl.pallas_call(
            first_kernel,
            out_shape=sent_shapes,
            in_specs=in_smem(2) + in_hbm(len(observed)),
            out_specs=tuple(in_vmem(2)),
            scratch_shapes=sums + buffers + [pltpu.SemaphoreType.DMA((13,))],
            compiler_params=ARRIVE_PARAMS,
            cost_estimate=PASS_COST,
            name="first_scatter",
        )(live_tiles, place, *observed)

    def middle(*received):
        observed = (obs_knot, obs_frac, att_coef, obs_star, star_coef, cal_coef, tile_row)
        return pl.pallas_call(
            functools.partial(middle_kernel, n_stars, n_seg),
            out_shape=(image_shape, table_shape, *sent_shapes),
            in_specs=in_smem(2) + in_vmem(len(observed) + len(received)),
            out_specs=tuple(in_vmem(4)),
            scratch_shapes=ready + sums,
            compiler_params=PARAMS,
            cost_estimate=PASS_COST,
            name="gather_and_scatter",
        )(live_tiles, place, *observed, *received)

    def last_gather(*received):
        observed = (obs_knot, obs_frac, att_coef, cal_coef, tile_row)
        return pl.pallas_call(
            functools.partial(last_kernel, n_stars, n_seg),
            out_shape=(image_shape, table_shape, shaped(n_stars * n_seg, 8, 128), shaped(8, 128)),
            in_specs=in_smem(2) + in_vmem(len(observed) + len(received)),
            out_specs=tuple(in_vmem(4)),
            scratch_shapes=ready,
            compiler_params=PARAMS,
            cost_estimate=PASS_COST,
            name="last_gather",
        )(live_tiles, place, *observed, *received)

    def star_forward(star):
        return pl.pallas_call(
            star_forward_kernel,
            out_shape=image_shape,
            in_specs=in_vmem(3),
            out_specs=in_vmem(1)[0],
            scratch_shapes=[pltpu.VMEM((2 * STAR_ROWS, COARSE), BF16)],
            compiler_params=PARAMS,
            cost_estimate=PASS_COST,
            name="star_forward",
        )(obs_star, star_coef, star)

    def swap(blocks, axes):
        return lax.all_to_all(blocks, axes, 0, 0)

    def partner(array, axis, distance):
        return lax.ppermute(array, axis, [(i, i ^ distance) for i in range(lax.axis_size(axis))])

    def reduced(table, star):
        distances = [1 << bit for bit in range(n_seg.bit_length() - 1)]
        for distance in distances[:-1]:
            star = star + partner(star, "seg", distance)
        blocks, star = pl.pallas_call(
            sum_kernel,
            out_shape=(shaped(n_stars, 2 * TABLE_ROWS // n_stars + 8, 128), star_shape),
            in_specs=in_vmem(3),
            out_specs=tuple(in_vmem(2)),
            compiler_params=PARAMS,
            cost_estimate=SMALL_COST,
            name="table_sum",
        )(swap(table, "stars"), star, partner(star, "seg", distances[-1]))
        return star_forward(star), star, swap(blocks, "stars")

    first = reduced(*first_scatter())
    star_0 = first[1]
    image_0, table_0, *sent = middle(*first)
    second = reduced(*sent)
    star_h = second[1]
    image_1, table_h, scalars, own_scalars = last_gather(*second, star_0, table_0, image_0)

    def star_order(star):
        return star.reshape(5, STAR_DEV)

    def att_order(table):
        att = table[:KNOT_ROWS].reshape(4, FINE, COARSE)
        return att.transpose(0, 2, 1).reshape(4, KNOT_DEV)

    return pl.pallas_call(
        output_kernel,
        out_shape=(shaped(5, STAR_DEV), shaped(4, KNOT_DEV), shaped(CALB_DEV, width), image_shape),
        in_specs=in_smem(1) + in_vmem(11),
        out_specs=tuple(in_vmem(4)),
        compiler_params=PARAMS,
        cost_estimate=SMALL_COST,
        name="outputs",
    )(
        live_tiles, own_scalars, swap(scalars, ("stars", "seg")), star_order(star_0), star_order(star_h),
        att_order(table_0), att_order(table_h), table_0, table_h, obs_value, image_0, image_1,
    )


def solution(mesh):
    placed = (
        P(("stars", "seg"), None),
        P(("stars", "seg"), None),
        P(("stars", "seg"), None),
        P(None, ("stars", "seg"), None),
        P(None, ("stars", "seg"), None),
        P(("stars", "seg"), None),
        P(("stars", "seg")),
        P(("stars", "seg")),
        P(("stars", "seg"), None),
    )
    return jax.shard_map(
        on_device,
        mesh=mesh,
        in_specs=placed,
        out_specs=(P(None, "stars"), P(None, "seg"), P("seg", None), P(("stars", "seg"), None)),
        check_vma=False,
    )
```

```python
import functools

import jax
import jax.numpy as jnp
from jax import lax
from jax.experimental import pallas as pl
from jax.experimental.pallas import tpu as pltpu
from jax.sharding import PartitionSpec as P

STAR_DEV = 8192
KNOT_DEV = 8192
CALB_DEV = 256
FINE = 32
COARSE = 256
GROUP = 16
WIDE_GROUP = 64
SLOT = 8
STAR_ROWS = 5 * FINE
KNOT_ROWS = 4 * FINE
TABLE_ROWS = KNOT_ROWS + CALB_DEV // 2
BF16 = jnp.bfloat16
F32 = jnp.float32
SCALAR_LANE = 64
PAST_ROWS = 16
KNOT_HALF = KNOT_ROWS + PAST_ROWS


def two_parts(values):
    high = values.astype(BF16)
    return high, (values - high.astype(F32)).astype(BF16)


def rows_and_columns(shape):
    return lax.broadcasted_iota(jnp.int32, shape, 0), lax.broadcasted_iota(jnp.int32, shape, 1)


def packed_rows(row, size):
    wide = jnp.broadcast_to(row.astype(F32), (16, row.shape[1])).astype(BF16)
    return jnp.concatenate([wide] * (size // 16), axis=0)


def matches(index_row, size):
    places, _ = rows_and_columns((size, index_row.shape[1]))
    return places.astype(F32).astype(BF16) == packed_rows(index_row, size)


def one_hot(index_row, size):
    return jnp.where(matches(index_row, size), jnp.ones((), BF16), jnp.zeros((), BF16))


def spline_weights(fraction):
    remain = 1.0 - fraction
    square = fraction * fraction
    cubed = square * fraction
    return (
        remain * remain * remain / 6.0,
        (3.0 * cubed - 6.0 * square + 4.0) / 6.0,
        (-3.0 * cubed + 3.0 * square + 3.0 * fraction + 1.0) / 6.0,
        cubed / 6.0,
    )


def weight_columns(weights, fine_row, tile, places):
    behind = places - fine_row
    result = jnp.zeros(behind.shape, F32)
    for offset in range(4):
        result = jnp.where(behind == offset, weights[offset][tile : tile + 1], result)
    return result


def near_and_past(weights, fine, tile):
    width = fine.shape[1]
    fine_row = fine[tile : tile + 1]
    near, _ = rows_and_columns((FINE, width))
    past, _ = rows_and_columns((PAST_ROWS, width))
    past = FINE + (past & 3)
    return weight_columns(weights, fine_row, tile, near), weight_columns(weights, fine_row, tile, past)


def past_terms(terms, here):
    rows, _ = rows_and_columns((PAST_ROWS, terms[0].shape[1]))
    result = jnp.broadcast_to(terms[3][here], rows.shape)
    for comp in range(2, -1, -1):
        result = jnp.where(rows < 4 * (comp + 1), terms[comp][here], result)
    return result


def product(left, right, contract):
    return lax.dot_general(left, right, (contract, ((), ())), preferred_element_type=F32)


def live_mask(live_ref, first, shape):
    rows, _ = rows_and_columns(shape)
    return (rows + first < live_ref[0]).astype(F32)


def store_rows(out_ref, begin, rows):
    block = out_ref.shape[1]
    for offset in range(0, rows.shape[0], 8):
        where = begin + offset
        out_ref[where // block, where % block : where % block + 8, :] = rows[offset : offset + 8]


def knot_factors(first, knot_ref, frac_ref):
    rows = pl.ds(first, WIDE_GROUP)
    knot = knot_ref[rows, :]
    coarse, fine = knot >> 5, knot & (FINE - 1)
    weights = spline_weights(frac_ref[rows, :])
    hot = [one_hot(coarse[tile : tile + 1], COARSE) for tile in range(WIDE_GROUP)]
    columns = [near_and_past(weights, fine, tile) for tile in range(WIDE_GROUP)]
    return jnp.concatenate(hot, axis=1), columns


def scatter(first, factors, values, observed, knot_acc, star_acc):
    att_coef_ref, star_ref, star_coef_ref = observed
    rows = pl.ds(first, WIDE_GROUP)
    knot_hot, columns = factors
    star = star_ref[rows, :]
    star_coarse, star_fine = star & (COARSE - 1), star >> 8
    terms = [att_coef_ref[comp, rows, :] * values for comp in range(4)]
    parts = [two_parts(star_coef_ref[comp, rows, :] * values) for comp in range(5)]
    parts = [pair[half].astype(F32) for half in range(2) for pair in parts]
    knot_left, star_left, star_right = [], [], []
    for tile in range(WIDE_GROUP):
        here = slice(tile, tile + 1)
        near, past = columns[tile]
        spread = jnp.concatenate(
            [term[here] * near for term in terms] + [past_terms(terms, here) * past], axis=0
        )
        knot_left.append(jnp.concatenate(two_parts(spread), axis=0))
        star_right.append(one_hot(star_coarse[here], COARSE))
        chosen = matches(star_fine[here], FINE)
        star_left.append(
            jnp.concatenate(
                [jnp.where(chosen, packed_rows(part[here], FINE), jnp.zeros((), BF16)) for part in parts],
                axis=0,
            )
        )
    knot_acc[...] += product(
        jnp.concatenate(knot_left, axis=1), knot_hot, ((1,), (1,))
    )
    star_acc[...] += product(
        jnp.concatenate(star_left, axis=1), jnp.concatenate(star_right, axis=1), ((1,), (1,))
    )


def scatter_calibration(values, tile_cal_ref, table_out):
    blocks = product(
        one_hot(tile_cal_ref[...], CALB_DEV), jnp.concatenate(two_parts(values), axis=1), ((1,), (0,))
    )
    width = values.shape[1]
    blocks = blocks[:, :width] + blocks[:, width:]
    blocks = jnp.concatenate([blocks[: CALB_DEV // 2], blocks[CALB_DEV // 2 :]], axis=1)
    store_rows(table_out, KNOT_ROWS, blocks)


def scatter_end(place_ref, scalars, knot_acc, star_acc, table_out, star_out):
    lane = lax.broadcasted_iota(jnp.int32, (8, 128), 1)
    row = lax.broadcasted_iota(jnp.int32, (8, 128), 0)
    wide_lane = lax.broadcasted_iota(jnp.int32, (8, COARSE), 1)
    wide_row = lax.broadcasted_iota(jnp.int32, (8, COARSE), 0)
    edges = jnp.zeros((8, 128), F32)
    for comp in range(4):
        begin, past = comp * FINE, KNOT_ROWS + comp // 2 * 8
        main = knot_acc[begin : begin + FINE] + knot_acc[KNOT_HALF + begin : KNOT_HALF + begin + FINE]
        beyond = knot_acc[past : past + 8] + knot_acc[KNOT_HALF + past : KNOT_HALF + past + 8]
        if comp % 2:
            beyond = pltpu.roll(beyond, 4, 0)
        moved = pltpu.roll(jnp.where(wide_row < 3, beyond, 0.0), 1, 1)
        top = main[:8] + jnp.where(wide_lane > 0, moved, 0.0)
        store_rows(table_out, begin, top)
        store_rows(table_out, begin + 8, main[8:])
        tail, head = moved[:, :128], top[:, :128]
        if comp:
            tail = pltpu.roll(tail, 2 * comp, 1)
        head = pltpu.roll(head, 2 * comp + 1, 1)
        edges = jnp.where((lane == 2 * comp) & (row < 3), tail, edges)
        edges = jnp.where((lane == 2 * comp + 1) & (row < 3), head, edges)
    edges = with_scalars(pltpu.roll(edges, SLOT * place_ref[0], 1), scalars)
    star_out[:STAR_ROWS] = star_acc[:STAR_ROWS] + star_acc[STAR_ROWS:]
    star_out[STAR_ROWS:] = jnp.concatenate([edges, jnp.zeros_like(edges)], axis=1)


def first_kernel(live_ref, place_ref, *refs):
    sources, (table_out, star_out, knot_acc, star_acc) = refs[:8], refs[8:12]
    buffers, sems = refs[12:20], refs[20]
    half = sources[0].shape[0] // 2
    copies = []

    def begin(source, target, *place):
        source, target = (source.at[place], target.at[place]) if place else (source, target)
        copies.append(pltpu.make_async_copy(source, target, sems.at[len(copies)]))
        copies[-1].start()

    for source, target in zip(sources[:3], buffers):
        begin(source, target)
    for rows in (slice(0, half), slice(half, 2 * half)):
        for source, target in zip(sources[3:], buffers[3:]):
            begin(source, target, *[slice(None)] * (len(source.shape) - 2), rows)
    value_ref, cal_coef_ref, tile_cal_ref, knot_ref, frac_ref, *observed = buffers
    knot_acc[...] = jnp.zeros_like(knot_acc)
    star_acc[...] = jnp.zeros_like(star_acc)
    for copy in copies[:3]:
        copy.wait()
    values = value_ref[...] * live_mask(live_ref, 0, value_ref.shape)
    scatter_calibration(values * cal_coef_ref[...], tile_cal_ref, table_out)
    for copy in copies[3:8]:
        copy.wait()

    @pl.loop(0, value_ref.shape[0] // WIDE_GROUP)
    def _(group):
        @pl.when(group * WIDE_GROUP == half)
        def _():
            for copy in copies[8:]:
                copy.wait()

        first = pl.multiple_of(group * WIDE_GROUP, WIDE_GROUP)
        values = value_ref[pl.ds(first, WIDE_GROUP), :]
        values = values * live_mask(live_ref, first, values.shape)
        scatter(first, knot_factors(first, knot_ref, frac_ref), values, observed, knot_acc, star_acc)

    scatter_end(place_ref, [], knot_acc, star_acc, table_out, star_out)


def sum_kernel(block_ref, own_ref, other_ref, out_ref, star_out):
    total = block_ref[0]
    for device in range(1, block_ref.shape[0]):
        total = total + block_ref[device]
    star = own_ref[...] + other_ref[...]
    star_out[...] = star[:STAR_ROWS]
    total = jnp.concatenate([total[:, :128], total[:, 128:], star[STAR_ROWS:, :128]], axis=0)
    for device in range(block_ref.shape[0]):
        out_ref[device] = total


def picked(array, which):
    row = lax.broadcasted_iota(jnp.int32, array.shape, 0)
    lane = lax.broadcasted_iota(jnp.int32, array.shape, 1)
    chosen = (row == 0) & (lane == SCALAR_LANE + which)
    return jnp.sum(jnp.where(chosen, array, 0.0), keepdims=True)


def with_scalars(array, scalars):
    row = lax.broadcasted_iota(jnp.int32, array.shape, 0)
    lane = lax.broadcasted_iota(jnp.int32, array.shape, 1)
    for which, value in scalars:
        array = jnp.where((row == 0) & (lane == SCALAR_LANE + which), value, array)
    return array


def first_step(edges):
    return picked(edges, 0), picked(edges, 1)


def star_forward_kernel(star_ref, star_coef_ref, star_x_ref, image_ref, star_parts_ref):
    star_x = star_x_ref[...]
    star_high, star_low = two_parts(star_x)
    star_parts_ref[:STAR_ROWS] = star_high
    star_parts_ref[STAR_ROWS:] = star_low

    @pl.loop(0, star_ref.shape[0] // GROUP)
    def _(group):
        rows = pl.ds(pl.multiple_of(group * GROUP, GROUP), GROUP)
        star = star_ref[rows, :]
        coarse, fine = star & (COARSE - 1), star >> 8
        coef = [star_coef_ref[comp, rows, :] for comp in range(5)]
        tiles = [slice(tile, tile + 1) for tile in range(GROUP)]
        hot = jnp.concatenate([one_hot(coarse[here], COARSE) for here in tiles], axis=1)
        found = product(star_parts_ref[...], hot, ((1,), (0,)))
        width = star.shape[1]
        fine_rows, _ = rows_and_columns((FINE, width))
        image_rows = []
        for tile, here in enumerate(tiles):
            across = slice(tile * width, (tile + 1) * width)

            def part(comp):
                begin = comp * FINE
                return (
                    found[begin : begin + FINE, across]
                    + found[STAR_ROWS + begin : STAR_ROWS + begin + FINE, across]
                )

            both = sum(coef[comp][here] * part(comp) for comp in range(5))
            both = jnp.where(fine_rows == fine[here], both, 0.0)
            both = both[:8] + both[8:16] + both[16:24] + both[24:]
            image_rows.append(jnp.sum(both, axis=0, keepdims=True))
        image_ref[rows, :] = jnp.concatenate(image_rows, axis=0)


def received_table(n_stars, n_seg, place_ref, block_ref):
    segment = place_ref[0]
    lane = lax.broadcasted_iota(jnp.int32, (8, 128), 1)
    row = lax.broadcasted_iota(jnp.int32, (8, 128), 0)
    edges = block_ref[0, -8:, :]
    for block in range(1, n_stars):
        edges = edges + block_ref[block, -8:, :]

    def slot(which):
        return pltpu.roll(edges, 128 - SLOT * jnp.clip(which, 0, n_seg - 1), 1)

    before, own, after = slot(segment - 1), slot(segment), slot(segment + 1)
    before = jnp.where(segment > 0, before, 0.0)
    ahead = jnp.where(lane % 2 == 0, own, 0.0) + pltpu.roll(jnp.where(lane % 2 == 1, after, 0.0), 127, 1)
    ahead = jnp.where((segment < n_seg - 1) & (lane < 8) & (row < 3), ahead, 0.0)

    size = TABLE_ROWS // n_stars
    table = jnp.concatenate([block_ref[:, :size, :], block_ref[:, size : 2 * size, :]], axis=2)
    table = table.reshape(TABLE_ROWS, COARSE)
    pieces = []
    for comp in range(4):
        shifted = pltpu.roll(before, 128 - 2 * comp, 1) if comp else before
        shifted = jnp.where((lane == 0) & (row < 3), shifted, 0.0)
        top = table[comp * FINE : comp * FINE + 8]
        pieces.append(top + jnp.concatenate([shifted, jnp.zeros_like(shifted)], axis=1))
        pieces.append(table[comp * FINE + 8 : (comp + 1) * FINE])
    return jnp.concatenate(pieces + [table[KNOT_ROWS:]], axis=0), ahead, edges


def gather_ready(table, ahead, cal_coef_ref, tile_cal_ref, star_image_ref, knot_parts_ref, cal_ref):
    wide_lane = lax.broadcasted_iota(jnp.int32, (8, COARSE), 1)
    row = lax.broadcasted_iota(jnp.int32, (8, COARSE), 0)
    beyond = []
    for comp in range(4):
        moved = pltpu.roll(table[comp * FINE : comp * FINE + 8], COARSE - 1, 1)
        last = pltpu.roll(ahead, 127 - 2 * comp, 1)
        moved = jnp.where(wide_lane == COARSE - 1, jnp.concatenate([last, last], axis=1), moved)
        beyond.append(pltpu.roll(moved, 4, 0) if comp % 2 else moved)
    beyond = [jnp.where(row < 4, beyond[0], beyond[1]), jnp.where(row < 4, beyond[2], beyond[3])]
    knot_high, knot_low = two_parts(jnp.concatenate([table[:KNOT_ROWS]] + beyond, axis=0))
    knot_parts_ref[:KNOT_HALF] = knot_high
    knot_parts_ref[KNOT_HALF:] = knot_low

    blocks = jnp.concatenate([table[KNOT_ROWS:, :128], table[KNOT_ROWS:, 128:]], axis=0)
    rows = product(
        one_hot(tile_cal_ref[...], CALB_DEV), jnp.concatenate(two_parts(blocks), axis=1), ((0,), (0,))
    )
    cal_ref[...] = (rows[:, :128] + rows[:, 128:]) * cal_coef_ref[...] + star_image_ref[...]


def gather(first, live_ref, factors, att_coef_ref, knot_parts_ref, cal_ref):
    rows = pl.ds(first, WIDE_GROUP)
    coef = [att_coef_ref[comp, rows, :] for comp in range(4)]
    hot, columns = factors
    found = product(knot_parts_ref[...], hot, ((1,), (0,)))
    width = cal_ref.shape[1]
    image_rows = []
    for tile in range(WIDE_GROUP):
        here = slice(tile, tile + 1)
        across = slice(tile * width, (tile + 1) * width)

        def part(begin, size):
            return (
                found[begin : begin + size, across]
                + found[KNOT_HALF + begin : KNOT_HALF + begin + size, across]
            )

        near, past = columns[tile]
        near = near * sum(coef[comp][here] * part(comp * FINE, FINE) for comp in range(4))
        past = past * past_terms(coef, here) * part(KNOT_ROWS, PAST_ROWS)
        both = near[:8] + near[8:16] + near[16:24] + near[24:] + past[:8] + past[8:]
        image_rows.append(jnp.sum(both, axis=0, keepdims=True))
    image = jnp.concatenate(image_rows, axis=0) + cal_ref[rows, :]
    return image * live_mask(live_ref, first, image.shape)


def squares(array):
    return jnp.sum(array * array, keepdims=True)


def middle_kernel(
    n_stars, n_seg, live_ref, place_ref, knot_ref, frac_ref, att_coef_ref, star_ref, star_coef_ref,
    cal_coef_ref, tile_cal_ref, star_image_ref, star_x_ref, block_ref, image_ref, table_out, scatter_out,
    star_out, knot_parts_ref, cal_ref, knot_acc, star_acc,
):
    table, ahead, _ = received_table(n_stars, n_seg, place_ref, block_ref)
    table_out[...] = table
    norm = squares(star_x_ref[...]) / n_seg + squares(table) / n_stars
    gather_ready(table, ahead, cal_coef_ref, tile_cal_ref, star_image_ref, knot_parts_ref, cal_ref)
    knot_acc[...] = jnp.zeros_like(knot_acc)
    star_acc[...] = jnp.zeros_like(star_acc)
    def one_group(group, total):
        first = pl.multiple_of(group * WIDE_GROUP, WIDE_GROUP)
        factors = knot_factors(first, knot_ref, frac_ref)
        image = gather(first, live_ref, factors, att_coef_ref, knot_parts_ref, cal_ref)
        image_ref[pl.ds(first, WIDE_GROUP), :] = image
        scatter(first, factors, image, (att_coef_ref, star_ref, star_coef_ref), knot_acc, star_acc)
        return total + image * image

    zero = jnp.zeros((WIDE_GROUP, knot_ref.shape[1]), F32)
    total = lax.fori_loop(0, knot_ref.shape[0] // WIDE_GROUP, one_group, zero)
    scatter_calibration(image_ref[...] * cal_coef_ref[...], tile_cal_ref, scatter_out)
    scalars = [(0, norm), (1, jnp.sum(total, keepdims=True))]
    scatter_end(place_ref, scalars, knot_acc, star_acc, scatter_out, star_out)


def last_kernel(
    n_stars, n_seg, live_ref, place_ref, knot_ref, frac_ref, att_coef_ref, cal_coef_ref, tile_cal_ref,
    star_image_ref, star_x_ref, block_ref, star_0_ref, table_0_ref, image_0_ref, image_ref, table_out,
    scalar_out, own_scalar_out, knot_parts_ref, cal_ref,
):
    table, ahead, edges = received_table(n_stars, n_seg, place_ref, block_ref)
    table_out[...] = table
    norm_0, square_0 = first_step(edges)
    step = norm_0 / square_0
    norm = (
        squares(star_0_ref[...] - step * star_x_ref[...]) / n_seg
        + squares(table_0_ref[...] - step * table) / n_stars
    )
    gather_ready(table, ahead, cal_coef_ref, tile_cal_ref, star_image_ref, knot_parts_ref, cal_ref)

    def one_group(group, sums):
        first = pl.multiple_of(group * WIDE_GROUP, WIDE_GROUP)
        rows = pl.ds(first, WIDE_GROUP)
        image_0 = image_0_ref[rows, :]
        factors = knot_factors(first, knot_ref, frac_ref)
        image = gather(first, live_ref, factors, att_coef_ref, knot_parts_ref, cal_ref)
        image = image_0 - step * image
        image_ref[rows, :] = image
        return sums[0] + image * image, sums[1] + image * image_0

    zero = jnp.zeros((WIDE_GROUP, knot_ref.shape[1]), F32)
    sums = lax.fori_loop(0, knot_ref.shape[0] // WIDE_GROUP, one_group, (zero, zero))
    scalars = [norm] + [jnp.sum(part, keepdims=True) for part in sums] + [norm_0, square_0]
    scalars = with_scalars(jnp.zeros((8, 128), F32), list(enumerate(scalars)))
    own_scalar_out[...] = scalars
    for device in range(scalar_out.shape[0]):
        scalar_out[device] = scalars[:1]


def output_kernel(
    live_ref, own_scalar_ref, scalar_ref, star_0_ref, star_h_ref, att_0_ref, att_h_ref, table_0_ref,
    table_h_ref, value_ref, image_0_ref, image_1_ref, star_out, att_out, cal_out, residual_out,
):
    norm_0, square_0 = [picked(own_scalar_ref[...], which) for which in (3, 4)]
    everyone = scalar_ref[0]
    for device in range(1, scalar_ref.shape[0]):
        everyone = everyone + scalar_ref[device]
    norm_1, square_1, cross = [picked(everyone, which) for which in range(3)]
    step_0 = norm_0 / square_0
    ratio = norm_1 / norm_0
    step_1 = norm_1 / (square_1 + 2.0 * ratio * cross + ratio * ratio * square_0)
    scale = step_0 + step_1 * ratio

    def combined(old, change):
        return scale * old + step_1 * (old - step_0 * change)

    star_out[...] = combined(star_0_ref[...], star_h_ref[...])
    att_out[...] = combined(att_0_ref[...], att_h_ref[...])
    cal = combined(table_0_ref[KNOT_ROWS:, :], table_h_ref[KNOT_ROWS:, :])
    cal_out[...] = jnp.concatenate([cal[:, :128], cal[:, 128:]], axis=0)
    values = value_ref[...] * live_mask(live_ref, 0, value_ref.shape)
    residual_out[...] = values - scale * image_0_ref[...] - step_1 * image_1_ref[...]


def in_vmem(count):
    return [pl.BlockSpec(memory_space=pltpu.VMEM)] * count


def in_smem(count):
    return [pl.BlockSpec(memory_space=pltpu.SMEM)] * count


def in_hbm(count):
    return [pl.BlockSpec(memory_space=pltpu.HBM)] * count


def shaped(*shape):
    return jax.ShapeDtypeStruct(shape, F32)


ARRIVE_PARAMS = pltpu.CompilerParams(vmem_limit_bytes=60 * 1024 * 1024)
PARAMS = pltpu.CompilerParams(vmem_limit_bytes=40 * 1024 * 1024)
PASS_COST = pl.CostEstimate(flops=3_000_000_000, bytes_accessed=1_000_000, transcendentals=0)
SMALL_COST = pl.CostEstimate(flops=1_000_000, bytes_accessed=600_000, transcendentals=0)


def on_device(
    obs_star, obs_knot, obs_frac, star_coef, att_coef, cal_coef, tile_cal, live_tiles, obs_value
):
    n_stars, n_seg = lax.axis_size("stars"), lax.axis_size("seg")
    tile_count, width = obs_star.shape
    tile_row = tile_cal[None, :]
    place = lax.axis_index("seg").astype(jnp.int32)[None]
    image_shape = shaped(tile_count, width)
    table_shape = shaped(TABLE_ROWS, COARSE)
    star_shape = shaped(STAR_ROWS, COARSE)
    sent_shapes = (shaped(n_stars, TABLE_ROWS // n_stars, COARSE), shaped(STAR_ROWS + 8, COARSE))
    sums = [pltpu.VMEM((2 * KNOT_HALF, COARSE), F32), pltpu.VMEM((2 * STAR_ROWS, COARSE), F32)]
    ready = [pltpu.VMEM((2 * KNOT_HALF, COARSE), BF16), pltpu.VMEM((tile_count, width), F32)]

    def first_scatter():
        observed = (obs_value, cal_coef, tile_row, obs_knot, obs_frac, att_coef, obs_star, star_coef)
        buffers = [pltpu.VMEM(array.shape, array.dtype) for array in observed]
        return pl.pallas_call(
            first_kernel,
            out_shape=sent_shapes,
            in_specs=in_smem(2) + in_hbm(len(observed)),
            out_specs=tuple(in_vmem(2)),
            scratch_shapes=sums + buffers + [pltpu.SemaphoreType.DMA((13,))],
            compiler_params=ARRIVE_PARAMS,
            cost_estimate=PASS_COST,
            name="first_scatter",
        )(live_tiles, place, *observed)

    def middle(*received):
        observed = (obs_knot, obs_frac, att_coef, obs_star, star_coef, cal_coef, tile_row)
        return pl.pallas_call(
            functools.partial(middle_kernel, n_stars, n_seg),
            out_shape=(image_shape, table_shape, *sent_shapes),
            in_specs=in_smem(2) + in_vmem(len(observed) + len(received)),
            out_specs=tuple(in_vmem(4)),
            scratch_shapes=ready + sums,
            compiler_params=PARAMS,
            cost_estimate=PASS_COST,
            name="gather_and_scatter",
        )(live_tiles, place, *observed, *received)

    def last_gather(*received):
        observed = (obs_knot, obs_frac, att_coef, cal_coef, tile_row)
        return pl.pallas_call(
            functools.partial(last_kernel, n_stars, n_seg),
            out_shape=(image_shape, table_shape, shaped(n_stars * n_seg, 1, 128), shaped(8, 128)),
            in_specs=in_smem(2) + in_vmem(len(observed) + len(received)),
            out_specs=tuple(in_vmem(4)),
            scratch_shapes=ready,
            compiler_params=PARAMS,
            cost_estimate=PASS_COST,
            name="last_gather",
        )(live_tiles, place, *observed, *received)

    def star_forward(star):
        return pl.pallas_call(
            star_forward_kernel,
            out_shape=image_shape,
            in_specs=in_vmem(3),
            out_specs=in_vmem(1)[0],
            scratch_shapes=[pltpu.VMEM((2 * STAR_ROWS, COARSE), BF16)],
            compiler_params=PARAMS,
            cost_estimate=PASS_COST,
            name="star_forward",
        )(obs_star, star_coef, star)

    def swap(blocks, axes):
        return lax.all_to_all(blocks, axes, 0, 0)

    def partner(array, axis, distance):
        return lax.ppermute(array, axis, [(i, i ^ distance) for i in range(lax.axis_size(axis))])

    def reduced(table, star):
        distances = [1 << bit for bit in range(n_seg.bit_length() - 1)]
        for distance in distances[:-1]:
            star = star + partner(star, "seg", distance)
        blocks, star = pl.pallas_call(
            sum_kernel,
            out_shape=(shaped(n_stars, 2 * TABLE_ROWS // n_stars + 8, 128), star_shape),
            in_specs=in_vmem(3),
            out_specs=tuple(in_vmem(2)),
            compiler_params=PARAMS,
            cost_estimate=SMALL_COST,
            name="table_sum",
        )(swap(table, "stars"), star, partner(star, "seg", distances[-1]))
        return star_forward(star), star, swap(blocks, "stars")

    first = reduced(*first_scatter())
    star_0 = first[1]
    image_0, table_0, *sent = middle(*first)
    second = reduced(*sent)
    star_h = second[1]
    image_1, table_h, scalars, own_scalars = last_gather(*second, star_0, table_0, image_0)

    def star_order(star):
        return star.reshape(5, STAR_DEV)

    def att_order(table):
        att = table[:KNOT_ROWS].reshape(4, FINE, COARSE)
        return att.transpose(0, 2, 1).reshape(4, KNOT_DEV)

    return pl.pallas_call(
        output_kernel,
        out_shape=(shaped(5, STAR_DEV), shaped(4, KNOT_DEV), shaped(CALB_DEV, width), image_shape),
        in_specs=in_smem(1) + in_vmem(11),
        out_specs=tuple(in_vmem(4)),
        compiler_params=PARAMS,
        cost_estimate=SMALL_COST,
        name="outputs",
    )(
        live_tiles, own_scalars, swap(scalars, ("stars", "seg")), star_order(star_0), star_order(star_h),
        att_order(table_0), att_order(table_h), table_0, table_h, obs_value, image_0, image_1,
    )


def solution(mesh):
    placed = (
        P(("stars", "seg"), None),
        P(("stars", "seg"), None),
        P(("stars", "seg"), None),
        P(None, ("stars", "seg"), None),
        P(None, ("stars", "seg"), None),
        P(("stars", "seg"), None),
        P(("stars", "seg")),
        P(("stars", "seg")),
        P(("stars", "seg"), None),
    )
    return jax.shard_map(
        on_device,
        mesh=mesh,
        in_specs=placed,
        out_specs=(P(None, "stars"), P(None, "seg"), P("seg", None), P(("stars", "seg"), None)),
        check_vma=False,
    )
```

```python
import functools

import jax
import jax.numpy as jnp
from jax import lax
from jax.experimental import pallas as pl
from jax.experimental.pallas import tpu as pltpu
from jax.sharding import PartitionSpec as P

STAR_DEV = 8192
KNOT_DEV = 8192
CALB_DEV = 256
FINE = 32
COARSE = 256
GROUP = 16
WIDE_GROUP = 64
SLOT = 8
STAR_ROWS = 5 * FINE
KNOT_ROWS = 4 * FINE
TABLE_ROWS = KNOT_ROWS + CALB_DEV // 2
BF16 = jnp.bfloat16
F32 = jnp.float32
SCALAR_LANE = 64
PAST_ROWS = 16
KNOT_HALF = KNOT_ROWS + PAST_ROWS


def two_parts(values):
    high = values.astype(BF16)
    return high, (values - high.astype(F32)).astype(BF16)


def rows_and_columns(shape):
    return lax.broadcasted_iota(jnp.int32, shape, 0), lax.broadcasted_iota(jnp.int32, shape, 1)


def packed_rows(row, size):
    wide = jnp.broadcast_to(row.astype(F32), (16, row.shape[1])).astype(BF16)
    return jnp.concatenate([wide] * (size // 16), axis=0)


def matches(index_row, size):
    places, _ = rows_and_columns((size, index_row.shape[1]))
    return places.astype(F32).astype(BF16) == packed_rows(index_row, size)


def one_hot(index_row, size):
    return jnp.where(matches(index_row, size), jnp.ones((), BF16), jnp.zeros((), BF16))


def spline_weights(fraction):
    remain = 1.0 - fraction
    square = fraction * fraction
    cubed = square * fraction
    return (
        remain * remain * remain / 6.0,
        (3.0 * cubed - 6.0 * square + 4.0) / 6.0,
        (-3.0 * cubed + 3.0 * square + 3.0 * fraction + 1.0) / 6.0,
        cubed / 6.0,
    )


def weight_columns(weights, fine_row, tile, places):
    behind = places - fine_row
    result = jnp.zeros(behind.shape, F32)
    for offset in range(4):
        result = jnp.where(behind == offset, weights[offset][tile : tile + 1], result)
    return result


def near_and_past(weights, fine, tile):
    width = fine.shape[1]
    fine_row = fine[tile : tile + 1]
    near, _ = rows_and_columns((FINE, width))
    past, _ = rows_and_columns((PAST_ROWS, width))
    past = FINE + (past & 3)
    return weight_columns(weights, fine_row, tile, near), weight_columns(weights, fine_row, tile, past)


def past_terms(terms, here):
    rows, _ = rows_and_columns((PAST_ROWS, terms[0].shape[1]))
    result = jnp.broadcast_to(terms[3][here], rows.shape)
    for comp in range(2, -1, -1):
        result = jnp.where(rows < 4 * (comp + 1), terms[comp][here], result)
    return result


def product(left, right, contract):
    return lax.dot_general(left, right, (contract, ((), ())), preferred_element_type=F32)


def live_mask(live_ref, first, shape):
    rows, _ = rows_and_columns(shape)
    return (rows + first < live_ref[0]).astype(F32)


def store_rows(out_ref, begin, rows):
    block = out_ref.shape[1]
    for offset in range(0, rows.shape[0], 8):
        where = begin + offset
        out_ref[where // block, where % block : where % block + 8, :] = rows[offset : offset + 8]


def knot_factors(first, size, knot_ref, frac_ref):
    rows = pl.ds(first, size)
    knot = knot_ref[rows, :]
    coarse, fine = knot >> 5, knot & (FINE - 1)
    weights = spline_weights(frac_ref[rows, :])
    hot = [one_hot(coarse[tile : tile + 1], COARSE) for tile in range(size)]
    columns = [near_and_past(weights, fine, tile) for tile in range(size)]
    return jnp.concatenate(hot, axis=1), columns


def scatter(first, factors, values, observed, knot_acc, star_acc):
    att_coef_ref, star_ref, star_coef_ref = observed
    knot_hot, columns = factors
    rows = pl.ds(first, len(columns))
    star = star_ref[rows, :]
    star_coarse, star_fine = star & (COARSE - 1), star >> 8
    terms = [att_coef_ref[comp, rows, :] * values for comp in range(4)]
    parts = [two_parts(star_coef_ref[comp, rows, :] * values) for comp in range(5)]
    parts = [pair[half].astype(F32) for half in range(2) for pair in parts]
    knot_left, star_left, star_right = [], [], []
    for tile in range(len(columns)):
        here = slice(tile, tile + 1)
        near, past = columns[tile]
        spread = jnp.concatenate(
            [term[here] * near for term in terms] + [past_terms(terms, here) * past], axis=0
        )
        knot_left.append(jnp.concatenate(two_parts(spread), axis=0))
        star_right.append(one_hot(star_coarse[here], COARSE))
        chosen = matches(star_fine[here], FINE)
        star_left.append(
            jnp.concatenate(
                [jnp.where(chosen, packed_rows(part[here], FINE), jnp.zeros((), BF16)) for part in parts],
                axis=0,
            )
        )
    knot_acc[...] += product(
        jnp.concatenate(knot_left, axis=1), knot_hot, ((1,), (1,))
    )
    star_acc[...] += product(
        jnp.concatenate(star_left, axis=1), jnp.concatenate(star_right, axis=1), ((1,), (1,))
    )


def scatter_calibration(values, tile_cal_ref, table_out):
    blocks = product(
        one_hot(tile_cal_ref[...], CALB_DEV), jnp.concatenate(two_parts(values), axis=1), ((1,), (0,))
    )
    width = values.shape[1]
    blocks = blocks[:, :width] + blocks[:, width:]
    blocks = jnp.concatenate([blocks[: CALB_DEV // 2], blocks[CALB_DEV // 2 :]], axis=1)
    store_rows(table_out, KNOT_ROWS, blocks)


def scatter_end(place_ref, scalars, knot_acc, star_acc, table_out, star_out):
    lane = lax.broadcasted_iota(jnp.int32, (8, 128), 1)
    row = lax.broadcasted_iota(jnp.int32, (8, 128), 0)
    wide_lane = lax.broadcasted_iota(jnp.int32, (8, COARSE), 1)
    wide_row = lax.broadcasted_iota(jnp.int32, (8, COARSE), 0)
    edges = jnp.zeros((8, 128), F32)
    for comp in range(4):
        begin, past = comp * FINE, KNOT_ROWS + comp // 2 * 8
        main = knot_acc[begin : begin + FINE] + knot_acc[KNOT_HALF + begin : KNOT_HALF + begin + FINE]
        beyond = knot_acc[past : past + 8] + knot_acc[KNOT_HALF + past : KNOT_HALF + past + 8]
        if comp % 2:
            beyond = pltpu.roll(beyond, 4, 0)
        moved = pltpu.roll(jnp.where(wide_row < 3, beyond, 0.0), 1, 1)
        top = main[:8] + jnp.where(wide_lane > 0, moved, 0.0)
        store_rows(table_out, begin, top)
        store_rows(table_out, begin + 8, main[8:])
        tail, head = moved[:, :128], top[:, :128]
        if comp:
            tail = pltpu.roll(tail, 2 * comp, 1)
        head = pltpu.roll(head, 2 * comp + 1, 1)
        edges = jnp.where((lane == 2 * comp) & (row < 3), tail, edges)
        edges = jnp.where((lane == 2 * comp + 1) & (row < 3), head, edges)
    edges = with_scalars(pltpu.roll(edges, SLOT * place_ref[0], 1), scalars)
    star_out[:STAR_ROWS] = star_acc[:STAR_ROWS] + star_acc[STAR_ROWS:]
    star_out[STAR_ROWS:] = jnp.concatenate([edges, jnp.zeros_like(edges)], axis=1)


def first_kernel(live_ref, place_ref, *refs):
    sources, (table_out, star_out, knot_acc, star_acc) = refs[:8], refs[8:12]
    buffers, sems = refs[12:20], refs[20]
    half = sources[0].shape[0] // 2
    copies = []

    def begin(source, target, *place):
        source, target = (source.at[place], target.at[place]) if place else (source, target)
        copies.append(pltpu.make_async_copy(source, target, sems.at[len(copies)]))
        copies[-1].start()

    for source, target in zip(sources[:3], buffers):
        begin(source, target)
    for rows in (slice(0, half), slice(half, 2 * half)):
        for source, target in zip(sources[3:], buffers[3:]):
            begin(source, target, *[slice(None)] * (len(source.shape) - 2), rows)
    value_ref, cal_coef_ref, tile_cal_ref, knot_ref, frac_ref, *observed = buffers
    knot_acc[...] = jnp.zeros_like(knot_acc)
    star_acc[...] = jnp.zeros_like(star_acc)
    for copy in copies[:3]:
        copy.wait()
    values = value_ref[...] * live_mask(live_ref, 0, value_ref.shape)
    scatter_calibration(values * cal_coef_ref[...], tile_cal_ref, table_out)
    for copy in copies[3:8]:
        copy.wait()

    @pl.loop(0, value_ref.shape[0] // WIDE_GROUP)
    def _(group):
        @pl.when(group * WIDE_GROUP == half)
        def _():
            for copy in copies[8:]:
                copy.wait()

        first = pl.multiple_of(group * WIDE_GROUP, WIDE_GROUP)
        values = value_ref[pl.ds(first, WIDE_GROUP), :]
        values = values * live_mask(live_ref, first, values.shape)
        scatter(first, knot_factors(first, WIDE_GROUP, knot_ref, frac_ref), values, observed, knot_acc, star_acc)

    scatter_end(place_ref, [], knot_acc, star_acc, table_out, star_out)


def sum_kernel(block_ref, own_ref, other_ref, out_ref, star_out):
    total = block_ref[0]
    for device in range(1, block_ref.shape[0]):
        total = total + block_ref[device]
    star = own_ref[...] + other_ref[...]
    star_out[...] = star[:STAR_ROWS]
    total = jnp.concatenate([total[:, :128], total[:, 128:], star[STAR_ROWS:, :128]], axis=0)
    for device in range(block_ref.shape[0]):
        out_ref[device] = total


def picked(array, which):
    row = lax.broadcasted_iota(jnp.int32, array.shape, 0)
    lane = lax.broadcasted_iota(jnp.int32, array.shape, 1)
    chosen = (row == 0) & (lane == SCALAR_LANE + which)
    return jnp.sum(jnp.where(chosen, array, 0.0), keepdims=True)


def with_scalars(array, scalars):
    row = lax.broadcasted_iota(jnp.int32, array.shape, 0)
    lane = lax.broadcasted_iota(jnp.int32, array.shape, 1)
    for which, value in scalars:
        array = jnp.where((row == 0) & (lane == SCALAR_LANE + which), value, array)
    return array


def first_step(edges):
    return picked(edges, 0), picked(edges, 1)


def star_forward_kernel(star_ref, star_coef_ref, star_x_ref, image_ref, star_parts_ref):
    star_x = star_x_ref[...]
    star_high, star_low = two_parts(star_x)
    star_parts_ref[:STAR_ROWS] = star_high
    star_parts_ref[STAR_ROWS:] = star_low

    @pl.loop(0, star_ref.shape[0] // GROUP)
    def _(group):
        rows = pl.ds(pl.multiple_of(group * GROUP, GROUP), GROUP)
        star = star_ref[rows, :]
        coarse, fine = star & (COARSE - 1), star >> 8
        coef = [star_coef_ref[comp, rows, :] for comp in range(5)]
        tiles = [slice(tile, tile + 1) for tile in range(GROUP)]
        hot = jnp.concatenate([one_hot(coarse[here], COARSE) for here in tiles], axis=1)
        found = product(star_parts_ref[...], hot, ((1,), (0,)))
        width = star.shape[1]
        fine_rows, _ = rows_and_columns((FINE, width))
        image_rows = []
        for tile, here in enumerate(tiles):
            across = slice(tile * width, (tile + 1) * width)

            def part(comp):
                begin = comp * FINE
                return (
                    found[begin : begin + FINE, across]
                    + found[STAR_ROWS + begin : STAR_ROWS + begin + FINE, across]
                )

            both = sum(coef[comp][here] * part(comp) for comp in range(5))
            both = jnp.where(fine_rows == fine[here], both, 0.0)
            both = both[:8] + both[8:16] + both[16:24] + both[24:]
            image_rows.append(jnp.sum(both, axis=0, keepdims=True))
        image_ref[rows, :] = jnp.concatenate(image_rows, axis=0)


def received_table(n_stars, n_seg, place_ref, block_ref):
    segment = place_ref[0]
    lane = lax.broadcasted_iota(jnp.int32, (8, 128), 1)
    row = lax.broadcasted_iota(jnp.int32, (8, 128), 0)
    edges = block_ref[0, -8:, :]
    for block in range(1, n_stars):
        edges = edges + block_ref[block, -8:, :]

    def slot(which):
        return pltpu.roll(edges, (128 - SLOT * jnp.clip(which, 0, n_seg - 1)) & 127, 1)

    before, own, after = slot(segment - 1), slot(segment), slot(segment + 1)
    before = jnp.where(segment > 0, before, 0.0)
    ahead = jnp.where(lane % 2 == 0, own, 0.0) + pltpu.roll(jnp.where(lane % 2 == 1, after, 0.0), 127, 1)
    ahead = jnp.where((segment < n_seg - 1) & (lane < 8) & (row < 3), ahead, 0.0)

    size = TABLE_ROWS // n_stars
    table = jnp.concatenate([block_ref[:, :size, :], block_ref[:, size : 2 * size, :]], axis=2)
    table = table.reshape(TABLE_ROWS, COARSE)
    pieces = []
    for comp in range(4):
        shifted = pltpu.roll(before, 128 - 2 * comp, 1) if comp else before
        shifted = jnp.where((lane == 0) & (row < 3), shifted, 0.0)
        top = table[comp * FINE : comp * FINE + 8]
        pieces.append(top + jnp.concatenate([shifted, jnp.zeros_like(shifted)], axis=1))
        pieces.append(table[comp * FINE + 8 : (comp + 1) * FINE])
    return jnp.concatenate(pieces + [table[KNOT_ROWS:]], axis=0), ahead, edges


def gather_ready(table, ahead, cal_coef_ref, tile_cal_ref, star_image_ref, knot_parts_ref, cal_ref):
    wide_lane = lax.broadcasted_iota(jnp.int32, (8, COARSE), 1)
    row = lax.broadcasted_iota(jnp.int32, (8, COARSE), 0)
    beyond = []
    for comp in range(4):
        moved = pltpu.roll(table[comp * FINE : comp * FINE + 8], COARSE - 1, 1)
        last = pltpu.roll(ahead, 127 - 2 * comp, 1)
        moved = jnp.where(wide_lane == COARSE - 1, jnp.concatenate([last, last], axis=1), moved)
        beyond.append(pltpu.roll(moved, 4, 0) if comp % 2 else moved)
    beyond = [jnp.where(row < 4, beyond[0], beyond[1]), jnp.where(row < 4, beyond[2], beyond[3])]
    knot_high, knot_low = two_parts(jnp.concatenate([table[:KNOT_ROWS]] + beyond, axis=0))
    knot_parts_ref[:KNOT_HALF] = knot_high
    knot_parts_ref[KNOT_HALF:] = knot_low

    blocks = jnp.concatenate([table[KNOT_ROWS:, :128], table[KNOT_ROWS:, 128:]], axis=0)
    rows = product(
        one_hot(tile_cal_ref[...], CALB_DEV), jnp.concatenate(two_parts(blocks), axis=1), ((0,), (0,))
    )
    cal_ref[...] = (rows[:, :128] + rows[:, 128:]) * cal_coef_ref[...] + star_image_ref[...]


def gather(first, live_ref, factors, att_coef_ref, knot_parts_ref, cal_ref):
    hot, columns = factors
    rows = pl.ds(first, len(columns))
    coef = [att_coef_ref[comp, rows, :] for comp in range(4)]
    found = product(knot_parts_ref[...], hot, ((1,), (0,)))
    width = cal_ref.shape[1]
    image_rows = []
    for tile in range(len(columns)):
        here = slice(tile, tile + 1)
        across = slice(tile * width, (tile + 1) * width)

        def part(begin, size):
            return (
                found[begin : begin + size, across]
                + found[KNOT_HALF + begin : KNOT_HALF + begin + size, across]
            )

        near, past = columns[tile]
        near = near * sum(coef[comp][here] * part(comp * FINE, FINE) for comp in range(4))
        past = past * past_terms(coef, here) * part(KNOT_ROWS, PAST_ROWS)
        both = near[:8] + near[8:16] + near[16:24] + near[24:] + past[:8] + past[8:]
        image_rows.append(jnp.sum(both, axis=0, keepdims=True))
    image = jnp.concatenate(image_rows, axis=0) + cal_ref[rows, :]
    return image * live_mask(live_ref, first, image.shape)


def squares(array):
    return jnp.sum(array * array, keepdims=True)


def middle_kernel(
    n_stars, n_seg, live_ref, place_ref, knot_ref, frac_ref, att_coef_ref, star_ref, star_coef_ref,
    cal_coef_ref, tile_cal_ref, star_image_ref, star_x_ref, block_ref, image_ref, table_out, scatter_out,
    star_out, knot_parts_ref, cal_ref, knot_acc, star_acc,
):
    table, ahead, _ = received_table(n_stars, n_seg, place_ref, block_ref)
    table_out[...] = table
    norm = squares(star_x_ref[...]) / n_seg + squares(table) / n_stars
    gather_ready(table, ahead, cal_coef_ref, tile_cal_ref, star_image_ref, knot_parts_ref, cal_ref)
    knot_acc[...] = jnp.zeros_like(knot_acc)
    star_acc[...] = jnp.zeros_like(star_acc)
    factors = knot_factors(0, knot_ref.shape[0], knot_ref, frac_ref)
    image = gather(0, live_ref, factors, att_coef_ref, knot_parts_ref, cal_ref)
    image_ref[...] = image
    scatter(0, factors, image, (att_coef_ref, star_ref, star_coef_ref), knot_acc, star_acc)
    scatter_calibration(image * cal_coef_ref[...], tile_cal_ref, scatter_out)
    scalars = [(0, norm), (1, squares(image))]
    scatter_end(place_ref, scalars, knot_acc, star_acc, scatter_out, star_out)


def last_kernel(
    n_stars, n_seg, live_ref, place_ref, knot_ref, frac_ref, att_coef_ref, cal_coef_ref, tile_cal_ref,
    star_image_ref, star_x_ref, block_ref, star_0_ref, table_0_ref, image_0_ref, image_ref, table_out,
    scalar_out, own_scalar_out, knot_parts_ref, cal_ref,
):
    table, ahead, edges = received_table(n_stars, n_seg, place_ref, block_ref)
    table_out[...] = table
    norm_0, square_0 = first_step(edges)
    step = norm_0 / square_0
    norm = (
        squares(star_0_ref[...] - step * star_x_ref[...]) / n_seg
        + squares(table_0_ref[...] - step * table) / n_stars
    )
    gather_ready(table, ahead, cal_coef_ref, tile_cal_ref, star_image_ref, knot_parts_ref, cal_ref)

    factors = knot_factors(0, knot_ref.shape[0], knot_ref, frac_ref)
    image_0 = image_0_ref[...]
    image = gather(0, live_ref, factors, att_coef_ref, knot_parts_ref, cal_ref)
    image = image_0 - step * image
    image_ref[...] = image
    cross = jnp.sum(image * image_0, keepdims=True)
    scalars = [norm, squares(image), cross, norm_0, square_0]
    scalars = with_scalars(jnp.zeros((8, 128), F32), list(enumerate(scalars)))
    own_scalar_out[...] = scalars
    for device in range(scalar_out.shape[0]):
        scalar_out[device] = scalars[:1]


def output_kernel(
    live_ref, own_scalar_ref, scalar_ref, star_0_ref, star_h_ref, att_0_ref, att_h_ref, table_0_ref,
    table_h_ref, value_ref, image_0_ref, image_1_ref, star_out, att_out, cal_out, residual_out,
):
    norm_0, square_0 = [picked(own_scalar_ref[...], which) for which in (3, 4)]
    everyone = scalar_ref[0]
    for device in range(1, scalar_ref.shape[0]):
        everyone = everyone + scalar_ref[device]
    norm_1, square_1, cross = [picked(everyone, which) for which in range(3)]
    step_0 = norm_0 / square_0
    ratio = norm_1 / norm_0
    step_1 = norm_1 / (square_1 + 2.0 * ratio * cross + ratio * ratio * square_0)
    scale = step_0 + step_1 * ratio

    def combined(old, change):
        return scale * old + step_1 * (old - step_0 * change)

    star_out[...] = combined(star_0_ref[...], star_h_ref[...])
    att_out[...] = combined(att_0_ref[...], att_h_ref[...])
    cal = combined(table_0_ref[KNOT_ROWS:, :], table_h_ref[KNOT_ROWS:, :])
    cal_out[...] = jnp.concatenate([cal[:, :128], cal[:, 128:]], axis=0)
    values = value_ref[...] * live_mask(live_ref, 0, value_ref.shape)
    residual_out[...] = values - scale * image_0_ref[...] - step_1 * image_1_ref[...]


def in_vmem(count):
    return [pl.BlockSpec(memory_space=pltpu.VMEM)] * count


def in_smem(count):
    return [pl.BlockSpec(memory_space=pltpu.SMEM)] * count


def in_hbm(count):
    return [pl.BlockSpec(memory_space=pltpu.HBM)] * count


def shaped(*shape):
    return jax.ShapeDtypeStruct(shape, F32)


ARRIVE_PARAMS = pltpu.CompilerParams(vmem_limit_bytes=60 * 1024 * 1024)
PARAMS = pltpu.CompilerParams(vmem_limit_bytes=40 * 1024 * 1024)
PASS_COST = pl.CostEstimate(flops=3_000_000_000, bytes_accessed=1_000_000, transcendentals=0)
SMALL_COST = pl.CostEstimate(flops=1_000_000, bytes_accessed=600_000, transcendentals=0)


def on_device(
    obs_star, obs_knot, obs_frac, star_coef, att_coef, cal_coef, tile_cal, live_tiles, obs_value
):
    n_stars, n_seg = lax.axis_size("stars"), lax.axis_size("seg")
    tile_count, width = obs_star.shape
    tile_row = tile_cal[None, :]
    place = lax.axis_index("seg").astype(jnp.int32)[None]
    image_shape = shaped(tile_count, width)
    table_shape = shaped(TABLE_ROWS, COARSE)
    star_shape = shaped(STAR_ROWS, COARSE)
    sent_shapes = (shaped(n_stars, TABLE_ROWS // n_stars, COARSE), shaped(STAR_ROWS + 8, COARSE))
    sums = [pltpu.VMEM((2 * KNOT_HALF, COARSE), F32), pltpu.VMEM((2 * STAR_ROWS, COARSE), F32)]
    ready = [pltpu.VMEM((2 * KNOT_HALF, COARSE), BF16), pltpu.VMEM((tile_count, width), F32)]

    def first_scatter():
        observed = (obs_value, cal_coef, tile_row, obs_knot, obs_frac, att_coef, obs_star, star_coef)
        buffers = [pltpu.VMEM(array.shape, array.dtype) for array in observed]
        return pl.pallas_call(
            first_kernel,
            out_shape=sent_shapes,
            in_specs=in_smem(2) + in_hbm(len(observed)),
            out_specs=tuple(in_vmem(2)),
            scratch_shapes=sums + buffers + [pltpu.SemaphoreType.DMA((13,))],
            compiler_params=ARRIVE_PARAMS,
            cost_estimate=PASS_COST,
            name="first_scatter",
        )(live_tiles, place, *observed)

    def middle(*received):
        observed = (obs_knot, obs_frac, att_coef, obs_star, star_coef, cal_coef, tile_row)
        return pl.pallas_call(
            functools.partial(middle_kernel, n_stars, n_seg),
            out_shape=(image_shape, table_shape, *sent_shapes),
            in_specs=in_smem(2) + in_vmem(len(observed) + len(received)),
            out_specs=tuple(in_vmem(4)),
            scratch_shapes=ready + sums,
            compiler_params=PARAMS,
            cost_estimate=PASS_COST,
            name="gather_and_scatter",
        )(live_tiles, place, *observed, *received)

    def last_gather(*received):
        observed = (obs_knot, obs_frac, att_coef, cal_coef, tile_row)
        return pl.pallas_call(
            functools.partial(last_kernel, n_stars, n_seg),
            out_shape=(image_shape, table_shape, shaped(n_stars * n_seg, 1, 128), shaped(8, 128)),
            in_specs=in_smem(2) + in_vmem(len(observed) + len(received)),
            out_specs=tuple(in_vmem(4)),
            scratch_shapes=ready,
            compiler_params=PARAMS,
            cost_estimate=PASS_COST,
            name="last_gather",
        )(live_tiles, place, *observed, *received)

    def star_forward(star):
        return pl.pallas_call(
            star_forward_kernel,
            out_shape=image_shape,
            in_specs=in_vmem(3),
            out_specs=in_vmem(1)[0],
            scratch_shapes=[pltpu.VMEM((2 * STAR_ROWS, COARSE), BF16)],
            compiler_params=PARAMS,
            cost_estimate=PASS_COST,
            name="star_forward",
        )(obs_star, star_coef, star)

    def swap(blocks, axes):
        return lax.all_to_all(blocks, axes, 0, 0)

    def partner(array, axis, distance):
        return lax.ppermute(array, axis, [(i, i ^ distance) for i in range(lax.axis_size(axis))])

    def reduced(table, star):
        distances = [1 << bit for bit in range(n_seg.bit_length() - 1)]
        for distance in distances[:-1]:
            star = star + partner(star, "seg", distance)
        blocks, star = pl.pallas_call(
            sum_kernel,
            out_shape=(shaped(n_stars, 2 * TABLE_ROWS // n_stars + 8, 128), star_shape),
            in_specs=in_vmem(3),
            out_specs=tuple(in_vmem(2)),
            compiler_params=PARAMS,
            cost_estimate=SMALL_COST,
            name="table_sum",
        )(swap(table, "stars"), star, partner(star, "seg", distances[-1]))
        return star_forward(star), star, swap(blocks, "stars")

    first = reduced(*first_scatter())
    star_0 = first[1]
    image_0, table_0, *sent = middle(*first)
    second = reduced(*sent)
    star_h = second[1]
    image_1, table_h, scalars, own_scalars = last_gather(*second, star_0, table_0, image_0)

    def star_order(star):
        return star.reshape(5, STAR_DEV)

    def att_order(table):
        att = table[:KNOT_ROWS].reshape(4, FINE, COARSE)
        return att.transpose(0, 2, 1).reshape(4, KNOT_DEV)

    return pl.pallas_call(
        output_kernel,
        out_shape=(shaped(5, STAR_DEV), shaped(4, KNOT_DEV), shaped(CALB_DEV, width), image_shape),
        in_specs=in_smem(1) + in_vmem(11),
        out_specs=tuple(in_vmem(4)),
        compiler_params=PARAMS,
        cost_estimate=SMALL_COST,
        name="outputs",
    )(
        live_tiles, own_scalars, swap(scalars, ("stars", "seg")), star_order(star_0), star_order(star_h),
        att_order(table_0), att_order(table_h), table_0, table_h, obs_value, image_0, image_1,
    )


def solution(mesh):
    placed = (
        P(("stars", "seg"), None),
        P(("stars", "seg"), None),
        P(("stars", "seg"), None),
        P(None, ("stars", "seg"), None),
        P(None, ("stars", "seg"), None),
        P(("stars", "seg"), None),
        P(("stars", "seg")),
        P(("stars", "seg")),
        P(("stars", "seg"), None),
    )
    return jax.shard_map(
        on_device,
        mesh=mesh,
        in_specs=placed,
        out_specs=(P(None, "stars"), P(None, "seg"), P("seg", None), P(("stars", "seg"), None)),
        check_vma=False,
    )
```

```python
import functools

import jax
import jax.numpy as jnp
from jax import lax
from jax.experimental import pallas as pl
from jax.experimental.pallas import tpu as pltpu
from jax.sharding import PartitionSpec as P

STAR_DEV = 8192
KNOT_DEV = 8192
CALB_DEV = 256
FINE = 32
COARSE = 256
GROUP = 16
WIDE_GROUP = 64
SLOT = 8
STAR_ROWS = 5 * FINE
KNOT_ROWS = 4 * FINE
TABLE_ROWS = KNOT_ROWS + CALB_DEV // 2
BF16 = jnp.bfloat16
F32 = jnp.float32
SCALAR_LANE = 64
PAST_ROWS = 16
KNOT_HALF = KNOT_ROWS + PAST_ROWS


def two_parts(values):
    high = values.astype(BF16)
    return high, (values - high.astype(F32)).astype(BF16)


def rows_and_columns(shape):
    return lax.broadcasted_iota(jnp.int32, shape, 0), lax.broadcasted_iota(jnp.int32, shape, 1)


def packed_rows(row, size):
    wide = jnp.broadcast_to(row.astype(F32), (16, row.shape[1])).astype(BF16)
    return jnp.concatenate([wide] * (size // 16), axis=0)


def matches(index_row, size):
    places, _ = rows_and_columns((size, index_row.shape[1]))
    return places.astype(F32).astype(BF16) == packed_rows(index_row, size)


def one_hot(index_row, size):
    return jnp.where(matches(index_row, size), jnp.ones((), BF16), jnp.zeros((), BF16))


def spline_weights(fraction):
    remain = 1.0 - fraction
    square = fraction * fraction
    cubed = square * fraction
    return (
        remain * remain * remain / 6.0,
        (3.0 * cubed - 6.0 * square + 4.0) / 6.0,
        (-3.0 * cubed + 3.0 * square + 3.0 * fraction + 1.0) / 6.0,
        cubed / 6.0,
    )


def weight_columns(weights, fine_row, tile, places):
    behind = places - fine_row
    result = jnp.zeros(behind.shape, F32)
    for offset in range(4):
        result = jnp.where(behind == offset, weights[offset][tile : tile + 1], result)
    return result


def near_and_past(weights, fine, tile):
    width = fine.shape[1]
    fine_row = fine[tile : tile + 1]
    near, _ = rows_and_columns((FINE, width))
    past, _ = rows_and_columns((PAST_ROWS, width))
    past = FINE + (past & 3)
    return weight_columns(weights, fine_row, tile, near), weight_columns(weights, fine_row, tile, past)


def past_terms(terms, here):
    rows, _ = rows_and_columns((PAST_ROWS, terms[0].shape[1]))
    result = jnp.broadcast_to(terms[3][here], rows.shape)
    for comp in range(2, -1, -1):
        result = jnp.where(rows < 4 * (comp + 1), terms[comp][here], result)
    return result


def product(left, right, contract):
    return lax.dot_general(left, right, (contract, ((), ())), preferred_element_type=F32)


def live_mask(live_ref, first, shape):
    rows, _ = rows_and_columns(shape)
    return (rows + first < live_ref[0]).astype(F32)


def store_rows(out_ref, begin, rows):
    block = out_ref.shape[1]
    for offset in range(0, rows.shape[0], 8):
        where = begin + offset
        out_ref[where // block, where % block : where % block + 8, :] = rows[offset : offset + 8]


def knot_factors(first, size, knot_ref, frac_ref):
    rows = pl.ds(first, size)
    knot = knot_ref[rows, :]
    coarse, fine = knot >> 5, knot & (FINE - 1)
    weights = spline_weights(frac_ref[rows, :])
    hot = [one_hot(coarse[tile : tile + 1], COARSE) for tile in range(size)]
    columns = [near_and_past(weights, fine, tile) for tile in range(size)]
    return jnp.concatenate(hot, axis=1), columns


def scatter(first, factors, values, observed, knot_acc, star_acc):
    att_coef_ref, star_ref, star_coef_ref = observed
    knot_hot, columns = factors
    rows = pl.ds(first, len(columns))
    star = star_ref[rows, :]
    star_coarse, star_fine = star & (COARSE - 1), star >> 8
    terms = [att_coef_ref[comp, rows, :] * values for comp in range(4)]
    parts = [two_parts(star_coef_ref[comp, rows, :] * values) for comp in range(5)]
    parts = [pair[half].astype(F32) for half in range(2) for pair in parts]
    knot_left, star_left, star_right = [], [], []
    for tile in range(len(columns)):
        here = slice(tile, tile + 1)
        near, past = columns[tile]
        spread = jnp.concatenate(
            [term[here] * near for term in terms] + [past_terms(terms, here) * past], axis=0
        )
        knot_left.append(jnp.concatenate(two_parts(spread), axis=0))
        star_right.append(one_hot(star_coarse[here], COARSE))
        chosen = matches(star_fine[here], FINE)
        star_left.append(
            jnp.concatenate(
                [jnp.where(chosen, packed_rows(part[here], FINE), jnp.zeros((), BF16)) for part in parts],
                axis=0,
            )
        )
    knot_acc[...] += product(
        jnp.concatenate(knot_left, axis=1), knot_hot, ((1,), (1,))
    )
    star_acc[...] += product(
        jnp.concatenate(star_left, axis=1), jnp.concatenate(star_right, axis=1), ((1,), (1,))
    )


def scatter_calibration(values, tile_cal_ref, table_out):
    blocks = product(
        one_hot(tile_cal_ref[...], CALB_DEV), jnp.concatenate(two_parts(values), axis=1), ((1,), (0,))
    )
    width = values.shape[1]
    blocks = blocks[:, :width] + blocks[:, width:]
    blocks = jnp.concatenate([blocks[: CALB_DEV // 2], blocks[CALB_DEV // 2 :]], axis=1)
    store_rows(table_out, KNOT_ROWS, blocks)


def scatter_end(place_ref, scalars, knot_acc, star_acc, table_out, star_out):
    lane = lax.broadcasted_iota(jnp.int32, (8, 128), 1)
    row = lax.broadcasted_iota(jnp.int32, (8, 128), 0)
    wide_lane = lax.broadcasted_iota(jnp.int32, (8, COARSE), 1)
    wide_row = lax.broadcasted_iota(jnp.int32, (8, COARSE), 0)
    edges = jnp.zeros((8, 128), F32)
    for comp in range(4):
        begin, past = comp * FINE, KNOT_ROWS + comp // 2 * 8
        main = knot_acc[begin : begin + FINE] + knot_acc[KNOT_HALF + begin : KNOT_HALF + begin + FINE]
        beyond = knot_acc[past : past + 8] + knot_acc[KNOT_HALF + past : KNOT_HALF + past + 8]
        if comp % 2:
            beyond = pltpu.roll(beyond, 4, 0)
        moved = pltpu.roll(jnp.where(wide_row < 3, beyond, 0.0), 1, 1)
        top = main[:8] + jnp.where(wide_lane > 0, moved, 0.0)
        store_rows(table_out, begin, top)
        store_rows(table_out, begin + 8, main[8:])
        tail, head = moved[:, :128], top[:, :128]
        if comp:
            tail = pltpu.roll(tail, 2 * comp, 1)
        head = pltpu.roll(head, 2 * comp + 1, 1)
        edges = jnp.where((lane == 2 * comp) & (row < 3), tail, edges)
        edges = jnp.where((lane == 2 * comp + 1) & (row < 3), head, edges)
    edges = with_scalars(pltpu.roll(edges, SLOT * place_ref[0], 1), scalars)
    star_out[:STAR_ROWS] = star_acc[:STAR_ROWS] + star_acc[STAR_ROWS:]
    star_out[STAR_ROWS:] = jnp.concatenate([edges, jnp.zeros_like(edges)], axis=1)


def first_kernel(live_ref, place_ref, *refs):
    sources, (table_out, star_out, knot_acc, star_acc) = refs[:8], refs[8:12]
    buffers, sems = refs[12:20], refs[20]
    half = sources[0].shape[0] // 2
    copies = []

    def begin(source, target, *place):
        source, target = (source.at[place], target.at[place]) if place else (source, target)
        copies.append(pltpu.make_async_copy(source, target, sems.at[len(copies)]))
        copies[-1].start()

    for source, target in zip(sources[:3], buffers):
        begin(source, target)
    for rows in (slice(0, half), slice(half, 2 * half)):
        for source, target in zip(sources[3:], buffers[3:]):
            begin(source, target, *[slice(None)] * (len(source.shape) - 2), rows)
    value_ref, cal_coef_ref, tile_cal_ref, knot_ref, frac_ref, *observed = buffers
    knot_acc[...] = jnp.zeros_like(knot_acc)
    star_acc[...] = jnp.zeros_like(star_acc)
    for copy in copies[:3]:
        copy.wait()
    values = value_ref[...] * live_mask(live_ref, 0, value_ref.shape)
    scatter_calibration(values * cal_coef_ref[...], tile_cal_ref, table_out)
    for copy in copies[3:8]:
        copy.wait()

    @pl.loop(0, value_ref.shape[0] // WIDE_GROUP)
    def _(group):
        @pl.when(group * WIDE_GROUP == half)
        def _():
            for copy in copies[8:]:
                copy.wait()

        first = pl.multiple_of(group * WIDE_GROUP, WIDE_GROUP)
        values = value_ref[pl.ds(first, WIDE_GROUP), :]
        values = values * live_mask(live_ref, first, values.shape)
        scatter(first, knot_factors(first, WIDE_GROUP, knot_ref, frac_ref), values, observed, knot_acc, star_acc)

    scatter_end(place_ref, [], knot_acc, star_acc, table_out, star_out)


def sum_kernel(block_ref, own_ref, other_ref, out_ref, star_out):
    total = block_ref[0]
    for device in range(1, block_ref.shape[0]):
        total = total + block_ref[device]
    star = own_ref[...] + other_ref[...]
    star_out[...] = star[:STAR_ROWS]
    total = jnp.concatenate([total[:, :128], total[:, 128:], star[STAR_ROWS:, :128]], axis=0)
    for device in range(block_ref.shape[0]):
        out_ref[device] = total


def picked(array, which):
    row = lax.broadcasted_iota(jnp.int32, array.shape, 0)
    lane = lax.broadcasted_iota(jnp.int32, array.shape, 1)
    chosen = (row == 0) & (lane == SCALAR_LANE + which)
    return jnp.sum(jnp.where(chosen, array, 0.0), keepdims=True)


def with_scalars(array, scalars):
    row = lax.broadcasted_iota(jnp.int32, array.shape, 0)
    lane = lax.broadcasted_iota(jnp.int32, array.shape, 1)
    for which, value in scalars:
        array = jnp.where((row == 0) & (lane == SCALAR_LANE + which), value, array)
    return array


def first_step(edges):
    return picked(edges, 0), picked(edges, 1)


def star_forward_kernel(star_ref, star_coef_ref, star_x_ref, image_ref, star_parts_ref):
    star_x = star_x_ref[...]
    star_high, star_low = two_parts(star_x)
    star_parts_ref[:STAR_ROWS] = star_high
    star_parts_ref[STAR_ROWS:] = star_low

    @pl.loop(0, star_ref.shape[0] // GROUP)
    def _(group):
        rows = pl.ds(pl.multiple_of(group * GROUP, GROUP), GROUP)
        star = star_ref[rows, :]
        coarse, fine = star & (COARSE - 1), star >> 8
        coef = [star_coef_ref[comp, rows, :] for comp in range(5)]
        tiles = [slice(tile, tile + 1) for tile in range(GROUP)]
        hot = jnp.concatenate([one_hot(coarse[here], COARSE) for here in tiles], axis=1)
        found = product(star_parts_ref[...], hot, ((1,), (0,)))
        width = star.shape[1]
        fine_rows, _ = rows_and_columns((FINE, width))
        image_rows = []
        for tile, here in enumerate(tiles):
            across = slice(tile * width, (tile + 1) * width)

            def part(comp):
                begin = comp * FINE
                return (
                    found[begin : begin + FINE, across]
                    + found[STAR_ROWS + begin : STAR_ROWS + begin + FINE, across]
                )

            both = sum(coef[comp][here] * part(comp) for comp in range(5))
            both = jnp.where(fine_rows == fine[here], both, 0.0)
            both = both[:8] + both[8:16] + both[16:24] + both[24:]
            image_rows.append(jnp.sum(both, axis=0, keepdims=True))
        image_ref[rows, :] = jnp.concatenate(image_rows, axis=0)


def received_table(n_stars, n_seg, place_ref, block_ref):
    segment = place_ref[0]
    lane = lax.broadcasted_iota(jnp.int32, (8, 128), 1)
    row = lax.broadcasted_iota(jnp.int32, (8, 128), 0)
    edges = block_ref[0, -8:, :]
    for block in range(1, n_stars):
        edges = edges + block_ref[block, -8:, :]

    def slot(which):
        return pltpu.roll(edges, (128 - SLOT * jnp.clip(which, 0, n_seg - 1)) & 127, 1)

    before, own, after = slot(segment - 1), slot(segment), slot(segment + 1)
    before = jnp.where(segment > 0, before, 0.0)
    ahead = jnp.where(lane % 2 == 0, own, 0.0) + pltpu.roll(jnp.where(lane % 2 == 1, after, 0.0), 127, 1)
    ahead = jnp.where((segment < n_seg - 1) & (lane < 8) & (row < 3), ahead, 0.0)

    size = TABLE_ROWS // n_stars
    table = jnp.concatenate([block_ref[:, :size, :], block_ref[:, size : 2 * size, :]], axis=2)
    table = table.reshape(TABLE_ROWS, COARSE)
    pieces = []
    for comp in range(4):
        shifted = pltpu.roll(before, 128 - 2 * comp, 1) if comp else before
        shifted = jnp.where((lane == 0) & (row < 3), shifted, 0.0)
        top = table[comp * FINE : comp * FINE + 8]
        pieces.append(top + jnp.concatenate([shifted, jnp.zeros_like(shifted)], axis=1))
        pieces.append(table[comp * FINE + 8 : (comp + 1) * FINE])
    return jnp.concatenate(pieces + [table[KNOT_ROWS:]], axis=0), ahead, edges


def gather_ready(table, ahead, cal_coef_ref, tile_cal_ref, star_image_ref, knot_parts_ref, cal_ref):
    wide_lane = lax.broadcasted_iota(jnp.int32, (8, COARSE), 1)
    row = lax.broadcasted_iota(jnp.int32, (8, COARSE), 0)
    beyond = []
    for comp in range(4):
        moved = pltpu.roll(table[comp * FINE : comp * FINE + 8], COARSE - 1, 1)
        last = pltpu.roll(ahead, 127 - 2 * comp, 1)
        moved = jnp.where(wide_lane == COARSE - 1, jnp.concatenate([last, last], axis=1), moved)
        beyond.append(pltpu.roll(moved, 4, 0) if comp % 2 else moved)
    beyond = [jnp.where(row < 4, beyond[0], beyond[1]), jnp.where(row < 4, beyond[2], beyond[3])]
    knot_high, knot_low = two_parts(jnp.concatenate([table[:KNOT_ROWS]] + beyond, axis=0))
    knot_parts_ref[:KNOT_HALF] = knot_high
    knot_parts_ref[KNOT_HALF:] = knot_low

    blocks = jnp.concatenate([table[KNOT_ROWS:, :128], table[KNOT_ROWS:, 128:]], axis=0)
    rows = product(
        one_hot(tile_cal_ref[...], CALB_DEV), jnp.concatenate(two_parts(blocks), axis=1), ((0,), (0,))
    )
    cal_ref[...] = (rows[:, :128] + rows[:, 128:]) * cal_coef_ref[...] + star_image_ref[...]


def gather(first, live_ref, factors, att_coef_ref, knot_parts_ref, cal_ref):
    hot, columns = factors
    rows = pl.ds(first, len(columns))
    coef = [att_coef_ref[comp, rows, :] for comp in range(4)]
    found = product(knot_parts_ref[...], hot, ((1,), (0,)))
    width = cal_ref.shape[1]
    image_rows = []
    for tile in range(len(columns)):
        here = slice(tile, tile + 1)
        across = slice(tile * width, (tile + 1) * width)

        def part(begin, size):
            return (
                found[begin : begin + size, across]
                + found[KNOT_HALF + begin : KNOT_HALF + begin + size, across]
            )

        near, past = columns[tile]
        near = near * sum(coef[comp][here] * part(comp * FINE, FINE) for comp in range(4))
        past = past * past_terms(coef, here) * part(KNOT_ROWS, PAST_ROWS)
        both = near[:8] + near[8:16] + near[16:24] + near[24:] + past[:8] + past[8:]
        image_rows.append(jnp.sum(both, axis=0, keepdims=True))
    image = jnp.concatenate(image_rows, axis=0) + cal_ref[rows, :]
    return image * live_mask(live_ref, first, image.shape)


def squares(array):
    return jnp.sum(array * array, keepdims=True)


def middle_kernel(
    n_stars, n_seg, live_ref, place_ref, knot_ref, frac_ref, att_coef_ref, star_ref, star_coef_ref,
    cal_coef_ref, tile_cal_ref, star_image_ref, star_x_ref, block_ref, image_ref, table_out, scatter_out,
    star_out, knot_parts_ref, cal_ref, knot_acc, star_acc,
):
    table, ahead, _ = received_table(n_stars, n_seg, place_ref, block_ref)
    table_out[...] = table
    norm = squares(star_x_ref[...]) / n_seg + squares(table) / n_stars
    gather_ready(table, ahead, cal_coef_ref, tile_cal_ref, star_image_ref, knot_parts_ref, cal_ref)
    knot_acc[...] = jnp.zeros_like(knot_acc)
    star_acc[...] = jnp.zeros_like(star_acc)
    factors = knot_factors(0, knot_ref.shape[0], knot_ref, frac_ref)
    image = gather(0, live_ref, factors, att_coef_ref, knot_parts_ref, cal_ref)
    image_ref[...] = image
    scatter(0, factors, image, (att_coef_ref, star_ref, star_coef_ref), knot_acc, star_acc)
    scatter_calibration(image * cal_coef_ref[...], tile_cal_ref, scatter_out)
    scalars = [(0, norm), (1, squares(image))]
    scatter_end(place_ref, scalars, knot_acc, star_acc, scatter_out, star_out)


def last_kernel(
    n_stars, n_seg, live_ref, place_ref, knot_ref, frac_ref, att_coef_ref, cal_coef_ref, tile_cal_ref,
    star_image_ref, star_x_ref, block_ref, star_0_ref, table_0_ref, image_0_ref, image_ref, table_out,
    scalar_out, own_scalar_out, knot_parts_ref, cal_ref,
):
    table, ahead, edges = received_table(n_stars, n_seg, place_ref, block_ref)
    table_out[...] = table
    norm_0, square_0 = first_step(edges)
    step = norm_0 / square_0
    norm = (
        squares(star_0_ref[...] - step * star_x_ref[...]) / n_seg
        + squares(table_0_ref[...] - step * table) / n_stars
    )
    gather_ready(table, ahead, cal_coef_ref, tile_cal_ref, star_image_ref, knot_parts_ref, cal_ref)

    factors = knot_factors(0, knot_ref.shape[0], knot_ref, frac_ref)
    image_0 = image_0_ref[...]
    image = gather(0, live_ref, factors, att_coef_ref, knot_parts_ref, cal_ref)
    image = image_0 - step * image
    image_ref[...] = image
    cross = jnp.sum(image * image_0, keepdims=True)
    scalars = [norm, squares(image), cross, norm_0, square_0]
    scalars = with_scalars(jnp.zeros((8, 128), F32), list(enumerate(scalars)))
    own_scalar_out[...] = scalars
    for device in range(scalar_out.shape[0]):
        scalar_out[device] = scalars[:1]


def output_kernel(
    live_ref, own_scalar_ref, scalar_ref, star_0_ref, star_h_ref, att_0_ref, att_h_ref, table_0_ref,
    table_h_ref, value_ref, image_0_ref, image_1_ref, star_out, att_out, cal_out, residual_out,
):
    norm_0, square_0 = [picked(own_scalar_ref[...], which) for which in (3, 4)]
    everyone = scalar_ref[0]
    for device in range(1, scalar_ref.shape[0]):
        everyone = everyone + scalar_ref[device]
    norm_1, square_1, cross = [picked(everyone, which) for which in range(3)]
    step_0 = norm_0 / square_0
    ratio = norm_1 / norm_0
    step_1 = norm_1 / (square_1 + 2.0 * ratio * cross + ratio * ratio * square_0)
    scale = step_0 + step_1 * ratio

    def combined(old, change):
        return scale * old + step_1 * (old - step_0 * change)

    star_out[...] = combined(star_0_ref[...], star_h_ref[...])
    att_out[...] = combined(att_0_ref[...], att_h_ref[...])
    cal = combined(table_0_ref[KNOT_ROWS:, :], table_h_ref[KNOT_ROWS:, :])
    cal_out[...] = jnp.concatenate([cal[:, :128], cal[:, 128:]], axis=0)
    values = value_ref[...] * live_mask(live_ref, 0, value_ref.shape)
    residual_out[...] = values - scale * image_0_ref[...] - step_1 * image_1_ref[...]


def in_vmem(count):
    return [pl.BlockSpec(memory_space=pltpu.VMEM)] * count


def in_smem(count):
    return [pl.BlockSpec(memory_space=pltpu.SMEM)] * count


def in_hbm(count):
    return [pl.BlockSpec(memory_space=pltpu.HBM)] * count


def shaped(*shape):
    return jax.ShapeDtypeStruct(shape, F32)


ARRIVE_PARAMS = pltpu.CompilerParams(vmem_limit_bytes=60 * 1024 * 1024)
PARAMS = pltpu.CompilerParams(vmem_limit_bytes=40 * 1024 * 1024)
PASS_COST = pl.CostEstimate(flops=3_000_000_000, bytes_accessed=1_000_000, transcendentals=0)
SMALL_COST = pl.CostEstimate(flops=1_000_000, bytes_accessed=600_000, transcendentals=0)


def on_device(
    obs_star, obs_knot, obs_frac, star_coef, att_coef, cal_coef, tile_cal, live_tiles, obs_value
):
    n_stars, n_seg = lax.axis_size("stars"), lax.axis_size("seg")
    tile_count, width = obs_star.shape
    tile_row = tile_cal[None, :]
    place = lax.axis_index("seg").astype(jnp.int32)[None]
    image_shape = shaped(tile_count, width)
    table_shape = shaped(TABLE_ROWS, COARSE)
    star_shape = shaped(STAR_ROWS, COARSE)
    sent_shapes = (shaped(n_stars, TABLE_ROWS // n_stars, COARSE), shaped(STAR_ROWS + 8, COARSE))
    sums = [pltpu.VMEM((2 * KNOT_HALF, COARSE), F32), pltpu.VMEM((2 * STAR_ROWS, COARSE), F32)]
    ready = [pltpu.VMEM((2 * KNOT_HALF, COARSE), BF16), pltpu.VMEM((tile_count, width), F32)]

    def first_scatter():
        observed = (obs_value, cal_coef, tile_row, obs_knot, obs_frac, att_coef, obs_star, star_coef)
        buffers = [pltpu.VMEM(array.shape, array.dtype) for array in observed]
        return pl.pallas_call(
            first_kernel,
            out_shape=sent_shapes,
            in_specs=in_smem(2) + in_hbm(len(observed)),
            out_specs=tuple(in_vmem(2)),
            scratch_shapes=sums + buffers + [pltpu.SemaphoreType.DMA((13,))],
            compiler_params=ARRIVE_PARAMS,
            cost_estimate=PASS_COST,
            name="first_scatter",
        )(live_tiles, place, *observed)

    def middle(*received):
        observed = (obs_knot, obs_frac, att_coef, obs_star, star_coef, cal_coef, tile_row)
        return pl.pallas_call(
            functools.partial(middle_kernel, n_stars, n_seg),
            out_shape=(image_shape, table_shape, *sent_shapes),
            in_specs=in_smem(2) + in_vmem(len(observed) + len(received)),
            out_specs=tuple(in_vmem(4)),
            scratch_shapes=ready + sums,
            compiler_params=PARAMS,
            cost_estimate=PASS_COST,
            name="gather_and_scatter",
        )(live_tiles, place, *observed, *received)

    def last_gather(*received):
        observed = (obs_knot, obs_frac, att_coef, cal_coef, tile_row)
        return pl.pallas_call(
            functools.partial(last_kernel, n_stars, n_seg),
            out_shape=(image_shape, table_shape, shaped(n_stars * n_seg, 1, 128), shaped(8, 128)),
            in_specs=in_smem(2) + in_vmem(len(observed) + len(received)),
            out_specs=tuple(in_vmem(4)),
            scratch_shapes=ready,
            compiler_params=PARAMS,
            cost_estimate=PASS_COST,
            name="last_gather",
        )(live_tiles, place, *observed, *received)

    def star_forward(star):
        return pl.pallas_call(
            star_forward_kernel,
            out_shape=image_shape,
            in_specs=in_vmem(3),
            out_specs=in_vmem(1)[0],
            scratch_shapes=[pltpu.VMEM((2 * STAR_ROWS, COARSE), BF16)],
            compiler_params=PARAMS,
            cost_estimate=PASS_COST,
            name="star_forward",
        )(obs_star, star_coef, star)

    def swap(blocks, groups=None):
        return lax.all_to_all(blocks, ("stars", "seg"), 0, 0, axis_index_groups=groups)

    def star_groups():
        forward = list(range(n_stars))
        turned = forward[n_stars // 2 :] + forward[: n_stars // 2]
        orders = (forward, forward[::-1], turned, turned[::-1])
        return [[star * n_seg + seg for star in orders[seg % 4]] for seg in range(n_seg)]

    def partner(array, axis, distance):
        return lax.ppermute(array, axis, [(i, i ^ distance) for i in range(lax.axis_size(axis))])

    def reduced(table, star):
        distances = [1 << bit for bit in range(n_seg.bit_length() - 1)]
        for distance in distances[:-1]:
            star = star + partner(star, "seg", distance)
        blocks, star = pl.pallas_call(
            sum_kernel,
            out_shape=(shaped(n_stars, 2 * TABLE_ROWS // n_stars + 8, 128), star_shape),
            in_specs=in_vmem(3),
            out_specs=tuple(in_vmem(2)),
            compiler_params=PARAMS,
            cost_estimate=SMALL_COST,
            name="table_sum",
        )(swap(table, star_groups()), star, partner(star, "seg", distances[-1]))
        return star_forward(star), star, swap(blocks, star_groups())

    first = reduced(*first_scatter())
    star_0 = first[1]
    image_0, table_0, *sent = middle(*first)
    second = reduced(*sent)
    star_h = second[1]
    image_1, table_h, scalars, own_scalars = last_gather(*second, star_0, table_0, image_0)

    def star_order(star):
        return star.reshape(5, STAR_DEV)

    def att_order(table):
        att = table[:KNOT_ROWS].reshape(4, FINE, COARSE)
        return att.transpose(0, 2, 1).reshape(4, KNOT_DEV)

    return pl.pallas_call(
        output_kernel,
        out_shape=(shaped(5, STAR_DEV), shaped(4, KNOT_DEV), shaped(CALB_DEV, width), image_shape),
        in_specs=in_smem(1) + in_vmem(11),
        out_specs=tuple(in_vmem(4)),
        compiler_params=PARAMS,
        cost_estimate=SMALL_COST,
        name="outputs",
    )(
        live_tiles, own_scalars, swap(scalars), star_order(star_0), star_order(star_h),
        att_order(table_0), att_order(table_h), table_0, table_h, obs_value, image_0, image_1,
    )


def solution(mesh):
    placed = (
        P(("stars", "seg"), None),
        P(("stars", "seg"), None),
        P(("stars", "seg"), None),
        P(None, ("stars", "seg"), None),
        P(None, ("stars", "seg"), None),
        P(("stars", "seg"), None),
        P(("stars", "seg")),
        P(("stars", "seg")),
        P(("stars", "seg"), None),
    )
    return jax.shard_map(
        on_device,
        mesh=mesh,
        in_specs=placed,
        out_specs=(P(None, "stars"), P(None, "seg"), P("seg", None), P(("stars", "seg"), None)),
        check_vma=False,
    )
```

```python
import functools

import jax
import jax.numpy as jnp
from jax import lax
from jax.experimental import pallas as pl
from jax.experimental.pallas import tpu as pltpu
from jax.sharding import PartitionSpec as P

STAR_DEV = 8192
KNOT_DEV = 8192
CALB_DEV = 256
FINE = 32
COARSE = 256
GROUP = 16
WIDE_GROUP = 64
SLOT = 8
STAR_ROWS = 5 * FINE
KNOT_ROWS = 4 * FINE
TABLE_ROWS = KNOT_ROWS + CALB_DEV // 2
BF16 = jnp.bfloat16
F32 = jnp.float32
SCALAR_LANE = 64
PAST_ROWS = 16
KNOT_HALF = KNOT_ROWS + PAST_ROWS


def two_parts(values):
    high = values.astype(BF16)
    return high, (values - high.astype(F32)).astype(BF16)


def rows_and_columns(shape):
    return lax.broadcasted_iota(jnp.int32, shape, 0), lax.broadcasted_iota(jnp.int32, shape, 1)


def packed_rows(row, size):
    wide = jnp.broadcast_to(row.astype(F32), (16, row.shape[1])).astype(BF16)
    return jnp.concatenate([wide] * (size // 16), axis=0)


def matches(index_row, size):
    places, _ = rows_and_columns((size, index_row.shape[1]))
    return places.astype(F32).astype(BF16) == packed_rows(index_row, size)


def one_hot(index_row, size):
    return jnp.where(matches(index_row, size), jnp.ones((), BF16), jnp.zeros((), BF16))


def spline_weights(fraction):
    remain = 1.0 - fraction
    square = fraction * fraction
    cubed = square * fraction
    return (
        remain * remain * remain / 6.0,
        (3.0 * cubed - 6.0 * square + 4.0) / 6.0,
        (-3.0 * cubed + 3.0 * square + 3.0 * fraction + 1.0) / 6.0,
        cubed / 6.0,
    )


def weight_columns(weights, fine_row, tile, places):
    behind = places - fine_row
    result = jnp.zeros(behind.shape, F32)
    for offset in range(4):
        result = jnp.where(behind == offset, weights[offset][tile : tile + 1], result)
    return result


def near_and_past(weights, fine, tile):
    width = fine.shape[1]
    fine_row = fine[tile : tile + 1]
    near, _ = rows_and_columns((FINE, width))
    past, _ = rows_and_columns((PAST_ROWS, width))
    past = FINE + (past & 3)
    return weight_columns(weights, fine_row, tile, near), weight_columns(weights, fine_row, tile, past)


def past_terms(terms, here):
    rows, _ = rows_and_columns((PAST_ROWS, terms[0].shape[1]))
    result = jnp.broadcast_to(terms[3][here], rows.shape)
    for comp in range(2, -1, -1):
        result = jnp.where(rows < 4 * (comp + 1), terms[comp][here], result)
    return result


def product(left, right, contract):
    return lax.dot_general(left, right, (contract, ((), ())), preferred_element_type=F32)


def live_mask(live_ref, first, shape):
    rows, _ = rows_and_columns(shape)
    return (rows + first < live_ref[0]).astype(F32)


def store_rows(out_ref, begin, rows):
    size = (out_ref.shape[1] - 8) // 2
    for offset in range(0, rows.shape[0], 8):
        block, place = divmod(begin + offset, size)
        out_ref[block, place : place + 8, :] = rows[offset : offset + 8, :128]
        out_ref[block, size + place : size + place + 8, :] = rows[offset : offset + 8, 128:]


def knot_factors(first, size, knot_ref, frac_ref):
    rows = pl.ds(first, size)
    knot = knot_ref[rows, :]
    coarse, fine = knot >> 5, knot & (FINE - 1)
    weights = spline_weights(frac_ref[rows, :])
    hot = [one_hot(coarse[tile : tile + 1], COARSE) for tile in range(size)]
    columns = [near_and_past(weights, fine, tile) for tile in range(size)]
    return jnp.concatenate(hot, axis=1), columns


def scatter(first, factors, values, observed, knot_acc, star_acc):
    att_coef_ref, star_ref, star_coef_ref = observed
    knot_hot, columns = factors
    rows = pl.ds(first, len(columns))
    star = star_ref[rows, :]
    star_coarse, star_fine = star & (COARSE - 1), star >> 8
    terms = [att_coef_ref[comp, rows, :] * values for comp in range(4)]
    parts = [two_parts(star_coef_ref[comp, rows, :] * values) for comp in range(5)]
    parts = [pair[half].astype(F32) for half in range(2) for pair in parts]
    knot_left, star_left, star_right = [], [], []
    for tile in range(len(columns)):
        here = slice(tile, tile + 1)
        near, past = columns[tile]
        spread = jnp.concatenate(
            [term[here] * near for term in terms] + [past_terms(terms, here) * past], axis=0
        )
        knot_left.append(jnp.concatenate(two_parts(spread), axis=0))
        star_right.append(one_hot(star_coarse[here], COARSE))
        chosen = matches(star_fine[here], FINE)
        star_left.append(
            jnp.concatenate(
                [jnp.where(chosen, packed_rows(part[here], FINE), jnp.zeros((), BF16)) for part in parts],
                axis=0,
            )
        )
    knot_acc[...] += product(
        jnp.concatenate(knot_left, axis=1), knot_hot, ((1,), (1,))
    )
    star_acc[...] += product(
        jnp.concatenate(star_left, axis=1), jnp.concatenate(star_right, axis=1), ((1,), (1,))
    )


def scatter_calibration(values, tile_cal_ref, table_out):
    blocks = product(
        one_hot(tile_cal_ref[...], CALB_DEV), jnp.concatenate(two_parts(values), axis=1), ((1,), (0,))
    )
    width = values.shape[1]
    blocks = blocks[:, :width] + blocks[:, width:]
    blocks = jnp.concatenate([blocks[: CALB_DEV // 2], blocks[CALB_DEV // 2 :]], axis=1)
    store_rows(table_out, KNOT_ROWS, blocks)


def scatter_end(place_ref, scalars, knot_acc, star_acc, table_out, star_out):
    lane = lax.broadcasted_iota(jnp.int32, (8, 128), 1)
    row = lax.broadcasted_iota(jnp.int32, (8, 128), 0)
    wide_lane = lax.broadcasted_iota(jnp.int32, (8, COARSE), 1)
    wide_row = lax.broadcasted_iota(jnp.int32, (8, COARSE), 0)
    edges = jnp.zeros((8, 128), F32)
    for comp in range(4):
        begin, past = comp * FINE, KNOT_ROWS + comp // 2 * 8
        main = knot_acc[begin : begin + FINE] + knot_acc[KNOT_HALF + begin : KNOT_HALF + begin + FINE]
        beyond = knot_acc[past : past + 8] + knot_acc[KNOT_HALF + past : KNOT_HALF + past + 8]
        if comp % 2:
            beyond = pltpu.roll(beyond, 4, 0)
        moved = pltpu.roll(jnp.where(wide_row < 3, beyond, 0.0), 1, 1)
        top = main[:8] + jnp.where(wide_lane > 0, moved, 0.0)
        store_rows(table_out, begin, top)
        store_rows(table_out, begin + 8, main[8:])
        tail, head = moved[:, :128], top[:, :128]
        if comp:
            tail = pltpu.roll(tail, 2 * comp, 1)
        head = pltpu.roll(head, 2 * comp + 1, 1)
        edges = jnp.where((lane == 2 * comp) & (row < 3), tail, edges)
        edges = jnp.where((lane == 2 * comp + 1) & (row < 3), head, edges)
    edges = with_scalars(pltpu.roll(edges, SLOT * place_ref[0], 1), scalars)
    for device in range(table_out.shape[0]):
        table_out[device, -8:, :] = edges
    star_out[...] = star_acc[:STAR_ROWS] + star_acc[STAR_ROWS:]


def first_kernel(live_ref, place_ref, *refs):
    sources, (table_out, star_out, knot_acc, star_acc) = refs[:8], refs[8:12]
    buffers, sems = refs[12:20], refs[20]
    half = sources[0].shape[0] // 2
    copies = []

    def begin(source, target, *place):
        source, target = (source.at[place], target.at[place]) if place else (source, target)
        copies.append(pltpu.make_async_copy(source, target, sems.at[len(copies)]))
        copies[-1].start()

    for source, target in zip(sources[:3], buffers):
        begin(source, target)
    for rows in (slice(0, half), slice(half, 2 * half)):
        for source, target in zip(sources[3:], buffers[3:]):
            begin(source, target, *[slice(None)] * (len(source.shape) - 2), rows)
    value_ref, cal_coef_ref, tile_cal_ref, knot_ref, frac_ref, *observed = buffers
    knot_acc[...] = jnp.zeros_like(knot_acc)
    star_acc[...] = jnp.zeros_like(star_acc)
    for copy in copies[:3]:
        copy.wait()
    values = value_ref[...] * live_mask(live_ref, 0, value_ref.shape)
    scatter_calibration(values * cal_coef_ref[...], tile_cal_ref, table_out)
    for copy in copies[3:8]:
        copy.wait()

    @pl.loop(0, value_ref.shape[0] // WIDE_GROUP)
    def _(group):
        @pl.when(group * WIDE_GROUP == half)
        def _():
            for copy in copies[8:]:
                copy.wait()

        first = pl.multiple_of(group * WIDE_GROUP, WIDE_GROUP)
        values = value_ref[pl.ds(first, WIDE_GROUP), :]
        values = values * live_mask(live_ref, first, values.shape)
        scatter(first, knot_factors(first, WIDE_GROUP, knot_ref, frac_ref), values, observed, knot_acc, star_acc)

    scatter_end(place_ref, [], knot_acc, star_acc, table_out, star_out)


def sum_kernel(block_ref, own_ref, other_ref, out_ref, star_out, edge_out):
    total = block_ref[0]
    for device in range(1, block_ref.shape[0]):
        total = total + block_ref[device]
    star_out[...] = own_ref[...] + other_ref[...]
    for device in range(block_ref.shape[0]):
        out_ref[device] = total[:-8]
    edge_out[...] = total[-8:]


def picked(array, which):
    row = lax.broadcasted_iota(jnp.int32, array.shape, 0)
    lane = lax.broadcasted_iota(jnp.int32, array.shape, 1)
    chosen = (row == 0) & (lane == SCALAR_LANE + which)
    return jnp.sum(jnp.where(chosen, array, 0.0), keepdims=True)


def with_scalars(array, scalars):
    row = lax.broadcasted_iota(jnp.int32, array.shape, 0)
    lane = lax.broadcasted_iota(jnp.int32, array.shape, 1)
    for which, value in scalars:
        array = jnp.where((row == 0) & (lane == SCALAR_LANE + which), value, array)
    return array


def first_step(edges):
    return picked(edges, 0), picked(edges, 1)


def star_forward_kernel(star_ref, star_coef_ref, star_x_ref, image_ref, star_parts_ref):
    star_x = star_x_ref[...]
    star_high, star_low = two_parts(star_x)
    star_parts_ref[:STAR_ROWS] = star_high
    star_parts_ref[STAR_ROWS:] = star_low

    @pl.loop(0, star_ref.shape[0] // GROUP)
    def _(group):
        rows = pl.ds(pl.multiple_of(group * GROUP, GROUP), GROUP)
        star = star_ref[rows, :]
        coarse, fine = star & (COARSE - 1), star >> 8
        coef = [star_coef_ref[comp, rows, :] for comp in range(5)]
        tiles = [slice(tile, tile + 1) for tile in range(GROUP)]
        hot = jnp.concatenate([one_hot(coarse[here], COARSE) for here in tiles], axis=1)
        found = product(star_parts_ref[...], hot, ((1,), (0,)))
        width = star.shape[1]
        fine_rows, _ = rows_and_columns((FINE, width))
        image_rows = []
        for tile, here in enumerate(tiles):
            across = slice(tile * width, (tile + 1) * width)

            def part(comp):
                begin = comp * FINE
                return (
                    found[begin : begin + FINE, across]
                    + found[STAR_ROWS + begin : STAR_ROWS + begin + FINE, across]
                )

            both = sum(coef[comp][here] * part(comp) for comp in range(5))
            both = jnp.where(fine_rows == fine[here], both, 0.0)
            both = both[:8] + both[8:16] + both[16:24] + both[24:]
            image_rows.append(jnp.sum(both, axis=0, keepdims=True))
        image_ref[rows, :] = jnp.concatenate(image_rows, axis=0)


def received_table(n_stars, n_seg, place_ref, block_ref, edges):
    segment = place_ref[0]
    lane = lax.broadcasted_iota(jnp.int32, (8, 128), 1)
    row = lax.broadcasted_iota(jnp.int32, (8, 128), 0)

    def slot(which):
        return pltpu.roll(edges, (128 - SLOT * jnp.clip(which, 0, n_seg - 1)) & 127, 1)

    before, own, after = slot(segment - 1), slot(segment), slot(segment + 1)
    before = jnp.where(segment > 0, before, 0.0)
    ahead = jnp.where(lane % 2 == 0, own, 0.0) + pltpu.roll(jnp.where(lane % 2 == 1, after, 0.0), 127, 1)
    ahead = jnp.where((segment < n_seg - 1) & (lane < 8) & (row < 3), ahead, 0.0)

    size = TABLE_ROWS // n_stars
    table = jnp.concatenate([block_ref[:, :size, :], block_ref[:, size : 2 * size, :]], axis=2)
    table = table.reshape(TABLE_ROWS, COARSE)
    pieces = []
    for comp in range(4):
        shifted = pltpu.roll(before, 128 - 2 * comp, 1) if comp else before
        shifted = jnp.where((lane == 0) & (row < 3), shifted, 0.0)
        top = table[comp * FINE : comp * FINE + 8]
        pieces.append(top + jnp.concatenate([shifted, jnp.zeros_like(shifted)], axis=1))
        pieces.append(table[comp * FINE + 8 : (comp + 1) * FINE])
    return jnp.concatenate(pieces + [table[KNOT_ROWS:]], axis=0), ahead


def gather_ready(table, ahead, cal_coef_ref, tile_cal_ref, star_image_ref, knot_parts_ref, cal_ref):
    wide_lane = lax.broadcasted_iota(jnp.int32, (8, COARSE), 1)
    row = lax.broadcasted_iota(jnp.int32, (8, COARSE), 0)
    beyond = []
    for comp in range(4):
        moved = pltpu.roll(table[comp * FINE : comp * FINE + 8], COARSE - 1, 1)
        last = pltpu.roll(ahead, 127 - 2 * comp, 1)
        moved = jnp.where(wide_lane == COARSE - 1, jnp.concatenate([last, last], axis=1), moved)
        beyond.append(pltpu.roll(moved, 4, 0) if comp % 2 else moved)
    beyond = [jnp.where(row < 4, beyond[0], beyond[1]), jnp.where(row < 4, beyond[2], beyond[3])]
    knot_high, knot_low = two_parts(jnp.concatenate([table[:KNOT_ROWS]] + beyond, axis=0))
    knot_parts_ref[:KNOT_HALF] = knot_high
    knot_parts_ref[KNOT_HALF:] = knot_low

    blocks = jnp.concatenate([table[KNOT_ROWS:, :128], table[KNOT_ROWS:, 128:]], axis=0)
    rows = product(
        one_hot(tile_cal_ref[...], CALB_DEV), jnp.concatenate(two_parts(blocks), axis=1), ((0,), (0,))
    )
    cal_ref[...] = (rows[:, :128] + rows[:, 128:]) * cal_coef_ref[...] + star_image_ref[...]


def gather(first, live_ref, factors, att_coef_ref, knot_parts_ref, cal_ref):
    hot, columns = factors
    rows = pl.ds(first, len(columns))
    coef = [att_coef_ref[comp, rows, :] for comp in range(4)]
    found = product(knot_parts_ref[...], hot, ((1,), (0,)))
    width = cal_ref.shape[1]
    image_rows = []
    for tile in range(len(columns)):
        here = slice(tile, tile + 1)
        across = slice(tile * width, (tile + 1) * width)

        def part(begin, size):
            return (
                found[begin : begin + size, across]
                + found[KNOT_HALF + begin : KNOT_HALF + begin + size, across]
            )

        near, past = columns[tile]
        near = near * sum(coef[comp][here] * part(comp * FINE, FINE) for comp in range(4))
        past = past * past_terms(coef, here) * part(KNOT_ROWS, PAST_ROWS)
        both = near[:8] + near[8:16] + near[16:24] + near[24:] + past[:8] + past[8:]
        image_rows.append(jnp.sum(both, axis=0, keepdims=True))
    image = jnp.concatenate(image_rows, axis=0) + cal_ref[rows, :]
    return image * live_mask(live_ref, first, image.shape)


def squares(array):
    return jnp.sum(array * array, keepdims=True)


def middle_kernel(
    n_stars, n_seg, live_ref, place_ref, knot_ref, frac_ref, att_coef_ref, star_ref, star_coef_ref,
    cal_coef_ref, tile_cal_ref, star_image_ref, star_x_ref, block_ref, edge_ref, other_edge_ref, image_ref, table_out, scatter_out,
    star_out, knot_parts_ref, cal_ref, knot_acc, star_acc,
):
    edges = edge_ref[...] + other_edge_ref[...]
    table, ahead = received_table(n_stars, n_seg, place_ref, block_ref, edges)
    table_out[...] = table
    norm = squares(star_x_ref[...]) / n_seg + squares(table) / n_stars
    gather_ready(table, ahead, cal_coef_ref, tile_cal_ref, star_image_ref, knot_parts_ref, cal_ref)
    knot_acc[...] = jnp.zeros_like(knot_acc)
    star_acc[...] = jnp.zeros_like(star_acc)
    factors = knot_factors(0, knot_ref.shape[0], knot_ref, frac_ref)
    image = gather(0, live_ref, factors, att_coef_ref, knot_parts_ref, cal_ref)
    image_ref[...] = image
    scatter(0, factors, image, (att_coef_ref, star_ref, star_coef_ref), knot_acc, star_acc)
    scatter_calibration(image * cal_coef_ref[...], tile_cal_ref, scatter_out)
    scalars = [(0, norm), (1, squares(image))]
    scatter_end(place_ref, scalars, knot_acc, star_acc, scatter_out, star_out)


def last_kernel(
    n_stars, n_seg, live_ref, place_ref, knot_ref, frac_ref, att_coef_ref, cal_coef_ref, tile_cal_ref,
    star_image_ref, star_x_ref, block_ref, edge_ref, other_edge_ref, star_0_ref, table_0_ref, image_0_ref, image_ref, table_out,
    scalar_out, own_scalar_out, knot_parts_ref, cal_ref,
):
    edges = edge_ref[...] + other_edge_ref[...]
    table, ahead = received_table(n_stars, n_seg, place_ref, block_ref, edges)
    table_out[...] = table
    norm_0, square_0 = first_step(edges)
    step = norm_0 / square_0
    norm = (
        squares(star_0_ref[...] - step * star_x_ref[...]) / n_seg
        + squares(table_0_ref[...] - step * table) / n_stars
    )
    gather_ready(table, ahead, cal_coef_ref, tile_cal_ref, star_image_ref, knot_parts_ref, cal_ref)

    factors = knot_factors(0, knot_ref.shape[0], knot_ref, frac_ref)
    image_0 = image_0_ref[...]
    image = gather(0, live_ref, factors, att_coef_ref, knot_parts_ref, cal_ref)
    image = image_0 - step * image
    image_ref[...] = image
    cross = jnp.sum(image * image_0, keepdims=True)
    scalars = [norm, squares(image), cross, norm_0, square_0]
    scalars = with_scalars(jnp.zeros((8, 128), F32), list(enumerate(scalars)))
    own_scalar_out[...] = scalars
    for device in range(scalar_out.shape[0]):
        scalar_out[device] = scalars[:1]


def output_kernel(
    live_ref, own_scalar_ref, scalar_ref, star_0_ref, star_h_ref, att_0_ref, att_h_ref, table_0_ref,
    table_h_ref, value_ref, image_0_ref, image_1_ref, star_out, att_out, cal_out, residual_out,
):
    norm_0, square_0 = [picked(own_scalar_ref[...], which) for which in (3, 4)]
    everyone = scalar_ref[0]
    for device in range(1, scalar_ref.shape[0]):
        everyone = everyone + scalar_ref[device]
    norm_1, square_1, cross = [picked(everyone, which) for which in range(3)]
    step_0 = norm_0 / square_0
    ratio = norm_1 / norm_0
    step_1 = norm_1 / (square_1 + 2.0 * ratio * cross + ratio * ratio * square_0)
    scale = step_0 + step_1 * ratio

    def combined(old, change):
        return scale * old + step_1 * (old - step_0 * change)

    star_out[...] = combined(star_0_ref[...], star_h_ref[...])
    att_out[...] = combined(att_0_ref[...], att_h_ref[...])
    cal = combined(table_0_ref[KNOT_ROWS:, :], table_h_ref[KNOT_ROWS:, :])
    cal_out[...] = jnp.concatenate([cal[:, :128], cal[:, 128:]], axis=0)
    values = value_ref[...] * live_mask(live_ref, 0, value_ref.shape)
    residual_out[...] = values - scale * image_0_ref[...] - step_1 * image_1_ref[...]


def in_vmem(count):
    return [pl.BlockSpec(memory_space=pltpu.VMEM)] * count


def in_smem(count):
    return [pl.BlockSpec(memory_space=pltpu.SMEM)] * count


def in_hbm(count):
    return [pl.BlockSpec(memory_space=pltpu.HBM)] * count


def shaped(*shape):
    return jax.ShapeDtypeStruct(shape, F32)


ARRIVE_PARAMS = pltpu.CompilerParams(vmem_limit_bytes=60 * 1024 * 1024)
PARAMS = pltpu.CompilerParams(vmem_limit_bytes=40 * 1024 * 1024)
PASS_COST = pl.CostEstimate(flops=3_000_000_000, bytes_accessed=1_000_000, transcendentals=0)
SMALL_COST = pl.CostEstimate(flops=1_000_000, bytes_accessed=600_000, transcendentals=0)


def on_device(
    obs_star, obs_knot, obs_frac, star_coef, att_coef, cal_coef, tile_cal, live_tiles, obs_value
):
    n_stars, n_seg = lax.axis_size("stars"), lax.axis_size("seg")
    tile_count, width = obs_star.shape
    tile_row = tile_cal[None, :]
    place = lax.axis_index("seg").astype(jnp.int32)[None]
    image_shape = shaped(tile_count, width)
    table_shape = shaped(TABLE_ROWS, COARSE)
    star_shape = shaped(STAR_ROWS, COARSE)
    sent_shapes = (shaped(n_stars, 2 * TABLE_ROWS // n_stars + 8, 128), star_shape)
    sums = [pltpu.VMEM((2 * KNOT_HALF, COARSE), F32), pltpu.VMEM((2 * STAR_ROWS, COARSE), F32)]
    ready = [pltpu.VMEM((2 * KNOT_HALF, COARSE), BF16), pltpu.VMEM((tile_count, width), F32)]

    def first_scatter():
        observed = (obs_value, cal_coef, tile_row, obs_knot, obs_frac, att_coef, obs_star, star_coef)
        buffers = [pltpu.VMEM(array.shape, array.dtype) for array in observed]
        return pl.pallas_call(
            first_kernel,
            out_shape=sent_shapes,
            in_specs=in_smem(2) + in_hbm(len(observed)),
            out_specs=tuple(in_vmem(2)),
            scratch_shapes=sums + buffers + [pltpu.SemaphoreType.DMA((13,))],
            compiler_params=ARRIVE_PARAMS,
            cost_estimate=PASS_COST,
            name="first_scatter",
        )(live_tiles, place, *observed)

    def middle(*received):
        observed = (obs_knot, obs_frac, att_coef, obs_star, star_coef, cal_coef, tile_row)
        return pl.pallas_call(
            functools.partial(middle_kernel, n_stars, n_seg),
            out_shape=(image_shape, table_shape, *sent_shapes),
            in_specs=in_smem(2) + in_vmem(len(observed) + len(received)),
            out_specs=tuple(in_vmem(4)),
            scratch_shapes=ready + sums,
            compiler_params=PARAMS,
            cost_estimate=PASS_COST,
            name="gather_and_scatter",
        )(live_tiles, place, *observed, *received)

    def last_gather(*received):
        observed = (obs_knot, obs_frac, att_coef, cal_coef, tile_row)
        return pl.pallas_call(
            functools.partial(last_kernel, n_stars, n_seg),
            out_shape=(image_shape, table_shape, shaped(n_stars * n_seg, 1, 128), shaped(8, 128)),
            in_specs=in_smem(2) + in_vmem(len(observed) + len(received)),
            out_specs=tuple(in_vmem(4)),
            scratch_shapes=ready,
            compiler_params=PARAMS,
            cost_estimate=PASS_COST,
            name="last_gather",
        )(live_tiles, place, *observed, *received)

    def star_forward(star):
        return pl.pallas_call(
            star_forward_kernel,
            out_shape=image_shape,
            in_specs=in_vmem(3),
            out_specs=in_vmem(1)[0],
            scratch_shapes=[pltpu.VMEM((2 * STAR_ROWS, COARSE), BF16)],
            compiler_params=PARAMS,
            cost_estimate=PASS_COST,
            name="star_forward",
        )(obs_star, star_coef, star)

    def swap(blocks, groups=None):
        return lax.all_to_all(blocks, ("stars", "seg"), 0, 0, axis_index_groups=groups)

    def star_groups():
        forward = list(range(n_stars))
        turned = forward[n_stars // 2 :] + forward[: n_stars // 2]
        orders = (forward, forward[::-1], turned, turned[::-1])
        return [[star * n_seg + seg for star in orders[seg % 4]] for seg in range(n_seg)]

    def partner(array, axis, distance):
        return lax.ppermute(array, axis, [(i, i ^ distance) for i in range(lax.axis_size(axis))])

    def reduced(table, star):
        distances = [1 << bit for bit in range(n_seg.bit_length() - 1)]
        for distance in distances[:-1]:
            star = star + partner(star, "seg", distance)
        blocks, star, edge = pl.pallas_call(
            sum_kernel,
            out_shape=(shaped(n_stars, 2 * TABLE_ROWS // n_stars, 128), star_shape, shaped(8, 128)),
            in_specs=in_vmem(3),
            out_specs=tuple(in_vmem(3)),
            compiler_params=PARAMS,
            cost_estimate=SMALL_COST,
            name="table_sum",
        )(swap(table, star_groups()), star, partner(star, "seg", distances[-1]))
        for distance in distances[:-1]:
            edge = edge + partner(edge, "seg", distance)
        gathered = swap(blocks, star_groups())
        return star_forward(star), star, gathered, edge, partner(edge, "seg", distances[-1])

    first = reduced(*first_scatter())
    star_0 = first[1]
    image_0, table_0, *sent = middle(*first)
    second = reduced(*sent)
    star_h = second[1]
    image_1, table_h, scalars, own_scalars = last_gather(*second, star_0, table_0, image_0)

    def star_order(star):
        return star.reshape(5, STAR_DEV)

    def att_order(table):
        att = table[:KNOT_ROWS].reshape(4, FINE, COARSE)
        return att.transpose(0, 2, 1).reshape(4, KNOT_DEV)

    return pl.pallas_call(
        output_kernel,
        out_shape=(shaped(5, STAR_DEV), shaped(4, KNOT_DEV), shaped(CALB_DEV, width), image_shape),
        in_specs=in_smem(1) + in_vmem(11),
        out_specs=tuple(in_vmem(4)),
        compiler_params=PARAMS,
        cost_estimate=SMALL_COST,
        name="outputs",
    )(
        live_tiles, own_scalars, swap(scalars), star_order(star_0), star_order(star_h),
        att_order(table_0), att_order(table_h), table_0, table_h, obs_value, image_0, image_1,
    )


def solution(mesh):
    placed = (
        P(("stars", "seg"), None),
        P(("stars", "seg"), None),
        P(("stars", "seg"), None),
        P(None, ("stars", "seg"), None),
        P(None, ("stars", "seg"), None),
        P(("stars", "seg"), None),
        P(("stars", "seg")),
        P(("stars", "seg")),
        P(("stars", "seg"), None),
    )
    return jax.shard_map(
        on_device,
        mesh=mesh,
        in_specs=placed,
        out_specs=(P(None, "stars"), P(None, "seg"), P("seg", None), P(("stars", "seg"), None)),
        check_vma=False,
    )
```

```python
import functools

import jax
import jax.numpy as jnp
from jax import lax
from jax.experimental import pallas as pl
from jax.experimental.pallas import tpu as pltpu
from jax.sharding import PartitionSpec as P

STAR_DEV = 8192
KNOT_DEV = 8192
CALB_DEV = 256
FINE = 32
COARSE = 256
GROUP = 64
WIDE_GROUP = 64
SLOT = 8
STAR_ROWS = 5 * FINE
KNOT_ROWS = 4 * FINE
TABLE_ROWS = KNOT_ROWS + CALB_DEV // 2
BF16 = jnp.bfloat16
F32 = jnp.float32
SCALAR_LANE = 64
PAST_ROWS = 16
KNOT_HALF = KNOT_ROWS + PAST_ROWS


def two_parts(values):
    high = values.astype(BF16)
    return high, (values - high.astype(F32)).astype(BF16)


def rows_and_columns(shape):
    return lax.broadcasted_iota(jnp.int32, shape, 0), lax.broadcasted_iota(jnp.int32, shape, 1)


def packed_rows(row, size):
    wide = jnp.broadcast_to(row.astype(F32), (16, row.shape[1])).astype(BF16)
    return jnp.concatenate([wide] * (size // 16), axis=0)


def matches(index_row, size):
    places, _ = rows_and_columns((size, index_row.shape[1]))
    return places.astype(F32).astype(BF16) == packed_rows(index_row, size)


def one_hot(index_row, size):
    return jnp.where(matches(index_row, size), jnp.ones((), BF16), jnp.zeros((), BF16))


def spline_weights(fraction):
    remain = 1.0 - fraction
    square = fraction * fraction
    cubed = square * fraction
    return (
        remain * remain * remain / 6.0,
        (3.0 * cubed - 6.0 * square + 4.0) / 6.0,
        (-3.0 * cubed + 3.0 * square + 3.0 * fraction + 1.0) / 6.0,
        cubed / 6.0,
    )


def weight_columns(weights, fine_row, tile, places):
    behind = places - fine_row
    result = jnp.zeros(behind.shape, F32)
    for offset in range(4):
        result = jnp.where(behind == offset, weights[offset][tile : tile + 1], result)
    return result


def near_and_past(weights, fine, tile):
    width = fine.shape[1]
    fine_row = fine[tile : tile + 1]
    near, _ = rows_and_columns((FINE, width))
    past, _ = rows_and_columns((PAST_ROWS, width))
    past = FINE + (past & 3)
    return weight_columns(weights, fine_row, tile, near), weight_columns(weights, fine_row, tile, past)


def past_terms(terms, here):
    rows, _ = rows_and_columns((PAST_ROWS, terms[0].shape[1]))
    result = jnp.broadcast_to(terms[3][here], rows.shape)
    for comp in range(2, -1, -1):
        result = jnp.where(rows < 4 * (comp + 1), terms[comp][here], result)
    return result


def product(left, right, contract):
    return lax.dot_general(left, right, (contract, ((), ())), preferred_element_type=F32)


def live_mask(live_ref, first, shape):
    rows, _ = rows_and_columns(shape)
    return (rows + first < live_ref[0]).astype(F32)


def store_rows(out_ref, begin, rows):
    size = (out_ref.shape[1] - 8) // 2
    for offset in range(0, rows.shape[0], 8):
        block, place = divmod(begin + offset, size)
        out_ref[block, place : place + 8, :] = rows[offset : offset + 8, :128]
        out_ref[block, size + place : size + place + 8, :] = rows[offset : offset + 8, 128:]


def knot_factors(first, size, knot_ref, frac_ref):
    rows = pl.ds(first, size)
    knot = knot_ref[rows, :]
    coarse, fine = knot >> 5, knot & (FINE - 1)
    weights = spline_weights(frac_ref[rows, :])
    hot = [one_hot(coarse[tile : tile + 1], COARSE) for tile in range(size)]
    columns = [near_and_past(weights, fine, tile) for tile in range(size)]
    return jnp.concatenate(hot, axis=1), columns


def scatter(first, factors, values, observed, knot_acc, star_acc):
    att_coef_ref, star_ref, star_coef_ref = observed
    knot_hot, columns = factors
    rows = pl.ds(first, len(columns))
    star = star_ref[rows, :]
    star_coarse, star_fine = star & (COARSE - 1), star >> 8
    terms = [att_coef_ref[comp, rows, :] * values for comp in range(4)]
    parts = [two_parts(star_coef_ref[comp, rows, :] * values) for comp in range(5)]
    parts = [pair[half].astype(F32) for half in range(2) for pair in parts]
    knot_left, star_left, star_right = [], [], []
    for tile in range(len(columns)):
        here = slice(tile, tile + 1)
        near, past = columns[tile]
        spread = jnp.concatenate(
            [term[here] * near for term in terms] + [past_terms(terms, here) * past], axis=0
        )
        knot_left.append(jnp.concatenate(two_parts(spread), axis=0))
        star_right.append(one_hot(star_coarse[here], COARSE))
        chosen = matches(star_fine[here], FINE)
        star_left.append(
            jnp.concatenate(
                [jnp.where(chosen, packed_rows(part[here], FINE), jnp.zeros((), BF16)) for part in parts],
                axis=0,
            )
        )
    knot_acc[...] += product(
        jnp.concatenate(knot_left, axis=1), knot_hot, ((1,), (1,))
    )
    star_acc[...] += product(
        jnp.concatenate(star_left, axis=1), jnp.concatenate(star_right, axis=1), ((1,), (1,))
    )


def scatter_calibration(values, tile_cal_ref, table_out):
    blocks = product(
        one_hot(tile_cal_ref[...], CALB_DEV), jnp.concatenate(two_parts(values), axis=1), ((1,), (0,))
    )
    width = values.shape[1]
    blocks = blocks[:, :width] + blocks[:, width:]
    blocks = jnp.concatenate([blocks[: CALB_DEV // 2], blocks[CALB_DEV // 2 :]], axis=1)
    store_rows(table_out, KNOT_ROWS, blocks)


def scatter_end(place_ref, scalars, knot_acc, star_acc, table_out, star_out):
    lane = lax.broadcasted_iota(jnp.int32, (8, 128), 1)
    row = lax.broadcasted_iota(jnp.int32, (8, 128), 0)
    wide_lane = lax.broadcasted_iota(jnp.int32, (8, COARSE), 1)
    wide_row = lax.broadcasted_iota(jnp.int32, (8, COARSE), 0)
    edges = jnp.zeros((8, 128), F32)
    for comp in range(4):
        begin, past = comp * FINE, KNOT_ROWS + comp // 2 * 8
        main = knot_acc[begin : begin + FINE] + knot_acc[KNOT_HALF + begin : KNOT_HALF + begin + FINE]
        beyond = knot_acc[past : past + 8] + knot_acc[KNOT_HALF + past : KNOT_HALF + past + 8]
        if comp % 2:
            beyond = pltpu.roll(beyond, 4, 0)
        moved = pltpu.roll(jnp.where(wide_row < 3, beyond, 0.0), 1, 1)
        top = main[:8] + jnp.where(wide_lane > 0, moved, 0.0)
        store_rows(table_out, begin, top)
        store_rows(table_out, begin + 8, main[8:])
        tail, head = moved[:, :128], top[:, :128]
        if comp:
            tail = pltpu.roll(tail, 2 * comp, 1)
        head = pltpu.roll(head, 2 * comp + 1, 1)
        edges = jnp.where((lane == 2 * comp) & (row < 3), tail, edges)
        edges = jnp.where((lane == 2 * comp + 1) & (row < 3), head, edges)
    edges = with_scalars(pltpu.roll(edges, SLOT * place_ref[0], 1), scalars)
    for device in range(table_out.shape[0]):
        table_out[device, -8:, :] = edges
    star_out[...] = star_acc[:STAR_ROWS] + star_acc[STAR_ROWS:]


def first_kernel(live_ref, place_ref, *refs):
    sources, (table_out, star_out, knot_acc, star_acc) = refs[:8], refs[8:12]
    buffers, sems = refs[12:20], refs[20]
    half = sources[0].shape[0] // 2
    copies = []

    def begin(source, target, *place):
        source, target = (source.at[place], target.at[place]) if place else (source, target)
        copies.append(pltpu.make_async_copy(source, target, sems.at[len(copies)]))
        copies[-1].start()

    for source, target in zip(sources[:3], buffers):
        begin(source, target)
    for rows in (slice(0, half), slice(half, 2 * half)):
        for source, target in zip(sources[3:], buffers[3:]):
            begin(source, target, *[slice(None)] * (len(source.shape) - 2), rows)
    value_ref, cal_coef_ref, tile_cal_ref, knot_ref, frac_ref, *observed = buffers
    knot_acc[...] = jnp.zeros_like(knot_acc)
    star_acc[...] = jnp.zeros_like(star_acc)
    for copy in copies[:3]:
        copy.wait()
    values = value_ref[...] * live_mask(live_ref, 0, value_ref.shape)
    scatter_calibration(values * cal_coef_ref[...], tile_cal_ref, table_out)
    for copy in copies[3:8]:
        copy.wait()

    @pl.loop(0, value_ref.shape[0] // WIDE_GROUP)
    def _(group):
        @pl.when(group * WIDE_GROUP == half)
        def _():
            for copy in copies[8:]:
                copy.wait()

        first = pl.multiple_of(group * WIDE_GROUP, WIDE_GROUP)
        values = value_ref[pl.ds(first, WIDE_GROUP), :]
        values = values * live_mask(live_ref, first, values.shape)
        scatter(first, knot_factors(first, WIDE_GROUP, knot_ref, frac_ref), values, observed, knot_acc, star_acc)

    scatter_end(place_ref, [], knot_acc, star_acc, table_out, star_out)


def sum_kernel(block_ref, own_ref, other_ref, out_ref, star_out, edge_out):
    total = block_ref[0]
    for device in range(1, block_ref.shape[0]):
        total = total + block_ref[device]
    star_out[...] = own_ref[...] + other_ref[...]
    for device in range(block_ref.shape[0]):
        out_ref[device] = total[:-8]
    edge_out[...] = total[-8:]


def picked(array, which):
    row = lax.broadcasted_iota(jnp.int32, array.shape, 0)
    lane = lax.broadcasted_iota(jnp.int32, array.shape, 1)
    chosen = (row == 0) & (lane == SCALAR_LANE + which)
    return jnp.sum(jnp.where(chosen, array, 0.0), keepdims=True)


def with_scalars(array, scalars):
    row = lax.broadcasted_iota(jnp.int32, array.shape, 0)
    lane = lax.broadcasted_iota(jnp.int32, array.shape, 1)
    for which, value in scalars:
        array = jnp.where((row == 0) & (lane == SCALAR_LANE + which), value, array)
    return array


def first_step(edges):
    return picked(edges, 0), picked(edges, 1)


def star_forward_kernel(star_ref, star_coef_ref, star_x_ref, image_ref, star_parts_ref):
    star_x = star_x_ref[...]
    star_high, star_low = two_parts(star_x)
    star_parts_ref[:STAR_ROWS] = star_high
    star_parts_ref[STAR_ROWS:] = star_low

    @pl.loop(0, star_ref.shape[0] // GROUP)
    def _(group):
        rows = pl.ds(pl.multiple_of(group * GROUP, GROUP), GROUP)
        star = star_ref[rows, :]
        coarse, fine = star & (COARSE - 1), star >> 8
        coef = [star_coef_ref[comp, rows, :] for comp in range(5)]
        tiles = [slice(tile, tile + 1) for tile in range(GROUP)]
        hot = jnp.concatenate([one_hot(coarse[here], COARSE) for here in tiles], axis=1)
        found = product(star_parts_ref[...], hot, ((1,), (0,)))
        width = star.shape[1]
        fine_rows, _ = rows_and_columns((FINE, width))
        image_rows = []
        for tile, here in enumerate(tiles):
            across = slice(tile * width, (tile + 1) * width)

            def part(comp):
                begin = comp * FINE
                return (
                    found[begin : begin + FINE, across]
                    + found[STAR_ROWS + begin : STAR_ROWS + begin + FINE, across]
                )

            both = sum(coef[comp][here] * part(comp) for comp in range(5))
            both = jnp.where(fine_rows == fine[here], both, 0.0)
            both = both[:8] + both[8:16] + both[16:24] + both[24:]
            image_rows.append(jnp.sum(both, axis=0, keepdims=True))
        image_ref[rows, :] = jnp.concatenate(image_rows, axis=0)


def received_table(n_stars, n_seg, place_ref, block_ref, edges):
    segment = place_ref[0]
    lane = lax.broadcasted_iota(jnp.int32, (8, 128), 1)
    row = lax.broadcasted_iota(jnp.int32, (8, 128), 0)

    def slot(which):
        return pltpu.roll(edges, (128 - SLOT * jnp.clip(which, 0, n_seg - 1)) & 127, 1)

    before, own, after = slot(segment - 1), slot(segment), slot(segment + 1)
    before = jnp.where(segment > 0, before, 0.0)
    ahead = jnp.where(lane % 2 == 0, own, 0.0) + pltpu.roll(jnp.where(lane % 2 == 1, after, 0.0), 127, 1)
    ahead = jnp.where((segment < n_seg - 1) & (lane < 8) & (row < 3), ahead, 0.0)

    size = TABLE_ROWS // n_stars
    table = jnp.concatenate([block_ref[:, :size, :], block_ref[:, size : 2 * size, :]], axis=2)
    table = table.reshape(TABLE_ROWS, COARSE)
    pieces = []
    for comp in range(4):
        shifted = pltpu.roll(before, 128 - 2 * comp, 1) if comp else before
        shifted = jnp.where((lane == 0) & (row < 3), shifted, 0.0)
        top = table[comp * FINE : comp * FINE + 8]
        pieces.append(top + jnp.concatenate([shifted, jnp.zeros_like(shifted)], axis=1))
        pieces.append(table[comp * FINE + 8 : (comp + 1) * FINE])
    return jnp.concatenate(pieces + [table[KNOT_ROWS:]], axis=0), ahead


def gather_ready(table, ahead, cal_coef_ref, tile_cal_ref, star_image_ref, knot_parts_ref, cal_ref):
    wide_lane = lax.broadcasted_iota(jnp.int32, (8, COARSE), 1)
    row = lax.broadcasted_iota(jnp.int32, (8, COARSE), 0)
    beyond = []
    for comp in range(4):
        moved = pltpu.roll(table[comp * FINE : comp * FINE + 8], COARSE - 1, 1)
        last = pltpu.roll(ahead, 127 - 2 * comp, 1)
        moved = jnp.where(wide_lane == COARSE - 1, jnp.concatenate([last, last], axis=1), moved)
        beyond.append(pltpu.roll(moved, 4, 0) if comp % 2 else moved)
    beyond = [jnp.where(row < 4, beyond[0], beyond[1]), jnp.where(row < 4, beyond[2], beyond[3])]
    knot_high, knot_low = two_parts(jnp.concatenate([table[:KNOT_ROWS]] + beyond, axis=0))
    knot_parts_ref[:KNOT_HALF] = knot_high
    knot_parts_ref[KNOT_HALF:] = knot_low

    blocks = jnp.concatenate([table[KNOT_ROWS:, :128], table[KNOT_ROWS:, 128:]], axis=0)
    rows = product(
        one_hot(tile_cal_ref[...], CALB_DEV), jnp.concatenate(two_parts(blocks), axis=1), ((0,), (0,))
    )
    cal_ref[...] = (rows[:, :128] + rows[:, 128:]) * cal_coef_ref[...] + star_image_ref[...]


def gather(first, live_ref, factors, att_coef_ref, knot_parts_ref, cal_ref):
    hot, columns = factors
    rows = pl.ds(first, len(columns))
    coef = [att_coef_ref[comp, rows, :] for comp in range(4)]
    found = product(knot_parts_ref[...], hot, ((1,), (0,)))
    width = cal_ref.shape[1]
    image_rows = []
    for tile in range(len(columns)):
        here = slice(tile, tile + 1)
        across = slice(tile * width, (tile + 1) * width)

        def part(begin, size):
            return (
                found[begin : begin + size, across]
                + found[KNOT_HALF + begin : KNOT_HALF + begin + size, across]
            )

        near, past = columns[tile]
        near = near * sum(coef[comp][here] * part(comp * FINE, FINE) for comp in range(4))
        past = past * past_terms(coef, here) * part(KNOT_ROWS, PAST_ROWS)
        both = near[:8] + near[8:16] + near[16:24] + near[24:] + past[:8] + past[8:]
        image_rows.append(jnp.sum(both, axis=0, keepdims=True))
    image = jnp.concatenate(image_rows, axis=0) + cal_ref[rows, :]
    return image * live_mask(live_ref, first, image.shape)


def squares(array):
    return jnp.sum(array * array, keepdims=True)


def middle_kernel(
    n_stars, n_seg, live_ref, place_ref, knot_ref, frac_ref, att_coef_ref, star_ref, star_coef_ref,
    cal_coef_ref, tile_cal_ref, star_image_ref, star_x_ref, block_ref, edge_ref, other_edge_ref, image_ref, table_out, scatter_out,
    star_out, knot_parts_ref, cal_ref, knot_acc, star_acc,
):
    edges = edge_ref[...] + other_edge_ref[...]
    table, ahead = received_table(n_stars, n_seg, place_ref, block_ref, edges)
    table_out[...] = table
    norm = squares(star_x_ref[...]) / n_seg + squares(table) / n_stars
    gather_ready(table, ahead, cal_coef_ref, tile_cal_ref, star_image_ref, knot_parts_ref, cal_ref)
    knot_acc[...] = jnp.zeros_like(knot_acc)
    star_acc[...] = jnp.zeros_like(star_acc)
    factors = knot_factors(0, knot_ref.shape[0], knot_ref, frac_ref)
    image = gather(0, live_ref, factors, att_coef_ref, knot_parts_ref, cal_ref)
    image_ref[...] = image
    scatter(0, factors, image, (att_coef_ref, star_ref, star_coef_ref), knot_acc, star_acc)
    scatter_calibration(image * cal_coef_ref[...], tile_cal_ref, scatter_out)
    scalars = [(0, norm), (1, squares(image))]
    scatter_end(place_ref, scalars, knot_acc, star_acc, scatter_out, star_out)


def last_kernel(
    n_stars, n_seg, live_ref, place_ref, knot_ref, frac_ref, att_coef_ref, cal_coef_ref, tile_cal_ref,
    star_image_ref, star_x_ref, block_ref, edge_ref, other_edge_ref, star_0_ref, table_0_ref, image_0_ref, image_ref, table_out,
    scalar_out, own_scalar_out, knot_parts_ref, cal_ref,
):
    edges = edge_ref[...] + other_edge_ref[...]
    table, ahead = received_table(n_stars, n_seg, place_ref, block_ref, edges)
    table_out[...] = table
    norm_0, square_0 = first_step(edges)
    step = norm_0 / square_0
    norm = (
        squares(star_0_ref[...] - step * star_x_ref[...]) / n_seg
        + squares(table_0_ref[...] - step * table) / n_stars
    )
    gather_ready(table, ahead, cal_coef_ref, tile_cal_ref, star_image_ref, knot_parts_ref, cal_ref)

    factors = knot_factors(0, knot_ref.shape[0], knot_ref, frac_ref)
    image_0 = image_0_ref[...]
    image = gather(0, live_ref, factors, att_coef_ref, knot_parts_ref, cal_ref)
    image = image_0 - step * image
    image_ref[...] = image
    cross = jnp.sum(image * image_0, keepdims=True)
    scalars = [norm, squares(image), cross, norm_0, square_0]
    scalars = with_scalars(jnp.zeros((8, 128), F32), list(enumerate(scalars)))
    own_scalar_out[...] = scalars
    for device in range(scalar_out.shape[0]):
        scalar_out[device] = scalars[:1]


def output_kernel(
    live_ref, own_scalar_ref, scalar_ref, star_0_ref, star_h_ref, att_0_ref, att_h_ref, table_0_ref,
    table_h_ref, value_ref, image_0_ref, image_1_ref, star_out, att_out, cal_out, residual_out,
):
    norm_0, square_0 = [picked(own_scalar_ref[...], which) for which in (3, 4)]
    everyone = scalar_ref[0]
    for device in range(1, scalar_ref.shape[0]):
        everyone = everyone + scalar_ref[device]
    norm_1, square_1, cross = [picked(everyone, which) for which in range(3)]
    step_0 = norm_0 / square_0
    ratio = norm_1 / norm_0
    step_1 = norm_1 / (square_1 + 2.0 * ratio * cross + ratio * ratio * square_0)
    scale = step_0 + step_1 * ratio

    def combined(old, change):
        return scale * old + step_1 * (old - step_0 * change)

    star_out[...] = combined(star_0_ref[...], star_h_ref[...])
    att_out[...] = combined(att_0_ref[...], att_h_ref[...])
    cal = combined(table_0_ref[KNOT_ROWS:, :], table_h_ref[KNOT_ROWS:, :])
    cal_out[...] = jnp.concatenate([cal[:, :128], cal[:, 128:]], axis=0)
    values = value_ref[...] * live_mask(live_ref, 0, value_ref.shape)
    residual_out[...] = values - scale * image_0_ref[...] - step_1 * image_1_ref[...]


def in_vmem(count):
    return [pl.BlockSpec(memory_space=pltpu.VMEM)] * count


def in_smem(count):
    return [pl.BlockSpec(memory_space=pltpu.SMEM)] * count


def in_hbm(count):
    return [pl.BlockSpec(memory_space=pltpu.HBM)] * count


def shaped(*shape):
    return jax.ShapeDtypeStruct(shape, F32)


ARRIVE_PARAMS = pltpu.CompilerParams(vmem_limit_bytes=60 * 1024 * 1024)
PARAMS = pltpu.CompilerParams(vmem_limit_bytes=40 * 1024 * 1024)
PASS_COST = pl.CostEstimate(flops=3_000_000_000, bytes_accessed=1_000_000, transcendentals=0)
SMALL_COST = pl.CostEstimate(flops=1_000_000, bytes_accessed=600_000, transcendentals=0)


def on_device(
    obs_star, obs_knot, obs_frac, star_coef, att_coef, cal_coef, tile_cal, live_tiles, obs_value
):
    n_stars, n_seg = lax.axis_size("stars"), lax.axis_size("seg")
    tile_count, width = obs_star.shape
    tile_row = tile_cal[None, :]
    place = lax.axis_index("seg").astype(jnp.int32)[None]
    image_shape = shaped(tile_count, width)
    table_shape = shaped(TABLE_ROWS, COARSE)
    star_shape = shaped(STAR_ROWS, COARSE)
    sent_shapes = (shaped(n_stars, 2 * TABLE_ROWS // n_stars + 8, 128), star_shape)
    sums = [pltpu.VMEM((2 * KNOT_HALF, COARSE), F32), pltpu.VMEM((2 * STAR_ROWS, COARSE), F32)]
    ready = [pltpu.VMEM((2 * KNOT_HALF, COARSE), BF16), pltpu.VMEM((tile_count, width), F32)]

    def first_scatter():
        observed = (obs_value, cal_coef, tile_row, obs_knot, obs_frac, att_coef, obs_star, star_coef)
        buffers = [pltpu.VMEM(array.shape, array.dtype) for array in observed]
        return pl.pallas_call(
            first_kernel,
            out_shape=sent_shapes,
            in_specs=in_smem(2) + in_hbm(len(observed)),
            out_specs=tuple(in_vmem(2)),
            scratch_shapes=sums + buffers + [pltpu.SemaphoreType.DMA((13,))],
            compiler_params=ARRIVE_PARAMS,
            cost_estimate=PASS_COST,
            name="first_scatter",
        )(live_tiles, place, *observed)

    def middle(*received):
        observed = (obs_knot, obs_frac, att_coef, obs_star, star_coef, cal_coef, tile_row)
        return pl.pallas_call(
            functools.partial(middle_kernel, n_stars, n_seg),
            out_shape=(image_shape, table_shape, *sent_shapes),
            in_specs=in_smem(2) + in_vmem(len(observed) + len(received)),
            out_specs=tuple(in_vmem(4)),
            scratch_shapes=ready + sums,
            compiler_params=PARAMS,
            cost_estimate=PASS_COST,
            name="gather_and_scatter",
        )(live_tiles, place, *observed, *received)

    def last_gather(*received):
        observed = (obs_knot, obs_frac, att_coef, cal_coef, tile_row)
        return pl.pallas_call(
            functools.partial(last_kernel, n_stars, n_seg),
            out_shape=(image_shape, table_shape, shaped(n_stars * n_seg, 1, 128), shaped(8, 128)),
            in_specs=in_smem(2) + in_vmem(len(observed) + len(received)),
            out_specs=tuple(in_vmem(4)),
            scratch_shapes=ready,
            compiler_params=PARAMS,
            cost_estimate=PASS_COST,
            name="last_gather",
        )(live_tiles, place, *observed, *received)

    def star_forward(star):
        return pl.pallas_call(
            star_forward_kernel,
            out_shape=image_shape,
            in_specs=in_vmem(3),
            out_specs=in_vmem(1)[0],
            scratch_shapes=[pltpu.VMEM((2 * STAR_ROWS, COARSE), BF16)],
            compiler_params=PARAMS,
            cost_estimate=PASS_COST,
            name="star_forward",
        )(obs_star, star_coef, star)

    def swap(blocks, groups=None):
        return lax.all_to_all(blocks, ("stars", "seg"), 0, 0, axis_index_groups=groups)

    def star_groups():
        forward = list(range(n_stars))
        turned = forward[n_stars // 2 :] + forward[: n_stars // 2]
        orders = (forward, forward[::-1], turned, turned[::-1])
        return [[star * n_seg + seg for star in orders[seg % 4]] for seg in range(n_seg)]

    def partner(array, axis, distance):
        return lax.ppermute(array, axis, [(i, i ^ distance) for i in range(lax.axis_size(axis))])

    def reduced(table, star):
        distances = [1 << bit for bit in range(n_seg.bit_length() - 1)]
        for distance in distances[:-1]:
            star = star + partner(star, "seg", distance)
        blocks, star, edge = pl.pallas_call(
            sum_kernel,
            out_shape=(shaped(n_stars, 2 * TABLE_ROWS // n_stars, 128), star_shape, shaped(8, 128)),
            in_specs=in_vmem(3),
            out_specs=tuple(in_vmem(3)),
            compiler_params=PARAMS,
            cost_estimate=SMALL_COST,
            name="table_sum",
        )(swap(table, star_groups()), star, partner(star, "seg", distances[-1]))
        for distance in distances[:-1]:
            edge = edge + partner(edge, "seg", distance)
        gathered = swap(blocks, star_groups())
        return star_forward(star), star, gathered, edge, partner(edge, "seg", distances[-1])

    first = reduced(*first_scatter())
    star_0 = first[1]
    image_0, table_0, *sent = middle(*first)
    second = reduced(*sent)
    star_h = second[1]
    image_1, table_h, scalars, own_scalars = last_gather(*second, star_0, table_0, image_0)

    def star_order(star):
        return star.reshape(5, STAR_DEV)

    def att_order(table):
        att = table[:KNOT_ROWS].reshape(4, FINE, COARSE)
        return att.transpose(0, 2, 1).reshape(4, KNOT_DEV)

    return pl.pallas_call(
        output_kernel,
        out_shape=(shaped(5, STAR_DEV), shaped(4, KNOT_DEV), shaped(CALB_DEV, width), image_shape),
        in_specs=in_smem(1) + in_vmem(11),
        out_specs=tuple(in_vmem(4)),
        compiler_params=PARAMS,
        cost_estimate=SMALL_COST,
        name="outputs",
    )(
        live_tiles, own_scalars, swap(scalars), star_order(star_0), star_order(star_h),
        att_order(table_0), att_order(table_h), table_0, table_h, obs_value, image_0, image_1,
    )


def solution(mesh):
    placed = (
        P(("stars", "seg"), None),
        P(("stars", "seg"), None),
        P(("stars", "seg"), None),
        P(None, ("stars", "seg"), None),
        P(None, ("stars", "seg"), None),
        P(("stars", "seg"), None),
        P(("stars", "seg")),
        P(("stars", "seg")),
        P(("stars", "seg"), None),
    )
    return jax.shard_map(
        on_device,
        mesh=mesh,
        in_specs=placed,
        out_specs=(P(None, "stars"), P(None, "seg"), P("seg", None), P(("stars", "seg"), None)),
        check_vma=False,
    )
```
